32 devices in a mesh: group: 4 (over z), sub: 8 (over y, x, core).
Axes of the slice: x: 2, y: 2, z: 4, core: 2. Of those that a mesh axis runs over, the one named last changes fastest.
Arguments:
- points: float32 [3, 65536], P(None, ('group', 'sub')), may hold values from 0 to 1
- leaf_basis: bfloat16 [65536, 64], P(('group', 'sub')), as said below
- inner_transfer: bfloat16 [61440, 64], P(('group', 'sub')), as said below
- device_transfer: float32 [2048, 64], P(('group', 'sub')), as said below
- vectors: bfloat16 [65536, 384], P(('group', 'sub')), may hold values from -0.75 to 0.75
- near_index: int32 [1024, 12], P(('group', 'sub')), may hold values from 0 to 1023, as said below
- near_count: int32 [1024], P(('group', 'sub')), may hold values from 6 to 12, as said below
- far_index: int32 [1024, 3], P(('group', 'sub')), may hold values from 0 to 1023, as said below
Outputs:
- near_product: bfloat16 [65536, 384], P(('group', 'sub'))
- coupling: bfloat16 [196608, 64], P(('group', 'sub'))
- device_factor: float32 [2048, 64], P(('group', 'sub'))
- group_factor: float32 [2048, 64], P(('group', 'sub'))
- root_factor: float32 [2048, 64], P(('group', 'sub'))
The draws below stay inside these ranges and needn't reach their ends.
Inputs may be any that keep to these rules, and one draw needn't show every extreme that they name: Slot 0 of near_index[t] is t; the first near_count[t] slots name distinct leaves of layers t // 4 - 1 to t // 4 + 1, all within 7 of t; the remaining slots hold t. far_index[t] names 3 distinct leaves of the window of 15 consecutive leaves centred on t (moved to lie inside 0 to 1023) whose layers differ from t's by two or more. near_count[t] is at most the number of leaves in layers t // 4 - 1 to t // 4 + 1. `inner_transfer`: each K x K block is the identity plus a full matrix, nonsingular. `device_transfer`: each K x K block is nonsingular. `leaf_basis`: each leaf's block has full column rank.
All inputs are finite; a program needn't handle non-finite values.
Results may differ from the reference program's by a relative error of at most 0.005.
Values may be sent and summed in bfloat16 or wider, within the bound.
No kernel may reach another device: no remote copies, remote signals or barrier semaphores. Data moves between devices by JAX's collectives and lax.ppermute only.
A program may use at most 64 MiB of HBM per device.

```python
import jax
import jax.numpy as jnp
from jax import lax

K = 64
P_SIZE = 64
LEAF_DEV = 32
NVEC = 384
LAYER = 4
RAD = 7
NEAR = 12
FAR = 3
NLEAF = 1024
N_GROUP = 4
N_SUB = 8


MIX_WEIGHT = 0.85


def near_lists(key):
    window = 2 * RAD + 1
    key_order, key_count, key_place, key_far = jax.random.split(jax.random.fold_in(key, 7), 4)
    leaf_ids = jnp.arange(NLEAF, dtype=jnp.int32)
    lowest = jnp.clip(leaf_ids - RAD, 0, NLEAF - window)
    columns = jnp.arange(window, dtype=jnp.int32)
    candidates = (lowest[:, None] + columns[None, :]).astype(jnp.int32)
    layer_gap = jnp.abs(candidates // LAYER - leaf_ids[:, None] // LAYER)
    adjacent = layer_gap <= 1
    is_self = candidates == leaf_ids[:, None]
    large_score = (1 << 16) * window + window
    near_scores = jax.random.randint(key_order, (NLEAF, window), 0, 1 << 16, dtype=jnp.int32) * window + columns[None, :]
    near_scores = jnp.where(adjacent, near_scores, large_score + columns[None, :])
    near_scores = jnp.where(is_self, -1, near_scores)
    near_order = jnp.argsort(near_scores, axis=1).astype(jnp.int32)
    near_listed = jnp.take_along_axis(candidates, near_order, axis=1)
    far_scores = jax.random.randint(key_far, (NLEAF, window), 0, 1 << 16, dtype=jnp.int32) * window + columns[None, :]
    far_scores = jnp.where(adjacent, large_score + columns[None, :], far_scores)
    far_order = jnp.argsort(far_scores, axis=1).astype(jnp.int32)
    far_listed = jnp.take_along_axis(candidates, far_order[:, :FAR], axis=1).astype(jnp.int32)
    adjacent_count = jnp.sum(adjacent.astype(jnp.int32), axis=1)
    counts = jax.random.randint(key_count, (NLEAF,), NEAR // 2, NEAR + 1, dtype=jnp.int32)
    chosen = jax.random.randint(key_place, (), LAYER, NLEAF - LAYER, dtype=jnp.int32)
    counts = jnp.where(leaf_ids == chosen, NEAR, counts)
    counts = jnp.minimum(counts, adjacent_count).astype(jnp.int32)
    slots = jnp.arange(NEAR, dtype=jnp.int32)
    near = jnp.where(slots[None, :] < counts[:, None], near_listed[:, :NEAR], leaf_ids[:, None]).astype(jnp.int32)
    return (near, counts, far_listed)


def draw_near_index(key, part):
    return near_lists(key)[0]


def draw_near_count(key, part):
    return near_lists(key)[1]


def draw_far_index(key, part):
    return near_lists(key)[2]


def noise_block(key, shape, fan_in, spread):
    values = jax.random.normal(key, shape, jnp.float32)
    return values * (spread / fan_in ** 0.5)


def column_mixing(values):
    return values + MIX_WEIGHT * jnp.roll(values, 1, axis=1)


def draw_leaf_basis(key, part):
    row_ids = jnp.arange(NLEAF * P_SIZE, dtype=jnp.int32)
    col_ids = jnp.arange(K, dtype=jnp.int32)
    identity = ((row_ids % P_SIZE)[:, None] == col_ids[None, :]).astype(jnp.float32)
    values = 1.5 * identity + noise_block(key, (NLEAF * P_SIZE, K), P_SIZE, 0.5)
    return column_mixing(values).astype(jnp.bfloat16)


def draw_inner_transfer(key, part):
    total_rows = N_GROUP * N_SUB * (LEAF_DEV - 2) * K
    row_ids = jnp.arange(total_rows, dtype=jnp.int32)
    col_ids = jnp.arange(K, dtype=jnp.int32)
    identity = ((row_ids % K)[:, None] == col_ids[None, :]).astype(jnp.float32)
    values = identity + noise_block(key, (total_rows, K), K, 0.35)
    return values.astype(jnp.bfloat16)


def draw_device_transfer(key, part):
    devices = N_GROUP * N_SUB
    key_noise = jax.random.fold_in(key, 0)
    row_ids = jnp.arange(devices * K, dtype=jnp.int32)
    col_ids = jnp.arange(K, dtype=jnp.int32)
    identity = ((row_ids % K)[:, None] == col_ids[None, :]).astype(jnp.float32)
    device_ids = (row_ids // K).astype(jnp.float32)
    rising = jnp.sqrt(1.0 + 2.0 * device_ids / (devices - 1))
    values = (identity + noise_block(key_noise, (devices * K, K), K, 0.35)) * rising[:, None]
    return column_mixing(values).astype(jnp.float32)


def level_of(key, extent, cuts, low, largest):
    loudness = 1.0
    for axis_at, shards_of in cuts:
        heights = jax.random.uniform(jax.random.fold_in(jax.random.fold_in(key, 6), axis_at), (shards_of,), jnp.float32, low / len(cuts), largest / len(cuts))
        loudness = loudness * jnp.repeat(jnp.exp(heights), extent[axis_at] // shards_of).reshape((-1,) + (1,) * (len(extent) - 1 - axis_at))
    return loudness


def noise(key, dims, scale, reach, cuts=(), kind=jnp.bfloat16):
    factor_of = level_of(key, dims, cuts, -0.22, 0.18) if cuts else 1.0
    values = jax.random.normal(key, dims, jnp.float32) * scale * factor_of
    return jnp.minimum(jnp.maximum(values, -reach), reach).astype(kind)


def setup_inputs(seed: int = 0) -> dict:
    arg_keys = jax.random.split(jax.random.key(seed), 9)
    points = jnp.clip(1.0 * jax.random.uniform(arg_keys[0], (3, NLEAF * P_SIZE), jnp.float32) ** level_of(arg_keys[0], (3, NLEAF * P_SIZE), ((1, 32),), -0.2, 0.2), 0.0, 1.0)
    leaf_basis = draw_leaf_basis(jax.random.fold_in(arg_keys[8], 71), 0)
    inner_transfer = draw_inner_transfer(jax.random.fold_in(arg_keys[8], 71), 0)
    device_transfer = draw_device_transfer(jax.random.fold_in(arg_keys[8], 71), 0)
    vectors = noise(arg_keys[4], (NLEAF * P_SIZE, NVEC), 0.125, 0.75, ((0, 32),))
    near_index = draw_near_index(jax.random.fold_in(arg_keys[8], 71), 0)
    near_count = draw_near_count(jax.random.fold_in(arg_keys[8], 71), 0)
    far_index = draw_far_index(jax.random.fold_in(arg_keys[8], 71), 0)
    return dict(points=points, leaf_basis=leaf_basis, inner_transfer=inner_transfer, device_transfer=device_transfer, vectors=vectors, near_index=near_index, near_count=near_count, far_index=far_index)


SHORT_SQ = 0.09
LONG_SQ = 2.25
LONG_WEIGHT = 0.5

def gram_matrix(matrix):
    return jnp.einsum('...ik,...il->...kl', matrix, matrix, precision=lax.Precision.HIGHEST)

def upper_factor(gram):
    return jnp.swapaxes(jnp.linalg.cholesky(gram), -1, -2)

def product(left_side, right_side):
    return jnp.einsum('...ij,...jk->...ik', left_side, right_side, precision=lax.Precision.HIGHEST)

def local_tree(leaf_factor, inner_blocks):
    factor = leaf_factor
    node_count = leaf_factor.shape[-3]
    levels = node_count.bit_length() - 1
    offset = 0
    for level in range(levels):
        merged = (gram_matrix(factor[..., 0::2, :, :]) + gram_matrix(factor[..., 1::2, :, :])) * 0.5
        factor = upper_factor(merged)
        node_count = node_count // 2
        if level + 1 < levels:
            factor = product(factor, inner_blocks[..., offset:offset + node_count, :, :])
            offset = offset + node_count
    return factor[..., 0, :, :]

def cell_offset(target, source):
    across = target % 2 - source % 2
    along = target // 2 % 2 - source // 2 % 2
    layer_gap = target // LAYER - source // LAYER
    return jnp.stack([across, along, layer_gap], axis=-1).astype(jnp.float32)

def leaf_kernel(first_pts, second_pts, offsets):
    differences = first_pts[..., :, :, None] - second_pts[..., :, None, :] + offsets[..., :, None, None]
    distance = jnp.sum(differences * differences, axis=-3)
    return jnp.exp(distance * (-0.5 / SHORT_SQ)) + LONG_WEIGHT * jnp.exp(distance * (-0.5 / LONG_SQ))

def reference(points, leaf_basis, inner_transfer, device_transfer, vectors, near_index, near_count, far_index):
    devices = N_GROUP * N_SUB
    basis_full = leaf_basis.astype(jnp.float32).reshape(NLEAF, P_SIZE, K)
    leaf_factor = upper_factor(gram_matrix(basis_full))
    inner_blocks = inner_transfer.astype(jnp.float32).reshape(devices, LEAF_DEV - 2, K, K)
    subtree_top = local_tree(leaf_factor.reshape(devices, LEAF_DEV, K, K), inner_blocks)
    device_factor = product(subtree_top, device_transfer.reshape(devices, K, K))
    grouped = device_factor.reshape(N_GROUP, N_SUB, K, K)
    group_factor = upper_factor(jnp.mean(gram_matrix(grouped), axis=1))
    root_factor = upper_factor(jnp.mean(gram_matrix(group_factor), axis=0))
    group_copies = jnp.repeat(group_factor, N_SUB, axis=0).reshape(devices * K, K)
    root_copies = jnp.broadcast_to(root_factor[None], (devices, K, K)).reshape(devices * K, K)
    coords = points.reshape(3, NLEAF, P_SIZE).transpose(1, 0, 2)
    blocks = vectors.reshape(NLEAF, P_SIZE, NVEC)

    def one_block(block_start):
        target = block_start + jnp.arange(LEAF_DEV, dtype=jnp.int32)
        near_rows = lax.dynamic_slice_in_dim(near_index, block_start, LEAF_DEV, 0)
        count_rows = lax.dynamic_slice_in_dim(near_count, block_start, LEAF_DEV, 0)
        far_rows = lax.dynamic_slice_in_dim(far_index, block_start, LEAF_DEV, 0)
        own_pts = jnp.take(coords, target, axis=0)
        running = jnp.zeros((LEAF_DEV, P_SIZE, NVEC), jnp.float32)
        for slot_index in range(NEAR):
            source = near_rows[:, slot_index]
            weights = leaf_kernel(own_pts, jnp.take(coords, source, axis=0), cell_offset(target, source))
            weights = jnp.where((slot_index < count_rows)[:, None, None], weights, 0.0).astype(jnp.bfloat16)
            gathered = jnp.take(blocks, source, axis=0)
            running = running + jnp.einsum('lij,ljv->liv', weights.astype(jnp.float32), gathered.astype(jnp.float32), precision=lax.Precision.HIGHEST)
        own_factor = jnp.take(leaf_factor, target, axis=0)
        pieces = []
        for slot_index in range(FAR):
            source = far_rows[:, slot_index]
            kernel_block = leaf_kernel(own_pts, jnp.take(coords, source, axis=0), cell_offset(target, source))
            other_factor = jnp.take(leaf_factor, source, axis=0)
            projected = product(product(own_factor, kernel_block), jnp.swapaxes(other_factor, -1, -2)) / K
            pieces.append(projected)
        return (running.astype(jnp.bfloat16), jnp.stack(pieces, axis=1).astype(jnp.bfloat16))
    starts = jnp.arange(NLEAF // LEAF_DEV, dtype=jnp.int32) * LEAF_DEV
    near_out, coupling_out = lax.map(one_block, starts)
    near_product = near_out.reshape(NLEAF * P_SIZE, NVEC)
    coupling = coupling_out.reshape(NLEAF * FAR * K, K)
    return (near_product, coupling, device_factor.reshape(devices * K, K), group_copies, root_copies)
```

```python
import math

import jax
import jax.numpy as jnp
from jax import lax
from jax.experimental import pallas as pl
from jax.experimental.pallas import tpu as pltpu
from jax.sharding import PartitionSpec as P

LAYER = 4
PAD = 8
LONG_SQ = 2.25
RATIO = 25.0
SCALE = 0.5 / LONG_SQ / math.log(2.0)
OFF = -16384.0
AXES = ("group", "sub")
F32 = jnp.float32
BF16 = jnp.bfloat16
BIG = pltpu.CompilerParams(vmem_limit_bytes=56 * 1024 * 1024)


def split2(value):
    high = value.astype(BF16)
    return high, (value - high.astype(F32)).astype(BF16)


def split3(value):
    high = value.astype(BF16)
    rest = value - high.astype(F32)
    middle = rest.astype(BF16)
    return high, middle, (rest - middle.astype(F32)).astype(BF16)


def mm(left, right):
    return jnp.dot(left, right, preferred_element_type=F32)


def mm_nt(left, right):
    return lax.dot_general(left, right, (((1,), (1,)), ((), ())), preferred_element_type=F32)


def exact(left, right):
    return jnp.dot(left, right, precision=lax.Precision.HIGHEST, preferred_element_type=F32)


def iota(shape, dim):
    return lax.broadcasted_iota(jnp.int32, shape, dim)


def tree_kernel(basis, inner, transfer, points, vectors, hot, top, to_next, to_prev, sems):
    width = basis.shape[0]
    count = basis.shape[1] // width
    halo = LAYER * width
    rows = vectors.shape[0]
    copies = [
        pltpu.make_async_copy(
            vectors.at[pl.ds(start, halo), :], target.at[pl.ds(0, halo), :], sems.at[n]
        )
        for n, (start, target) in enumerate(((rows - halo, to_next), (0, to_prev)))
    ]
    for copy in copies:
        copy.start()

    for target, first, skip in ((to_next, count - PAD, 1), (to_prev, 0, 0)):
        block = basis[:, first * width : (first + PAD) * width]
        pieces = [
            block[:, (at + skip) * width : (at + skip + 3) * width] for at in (0, LAYER)
        ]
        target[halo : halo + width, :] = jnp.concatenate(pieces, axis=1)
        for n in range(2):
            start = (first + n * LAYER) * width
            coords = points[:, start : start + halo]
            high, low = split2(coords)
            base = halo + width + 16 * n
            target[base : base + 16, :] = jnp.zeros((16, target.shape[1]), BF16)
            target[base : base + 3, 0:halo] = high
            target[base + 8 : base + 11, 0:halo] = low

    both = 2 * width
    same = iota((both, both), 0) // width == iota((both, both), 1) // width
    half_block = jnp.where(same, 0.5, 0.0).astype(F32)

    def pair(index):
        return inner[:, index * both : (index + 1) * both]

    blocks = []
    for n in range(count // 4):
        stacked = jnp.concatenate(
            [basis[:, (2 * n + m) * both : (2 * n + m + 1) * both] for m in range(2)], axis=0
        )
        blocks.append(mm_nt(stacked, stacked) * half_block)
    offset = 0
    while True:
        nodes = len(blocks)
        xs, ts = [], []
        for n in range(nodes):
            t = pair(offset + n)
            parts = jnp.concatenate(split3(blocks[n]), axis=0)
            xs.append(mm(jnp.concatenate([t, t, t], axis=1), parts))
            ts.append(t)
        offset += nodes
        if nodes == 1:
            break
        blocks = []
        for n in range(nodes // 2):
            x = jnp.concatenate(split3(jnp.concatenate(xs[2 * n : 2 * n + 2], axis=0)), axis=1)
            t = jnp.concatenate(ts[2 * n : 2 * n + 2], axis=0)
            blocks.append(mm_nt(x, jnp.concatenate([t, t, t], axis=1)) * half_block)
    t = ts[0]
    x = jnp.concatenate(split3(xs[0]), axis=1)
    top_gram = mm_nt(x, jnp.concatenate([t, t, t], axis=1)) * 0.5
    top[...] = top_gram
    matrix = transfer[...]
    gram = exact(exact(matrix.T, top_gram), matrix)
    group = lax.axis_index("group")
    for g in range(hot.shape[0] // width):
        hot[g * width : (g + 1) * width, :] = jnp.where(group == g, gram, 0.0)
    for copy in copies:
        copy.wait()


def factor_lanes(work, width):
    panels = width // 8
    row = iota((8, 128), 0)

    def spread(value, k):
        return jnp.broadcast_to(value[k : k + 1, :], (8, 128))

    for p in range(panels):
        tiles = list(range(p, panels))
        for at in range(0, len(tiles), 3):
            group = tiles[at : at + 3]
            accs = [work[8 * p + k, 8 * i : 8 * i + 8, :] for i in group for k in range(8)]

            def step(j, accs, group=group, p=p):
                factors = [
                    jnp.broadcast_to(work[j, 8 * p + k : 8 * p + k + 1, :], (8, 128))
                    for k in range(8)
                ]
                out = []
                for n, i in enumerate(group):
                    column = work[j, 8 * i : 8 * i + 8, :]
                    out += [accs[8 * n + k] - column * factors[k] for k in range(8)]
                return out

            if p:
                accs = lax.fori_loop(0, 8 * p, step, accs, unroll=4)
                for n, i in enumerate(group):
                    for k in range(8):
                        work[8 * p + k, 8 * i : 8 * i + 8, :] = accs[8 * n + k]
        diag = [work[8 * p + k, 8 * p : 8 * p + 8, :] for k in range(8)]
        scales, mults = [], []
        for k in range(8):
            scale = lax.rsqrt(spread(diag[k], k))
            scales.append(scale)
            diag[k] = jnp.where(row >= k, diag[k] * scale, 0.0)
            mults.append([spread(diag[k], m) for m in range(k + 1, 8)])
            for m in range(k + 1, 8):
                diag[m] = diag[m] - diag[k] * mults[k][m - k - 1]
        for k in range(8):
            work[8 * p + k, 8 * p : 8 * p + 8, :] = diag[k]
            for i in range(p):
                work[8 * p + k, 8 * i : 8 * i + 8, :] = jnp.zeros((8, 128), F32)
        for i in range(p + 1, panels):
            tile = [work[8 * p + k, 8 * i : 8 * i + 8, :] for k in range(8)]
            for k in range(8):
                tile[k] = tile[k] * scales[k]
                for m in range(k + 1, 8):
                    tile[m] = tile[m] - tile[k] * mults[k][m - k - 1]
            for k in range(8):
                work[8 * p + k, 8 * i : 8 * i + 8, :] = tile[k]


def to_lanes(grams, work, width, many):
    for i in range(width):
        work[i, :, 0:many] = grams[pl.ds(i, many, stride=width), :].T


def from_lanes(work, factors, width, many):
    for j in range(width):
        column = work[j, :, 0:many]
        factors[pl.ds(j, many, stride=width), :] = jnp.concatenate([column, column], axis=0).T


def gaussians(exponent):
    return jnp.exp2(exponent) + jnp.exp2(exponent * RATIO + RATIO)


def main_kernel(
    points,
    basis,
    near_list,
    near_used,
    far_list,
    top,
    transfer,
    left,
    right,
    vectors,
    near,
    coupling,
    device_factor,
    wide,
    coords,
    first_rows,
    second_rows,
    second_cols,
    first_cols,
    switches,
    grams,
    work,
    factors,
    high,
    low,
    sem,
):
    width = basis.shape[0]
    own = basis.shape[1] // width
    total = own + 2 * PAD
    halo = LAYER * width
    rows = own * width
    both = 2 * width
    copy = pltpu.make_async_copy(vectors, wide.at[pl.ds(halo, rows), :], sem)
    copy.start()
    wide[0:halo, :] = left[0:halo, :]
    wide[halo + rows : 2 * halo + rows, :] = right[0:halo, :]

    coords[...] = jnp.zeros(coords.shape, F32)
    coords[0:3, PAD * width : PAD * width + rows] = points[...]
    for side, block in ((0, left), (PAD * width + rows, right)):
        for n in range(2):
            base = halo + width + 16 * n
            values = block[base : base + 16, 0:halo].astype(F32)
            coords[0:3, side + n * halo : side + (n + 1) * halo] = (
                values[0:3, :] + values[8:11, :]
            )
    lanes = coords.shape[1]
    sub = iota((8, lanes), 0)
    leaf = iota((8, lanes), 1) // width
    corner = jnp.where(sub == 0, leaf % 2 - 1, leaf // 2 % 2 - 1)
    corner = jnp.where(sub == 2, leaf // LAYER - total // LAYER // 2, corner)
    place = jnp.where(sub < 3, coords[...] + corner.astype(F32), 0.0)
    norm = jnp.sum(place * place, axis=0, keepdims=True) * SCALE
    first = jnp.where(sub == 3, -norm, jnp.where(sub == 4, 1.0, place))
    second = jnp.where(
        sub == 3, 1.0, jnp.where(sub == 4, -norm - 1.0, place * (2.0 * SCALE))
    )
    fh, fm, fl = [v.astype(F32) for v in split3(first)]
    sh, sm, sl = [v.astype(F32) for v in split3(second)]
    hot_row = iota((16, lanes), 0)
    hot_leaf = iota((16, lanes), 1) // width
    hot = jnp.where((hot_leaf + 16 - PAD) % 16 == hot_row, 1.0, 0.0).astype(F32)
    first_all = jnp.concatenate([fh, fh, fh, fm, fm, fl, hot], axis=0)
    second_all = jnp.concatenate([sh, sm, sl, sh, sm, sh, jnp.zeros_like(hot)], axis=0)
    first_cols[...] = first_all.astype(BF16)
    second_cols[...] = second_all[0:48, :].astype(BF16)
    first_rows[...] = first_all[:, PAD * width : PAD * width + rows].T.astype(BF16)
    second_rows[...] = jnp.concatenate([second_all, second_all], axis=0).T.astype(BF16)

    start_leaf = lax.axis_index(AXES) * own
    target = iota((1, own), 1)
    base_leaf = start_leaf + target // LAYER * LAYER - LAYER
    window = 3 * LAYER
    found = jnp.zeros((16, own), jnp.bool_)
    place_row = iota((16, own), 0)
    for n in range(near_list.shape[0]):
        spot = jnp.where(near_used[...] > n, near_list[n : n + 1, :] - base_leaf, -1)
        found = jnp.logical_or(found, place_row == spot)
    bias = jnp.where(found, 0.0, OFF).astype(F32)
    span = window * width
    expand = jnp.where(iota((16, span), 0) == iota((16, span), 1) // width, 1.0, 0.0)
    switches[...] = mm(bias.T.astype(BF16), expand.astype(BF16)).astype(BF16)

    lane = iota((width, both), 1)
    for n in range(own // 2):
        block = basis[:, n * both : (n + 1) * both]
        zero = jnp.zeros_like(block)
        stacked = jnp.concatenate(
            [jnp.where(lane < width, block, zero), jnp.where(lane < width, zero, block)], axis=0
        )
        at = (PAD + 2 * n) * width
        grams[at : at + both, :] = mm_nt(stacked, block)
    for block, spots in (
        (left, (1, 2, 3, 5, 6, 7)),
        (right, tuple(PAD + own + m for m in (0, 1, 2, 4, 5, 6))),
    ):
        for n, spot in enumerate(spots):
            piece = block[halo : halo + width, n * width : (n + 1) * width]
            grams[spot * width : (spot + 1) * width, :] = mm_nt(piece, piece)
    for spot in (0, 4, total - 5, total - 1):
        grams[spot * width : (spot + 1) * width, :] = top[...]

    to_lanes(grams, work, width, total)
    factor_lanes(work, width)
    from_lanes(work, factors, width, total)
    device_factor[...] = exact(factors[0:width, 0:width], transfer[...])
    high_part, low_part = split2(factors[...])
    high[...] = high_part
    low[...] = low_part

    copy.wait()

    def layer(index, carry):
        at = pl.multiple_of(index * halo, halo)
        around = pl.multiple_of(index * halo + halo, halo)
        group = pl.multiple_of(index // 4 * 16, 16)
        columns = jnp.concatenate(
            [second_cols[:, pl.ds(around, 3 * halo)], switches[pl.ds(group, 16), :]], axis=0
        )
        weights = gaussians(mm(first_rows[pl.ds(at, halo), :], columns)).astype(BF16)
        near[pl.ds(at, halo), :] = mm(weights, wide[pl.ds(at, 3 * halo), :]).astype(BF16)
        return carry

    lax.fori_loop(0, own // LAYER, layer, 0)

    far = far_list.shape[0]
    square = iota((both, both), 0) // width == iota((both, both), 1) // width
    lane_far = iota((width, both), 1) < width
    lane_wide = iota((far * width, both), 1) < width

    def far_pair(index, carry):
        t = 2 * index
        spots = [
            [
                pl.multiple_of((far_list[f, t + m] - start_leaf + PAD) * width, width)
                for f in range(far)
            ]
            for m in range(2)
        ]
        picked = [
            jnp.concatenate([second_rows[pl.ds(s, width), :] for s in spots[m]], axis=0)
            for m in range(2)
        ]
        sources = jnp.where(lane_wide, picked[0], picked[1])
        at = pl.multiple_of((PAD + t) * width, both)
        own_cols = first_cols[:, pl.ds(at, both)]
        zero = jnp.zeros((both, both), BF16)
        targets = jnp.where(square, jnp.concatenate([own_cols, own_cols], axis=0), zero)
        kernel_block = gaussians(mm(sources, targets))
        kh, kl = split2(kernel_block)
        rh = jnp.where(square, high[pl.ds(at, both), :], zero)
        rl = jnp.where(square, low[pl.ds(at, both), :], zero)
        half = mm_nt(
            jnp.concatenate([kh, kl, kh], axis=1), jnp.concatenate([rh, rh, rl], axis=1)
        ) * (1.0 / width)
        zh, zl = split2(half)
        outs = []
        for f in range(far):
            a = slice(f * width, (f + 1) * width)
            sh = jnp.where(
                lane_far, high[pl.ds(spots[0][f], width), :], high[pl.ds(spots[1][f], width), :]
            )
            sl = jnp.where(
                lane_far, low[pl.ds(spots[0][f], width), :], low[pl.ds(spots[1][f], width), :]
            )
            ph = jnp.where(square, jnp.concatenate([zh[a], zh[a]], axis=0), zero)
            plow = jnp.where(square, jnp.concatenate([zl[a], zl[a]], axis=0), zero)
            outs.append(
                mm(jnp.concatenate([sh, sh, sl], axis=1), jnp.concatenate([ph, plow, ph], axis=0))
            )
        line = jnp.concatenate(
            [out[:, 0:width] for out in outs] + [out[:, width:both] for out in outs], axis=1
        )
        where = pl.multiple_of(index * (2 * far * width), both)
        coupling[:, pl.ds(where, 2 * far * width)] = line.astype(BF16)
        return carry

    lax.fori_loop(0, own // 2, far_pair, 0)


def upper_kernel(sums, group_factor, root_factor, grams, work, factors):
    width = sums.shape[1]
    groups = sums.shape[0] // width
    members = lax.axis_size("sub")
    group = lax.axis_index("group")
    total = sums[0:width, :]
    for g in range(1, groups):
        total = total + sums[g * width : (g + 1) * width, :]
    mine = sums[pl.ds(pl.multiple_of(group * width, width), width), :]
    for n in range(8):
        grams[n * width : (n + 1) * width, :] = (
            mine * (1.0 / members) if n == 0 else total * (1.0 / (members * groups))
        )
    to_lanes(grams, work, width, 8)
    factor_lanes(work, width)
    from_lanes(work, factors, width, 8)
    group_factor[...] = factors[0:width, 0:width]
    root_factor[...] = factors[width : 2 * width, 0:width]


def shift(block, distance):
    devices = range(lax.axis_size(AXES))
    route = [(i - distance, i) for i in devices if i - distance in devices]
    return lax.ppermute(block, AXES, route)


def per_device(
    points, leaf_basis, inner_transfer, device_transfer, vectors, near_index, near_count, far_index
):
    own = near_index.shape[0]
    width = leaf_basis.shape[1]
    columns = vectors.shape[1]
    halo = LAYER * width
    total = own + 2 * PAD
    groups = lax.axis_size("group")
    vmem = pl.BlockSpec(memory_space=pltpu.VMEM)
    smem = pl.BlockSpec(memory_space=pltpu.SMEM)
    hbm = pl.BlockSpec(memory_space=pl.ANY)
    square = jax.ShapeDtypeStruct((width, width), F32)
    sent = jax.ShapeDtypeStruct((halo + width + 32, columns), BF16)
    basis = leaf_basis.T

    hot, top, to_next, to_prev = pl.pallas_call(
        tree_kernel,
        out_shape=(jax.ShapeDtypeStruct((groups * width, width), F32), square, sent, sent),
        in_specs=[vmem, vmem, vmem, vmem, hbm],
        out_specs=(vmem, vmem, vmem, vmem),
        scratch_shapes=[pltpu.SemaphoreType.DMA((2,))],
        compiler_params=BIG,
        name="tree",
    )(basis, inner_transfer.T, device_transfer, points, vectors)
    left = shift(to_next, 1)
    right = shift(to_prev, -1)
    sums = lax.psum(hot, AXES)

    near, coupling, device_factor = pl.pallas_call(
        main_kernel,
        out_shape=(
            jax.ShapeDtypeStruct(vectors.shape, BF16),
            jax.ShapeDtypeStruct((width, own * far_index.shape[1] * width), BF16),
            square,
        ),
        in_specs=[vmem] * 4 + [smem] + [vmem] * 4 + [hbm],
        out_specs=(vmem, vmem, vmem),
        scratch_shapes=[
            pltpu.VMEM((own * width + 2 * halo, columns), BF16),
            pltpu.VMEM((8, total * width), F32),
            pltpu.VMEM((own * width, 64), BF16),
            pltpu.VMEM((total * width, 128), BF16),
            pltpu.VMEM((48, total * width), BF16),
            pltpu.VMEM((64, total * width), BF16),
            pltpu.VMEM((own, 3 * halo), BF16),
            pltpu.VMEM((total * width, width), F32),
            pltpu.VMEM((width, width, 128), F32),
            pltpu.VMEM((total * width, 2 * width), F32),
            pltpu.VMEM((total * width, 2 * width), BF16),
            pltpu.VMEM((total * width, 2 * width), BF16),
            pltpu.SemaphoreType.DMA,
        ],
        compiler_params=BIG,
        name="leaves",
    )(
        points,
        basis,
        near_index.T,
        near_count.reshape(1, own),
        far_index.T,
        top,
        device_transfer,
        left,
        right,
        vectors,
    )

    group_factor, root_factor = pl.pallas_call(
        upper_kernel,
        out_shape=(square, square),
        in_specs=[vmem],
        out_specs=(vmem, vmem),
        scratch_shapes=[
            pltpu.VMEM((8 * width, width), F32),
            pltpu.VMEM((width, width, 128), F32),
            pltpu.VMEM((8 * width, 2 * width), F32),
        ],
        compiler_params=BIG,
        name="upper",
    )(sums)
    return near, coupling.T, device_factor, group_factor, root_factor


def solution(mesh):
    split = P(AXES, None)
    return jax.shard_map(
        per_device,
        mesh=mesh,
        in_specs=(P(None, AXES), split, split, split, split, split, P(AXES), split),
        out_specs=(split, split, split, split, split),
        check_vma=False,
    )
```

```python
import math

import jax
import jax.numpy as jnp
from jax import lax
from jax.experimental import pallas as pl
from jax.experimental.pallas import tpu as pltpu
from jax.sharding import PartitionSpec as P

LAYER = 4
PAD = 8
LONG_SQ = 2.25
RATIO = 25.0
SCALE = 0.5 / LONG_SQ / math.log(2.0)
OFF = -16384.0
AXES = ("group", "sub")
F32 = jnp.float32
BF16 = jnp.bfloat16
BIG = pltpu.CompilerParams(vmem_limit_bytes=56 * 1024 * 1024)


def split2(value):
    high = value.astype(BF16)
    return high, (value - high.astype(F32)).astype(BF16)


def split3(value):
    high = value.astype(BF16)
    rest = value - high.astype(F32)
    middle = rest.astype(BF16)
    return high, middle, (rest - middle.astype(F32)).astype(BF16)


def mm(left, right):
    return jnp.dot(left, right, preferred_element_type=F32)


def mm_nt(left, right):
    return lax.dot_general(left, right, (((1,), (1,)), ((), ())), preferred_element_type=F32)


def exact(left, right):
    return jnp.dot(left, right, precision=lax.Precision.HIGHEST, preferred_element_type=F32)


def iota(shape, dim):
    return lax.broadcasted_iota(jnp.int32, shape, dim)


def tree_kernel(basis, inner, transfer, points, vectors, fan, top, to_next, to_prev, sems):
    width = basis.shape[0]
    count = basis.shape[1] // width
    halo = LAYER * width
    rows = vectors.shape[0]
    copies = [
        pltpu.make_async_copy(
            vectors.at[pl.ds(start, halo), :], target.at[pl.ds(0, halo), :], sems.at[n]
        )
        for n, (start, target) in enumerate(((rows - halo, to_next), (0, to_prev)))
    ]
    for copy in copies:
        copy.start()

    for target, first, skip in ((to_next, count - PAD, 1), (to_prev, 0, 0)):
        block = basis[:, first * width : (first + PAD) * width]
        pieces = [
            block[:, (at + skip) * width : (at + skip + 3) * width] for at in (0, LAYER)
        ]
        target[halo : halo + width, :] = jnp.concatenate(pieces, axis=1)
        for n in range(2):
            start = (first + n * LAYER) * width
            coords = points[:, start : start + halo]
            high, low = split2(coords)
            base = halo + width + 16 * n
            target[base : base + 16, :] = jnp.zeros((16, target.shape[1]), BF16)
            target[base : base + 3, 0:halo] = high
            target[base + 8 : base + 11, 0:halo] = low

    both = 2 * width
    same = iota((both, both), 0) // width == iota((both, both), 1) // width
    half_block = jnp.where(same, 0.5, 0.0).astype(F32)

    def pair(index):
        return inner[:, index * both : (index + 1) * both]

    blocks = []
    for n in range(count // 4):
        stacked = jnp.concatenate(
            [basis[:, (2 * n + m) * both : (2 * n + m + 1) * both] for m in range(2)], axis=0
        )
        blocks.append(mm_nt(stacked, stacked) * half_block)
    offset = 0
    while True:
        nodes = len(blocks)
        xs, ts = [], []
        for n in range(nodes):
            t = pair(offset + n)
            parts = jnp.concatenate(split3(blocks[n]), axis=0)
            xs.append(mm(jnp.concatenate([t, t, t], axis=1), parts))
            ts.append(t)
        offset += nodes
        if nodes == 1:
            break
        blocks = []
        for n in range(nodes // 2):
            x = jnp.concatenate(split3(jnp.concatenate(xs[2 * n : 2 * n + 2], axis=0)), axis=1)
            t = jnp.concatenate(ts[2 * n : 2 * n + 2], axis=0)
            blocks.append(mm_nt(x, jnp.concatenate([t, t, t], axis=1)) * half_block)
    t = ts[0]
    x = jnp.concatenate(split3(xs[0]), axis=1)
    top_gram = mm_nt(x, jnp.concatenate([t, t, t], axis=1)) * 0.5
    top[...] = top_gram
    matrix = transfer[...]
    gram = exact(exact(matrix.T, top_gram), matrix)
    for n in range(fan.shape[0]):
        fan[n, :, :] = jnp.concatenate([gram[: width // 2], gram[width // 2 :]], axis=1)
    for copy in copies:
        copy.wait()


def factor_lanes(work, width, beside):
    panels = width // 8
    row = iota((8, 128), 0)

    def spread(j, i):
        return jnp.broadcast_to(work[j, i : i + 1, :], (8, 128))

    for p in range(panels):
        at = 8 * p
        tiles = list(range(p, panels))
        if p:
            for start in range(0, len(tiles), 3):
                group = tiles[start : start + 3]
                accs = [work[at + k, 8 * i : 8 * i + 8, :] for i in group for k in range(8)]

                def step(j, accs, group=group, at=at):
                    factors = [spread(j, at + k) for k in range(8)]
                    out = []
                    for n, i in enumerate(group):
                        column = work[j, 8 * i : 8 * i + 8, :]
                        out += [accs[8 * n + k] - column * factors[k] for k in range(8)]
                    return out

                accs = lax.fori_loop(0, at, step, accs, unroll=4)
                for n, i in enumerate(group):
                    for k in range(8):
                        work[at + k, 8 * i : 8 * i + 8, :] = accs[8 * n + k]
        entry = {(k, m): spread(at + k, at + m) for k in range(8) for m in range(k, 8)}
        scales = []
        for k in range(8):
            scales.append(lax.rsqrt(entry[k, k]))
            for m in range(k + 1, 8):
                entry[k, m] = entry[k, m] * scales[k]
            for m in range(k + 1, 8):
                for q in range(m, 8):
                    entry[m, q] = entry[m, q] - entry[k, m] * entry[k, q]
        for i in tiles:
            tile = [work[at + k, 8 * i : 8 * i + 8, :] for k in range(8)]
            for k in range(8):
                tile[k] = tile[k] * scales[k]
                for m in range(k + 1, 8):
                    tile[m] = tile[m] - tile[k] * entry[k, m]
            for k in range(8):
                work[at + k, 8 * i : 8 * i + 8, :] = (
                    jnp.where(row >= k, tile[k], 0.0) if i == p else tile[k]
                )
        for i in range(p):
            for k in range(8):
                work[at + k, 8 * i : 8 * i + 8, :] = jnp.zeros((8, 128), F32)
        beside(p)


def to_lanes(grams, work, width, many):
    for i in range(width):
        work[i, :, 0:many] = grams[pl.ds(i, many, stride=width), :].T


def from_lanes(work, factors, width, many):
    for j in range(width):
        column = work[j, :, 0:many]
        factors[pl.ds(j, many, stride=width), :] = jnp.concatenate([column, column], axis=0).T


def gaussians(exponent):
    return jnp.exp2(exponent) + jnp.exp2(exponent * RATIO + RATIO)


def main_kernel(
    points,
    basis,
    near_list,
    near_used,
    far_list,
    top,
    sums,
    transfer,
    left,
    right,
    vectors,
    near,
    coupling,
    device_factor,
    group_factor,
    root_factor,
    wide,
    sides,
    coords,
    first_rows,
    second_rows,
    second_cols,
    first_cols,
    switches,
    grams,
    work,
    factors,
    high,
    low,
    sems,
):
    width = basis.shape[0]
    own = basis.shape[1] // width
    total = own + 2 * PAD
    halo = LAYER * width
    rows = own * width
    both = 2 * width
    extra = sides.shape[1]
    side_copies = [
        pltpu.make_async_copy(side.at[pl.ds(halo, extra), :], sides.at[n], sems.at[n])
        for n, side in enumerate((left, right))
    ]
    copies = [
        pltpu.make_async_copy(source, wide.at[pl.ds(start, many), :], sems.at[2 + n])
        for n, (source, start, many) in enumerate(
            (
                (left.at[pl.ds(0, halo), :], 0, halo),
                (right.at[pl.ds(0, halo), :], halo + rows, halo),
                (vectors, halo, rows),
            )
        )
    ]
    for copy in side_copies + copies:
        copy.start()

    coords[...] = jnp.zeros(coords.shape, F32)
    coords[0:3, PAD * width : PAD * width + rows] = points[...]
    for copy in side_copies:
        copy.wait()
    for block, side in enumerate((0, PAD * width + rows)):
        for n in range(2):
            base = width + 16 * n
            values = sides[block, base : base + 16, 0:halo].astype(F32)
            coords[0:3, side + n * halo : side + (n + 1) * halo] = (
                values[0:3, :] + values[8:11, :]
            )
    lanes = coords.shape[1]
    sub = iota((8, lanes), 0)
    leaf = iota((8, lanes), 1) // width
    corner = jnp.where(sub == 0, leaf % 2 - 1, leaf // 2 % 2 - 1)
    corner = jnp.where(sub == 2, leaf // LAYER - total // LAYER // 2, corner)
    place = jnp.where(sub < 3, coords[...] + corner.astype(F32), 0.0)
    norm = jnp.sum(place * place, axis=0, keepdims=True) * SCALE
    first = jnp.where(sub == 3, -norm, jnp.where(sub == 4, 1.0, place))
    second = jnp.where(
        sub == 3, 1.0, jnp.where(sub == 4, -norm - 1.0, place * (2.0 * SCALE))
    )
    fh, fm, fl = [v.astype(F32) for v in split3(first)]
    sh, sm, sl = [v.astype(F32) for v in split3(second)]
    hot_row = iota((16, lanes), 0)
    hot_leaf = iota((16, lanes), 1) // width
    hot = jnp.where((hot_leaf + 16 - PAD) % 16 == hot_row, 1.0, 0.0).astype(F32)
    first_all = jnp.concatenate([fh, fh, fh, fm, fm, fl, hot], axis=0)
    second_all = jnp.concatenate([sh, sm, sl, sh, sm, sh, jnp.zeros_like(hot)], axis=0)
    first_cols[...] = first_all.astype(BF16)
    second_cols[...] = second_all[0:48, :].astype(BF16)
    first_rows[...] = first_all[:, PAD * width : PAD * width + rows].T.astype(BF16)
    second_rows[...] = jnp.concatenate([second_all, second_all], axis=0).T.astype(BF16)

    start_leaf = lax.axis_index(AXES) * own
    target = iota((1, own), 1)
    base_leaf = start_leaf + target // LAYER * LAYER - LAYER
    window = 3 * LAYER
    found = jnp.zeros((16, own), jnp.bool_)
    place_row = iota((16, own), 0)
    for n in range(near_list.shape[0]):
        spot = jnp.where(near_used[...] > n, near_list[n : n + 1, :] - base_leaf, -1)
        found = jnp.logical_or(found, place_row == spot)
    bias = jnp.where(found, 0.0, OFF).astype(F32)
    span = window * width
    expand = jnp.where(iota((16, span), 0) == iota((16, span), 1) // width, 1.0, 0.0)
    switches[...] = mm(bias.T.astype(BF16), expand.astype(BF16)).astype(BF16)

    lane = iota((width, both), 1)
    for n in range(own // 2):
        block = basis[:, n * both : (n + 1) * both]
        zero = jnp.zeros_like(block)
        stacked = jnp.concatenate(
            [jnp.where(lane < width, block, zero), jnp.where(lane < width, zero, block)], axis=0
        )
        at = (PAD + 2 * n) * width
        grams[at : at + both, :] = mm_nt(stacked, block)
    for block, spots in enumerate(
        ((1, 2, 3, 5, 6, 7), tuple(PAD + own + m for m in (0, 1, 2, 4, 5, 6)))
    ):
        for n, spot in enumerate(spots):
            piece = sides[block, 0:width, n * width : (n + 1) * width]
            grams[spot * width : (spot + 1) * width, :] = mm_nt(piece, piece)
    members, groups = lax.axis_size("sub"), lax.axis_size("group")
    root = sums[0, :, :]
    for g in range(1, groups):
        root = root + sums[g, :, :]
    mine = sums[lax.axis_index("group"), :, :]
    root, mine = (
        jnp.concatenate([v[:, :width], v[:, width:]], axis=0) for v in (root, mine)
    )
    spare = (0, 4, total - 5, total - 1)
    for spot, gram in zip(
        spare,
        (top[...], mine * (1.0 / members), root * (1.0 / (members * groups)), top[...]),
    ):
        grams[spot * width : (spot + 1) * width, :] = gram

    for copy in copies:
        copy.wait()

    def layer(index):
        at = index * halo
        around = index * halo + halo
        group = index // 4 * 16
        columns = jnp.concatenate(
            [second_cols[:, pl.ds(around, 3 * halo)], switches[pl.ds(group, 16), :]], axis=0
        )
        weights = gaussians(mm(first_rows[pl.ds(at, halo), :], columns)).astype(BF16)
        near[pl.ds(at, halo), :] = mm(weights, wide[pl.ds(at, 3 * halo), :]).astype(BF16)

    to_lanes(grams, work, width, total)
    layers = own // LAYER
    panels = width // 8

    def some_layers(p):
        for index in range(p * layers // panels, (p + 1) * layers // panels):
            layer(index)

    factor_lanes(work, width, some_layers)
    from_lanes(work, factors, width, total)
    device_factor[...] = exact(factors[0:width, 0:width], transfer[...])
    for target, spot in ((group_factor, spare[1]), (root_factor, spare[2])):
        target[...] = factors[spot * width : (spot + 1) * width, 0:width]
    high_part, low_part = split2(factors[...])
    high[...] = high_part
    low[...] = low_part

    far = far_list.shape[0]
    square = iota((both, both), 0) // width == iota((both, both), 1) // width
    lane_far = iota((width, both), 1) < width
    lane_wide = iota((far * width, both), 1) < width

    def far_pair(index, carry):
        t = 2 * index
        spots = [
            [
                pl.multiple_of((far_list[f, t + m] - start_leaf + PAD) * width, width)
                for f in range(far)
            ]
            for m in range(2)
        ]
        picked = [
            jnp.concatenate([second_rows[pl.ds(s, width), :] for s in spots[m]], axis=0)
            for m in range(2)
        ]
        sources = jnp.where(lane_wide, picked[0], picked[1])
        at = pl.multiple_of((PAD + t) * width, both)
        own_cols = first_cols[:, pl.ds(at, both)]
        zero = jnp.zeros((both, both), BF16)
        targets = jnp.where(square, jnp.concatenate([own_cols, own_cols], axis=0), zero)
        kernel_block = gaussians(mm(sources, targets))
        kh, kl = split2(kernel_block)
        rh = jnp.where(square, high[pl.ds(at, both), :], zero)
        rl = jnp.where(square, low[pl.ds(at, both), :], zero)
        half = mm_nt(
            jnp.concatenate([kh, kl, kh], axis=1), jnp.concatenate([rh, rh, rl], axis=1)
        ) * (1.0 / width)
        zh, zl = split2(half)
        outs = []
        for f in range(far):
            a = slice(f * width, (f + 1) * width)
            sh = jnp.where(
                lane_far, high[pl.ds(spots[0][f], width), :], high[pl.ds(spots[1][f], width), :]
            )
            sl = jnp.where(
                lane_far, low[pl.ds(spots[0][f], width), :], low[pl.ds(spots[1][f], width), :]
            )
            ph = jnp.where(square, jnp.concatenate([zh[a], zh[a]], axis=0), zero)
            plow = jnp.where(square, jnp.concatenate([zl[a], zl[a]], axis=0), zero)
            outs.append(
                mm(jnp.concatenate([sh, sh, sl], axis=1), jnp.concatenate([ph, plow, ph], axis=0))
            )
        line = jnp.concatenate(
            [out[:, 0:width] for out in outs] + [out[:, width:both] for out in outs], axis=1
        )
        where = pl.multiple_of(index * (2 * far * width), both)
        coupling[:, pl.ds(where, 2 * far * width)] = line.astype(BF16)
        return carry

    lax.fori_loop(0, own // 2, far_pair, 0, unroll=4)


def shift(block, distance):
    devices = range(lax.axis_size(AXES))
    route = [(i - distance, i) for i in devices if i - distance in devices]
    return lax.ppermute(block, AXES, route)


def per_device(
    points, leaf_basis, inner_transfer, device_transfer, vectors, near_index, near_count, far_index
):
    own = near_index.shape[0]
    width = leaf_basis.shape[1]
    columns = vectors.shape[1]
    halo = LAYER * width
    total = own + 2 * PAD
    members, groups = lax.axis_size("sub"), lax.axis_size("group")
    vmem = pl.BlockSpec(memory_space=pltpu.VMEM)
    smem = pl.BlockSpec(memory_space=pltpu.SMEM)
    hbm = pl.BlockSpec(memory_space=pl.ANY)
    square = jax.ShapeDtypeStruct((width, width), F32)
    sent = jax.ShapeDtypeStruct((halo + width + 32, columns), BF16)
    basis = leaf_basis.T

    fan, top, to_next, to_prev = pl.pallas_call(
        tree_kernel,
        out_shape=(jax.ShapeDtypeStruct((members, width // 2, 2 * width), F32), square, sent, sent),
        in_specs=[vmem, vmem, vmem, vmem, hbm],
        out_specs=(vmem, vmem, vmem, vmem),
        scratch_shapes=[pltpu.SemaphoreType.DMA((2,))],
        compiler_params=BIG,
        name="tree",
    )(basis, inner_transfer.T, device_transfer, points, vectors)
    left = shift(to_next, 1)
    right = shift(to_prev, -1)
    fan = lax.all_to_all(fan, "sub", 0, 0, tiled=True)
    gram = jnp.broadcast_to(jnp.sum(fan, axis=0, keepdims=True), (groups, *fan.shape[1:]))
    sums = lax.all_to_all(gram, "group", 0, 0, tiled=True)

    near, coupling, device_factor, group_factor, root_factor = pl.pallas_call(
        main_kernel,
        out_shape=(
            jax.ShapeDtypeStruct(vectors.shape, BF16),
            jax.ShapeDtypeStruct((width, own * far_index.shape[1] * width), BF16),
            square,
            square,
            square,
        ),
        in_specs=[vmem] * 4 + [smem] + [vmem] * 3 + [hbm] * 3,
        out_specs=(vmem,) * 5,
        scratch_shapes=[
            pltpu.VMEM((own * width + 2 * halo, columns), BF16),
            pltpu.VMEM((2, width + 32, columns), BF16),
            pltpu.VMEM((8, total * width), F32),
            pltpu.VMEM((own * width, 64), BF16),
            pltpu.VMEM((total * width, 128), BF16),
            pltpu.VMEM((48, total * width), BF16),
            pltpu.VMEM((64, total * width), BF16),
            pltpu.VMEM((own, 3 * halo), BF16),
            pltpu.VMEM((total * width, width), F32),
            pltpu.VMEM((width, width, 128), F32),
            pltpu.VMEM((total * width, 2 * width), F32),
            pltpu.VMEM((total * width, 2 * width), BF16),
            pltpu.VMEM((total * width, 2 * width), BF16),
            pltpu.SemaphoreType.DMA((5,)),
        ],
        compiler_params=BIG,
        name="leaves",
    )(
        points,
        basis,
        near_index.T,
        near_count.reshape(1, own),
        far_index.T,
        top,
        sums,
        device_transfer,
        left,
        right,
        vectors,
    )
    return near, coupling.T, device_factor, group_factor, root_factor


def solution(mesh):
    split = P(AXES, None)
    return jax.shard_map(
        per_device,
        mesh=mesh,
        in_specs=(P(None, AXES), split, split, split, split, split, P(AXES), split),
        out_specs=(split, split, split, split, split),
        check_vma=False,
    )
```

```python
import math

import jax
import jax.numpy as jnp
from jax import lax
from jax.experimental import pallas as pl
from jax.experimental.pallas import tpu as pltpu
from jax.sharding import PartitionSpec as P

LAYER = 4
PAD = 8
LONG_SQ = 2.25
RATIO = 25.0
SCALE = 0.5 / LONG_SQ
HALF = math.log(0.5)
OFF = -16384.0
AXES = ("group", "sub")
F32 = jnp.float32
BF16 = jnp.bfloat16


def room(megabytes):
    return pltpu.CompilerParams(vmem_limit_bytes=megabytes * 1024 * 1024)


def split2(value):
    high = value.astype(BF16)
    return high, (value - high.astype(F32)).astype(BF16)


def split3(value):
    high = value.astype(BF16)
    rest = value - high.astype(F32)
    middle = rest.astype(BF16)
    return high, middle, (rest - middle.astype(F32)).astype(BF16)


def mm(left, right):
    return jnp.dot(left, right, preferred_element_type=F32)


def mm_nt(left, right):
    return lax.dot_general(left, right, (((1,), (1,)), ((), ())), preferred_element_type=F32)


def exact(left, right):
    return jnp.dot(left, right, precision=lax.Precision.HIGHEST, preferred_element_type=F32)


def iota(shape, dim):
    return lax.broadcasted_iota(jnp.int32, shape, dim)


def tree_kernel(basis, inner, transfer, points, vectors, dense, top, to_next, to_prev, sems):
    width = basis.shape[0]
    count = basis.shape[1] // width
    halo = LAYER * width
    rows = vectors.shape[0]
    copies = [
        pltpu.make_async_copy(
            vectors.at[pl.ds(start, halo), :], target.at[pl.ds(0, halo), :], sems.at[n]
        )
        for n, (start, target) in enumerate(((rows - halo, to_next), (0, to_prev)))
    ]
    for copy in copies:
        copy.start()

    for target, first, skip in ((to_next, count - PAD, 1), (to_prev, 0, 0)):
        block = basis[:, first * width : (first + PAD) * width]
        pieces = [
            block[:, (at + skip) * width : (at + skip + 3) * width] for at in (0, LAYER)
        ]
        target[halo : halo + width, :] = jnp.concatenate(pieces, axis=1)
        for n in range(2):
            start = (first + n * LAYER) * width
            coords = points[:, start : start + halo]
            high, low = split2(coords)
            base = halo + width + 16 * n
            target[base : base + 16, :] = jnp.zeros((16, target.shape[1]), BF16)
            target[base : base + 3, 0:halo] = high
            target[base + 8 : base + 11, 0:halo] = low

    both = 2 * width
    same = iota((both, both), 0) // width == iota((both, both), 1) // width
    half_block = jnp.where(same, 0.5, 0.0).astype(F32)

    def pair(index):
        return inner[:, index * both : (index + 1) * both]

    blocks = []
    for n in range(count // 4):
        stacked = jnp.concatenate(
            [basis[:, (2 * n + m) * both : (2 * n + m + 1) * both] for m in range(2)], axis=0
        )
        blocks.append(mm_nt(stacked, stacked) * half_block)
    offset = 0
    while True:
        nodes = len(blocks)
        xs, ts = [], []
        for n in range(nodes):
            t = pair(offset + n)
            parts = jnp.concatenate(split3(blocks[n]), axis=0)
            xs.append(mm(jnp.concatenate([t, t, t], axis=1), parts))
            ts.append(t)
        offset += nodes
        if nodes == 1:
            break
        blocks = []
        for n in range(nodes // 2):
            x = jnp.concatenate(split3(jnp.concatenate(xs[2 * n : 2 * n + 2], axis=0)), axis=1)
            t = jnp.concatenate(ts[2 * n : 2 * n + 2], axis=0)
            blocks.append(mm_nt(x, jnp.concatenate([t, t, t], axis=1)) * half_block)
    t = ts[0]
    x = jnp.concatenate(split3(xs[0]), axis=1)
    top_gram = mm_nt(x, jnp.concatenate([t, t, t], axis=1)) * 0.5
    top[...] = top_gram
    matrix = transfer[...]
    gram = exact(exact(matrix.T, top_gram), matrix)
    dense[...] = jnp.concatenate([gram[: width // 2], gram[width // 2 :]], axis=1)
    for copy in copies:
        copy.wait()


def factor_lanes(work, width, beside):
    panels = width // 8
    row = iota((8, 128), 0)

    def spread(j, i):
        return jnp.broadcast_to(work[j, i : i + 1, :], (8, 128))

    for p in range(panels):
        at = 8 * p
        tiles = list(range(p, panels))
        if p:
            for start in range(0, len(tiles), 3):
                group = tiles[start : start + 3]
                accs = [work[at + k, 8 * i : 8 * i + 8, :] for i in group for k in range(8)]

                def step(j, accs, group=group, at=at):
                    factors = [spread(j, at + k) for k in range(8)]
                    out = []
                    for n, i in enumerate(group):
                        column = work[j, 8 * i : 8 * i + 8, :]
                        out += [accs[8 * n + k] - column * factors[k] for k in range(8)]
                    return out

                accs = lax.fori_loop(0, at, step, accs, unroll=4)
                for n, i in enumerate(group):
                    for k in range(8):
                        work[at + k, 8 * i : 8 * i + 8, :] = accs[8 * n + k]
        entry = {(k, m): spread(at + k, at + m) for k in range(8) for m in range(k, 8)}
        scales = []
        for k in range(8):
            scales.append(lax.rsqrt(entry[k, k]))
            for m in range(k + 1, 8):
                entry[k, m] = entry[k, m] * scales[k]
            for m in range(k + 1, 8):
                for q in range(m, 8):
                    entry[m, q] = entry[m, q] - entry[k, m] * entry[k, q]
        for i in tiles:
            tile = [work[at + k, 8 * i : 8 * i + 8, :] for k in range(8)]
            for k in range(8):
                tile[k] = tile[k] * scales[k]
                for m in range(k + 1, 8):
                    tile[m] = tile[m] - tile[k] * entry[k, m]
            for k in range(8):
                work[at + k, 8 * i : 8 * i + 8, :] = (
                    jnp.where(row >= k, tile[k], 0.0) if i == p else tile[k]
                )
        for i in range(p):
            for k in range(8):
                work[at + k, 8 * i : 8 * i + 8, :] = jnp.zeros((8, 128), F32)
        beside(p)


def to_lanes(grams, work, width, many):
    for i in range(width):
        work[i, :, 0:many] = grams[pl.ds(i, many, stride=width), :].T


def from_lanes(work, factors, width, many):
    for j in range(width):
        column = work[j, :, 0:many]
        factors[pl.ds(j, many, stride=width), :] = jnp.concatenate([column, column], axis=0).T


def gaussians(exponent):
    return jnp.exp(exponent) + jnp.exp(exponent * RATIO - RATIO * HALF)


def leaves_kernel(
    points,
    basis,
    near_list,
    near_used,
    top,
    transfer,
    left,
    right,
    vectors,
    near,
    high,
    low,
    second_rows,
    first_cols,
    device_factor,
    wide,
    sides,
    coords,
    first_rows,
    second_cols,
    switches,
    grams,
    work,
    factors,
    sems,
):
    width = basis.shape[0]
    own = basis.shape[1] // width
    total = own + 2 * PAD
    halo = LAYER * width
    rows = own * width
    both = 2 * width
    extra = sides.shape[1]
    side_copies = [
        pltpu.make_async_copy(side.at[pl.ds(halo, extra), :], sides.at[n], sems.at[n])
        for n, side in enumerate((left, right))
    ]
    copies = [
        pltpu.make_async_copy(source, wide.at[pl.ds(start, many), :], sems.at[2 + n])
        for n, (source, start, many) in enumerate(
            (
                (left.at[pl.ds(0, halo), :], 0, halo),
                (right.at[pl.ds(0, halo), :], halo + rows, halo),
                (vectors, halo, rows),
            )
        )
    ]
    for copy in side_copies + copies:
        copy.start()

    coords[...] = jnp.zeros(coords.shape, F32)
    coords[0:3, PAD * width : PAD * width + rows] = points[...]
    for copy in side_copies:
        copy.wait()
    for block, side in enumerate((0, PAD * width + rows)):
        for n in range(2):
            base = width + 16 * n
            values = sides[block, base : base + 16, 0:halo].astype(F32)
            coords[0:3, side + n * halo : side + (n + 1) * halo] = (
                values[0:3, :] + values[8:11, :]
            )
    lanes = coords.shape[1]
    sub = iota((8, lanes), 0)
    leaf = iota((8, lanes), 1) // width
    corner = jnp.where(sub == 0, leaf % 2 - 1, leaf // 2 % 2 - 1)
    corner = jnp.where(sub == 2, leaf // LAYER - total // LAYER // 2, corner)
    place = jnp.where(sub < 3, coords[...] + corner.astype(F32), 0.0)
    norm = jnp.sum(place * place, axis=0, keepdims=True) * SCALE
    first = jnp.where(sub == 3, -norm, jnp.where(sub == 4, 1.0, place))
    second = jnp.where(
        sub == 3, 1.0, jnp.where(sub == 4, HALF - norm, place * (2.0 * SCALE))
    )
    fh, fm, fl = [v.astype(F32) for v in split3(first)]
    sh, sm, sl = [v.astype(F32) for v in split3(second)]
    hot_row = iota((16, lanes), 0)
    hot_leaf = iota((16, lanes), 1) // width
    hot = jnp.where((hot_leaf + 16 - PAD) % 16 == hot_row, 1.0, 0.0).astype(F32)
    first_all = jnp.concatenate([fh, fh, fh, fm, fm, fl, hot], axis=0)
    second_all = jnp.concatenate([sh, sm, sl, sh, sm, sh, jnp.zeros_like(hot)], axis=0)
    first_cols[...] = first_all.astype(BF16)
    second_cols[...] = second_all[0:48, :].astype(BF16)
    first_rows[...] = first_all[:, PAD * width : PAD * width + rows].T.astype(BF16)
    second_rows[...] = jnp.concatenate([second_all, second_all], axis=0).T.astype(BF16)

    start_leaf = lax.axis_index(AXES) * own
    target = iota((1, own), 1)
    base_leaf = start_leaf + target // LAYER * LAYER - LAYER
    window = 3 * LAYER
    found = jnp.zeros((16, own), jnp.bool_)
    place_row = iota((16, own), 0)
    for n in range(near_list.shape[0]):
        spot = jnp.where(near_used[...] > n, near_list[n : n + 1, :] - base_leaf, -1)
        found = jnp.logical_or(found, place_row == spot)
    bias = jnp.where(found, 0.0, OFF).astype(F32)
    span = window * width
    expand = jnp.where(iota((16, span), 0) == iota((16, span), 1) // width, 1.0, 0.0)
    switches[...] = mm(bias.T.astype(BF16), expand.astype(BF16)).astype(BF16)

    lane = iota((width, both), 1)
    for n in range(own // 2):
        block = basis[:, n * both : (n + 1) * both]
        zero = jnp.zeros_like(block)
        stacked = jnp.concatenate(
            [jnp.where(lane < width, block, zero), jnp.where(lane < width, zero, block)], axis=0
        )
        at = (PAD + 2 * n) * width
        grams[at : at + both, :] = mm_nt(stacked, block)
    for block, spots in enumerate(
        ((1, 2, 3, 5, 6, 7), tuple(PAD + own + m for m in (0, 1, 2, 4, 5, 6)))
    ):
        for n, spot in enumerate(spots):
            piece = sides[block, 0:width, n * width : (n + 1) * width]
            grams[spot * width : (spot + 1) * width, :] = mm_nt(piece, piece)
    for spot in (0, LAYER, total - LAYER - 1, total - 1):
        grams[spot * width : (spot + 1) * width, :] = top[...]

    for copy in copies:
        copy.wait()

    def layer(index):
        at = index * halo
        around = index * halo + halo
        group = index // 4 * 16
        columns = jnp.concatenate(
            [second_cols[:, pl.ds(around, 3 * halo)], switches[pl.ds(group, 16), :]], axis=0
        )
        weights = gaussians(mm(first_rows[pl.ds(at, halo), :], columns)).astype(BF16)
        near[pl.ds(at, halo), :] = mm(weights, wide[pl.ds(at, 3 * halo), :]).astype(BF16)

    to_lanes(grams, work, width, total)
    layers = own // LAYER
    panels = width // 8

    def some_layers(p):
        for index in range(p * layers // panels, (p + 1) * layers // panels):
            layer(index)

    factor_lanes(work, width, some_layers)
    from_lanes(work, factors, width, total)
    device_factor[...] = exact(factors[0:width, 0:width], transfer[...])
    high_part, low_part = split2(factors[...])
    high[...] = high_part
    low[...] = low_part


def far_kernel(
    far_list,
    all_grams,
    high,
    low,
    second_rows,
    first_cols,
    coupling,
    group_factor,
    root_factor,
    grams,
    work,
    factors,
):
    width = group_factor.shape[0]
    far, own = far_list.shape
    both = 2 * width
    start_leaf = lax.axis_index(AXES) * own
    members, groups = lax.axis_size("sub"), lax.axis_size("group")

    group = lax.axis_index("group")
    mine = all_grams[group * members, :, :]
    for m in range(1, members):
        mine = mine + all_grams[group * members + m, :, :]
    everyone = all_grams[0, :, :]
    for m in range(1, members * groups):
        everyone = everyone + all_grams[m, :, :]
    for n in range(8):
        value = everyone * (1.0 / (members * groups)) if n else mine * (1.0 / members)
        grams[n * width : (n + 1) * width, :] = jnp.concatenate(
            [value[:, :width], value[:, width:]], axis=0
        )
    to_lanes(grams, work, width, 8)

    square = iota((both, both), 0) // width == iota((both, both), 1) // width
    lane_far = iota((width, both), 1) < width
    lane_wide = iota((far * width, both), 1) < width

    def far_pair(index):
        t = 2 * index
        spots = [
            [
                pl.multiple_of((far_list[f, t + m] - start_leaf + PAD) * width, width)
                for f in range(far)
            ]
            for m in range(2)
        ]
        picked = [
            jnp.concatenate([second_rows[pl.ds(s, width), :] for s in spots[m]], axis=0)
            for m in range(2)
        ]
        sources = jnp.where(lane_wide, picked[0], picked[1])
        at = (PAD + t) * width
        own_cols = first_cols[:, pl.ds(at, both)]
        zero = jnp.zeros((both, both), BF16)
        targets = jnp.where(square, jnp.concatenate([own_cols, own_cols], axis=0), zero)
        kernel_block = gaussians(mm(sources, targets))
        kh, kl = split2(kernel_block)
        rh = jnp.where(square, high[pl.ds(at, both), :], zero)
        rl = jnp.where(square, low[pl.ds(at, both), :], zero)
        half = mm_nt(
            jnp.concatenate([kh, kl, kh], axis=1), jnp.concatenate([rh, rh, rl], axis=1)
        ) * (1.0 / width)
        zh, zl = split2(half)
        outs = []
        for f in range(far):
            a = slice(f * width, (f + 1) * width)
            sh = jnp.where(
                lane_far, high[pl.ds(spots[0][f], width), :], high[pl.ds(spots[1][f], width), :]
            )
            sl = jnp.where(
                lane_far, low[pl.ds(spots[0][f], width), :], low[pl.ds(spots[1][f], width), :]
            )
            ph = jnp.where(square, jnp.concatenate([zh[a], zh[a]], axis=0), zero)
            plow = jnp.where(square, jnp.concatenate([zl[a], zl[a]], axis=0), zero)
            outs.append(
                mm(jnp.concatenate([sh, sh, sl], axis=1), jnp.concatenate([ph, plow, ph], axis=0))
            )
        line = jnp.concatenate(
            [out[:, 0:width] for out in outs] + [out[:, width:both] for out in outs], axis=1
        )
        coupling[:, pl.ds(index * 2 * far * width, 2 * far * width)] = line.astype(BF16)

    pairs = own // 2
    panels = width // 8

    def some_pairs(p):
        for index in range(p * pairs // panels, (p + 1) * pairs // panels):
            far_pair(index)

    factor_lanes(work, width, some_pairs)
    from_lanes(work, factors, width, 8)
    group_factor[...] = factors[0:width, 0:width]
    root_factor[...] = factors[width : 2 * width, 0:width]


def shift(block, distance):
    devices = range(lax.axis_size(AXES))
    route = [(i - distance, i) for i in devices if i - distance in devices]
    return lax.ppermute(block, AXES, route)


def per_device(
    points, leaf_basis, inner_transfer, device_transfer, vectors, near_index, near_count, far_index
):
    own = near_index.shape[0]
    width = leaf_basis.shape[1]
    columns = vectors.shape[1]
    halo = LAYER * width
    total = own + 2 * PAD
    vmem = pl.BlockSpec(memory_space=pltpu.VMEM)
    smem = pl.BlockSpec(memory_space=pltpu.SMEM)
    hbm = pl.BlockSpec(memory_space=pl.ANY)
    square = jax.ShapeDtypeStruct((width, width), F32)
    sent = jax.ShapeDtypeStruct((halo + width + 32, columns), BF16)
    basis = leaf_basis.T

    dense, top, to_next, to_prev = pl.pallas_call(
        tree_kernel,
        out_shape=(jax.ShapeDtypeStruct((width // 2, 2 * width), F32), square, sent, sent),
        in_specs=[vmem, vmem, vmem, vmem, hbm],
        out_specs=(vmem, vmem, vmem, vmem),
        scratch_shapes=[pltpu.SemaphoreType.DMA((2,))],
        compiler_params=room(8),
        name="tree",
    )(basis, inner_transfer.T, device_transfer, points, vectors)
    left = shift(to_next, 1)
    right = shift(to_prev, -1)
    all_grams = lax.all_gather(dense, AXES)

    split_factors = jax.ShapeDtypeStruct((total * width, 2 * width), BF16)
    near, high, low, second_rows, first_cols, device_factor = pl.pallas_call(
        leaves_kernel,
        out_shape=(
            jax.ShapeDtypeStruct(vectors.shape, BF16),
            split_factors,
            split_factors,
            split_factors,
            jax.ShapeDtypeStruct((64, total * width), BF16),
            square,
        ),
        in_specs=[vmem] * 6 + [hbm] * 3,
        out_specs=(vmem,) * 6,
        scratch_shapes=[
            pltpu.VMEM((own * width + 2 * halo, columns), BF16),
            pltpu.VMEM((2, width + 32, columns), BF16),
            pltpu.VMEM((8, total * width), F32),
            pltpu.VMEM((own * width, 64), BF16),
            pltpu.VMEM((48, total * width), BF16),
            pltpu.VMEM((own, 3 * halo), BF16),
            pltpu.VMEM((total * width, width), F32),
            pltpu.VMEM((width, width, 128), F32),
            pltpu.VMEM((total * width, 2 * width), F32),
            pltpu.SemaphoreType.DMA((5,)),
        ],
        compiler_params=room(28),
        name="leaves",
    )(
        points,
        basis,
        near_index.T,
        near_count.reshape(1, own),
        top,
        device_transfer,
        left,
        right,
        vectors,
    )

    coupling, group_factor, root_factor = pl.pallas_call(
        far_kernel,
        out_shape=(
            jax.ShapeDtypeStruct((width, own * far_index.shape[1] * width), BF16),
            square,
            square,
        ),
        in_specs=[smem] + [vmem] * 5,
        out_specs=(vmem,) * 3,
        scratch_shapes=[
            pltpu.VMEM((8 * width, width), F32),
            pltpu.VMEM((width, width, 128), F32),
            pltpu.VMEM((8 * width, 2 * width), F32),
        ],
        compiler_params=room(20),
        name="far",
    )(far_index.T, all_grams, high, low, second_rows, first_cols)
    return near, coupling.T, device_factor, group_factor, root_factor


def solution(mesh):
    split = P(AXES, None)
    return jax.shard_map(
        per_device,
        mesh=mesh,
        in_specs=(P(None, AXES), split, split, split, split, split, P(AXES), split),
        out_specs=(split, split, split, split, split),
        check_vma=False,
    )
```

```python
import math

import jax
import jax.numpy as jnp
from jax import lax
from jax.experimental import pallas as pl
from jax.experimental.pallas import tpu as pltpu
from jax.sharding import PartitionSpec as P

LAYER = 4
PAD = 8
LONG_SQ = 2.25
RATIO = 25.0
SCALE = 0.5 / LONG_SQ
HALF = math.log(0.5)
OFF = -16384.0
AXES = ("group", "sub")
F32 = jnp.float32
BF16 = jnp.bfloat16


def room(megabytes):
    return pltpu.CompilerParams(vmem_limit_bytes=megabytes * 1024 * 1024)


def split2(value):
    high = value.astype(BF16)
    return high, (value - high.astype(F32)).astype(BF16)


def split3(value):
    high = value.astype(BF16)
    rest = value - high.astype(F32)
    middle = rest.astype(BF16)
    return high, middle, (rest - middle.astype(F32)).astype(BF16)


def mm(left, right):
    return jnp.dot(left, right, preferred_element_type=F32)


def mm_nt(left, right):
    return lax.dot_general(left, right, (((1,), (1,)), ((), ())), preferred_element_type=F32)


def exact(left, right):
    return jnp.dot(left, right, precision=lax.Precision.HIGHEST, preferred_element_type=F32)


def iota(shape, dim):
    return lax.broadcasted_iota(jnp.int32, shape, dim)


def tree_kernel(basis, inner, transfer, points, vectors, dense, top, to_next, to_prev, sems):
    width = basis.shape[0]
    count = basis.shape[1] // width
    halo = LAYER * width
    rows = vectors.shape[0]
    copies = [
        pltpu.make_async_copy(
            vectors.at[pl.ds(start, halo), :], target.at[pl.ds(0, halo), :], sems.at[n]
        )
        for n, (start, target) in enumerate(((rows - halo, to_next), (0, to_prev)))
    ]
    for copy in copies:
        copy.start()

    for target, first, skip in ((to_next, count - PAD, 1), (to_prev, 0, 0)):
        block = basis[:, first * width : (first + PAD) * width]
        pieces = [
            block[:, (at + skip) * width : (at + skip + 3) * width] for at in (0, LAYER)
        ]
        target[halo : halo + width, :] = jnp.concatenate(pieces, axis=1)
        for n in range(2):
            start = (first + n * LAYER) * width
            coords = points[:, start : start + halo]
            high, low = split2(coords)
            base = halo + width + 16 * n
            target[base : base + 16, :] = jnp.zeros((16, target.shape[1]), BF16)
            target[base : base + 3, 0:halo] = high
            target[base + 8 : base + 11, 0:halo] = low

    both = 2 * width
    same = iota((both, both), 0) // width == iota((both, both), 1) // width
    half_block = jnp.where(same, 0.5, 0.0).astype(F32)

    def pair(index):
        return inner[:, index * both : (index + 1) * both]

    blocks = []
    for n in range(count // 4):
        stacked = jnp.concatenate(
            [basis[:, (2 * n + m) * both : (2 * n + m + 1) * both] for m in range(2)], axis=0
        )
        blocks.append(mm_nt(stacked, stacked) * half_block)
    offset = 0
    while True:
        nodes = len(blocks)
        xs, ts = [], []
        for n in range(nodes):
            t = pair(offset + n)
            parts = jnp.concatenate(split3(blocks[n]), axis=0)
            xs.append(mm(jnp.concatenate([t, t, t], axis=1), parts))
            ts.append(t)
        offset += nodes
        if nodes == 1:
            break
        blocks = []
        for n in range(nodes // 2):
            x = jnp.concatenate(split3(jnp.concatenate(xs[2 * n : 2 * n + 2], axis=0)), axis=1)
            t = jnp.concatenate(ts[2 * n : 2 * n + 2], axis=0)
            blocks.append(mm_nt(x, jnp.concatenate([t, t, t], axis=1)) * half_block)
    t = ts[0]
    x = jnp.concatenate(split3(xs[0]), axis=1)
    top_gram = mm_nt(x, jnp.concatenate([t, t, t], axis=1)) * 0.5
    top[...] = top_gram
    matrix = transfer[...]
    gram = exact(exact(matrix.T, top_gram), matrix)
    halves = jnp.concatenate([gram[: width // 2], gram[width // 2 :]], axis=1)
    dense[...] = halves
    parts = jnp.concatenate(split3(halves), axis=1)
    for target in (to_next, to_prev):
        target[halo + width + 32 :, :] = parts
    for copy in copies:
        copy.wait()


def factor_lanes(work, width, beside):
    panels = width // 8
    row = iota((8, 128), 0)

    def spread(j, i):
        return jnp.broadcast_to(work[j, i : i + 1, :], (8, 128))

    for p in range(panels):
        at = 8 * p
        tiles = list(range(p, panels))
        if p:
            for start in range(0, len(tiles), 3):
                group = tiles[start : start + 3]
                accs = [work[at + k, 8 * i : 8 * i + 8, :] for i in group for k in range(8)]

                def step(j, accs, group=group, at=at):
                    factors = [spread(j, at + k) for k in range(8)]
                    out = []
                    for n, i in enumerate(group):
                        column = work[j, 8 * i : 8 * i + 8, :]
                        out += [accs[8 * n + k] - column * factors[k] for k in range(8)]
                    return out

                accs = lax.fori_loop(0, at, step, accs, unroll=4)
                for n, i in enumerate(group):
                    for k in range(8):
                        work[at + k, 8 * i : 8 * i + 8, :] = accs[8 * n + k]
        entry = {(k, m): spread(at + k, at + m) for k in range(8) for m in range(k, 8)}
        scales = []
        for k in range(8):
            scales.append(lax.rsqrt(entry[k, k]))
            for m in range(k + 1, 8):
                entry[k, m] = entry[k, m] * scales[k]
            for m in range(k + 1, 8):
                for q in range(m, 8):
                    entry[m, q] = entry[m, q] - entry[k, m] * entry[k, q]
        for i in tiles:
            tile = [work[at + k, 8 * i : 8 * i + 8, :] for k in range(8)]
            for k in range(8):
                tile[k] = tile[k] * scales[k]
                for m in range(k + 1, 8):
                    tile[m] = tile[m] - tile[k] * entry[k, m]
            for k in range(8):
                work[at + k, 8 * i : 8 * i + 8, :] = (
                    jnp.where(row >= k, tile[k], 0.0) if i == p else tile[k]
                )
        for i in range(p):
            for k in range(8):
                work[at + k, 8 * i : 8 * i + 8, :] = jnp.zeros((8, 128), F32)
        beside(p)


def to_lanes(grams, work, width, many):
    for i in range(width):
        work[i, :, 0:many] = grams[pl.ds(i, many, stride=width), :].T


def from_lanes(work, factors, width, many):
    for j in range(width):
        column = work[j, :, 0:many]
        factors[pl.ds(j, many, stride=width), :] = jnp.concatenate([column, column], axis=0).T


def gaussians(exponent):
    return jnp.exp(exponent) + jnp.exp(exponent * RATIO - RATIO * HALF)


def features(place, leaf, center):
    sub = iota(place.shape, 0)
    corner = jnp.where(sub == 0, leaf % 2 - 1, leaf // 2 % 2 - 1)
    corner = jnp.where(sub == 2, leaf // LAYER - center, corner)
    place = jnp.where(sub < 3, place + corner.astype(F32), 0.0)
    norm = jnp.sum(place * place, axis=0, keepdims=True) * SCALE
    first = jnp.where(sub == 3, -norm, jnp.where(sub == 4, 1.0, place))
    second = jnp.where(
        sub == 3, 1.0, jnp.where(sub == 4, HALF - norm, place * (2.0 * SCALE))
    )
    fh, fm, fl = [v.astype(F32) for v in split3(first)]
    sh, sm, sl = [v.astype(F32) for v in split3(second)]
    return (
        jnp.concatenate([fh, fh, fh, fm, fm, fl], axis=0),
        jnp.concatenate([sh, sm, sl, sh, sm, sh], axis=0),
    )


def rows_of(second):
    blank = jnp.zeros((16, second.shape[1]), F32)
    return jnp.concatenate([second, blank, second, blank], axis=0).T.astype(BF16)


def near_weights(first_rows, second, switches, index, halo):
    group = index // 4 * 16
    columns = jnp.concatenate([second, switches[group : group + 16, :]], axis=0)
    return gaussians(mm(first_rows[index * halo : (index + 1) * halo, :], columns)).astype(BF16)


def prepare(points, near_list, near_used, first_rows, first_cols, second_cols, switches, place):
    rows = points.shape[1]
    own = near_list.shape[1]
    width = rows // own
    place[...] = jnp.zeros(place.shape, F32)
    place[0:3, :] = points[...]
    leaf = iota((8, rows), 1) // width
    first, second = features(place[...], leaf, own // LAYER // 2)
    hot_leaf = iota((16, rows), 1) // width
    hot = jnp.where(hot_leaf % 16 == iota((16, rows), 0), 1.0, 0.0).astype(F32)
    first = jnp.concatenate([first, hot], axis=0)
    first_cols[...] = first.astype(BF16)
    second_cols[...] = second.astype(BF16)
    first_rows[...] = first.T.astype(BF16)

    start_leaf = lax.axis_index(AXES) * own
    target = iota((1, own), 1)
    base_leaf = start_leaf + target // LAYER * LAYER - LAYER
    found = jnp.zeros((16, own), jnp.bool_)
    place_row = iota((16, own), 0)
    for n in range(near_list.shape[0]):
        spot = jnp.where(near_used[...] > n, near_list[n : n + 1, :] - base_leaf, -1)
        found = jnp.logical_or(found, place_row == spot)
    bias = jnp.where(found, 0.0, OFF).astype(F32)
    span = 3 * LAYER * width
    expand = jnp.where(iota((16, span), 0) == iota((16, span), 1) // width, 1.0, 0.0)
    switches[...] = mm(bias.T.astype(BF16), expand.astype(BF16)).astype(BF16)


def inner_layers(layers, vectors, first_rows, second_cols, switches, near, block, sems, halo):
    copies = []
    for n, index in enumerate(layers):
        around = slice((index - 1) * halo, (index + 2) * halo)
        weights = near_weights(first_rows, second_cols[:, around], switches, index, halo)
        block[n, :, :] = mm(weights, vectors[around, :]).astype(BF16)
        copies.append(
            pltpu.make_async_copy(block.at[n], near.at[pl.ds(index * halo, halo), :], sems.at[n])
        )
        copies[-1].start()
    for copy in copies:
        copy.wait()


def first_near_kernel(layers):
    def body(
        points, near_list, near_used, vectors,
        near, first_rows, first_cols, second_cols, switches, place, block, sems,
    ):
        prepare(
            points, near_list, near_used, first_rows, first_cols, second_cols, switches, place
        )
        halo = block.shape[1]
        inner_layers(layers, vectors, first_rows, second_cols, switches, near, block, sems, halo)

    return body


def next_near_kernel(layers):
    def body(after, old, first_rows, second_cols, switches, vectors, near, block, sems):
        halo = block.shape[1]
        inner_layers(layers, vectors, first_rows, second_cols, switches, near, block, sems, halo)

    return body


def leaves_kernel(
    old,
    basis,
    top,
    group_gram,
    root_gram,
    transfer,
    first_rows,
    second_cols,
    switches,
    left,
    right,
    vectors,
    near,
    high,
    low,
    second_rows,
    device_factor,
    group_factor,
    root_factor,
    ends,
    sides,
    place,
    halo_cols,
    block,
    grams,
    work,
    factors,
    sems,
    *,
    members,
    groups,
):
    width = basis.shape[0]
    own = basis.shape[1] // width
    total = own + 2 * PAD
    halo = LAYER * width
    layers = own // LAYER
    both = 2 * width
    extra = sides.shape[1]
    side_copies = [
        pltpu.make_async_copy(side.at[pl.ds(halo, extra), :], sides.at[n], sems.at[n])
        for n, side in enumerate((left, right))
    ]
    end_copies = [
        pltpu.make_async_copy(side.at[pl.ds(0, halo), :], ends.at[n], sems.at[2 + n])
        for n, side in enumerate((left, right))
    ]
    for copy in side_copies + end_copies:
        copy.start()

    lane = iota((width, both), 1)
    for n in range(own // 2):
        pair = basis[:, n * both : (n + 1) * both]
        zero = jnp.zeros_like(pair)
        stacked = jnp.concatenate(
            [jnp.where(lane < width, pair, zero), jnp.where(lane < width, zero, pair)], axis=0
        )
        at = (PAD + 2 * n) * width
        grams[at : at + both, :] = mm_nt(stacked, pair)
    spare = (0, LAYER, total - LAYER - 1, total - 1)
    for spot, gram in zip(
        spare,
        (
            top[...],
            group_gram[...] * (1.0 / members),
            root_gram[...] * (1.0 / (members * groups)),
            top[...],
        ),
    ):
        if gram.shape[0] < width:
            gram = jnp.concatenate([gram[:, :width], gram[:, width:]], axis=0)
        grams[spot * width : (spot + 1) * width, :] = gram
    for copy in side_copies:
        copy.wait()
    for side, spots in enumerate(
        ((1, 2, 3, 5, 6, 7), tuple(PAD + own + m for m in (0, 1, 2, 4, 5, 6)))
    ):
        for n, spot in enumerate(spots):
            piece = sides[side, 0:width, n * width : (n + 1) * width]
            grams[spot * width : (spot + 1) * width, :] = mm_nt(piece, piece)

    lanes = PAD * width
    place[...] = jnp.zeros(place.shape, F32)
    for side, first_leaf in enumerate((-PAD, own)):
        for n in range(2):
            base = width + 16 * n
            values = sides[side, base : base + 16, 0:halo].astype(F32)
            place[0:3, n * halo : (n + 1) * halo] = values[0:3, :] + values[8:11, :]
        leaf = iota((8, lanes), 1) // width + (first_leaf + PAD)
        second = features(place[...], leaf, layers // 2 + PAD // LAYER)[1]
        halo_cols[side, :, :] = second.astype(BF16)
        at = (PAD + first_leaf) * width
        second_rows[at : at + lanes, :] = rows_of(second)
    for n in range(own * width // 512):
        at = PAD * width + n * 512
        second_rows[at : at + 512, :] = rows_of(
            second_cols[:, n * 512 : (n + 1) * 512].astype(F32)
        )

    copies = [
        pltpu.make_async_copy(block.at[n], near.at[pl.ds(index * halo, halo), :], sems.at[4 + n])
        for n, index in enumerate((0, layers - 1))
    ]

    def edge(n):
        if n == 0:
            columns = [halo_cols[0, :, halo:], second_cols[:, 0 : 2 * halo]]
            index = 0
        else:
            columns = [second_cols[:, (layers - 2) * halo :], halo_cols[1, :, 0:halo]]
            index = layers - 1
        weights = near_weights(
            first_rows, jnp.concatenate(columns, axis=1), switches, index, halo
        )
        if n == 0:
            value = mm(weights[:, 0:halo], ends[0, :, :])
            value = value + mm(weights[:, halo:], vectors[0 : 2 * halo, :])
        else:
            value = mm(weights[:, 0 : 2 * halo], vectors[(layers - 2) * halo :, :])
            value = value + mm(weights[:, 2 * halo :], ends[1, :, :])
        block[n, :, :] = value.astype(BF16)
        copies[n].start()

    def beside(p):
        if p in (1, 3):
            edge(p // 2)

    to_lanes(grams, work, width, total)
    for copy in end_copies:
        copy.wait()
    factor_lanes(work, width, beside)
    from_lanes(work, factors, width, total)
    device_factor[...] = exact(factors[0:width, 0:width], transfer[...])
    for target, spot in ((group_factor, spare[1]), (root_factor, spare[2])):
        target[...] = factors[spot * width : (spot + 1) * width, 0:width]
    high_part, low_part = split2(factors[...])
    high[...] = high_part
    low[...] = low_part
    for copy in copies:
        copy.wait()


def far_kernel(far_list, high, low, second_rows, first_cols, coupling):
    width = coupling.shape[0]
    far, own = far_list.shape
    both = 2 * width
    start_leaf = lax.axis_index(AXES) * own
    square = iota((both, both), 0) // width == iota((both, both), 1) // width
    lane_far = iota((width, both), 1) < width
    lane_wide = iota((far * width, both), 1) < width

    def far_pair(index):
        t = 2 * index
        spots = [
            [
                pl.multiple_of((far_list[f, t + m] - start_leaf + PAD) * width, width)
                for f in range(far)
            ]
            for m in range(2)
        ]
        picked = [
            jnp.concatenate([second_rows[pl.ds(s, width), :] for s in spots[m]], axis=0)
            for m in range(2)
        ]
        sources = jnp.where(lane_wide, picked[0], picked[1])
        at = (PAD + t) * width
        own_cols = first_cols[:, t * width : t * width + both]
        zero = jnp.zeros((both, both), BF16)
        targets = jnp.where(square, jnp.concatenate([own_cols, own_cols], axis=0), zero)
        kernel_block = gaussians(mm(sources, targets))
        kh, kl = split2(kernel_block)
        rh = jnp.where(square, high[pl.ds(at, both), :], zero)
        rl = jnp.where(square, low[pl.ds(at, both), :], zero)
        half = mm_nt(
            jnp.concatenate([kh, kl, kh], axis=1), jnp.concatenate([rh, rh, rl], axis=1)
        ) * (1.0 / width)
        zh, zl = split2(half)
        outs = []
        for f in range(far):
            a = slice(f * width, (f + 1) * width)
            sh = jnp.where(
                lane_far, high[pl.ds(spots[0][f], width), :], high[pl.ds(spots[1][f], width), :]
            )
            sl = jnp.where(
                lane_far, low[pl.ds(spots[0][f], width), :], low[pl.ds(spots[1][f], width), :]
            )
            ph = jnp.where(square, jnp.concatenate([zh[a], zh[a]], axis=0), zero)
            plow = jnp.where(square, jnp.concatenate([zl[a], zl[a]], axis=0), zero)
            outs.append(
                mm(jnp.concatenate([sh, sh, sl], axis=1), jnp.concatenate([ph, plow, ph], axis=0))
            )
        line = jnp.concatenate(
            [out[:, 0:width] for out in outs] + [out[:, width:both] for out in outs], axis=1
        )
        coupling[:, pl.ds(index * 2 * far * width, 2 * far * width)] = line.astype(BF16)

    for index in range(own // 2):
        far_pair(index)


def shift(block, distance):
    devices = range(lax.axis_size(AXES))
    route = [(i - distance, i) for i in devices if i - distance in devices]
    return lax.ppermute(block, AXES, route)


def exchange(value, axis, bit):
    mask = 2**bit
    pairs = [(source, source ^ mask) for source in range(lax.axis_size(axis))]
    return value + lax.ppermute(value, axis, pairs)


def per_device(
    points, leaf_basis, inner_transfer, device_transfer, vectors, near_index, near_count, far_index
):
    own = near_index.shape[0]
    width = leaf_basis.shape[1]
    columns = vectors.shape[1]
    halo = LAYER * width
    half = width // 2
    layers = own // LAYER
    total = own + 2 * PAD
    members, groups = lax.axis_size("sub"), lax.axis_size("group")
    vmem = pl.BlockSpec(memory_space=pltpu.VMEM)
    smem = pl.BlockSpec(memory_space=pltpu.SMEM)
    hbm = pl.BlockSpec(memory_space=pl.ANY)
    square = jax.ShapeDtypeStruct((width, width), F32)
    sent = jax.ShapeDtypeStruct((halo + width + 32 + half, columns), BF16)
    product = jax.ShapeDtypeStruct(vectors.shape, BF16)
    basis = leaf_basis.T

    dense, top, to_next, to_prev = pl.pallas_call(
        tree_kernel,
        out_shape=(jax.ShapeDtypeStruct((half, 2 * width), F32), square, sent, sent),
        in_specs=[vmem, vmem, vmem, vmem, hbm],
        out_specs=(vmem, vmem, vmem, vmem),
        scratch_shapes=[pltpu.SemaphoreType.DMA((2,))],
        compiler_params=room(8),
        name="tree",
    )(basis, inner_transfer.T, device_transfer, points, vectors)
    left = shift(to_next, 1)
    right = shift(to_prev, -1)

    steps = [("sub", bit) for bit in range(1, members.bit_length() - 1)]
    steps += [("group", bit) for bit in range(groups.bit_length() - 1)]
    inner = list(range(1, layers - 1))
    chunks = [inner[:2]] + [[index] for index in inner[2:]]
    scratch = [
        pltpu.VMEM((2, halo, columns), BF16),
        pltpu.SemaphoreType.DMA((2,)),
    ]
    near, first_rows, first_cols, second_cols, switches = pl.pallas_call(
        first_near_kernel(chunks[0]),
        out_shape=(
            product,
            jax.ShapeDtypeStruct((own * width, 64), BF16),
            jax.ShapeDtypeStruct((64, own * width), BF16),
            jax.ShapeDtypeStruct((48, own * width), BF16),
            jax.ShapeDtypeStruct((own, 3 * halo), BF16),
        ),
        in_specs=[vmem] * 4,
        out_specs=(hbm,) + (vmem,) * 4,
        scratch_shapes=[pltpu.VMEM((8, own * width), F32)] + scratch,
        compiler_params=room(10),
        cost_estimate=pl.CostEstimate(
            flops=10**9, bytes_accessed=4 * 10**6, transcendentals=10**6
        ),
        name="near_0",
    )(points, near_index.T, near_count.reshape(1, own), vectors)

    odd = lax.axis_index("sub") % 2 == 1
    other = jnp.where(odd, left[halo + width + 32 :, :], right[halo + width + 32 :, :])
    parts = [other[:, n * 2 * width : (n + 1) * 2 * width].astype(F32) for n in range(3)]
    gram = dense + (parts[0] + (parts[1] + parts[2]))
    group_gram = gram
    for n, (axis, bit) in enumerate(steps):
        before = gram
        gram = exchange(gram, axis, bit)
        if axis == "sub":
            group_gram = gram
        if n + 1 < len(chunks):
            near = pl.pallas_call(
                next_near_kernel(chunks[n + 1]),
                out_shape=product,
                in_specs=[hbm, hbm] + [vmem] * 4,
                out_specs=hbm,
                scratch_shapes=scratch,
                input_output_aliases={1: 0},
                compiler_params=room(10),
                cost_estimate=pl.CostEstimate(
                    flops=10**9, bytes_accessed=4 * 10**6, transcendentals=10**6
                ),
                name=f"near_{n + 1}",
            )(before, near, first_rows, second_cols, switches, vectors)
            gram, near = lax.optimization_barrier((gram, near))

    split_factors = jax.ShapeDtypeStruct((total * width, 2 * width), BF16)
    near, high, low, second_rows, device_factor, group_factor, root_factor = pl.pallas_call(
        lambda *refs: leaves_kernel(*refs, members=members, groups=groups),
        out_shape=(product, split_factors, split_factors, split_factors, square, square, square),
        in_specs=[hbm] + [vmem] * 8 + [hbm] * 2 + [vmem],
        out_specs=(hbm,) + (vmem,) * 6,
        scratch_shapes=[
            pltpu.VMEM((2, halo, columns), BF16),
            pltpu.VMEM((2, width + 32, columns), BF16),
            pltpu.VMEM((8, PAD * width), F32),
            pltpu.VMEM((2, 48, PAD * width), BF16),
            pltpu.VMEM((2, halo, columns), BF16),
            pltpu.VMEM((total * width, width), F32),
            pltpu.VMEM((width, width, 128), F32),
            pltpu.VMEM((total * width, 2 * width), F32),
            pltpu.SemaphoreType.DMA((6,)),
        ],
        input_output_aliases={0: 0},
        compiler_params=room(24),
        name="leaves",
    )(
        near,
        basis,
        top,
        group_gram,
        gram,
        device_transfer,
        first_rows,
        second_cols,
        switches,
        left,
        right,
        vectors,
    )

    coupling = pl.pallas_call(
        far_kernel,
        out_shape=jax.ShapeDtypeStruct((width, own * far_index.shape[1] * width), BF16),
        in_specs=[smem] + [vmem] * 4,
        out_specs=vmem,
        compiler_params=room(16),
        name="far",
    )(far_index.T, high, low, second_rows, first_cols)
    return near, coupling.T, device_factor, group_factor, root_factor


def solution(mesh):
    split = P(AXES, None)
    return jax.shard_map(
        per_device,
        mesh=mesh,
        in_specs=(P(None, AXES), split, split, split, split, split, P(AXES), split),
        out_specs=(split, split, split, split, split),
        check_vma=False,
    )
```

```python
import functools
import math

import jax
import jax.numpy as jnp
from jax import lax
from jax.experimental import pallas as pl
from jax.experimental.pallas import tpu as pltpu
from jax.sharding import PartitionSpec as P

LAYER = 4
PAD = 8
LONG_SQ = 2.25
RATIO = 25.0
SCALE = 0.5 / LONG_SQ
HALF = math.log(0.5)
OFF = -16384.0
STRIDE = 72
AXES = ("group", "sub")
F32 = jnp.float32
BF16 = jnp.bfloat16


def room(megabytes):
    return pltpu.CompilerParams(vmem_limit_bytes=megabytes * 1024 * 1024)


def split2(value):
    high = value.astype(BF16)
    return high, (value - high.astype(F32)).astype(BF16)


def split3(value):
    high = value.astype(BF16)
    rest = value - high.astype(F32)
    middle = rest.astype(BF16)
    return high, middle, (rest - middle.astype(F32)).astype(BF16)


def mm(left, right):
    return jnp.dot(left, right, preferred_element_type=F32)


def mm_nt(left, right):
    return lax.dot_general(left, right, (((1,), (1,)), ((), ())), preferred_element_type=F32)


def exact(left, right):
    return jnp.dot(left, right, precision=lax.Precision.HIGHEST, preferred_element_type=F32)


def iota(shape, dim):
    return lax.broadcasted_iota(jnp.int32, shape, dim)


def tree_kernel(
    points_in, basis_in, inner_in, transfer_in, vectors,
    dense, top, to_next, to_prev, points, basis, inner, transfer, sems,
):
    width = basis.shape[0]
    count = basis.shape[1] // width
    halo = LAYER * width
    rows = vectors.shape[0]
    sides = ((to_next, rows - halo, (count - PAD) * width, 1), (to_prev, 0, 0, 0))
    basis_copy, inner_copy, points_copy, transfer_copy = loads = [
        pltpu.make_async_copy(source, target, sems.at[n])
        for n, (source, target) in enumerate(
            (
                (basis_in, basis),
                (inner_in, inner),
                (points_in, points),
                (transfer_in, transfer),
            )
        )
    ]
    copies = [
        pltpu.make_async_copy(
            vectors.at[pl.ds(start, halo), :], target.at[pl.ds(0, halo), :], sems.at[4 + n]
        )
        for n, (target, start, _, _) in enumerate(sides)
    ]
    for copy in loads + copies:
        copy.start()
    basis_copy.wait()
    points_copy.wait()
    transfer_copy.wait()

    for target, _, start, skip in sides:
        pieces = [
            basis[:, start + (at + skip) * width : start + (at + skip + 3) * width]
            for at in (0, LAYER)
        ]
        target[halo : halo + width, :] = jnp.concatenate(pieces, axis=1)
        for n in range(2):
            high, low = split2(points[:, start + n * halo : start + (n + 1) * halo])
            base = halo + width + 16 * n
            target[base : base + 16, :] = jnp.zeros((16, target.shape[1]), BF16)
            target[base : base + 3, 0:halo] = high
            target[base + 8 : base + 11, 0:halo] = low

    both = 2 * width
    same = iota((both, both), 0) // width == iota((both, both), 1) // width
    half_block = jnp.where(same, 0.5, 0.0).astype(F32)

    def pair(index):
        return inner[:, index * both : (index + 1) * both]

    blocks = []
    for n in range(count // 4):
        stacked = jnp.concatenate(
            [basis[:, (2 * n + m) * both : (2 * n + m + 1) * both] for m in range(2)], axis=0
        )
        blocks.append(mm_nt(stacked, stacked) * half_block)
    inner_copy.wait()
    offset = 0
    while True:
        nodes = len(blocks)
        xs, ts = [], []
        for n in range(nodes):
            t = pair(offset + n)
            parts = jnp.concatenate(split3(blocks[n]), axis=0)
            xs.append(mm(jnp.concatenate([t, t, t], axis=1), parts))
            ts.append(t)
        offset += nodes
        if nodes == 1:
            break
        blocks = []
        for n in range(nodes // 2):
            x = jnp.concatenate(split3(jnp.concatenate(xs[2 * n : 2 * n + 2], axis=0)), axis=1)
            t = jnp.concatenate(ts[2 * n : 2 * n + 2], axis=0)
            blocks.append(mm_nt(x, jnp.concatenate([t, t, t], axis=1)) * half_block)
    t = ts[0]
    x = jnp.concatenate(split3(xs[0]), axis=1)
    top_gram = mm_nt(x, jnp.concatenate([t, t, t], axis=1)) * 0.5
    top[...] = top_gram
    matrix = transfer[...]
    gram = exact(exact(matrix.T, top_gram), matrix)
    dense[...] = jnp.concatenate([gram[: width // 2], gram[width // 2 :]], axis=1)
    for copy in copies:
        copy.wait()


def factor_lanes(work, width, beside):
    panels = width // 8
    row = iota((8, 128), 0)

    def spread(j, i):
        return jnp.broadcast_to(work[j, i : i + 1, :], (8, 128))

    for p in range(panels):
        at = 8 * p
        tiles = list(range(p, panels))
        if p:
            for start in range(0, len(tiles), 3):
                group = tiles[start : start + 3]
                accs = [work[at + k, 8 * i : 8 * i + 8, :] for i in group for k in range(8)]

                def step(j, accs, group=group, at=at):
                    factors = [spread(j, at + k) for k in range(8)]
                    out = []
                    for n, i in enumerate(group):
                        column = work[j, 8 * i : 8 * i + 8, :]
                        out += [accs[8 * n + k] - column * factors[k] for k in range(8)]
                    return out

                accs = lax.fori_loop(0, at, step, accs, unroll=4)
                for n, i in enumerate(group):
                    for k in range(8):
                        work[at + k, 8 * i : 8 * i + 8, :] = accs[8 * n + k]
        entry = {(k, m): spread(at + k, at + m) for k in range(8) for m in range(k, 8)}
        scales = []
        for k in range(8):
            scales.append(lax.rsqrt(entry[k, k]))
            for m in range(k + 1, 8):
                entry[k, m] = entry[k, m] * scales[k]
            for m in range(k + 1, 8):
                for q in range(m, 8):
                    entry[m, q] = entry[m, q] - entry[k, m] * entry[k, q]
        for i in tiles:
            tile = [work[at + k, 8 * i : 8 * i + 8, :] for k in range(8)]
            for k in range(8):
                tile[k] = tile[k] * scales[k]
                for m in range(k + 1, 8):
                    tile[m] = tile[m] - tile[k] * entry[k, m]
            for k in range(8):
                work[at + k, 8 * i : 8 * i + 8, :] = (
                    jnp.where(row >= k, tile[k], 0.0) if i == p else tile[k]
                )
        for i in range(p):
            for k in range(8):
                work[at + k, 8 * i : 8 * i + 8, :] = jnp.zeros((8, 128), F32)
        beside(p)


def to_lanes(grams, work, width, many):
    for i in range(width):
        work[i, :, 0:many] = grams[pl.ds(i, many, stride=STRIDE), :].T


def from_lanes(work, factors, width, many):
    for j in range(width):
        column = work[j, :, 0:many]
        factors[pl.ds(j, many, stride=STRIDE), :] = jnp.concatenate([column, column], axis=0).T


def gaussians(exponent):
    return jnp.exp(exponent) + jnp.exp(exponent * RATIO - RATIO * HALF)


def features(place, leaf, center):
    sub = iota(place.shape, 0)
    corner = jnp.where(sub == 0, leaf % 2 - 1, leaf // 2 % 2 - 1)
    corner = jnp.where(sub == 2, leaf // LAYER - center, corner)
    place = jnp.where(sub < 3, place + corner.astype(F32), 0.0)
    norm = jnp.sum(place * place, axis=0, keepdims=True) * SCALE
    first = jnp.where(sub == 3, -norm, jnp.where(sub == 4, 1.0, place))
    second = jnp.where(
        sub == 3, 1.0, jnp.where(sub == 4, HALF - norm, place * (2.0 * SCALE))
    )
    fh, fm, fl = [v.astype(F32) for v in split3(first)]
    sh, sm, sl = [v.astype(F32) for v in split3(second)]
    return (
        jnp.concatenate([fh, fh, fh, fm, fm, fl], axis=0),
        jnp.concatenate([sh, sm, sl, sh, sm, sh], axis=0),
    )


def rows_of(second):
    blank = jnp.zeros((16, second.shape[1]), F32)
    return jnp.concatenate([second, blank, second, blank], axis=0).T.astype(BF16)


def near_weights(first_rows, second, switches, index, halo):
    group = index // 4 * 16
    columns = jnp.concatenate([second, switches[group : group + 16, :]], axis=0)
    return gaussians(mm(first_rows[index * halo : (index + 1) * halo, :], columns)).astype(BF16)


def prepare(
    points, near_list, near_used, first_rows, first_cols, second_cols, second_rows, switches, place
):
    rows = points.shape[1]
    own = near_list.shape[1]
    width = rows // own
    place[...] = jnp.zeros(place.shape, F32)
    place[0:3, :] = points[...]
    leaf = iota((8, rows), 1) // width
    first, second = features(place[...], leaf, own // LAYER // 2)
    hot_leaf = iota((16, rows), 1) // width
    hot = jnp.where(hot_leaf % 16 == iota((16, rows), 0), 1.0, 0.0).astype(F32)
    first = jnp.concatenate([first, hot], axis=0)
    first_cols[...] = first.astype(BF16)
    second_cols[...] = second.astype(BF16)
    first_rows[...] = first.T.astype(BF16)
    second_rows[...] = rows_of(second)

    start_leaf = lax.axis_index(AXES) * own
    target = iota((1, own), 1)
    base_leaf = start_leaf + target // LAYER * LAYER - LAYER
    found = jnp.zeros((16, own), jnp.bool_)
    place_row = iota((16, own), 0)
    for n in range(near_list.shape[0]):
        spot = jnp.where(near_used[...] > n, near_list[n : n + 1, :] - base_leaf, -1)
        found = jnp.logical_or(found, place_row == spot)
    bias = jnp.where(found, 0.0, OFF).astype(F32)
    span = 3 * LAYER * width
    expand = jnp.where(iota((16, span), 0) == iota((16, span), 1) // width, 1.0, 0.0)
    switches[...] = mm(bias.T.astype(BF16), expand.astype(BF16)).astype(BF16)


def inner_layers(layers, vectors, first_rows, second_cols, switches, out, halo):
    for n, index in enumerate(layers):
        around = slice((index - 1) * halo, (index + 2) * halo)
        weights = near_weights(first_rows, second_cols[:, around], switches, index, halo)
        out[n * halo : (n + 1) * halo, :] = mm(weights, vectors[around, :]).astype(BF16)


def far_blocks(pairs, far_list, second_rows, first_cols, out, width, base, places):
    far, own = far_list.shape
    both = 2 * width
    start_leaf = lax.axis_index(AXES) * own
    square = iota((both, both), 0) // width == iota((both, both), 1) // width
    lane = iota((far * width, both), 1) < width
    exponents = []
    for index in pairs:
        t = 2 * index
        picked = []
        for m in range(2):
            spots = [
                pl.multiple_of((far_list[f, t + m] - start_leaf + base) * width, width)
                for f in range(far)
            ]
            picked.append(
                jnp.concatenate([second_rows[pl.ds(spot, width), :] for spot in spots], axis=0)
            )
        cols = first_cols[:, t * width : t * width + both]
        targets = jnp.where(
            square, jnp.concatenate([cols, cols], axis=0), jnp.zeros((both, both), BF16)
        )
        exponents.append(mm(jnp.where(lane, picked[0], picked[1]), targets))
    for place, exponent in zip(places, exponents):
        high, low = split2(gaussians(exponent))
        at = place * far * width
        out[at : at + far * width, 0:both] = high
        out[at : at + far * width, both : 2 * both] = low


def first_chunk_kernel(layers):
    def body(
        points, near_list, near_used, vectors,
        out, first_rows, first_cols, second_cols, second_rows, switches, place,
    ):
        prepare(
            points,
            near_list,
            near_used,
            first_rows,
            first_cols,
            second_cols,
            second_rows,
            switches,
            place,
        )
        halo = LAYER * points.shape[1] // near_list.shape[1]
        inner_layers(layers, vectors, first_rows, second_cols, switches, out, halo)

    return body


def next_chunk_kernel(layers, pairs):
    def body(
        after, far_list, first_rows, first_cols, second_cols, second_rows, switches, vectors, *outs
    ):
        width = vectors.shape[0] // far_list.shape[1]
        if layers:
            inner_layers(
                layers, vectors, first_rows, second_cols, switches, outs[0], LAYER * width
            )
        if pairs:
            far_blocks(
                pairs, far_list, second_rows, first_cols, outs[-1], width, 0, range(len(pairs))
            )

    return body


def leaves_kernel(chunks, edge_pairs, members, groups, *refs):
    outer = len(chunks)
    inner_near = refs[:outer]
    (
        far_list,
        basis,
        top,
        group_gram,
        root_gram,
        transfer,
        first_rows,
        first_cols,
        second_cols,
        own_rows,
        switches,
        left,
        right,
        vectors,
        near,
        high,
        low,
        edge_blocks,
        device_factor,
        group_factor,
        root_factor,
        ends,
        sides,
        place,
        halo_cols,
        second_rows,
        block,
        grams,
        work,
        factors,
        sems,
    ) = refs[outer:]
    width = basis.shape[0]
    own = basis.shape[1] // width
    total = own + 2 * PAD
    halo = LAYER * width
    layers = own // LAYER
    both = 2 * width
    extra = sides.shape[1]
    side_copies = [
        pltpu.make_async_copy(side.at[pl.ds(halo, extra), :], sides.at[n], sems.at[n])
        for n, side in enumerate((left, right))
    ]
    end_copies = [
        pltpu.make_async_copy(side.at[pl.ds(0, halo), :], ends.at[n], sems.at[2 + n])
        for n, side in enumerate((left, right))
    ]
    near_copies = [
        pltpu.make_async_copy(
            part, near.at[pl.ds(chunk[0] * halo, len(chunk) * halo), :], sems.at[6 + n]
        )
        for n, (part, chunk) in enumerate(zip(inner_near, chunks))
    ]
    for copy in side_copies + end_copies + near_copies:
        copy.start()

    lane = iota((width, both), 1)
    for n in range(own // 2):
        pair = basis[:, n * both : (n + 1) * both]
        zero = jnp.zeros_like(pair)
        stacked = jnp.concatenate(
            [jnp.where(lane < width, pair, zero), jnp.where(lane < width, zero, pair)], axis=0
        )
        value = mm_nt(stacked, pair)
        for m in range(2):
            at = (PAD + 2 * n + m) * STRIDE
            grams[at : at + width, :] = value[m * width : (m + 1) * width]
    spare = (0, LAYER, total - LAYER - 1, total - 1)
    for spot, gram in zip(
        spare,
        (
            top[...],
            group_gram[...] * (1.0 / members),
            root_gram[...] * (1.0 / (members * groups)),
            top[...],
        ),
    ):
        if gram.shape[0] < width:
            gram = jnp.concatenate([gram[:, :width], gram[:, width:]], axis=0)
        grams[spot * STRIDE : spot * STRIDE + width, :] = gram
    for copy in side_copies:
        copy.wait()
    for side, spots in enumerate(
        ((1, 2, 3, 5, 6, 7), tuple(PAD + own + m for m in (0, 1, 2, 4, 5, 6)))
    ):
        for n, spot in enumerate(spots):
            piece = sides[side, 0:width, n * width : (n + 1) * width]
            grams[spot * STRIDE : spot * STRIDE + width, :] = mm_nt(piece, piece)

    lanes = PAD * width
    place[...] = jnp.zeros(place.shape, F32)
    for side, first_leaf in enumerate((-PAD, own)):
        for n in range(2):
            base = width + 16 * n
            values = sides[side, base : base + 16, 0:halo].astype(F32)
            place[0:3, n * halo : (n + 1) * halo] = values[0:3, :] + values[8:11, :]
        leaf = iota((8, lanes), 1) // width + (first_leaf + PAD)
        second = features(place[...], leaf, layers // 2 + PAD // LAYER)[1]
        halo_cols[side, :, :] = second.astype(BF16)
        at = (PAD + first_leaf) * width
        second_rows[at : at + lanes, :] = rows_of(second)
    second_rows[lanes : lanes + own * width, :] = own_rows[...]

    copies = [
        pltpu.make_async_copy(block.at[n], near.at[pl.ds(index * halo, halo), :], sems.at[4 + n])
        for n, index in enumerate((0, layers - 1))
    ]

    def edge(n):
        if n == 0:
            columns = [halo_cols[0, :, halo:], second_cols[:, 0 : 2 * halo]]
            index = 0
        else:
            columns = [second_cols[:, (layers - 2) * halo :], halo_cols[1, :, 0:halo]]
            index = layers - 1
        weights = near_weights(
            first_rows, jnp.concatenate(columns, axis=1), switches, index, halo
        )
        if n == 0:
            value = mm(weights[:, 0:halo], ends[0, :, :])
            value = value + mm(weights[:, halo:], vectors[0 : 2 * halo, :])
        else:
            value = mm(weights[:, 0 : 2 * halo], vectors[(layers - 2) * halo :, :])
            value = value + mm(weights[:, 2 * halo :], ends[1, :, :])
        block[n, :, :] = value.astype(BF16)
        copies[n].start()

    panels = width // 8

    def beside(p):
        if p in (1, 3):
            edge(p // 2)
        places = range(p * len(edge_pairs) // panels, (p + 1) * len(edge_pairs) // panels)
        far_blocks(
            [edge_pairs[n] for n in places],
            far_list,
            second_rows,
            first_cols,
            edge_blocks,
            width,
            PAD,
            places,
        )

    to_lanes(grams, work, width, total)
    for copy in end_copies:
        copy.wait()
    factor_lanes(work, width, beside)
    from_lanes(work, factors, width, total)
    device_factor[...] = exact(factors[0:width, 0:width], transfer[...])
    for target, spot in ((group_factor, spare[1]), (root_factor, spare[2])):
        target[...] = factors[spot * STRIDE : spot * STRIDE + width, 0:width]
    for spot in range(total):
        at = slice(spot * width, (spot + 1) * width)
        high[at, :], low[at, :] = split2(factors[spot * STRIDE : spot * STRIDE + width, :])
    for copy in copies + near_copies:
        copy.wait()


def far_kernel(plan, far_list, high, low, *refs):
    blocks, coupling = refs[:-1], refs[-1]
    width = coupling.shape[0]
    far, own = far_list.shape
    both = 2 * width
    start_leaf = lax.axis_index(AXES) * own
    square = iota((both, both), 0) // width == iota((both, both), 1) // width
    lane = iota((width, both), 1) < width
    zero = jnp.zeros((both, both), BF16)

    def diagonal(value):
        return jnp.where(square, value, zero)

    for start in range(0, own // 2, 4):
        indices = range(start, start + 4)
        halves = []
        for index in indices:
            source, place = plan[index]
            at = place * far * width
            kh = blocks[source][at : at + far * width, 0:both]
            kl = blocks[source][at : at + far * width, both : 2 * both]
            at = (PAD + 2 * index) * width
            rh = diagonal(high[at : at + both, :])
            rl = diagonal(low[at : at + both, :])
            halves.append(
                mm_nt(
                    jnp.concatenate([kh, kl, kh], axis=1), jnp.concatenate([rh, rh, rl], axis=1)
                )
            )
        outs = []
        for index, half in zip(indices, halves):
            zh, zl = split2(half * (1.0 / width))
            for f in range(far):
                spots = [
                    pl.multiple_of((far_list[f, 2 * index + m] - start_leaf + PAD) * width, width)
                    for m in range(2)
                ]
                sh, sl = (
                    jnp.where(lane, *(part[pl.ds(spot, width), :] for spot in spots))
                    for part in (high, low)
                )
                a = slice(f * width, (f + 1) * width)
                ph = diagonal(jnp.concatenate([zh[a], zh[a]], axis=0))
                plow = diagonal(jnp.concatenate([zl[a], zl[a]], axis=0))
                outs.append(
                    mm(
                        jnp.concatenate([sh, sh, sl], axis=1),
                        jnp.concatenate([ph, plow, ph], axis=0),
                    )
                )
        for n, index in enumerate(indices):
            three = outs[n * far : (n + 1) * far]
            line = jnp.concatenate(
                [out[:, 0:width] for out in three] + [out[:, width:both] for out in three], axis=1
            )
            at = index * 2 * far * width
            coupling[:, at : at + 2 * far * width] = line.astype(BF16)


def shift(block, distance):
    devices = range(lax.axis_size(AXES))
    route = [(i - distance, i) for i in devices if i - distance in devices]
    return lax.ppermute(block, AXES, route)


def exchange(value, axis, bit):
    mask = 2**bit
    pairs = [(source, source ^ mask) for source in range(lax.axis_size(axis))]
    return value + lax.ppermute(value, axis, pairs)


def per_device(
    points, leaf_basis, inner_transfer, device_transfer, vectors, near_index, near_count, far_index
):
    own = near_index.shape[0]
    width = leaf_basis.shape[1]
    columns = vectors.shape[1]
    halo = LAYER * width
    half = width // 2
    layers = own // LAYER
    total = own + 2 * PAD
    members, groups = lax.axis_size("sub"), lax.axis_size("group")
    vmem = pl.BlockSpec(memory_space=pltpu.VMEM)
    smem = pl.BlockSpec(memory_space=pltpu.SMEM)
    hbm = pl.BlockSpec(memory_space=pl.ANY)
    square = jax.ShapeDtypeStruct((width, width), F32)
    sent = jax.ShapeDtypeStruct((halo + width + 32, columns), BF16)
    basis = leaf_basis.T
    near_list, far_list = near_index.T, far_index.T
    cost = pl.CostEstimate(flops=10**9, bytes_accessed=4 * 10**6, transcendentals=10**6)

    dense, top, to_next, to_prev = pl.pallas_call(
        tree_kernel,
        out_shape=(jax.ShapeDtypeStruct((half, 2 * width), F32), square, sent, sent),
        in_specs=[hbm] * 5,
        out_specs=(vmem,) * 4,
        scratch_shapes=[
            pltpu.VMEM((3, own * width), F32),
            pltpu.VMEM((width, own * width), BF16),
            pltpu.VMEM((width, (own - 2) * width), BF16),
            pltpu.VMEM((width, width), F32),
            pltpu.SemaphoreType.DMA((6,)),
        ],
        compiler_params=room(60),
        name="tree",
    )(points, basis, inner_transfer.T, device_transfer, vectors)
    left = shift(to_next, 1)
    right = shift(to_prev, -1)

    steps = [("sub", bit) for bit in range(members.bit_length() - 1)]
    steps += [("group", bit) for bit in range(groups.bit_length() - 1)]
    chunks = [[1], [2, 3], [4, 5], [6], []]
    inner_pairs = list(range(PAD // 2, (own - PAD) // 2))
    few = len(inner_pairs) // 2 - 1
    pair_chunks = [[], [], [], inner_pairs[:few], inner_pairs[few:]]
    blocks, plan, parts = [], {}, []

    def part_shape(count):
        return jax.ShapeDtypeStruct((count * halo, columns), BF16)

    def block_shape(count):
        return jax.ShapeDtypeStruct((count * far_index.shape[1] * width, 4 * width), BF16)

    late_points, dense = lax.optimization_barrier((points, dense))
    part, *shared = pl.pallas_call(
        first_chunk_kernel(chunks[0]),
        out_shape=(
            part_shape(len(chunks[0])),
            jax.ShapeDtypeStruct((own * width, 64), BF16),
            jax.ShapeDtypeStruct((64, own * width), BF16),
            jax.ShapeDtypeStruct((48, own * width), BF16),
            jax.ShapeDtypeStruct((own * width, 128), BF16),
            jax.ShapeDtypeStruct((own, 3 * halo), BF16),
        ),
        in_specs=[vmem] * 4,
        out_specs=(vmem,) * 6,
        scratch_shapes=[pltpu.VMEM((8, own * width), F32)],
        compiler_params=room(10),
        cost_estimate=cost,
        name="chunk_0",
    )(late_points, near_list, near_count.reshape(1, own), vectors)
    parts.append(part)
    gram = group_gram = dense
    for n in range(max(len(steps), len(chunks))):
        before = gram
        if n < len(steps):
            axis, bit = steps[n]
            gram = exchange(gram, axis, bit)
            if axis == "sub":
                group_gram = gram
        if n == 0:
            gram, parts[0] = lax.optimization_barrier((gram, parts[0]))
        elif n < len(chunks):
            layer_chunk, pair_chunk = chunks[n], pair_chunks[n]
            shapes = [part_shape(len(layer_chunk))] * bool(layer_chunk)
            shapes += [block_shape(len(pair_chunk))] * bool(pair_chunk)
            outs = pl.pallas_call(
                next_chunk_kernel(layer_chunk, pair_chunk),
                out_shape=tuple(shapes),
                in_specs=[hbm, smem] + [vmem] * 6,
                out_specs=(vmem,) * len(shapes),
                compiler_params=room(10),
                cost_estimate=cost,
                name=f"chunk_{n}",
            )(before, far_list, *shared, vectors)
            gram, outs = lax.optimization_barrier((gram, outs))
            if layer_chunk:
                parts.append(outs[0])
            if pair_chunk:
                plan.update((index, (len(blocks), m)) for m, index in enumerate(pair_chunk))
                blocks.append(outs[-1])

    edge_pairs = [index for index in range(own // 2) if index not in plan]
    plan.update((index, (len(blocks), m)) for m, index in enumerate(edge_pairs))
    near_chunks = [chunk for chunk in chunks if chunk]
    split_factors = jax.ShapeDtypeStruct((total * width, 2 * width), BF16)
    near, high, low, edge_blocks, device_factor, group_factor, root_factor = pl.pallas_call(
        functools.partial(leaves_kernel, near_chunks, edge_pairs, members, groups),
        out_shape=(
            jax.ShapeDtypeStruct(vectors.shape, BF16),
            split_factors,
            split_factors,
            block_shape(len(edge_pairs)),
            square,
            square,
            square,
        ),
        in_specs=[hbm] * len(parts) + [smem] + [vmem] * 10 + [hbm] * 2 + [vmem],
        out_specs=(hbm,) + (vmem,) * 6,
        scratch_shapes=[
            pltpu.VMEM((2, halo, columns), BF16),
            pltpu.VMEM((2, width + 32, columns), BF16),
            pltpu.VMEM((8, PAD * width), F32),
            pltpu.VMEM((2, 48, PAD * width), BF16),
            pltpu.VMEM((total * width, 2 * width), BF16),
            pltpu.VMEM((2, halo, columns), BF16),
            pltpu.VMEM((total * STRIDE, width), F32),
            pltpu.VMEM((width, width, 128), F32),
            pltpu.VMEM((total * STRIDE, 2 * width), F32),
            pltpu.SemaphoreType.DMA((6 + len(parts),)),
        ],
        compiler_params=room(24),
        name="leaves",
    )(
        *parts,
        far_list,
        basis,
        top,
        group_gram,
        gram,
        device_transfer,
        *shared,
        left,
        right,
        vectors,
    )

    coupling = pl.pallas_call(
        functools.partial(far_kernel, plan),
        out_shape=jax.ShapeDtypeStruct((width, own * far_index.shape[1] * width), BF16),
        in_specs=[smem] + [vmem] * (3 + len(blocks)),
        out_specs=vmem,
        compiler_params=room(16),
        name="far",
    )(far_list, high, low, *blocks, edge_blocks)
    return near, coupling.T, device_factor, group_factor, root_factor


def solution(mesh):
    split = P(AXES, None)
    return jax.shard_map(
        per_device,
        mesh=mesh,
        in_specs=(P(None, AXES), split, split, split, split, split, P(AXES), split),
        out_specs=(split, split, split, split, split),
        check_vma=False,
    )
```

```python
import functools
import math

import jax
import jax.numpy as jnp
from jax import lax
from jax.experimental import pallas as pl
from jax.experimental.pallas import tpu as pltpu
from jax.sharding import PartitionSpec as P

LAYER = 4
PAD = 8
LONG_SQ = 2.25
RATIO = 25.0
SCALE = 0.5 / LONG_SQ
HALF = math.log(0.5)
OFF = -16384.0
STRIDE = 72
AXES = ("group", "sub")
F32 = jnp.float32
BF16 = jnp.bfloat16


def room(megabytes):
    return pltpu.CompilerParams(vmem_limit_bytes=int(megabytes * 1024 * 1024))


def split2(value):
    high = value.astype(BF16)
    return high, (value - high.astype(F32)).astype(BF16)


def split3(value):
    high = value.astype(BF16)
    rest = value - high.astype(F32)
    middle = rest.astype(BF16)
    return high, middle, (rest - middle.astype(F32)).astype(BF16)


def mm(left, right):
    return jnp.dot(left, right, preferred_element_type=F32)


def mm_nt(left, right):
    return lax.dot_general(left, right, (((1,), (1,)), ((), ())), preferred_element_type=F32)


def exact(left, right):
    return jnp.dot(left, right, precision=lax.Precision.HIGHEST, preferred_element_type=F32)


def iota(shape, dim):
    return lax.broadcasted_iota(jnp.int32, shape, dim)


def tree_kernel(
    points_in, basis_in, below_in, transfer_in, vectors,
    dense, top, outer, inner, points, basis, below, transfer, sems,
):
    width = basis.shape[0]
    count = basis.shape[1] // width
    halo = LAYER * width
    span = PAD * width
    rows = vectors.shape[0]
    odd = lax.axis_index("sub") % 2
    sides = ((outer, odd), (inner, 1 - odd))
    basis_copy, below_copy, points_copy, transfer_copy = loads = [
        pltpu.make_async_copy(source, target, sems.at[n])
        for n, (source, target) in enumerate(
            (
                (basis_in, basis),
                (below_in, below),
                (points_in, points),
                (transfer_in, transfer),
            )
        )
    ]
    copies = [
        pltpu.make_async_copy(
            vectors.at[pl.ds(pl.multiple_of(last * (rows - halo), 16), halo), :],
            target.at[pl.ds(0, halo), :],
            sems.at[4 + n],
        )
        for n, (target, last) in enumerate(sides)
    ]
    for copy in loads + copies:
        copy.start()
    basis_copy.wait()
    points_copy.wait()
    transfer_copy.wait()

    for target, last in sides:
        bases = basis[:, count * width - span :], basis[:, 0:span]
        last_three, first_three = (
            jnp.concatenate(
                [block[:, (at + skip) * width : (at + skip + 3) * width] for at in (0, LAYER)],
                axis=1,
            )
            for skip, block in zip((1, 0), bases)
        )
        target[halo : halo + width, :] = jnp.where(last == 1, last_three, first_three)
        coords = jnp.where(last == 1, points[:, count * width - span :], points[:, 0:span])
        for m in range(2):
            high, low = split2(coords[:, m * halo : (m + 1) * halo])
            base = halo + width + 16 * m
            target[base : base + 16, :] = jnp.zeros((16, target.shape[1]), BF16)
            target[base : base + 3, 0:halo] = high
            target[base + 8 : base + 11, 0:halo] = low

    both = 2 * width
    same = iota((both, both), 0) // width == iota((both, both), 1) // width
    half_block = jnp.where(same, 0.5, 0.0).astype(F32)

    def pair(index):
        return below[:, index * both : (index + 1) * both]

    blocks = []
    for n in range(count // 4):
        stacked = jnp.concatenate(
            [basis[:, (2 * n + m) * both : (2 * n + m + 1) * both] for m in range(2)], axis=0
        )
        blocks.append(mm_nt(stacked, stacked) * half_block)
    below_copy.wait()
    offset = 0
    while True:
        nodes = len(blocks)
        xs, ts = [], []
        for n in range(nodes):
            t = pair(offset + n)
            parts = jnp.concatenate(split3(blocks[n]), axis=0)
            xs.append(mm(jnp.concatenate([t, t, t], axis=1), parts))
            ts.append(t)
        offset += nodes
        if nodes == 1:
            break
        blocks = []
        for n in range(nodes // 2):
            x = jnp.concatenate(split3(jnp.concatenate(xs[2 * n : 2 * n + 2], axis=0)), axis=1)
            t = jnp.concatenate(ts[2 * n : 2 * n + 2], axis=0)
            blocks.append(mm_nt(x, jnp.concatenate([t, t, t], axis=1)) * half_block)
    t = ts[0]
    x = jnp.concatenate(split3(xs[0]), axis=1)
    top_gram = mm_nt(x, jnp.concatenate([t, t, t], axis=1)) * 0.5
    top[...] = top_gram
    matrix = transfer[...]
    gram = exact(exact(matrix.T, top_gram), matrix)
    halves = jnp.concatenate([gram[: width // 2], gram[width // 2 :]], axis=1)
    dense[...] = halves
    inner[halo + width + 32 :, :] = jnp.concatenate(split3(halves), axis=1)
    for copy in copies:
        copy.wait()


def factor_lanes(work, width, beside):
    panels = width // 8
    row = iota((8, 128), 0)

    def spread(j, i):
        return jnp.broadcast_to(work[j, i : i + 1, :], (8, 128))

    for p in range(panels):
        at = 8 * p
        entry = {(k, m): spread(at + k, at + m) for k in range(8) for m in range(k, 8)}
        scales = []
        for k in range(8):
            scales.append(lax.rsqrt(entry[k, k]))
            for m in range(k + 1, 8):
                entry[k, m] = entry[k, m] * scales[k]
            for m in range(k + 1, 8):
                for q in range(m, 8):
                    entry[m, q] = entry[m, q] - entry[k, m] * entry[k, q]
        for i in range(p, panels):
            tile = [work[at + k, 8 * i : 8 * i + 8, :] for k in range(8)]
            for k in range(8):
                tile[k] = tile[k] * scales[k]
                for m in range(k + 1, 8):
                    tile[m] = tile[m] - tile[k] * entry[k, m]
            for k in range(8):
                work[at + k, 8 * i : 8 * i + 8, :] = (
                    jnp.where(row >= k, tile[k], 0.0) if i == p else tile[k]
                )
        beside(p)
        for q in range(p + 1, panels):
            for start in range(q, panels, 2):
                group = range(start, min(start + 2, panels))
                accs = {
                    (i, k): work[8 * q + k, 8 * i : 8 * i + 8, :] for i in group for k in range(8)
                }
                for j in range(at, at + 8):
                    factors = [spread(j, 8 * q + k) for k in range(8)]
                    for i in group:
                        column = work[j, 8 * i : 8 * i + 8, :]
                        for k in range(8):
                            accs[i, k] = accs[i, k] - column * factors[k]
                for (i, k), value in accs.items():
                    work[8 * q + k, 8 * i : 8 * i + 8, :] = value


def to_lanes(grams, work, width, many):
    for i in range(width):
        work[i, :, 0:many] = grams[pl.ds(i, many, stride=STRIDE), :].T


def from_lanes(work, factors, width, many):
    for j in range(width):
        skip = j // 8 * 8
        column = work[j, skip:, 0:many]
        if skip:
            column = jnp.concatenate([jnp.zeros((skip, many), F32), column], axis=0)
        factors[pl.ds(j, many, stride=STRIDE), :] = jnp.concatenate([column, column], axis=0).T


def gaussians(exponent):
    return jnp.exp(exponent) + jnp.exp(exponent * RATIO - RATIO * HALF)


def features(place, leaf, center):
    sub = iota(place.shape, 0)
    corner = jnp.where(sub == 0, leaf % 2 - 1, leaf // 2 % 2 - 1)
    corner = jnp.where(sub == 2, leaf // LAYER - center, corner)
    place = jnp.where(sub < 3, place + corner.astype(F32), 0.0)
    norm = jnp.sum(place * place, axis=0, keepdims=True) * SCALE
    first = jnp.where(sub == 3, -norm, jnp.where(sub == 4, 1.0, place))
    second = jnp.where(
        sub == 3, 1.0, jnp.where(sub == 4, HALF - norm, place * (2.0 * SCALE))
    )
    fh, fm, fl = [v.astype(F32) for v in split3(first)]
    sh, sm, sl = [v.astype(F32) for v in split3(second)]
    return (
        jnp.concatenate([fh, fh, fh, fm, fm, fl], axis=0),
        jnp.concatenate([sh, sm, sl, sh, sm, sh], axis=0),
    )


def rows_of(second):
    blank = jnp.zeros((16, second.shape[1]), F32)
    return jnp.concatenate([second, blank, second, blank], axis=0).T.astype(BF16)


def near_weights(first_rows, second, switches, index, halo):
    group = index // 4 * 16
    columns = jnp.concatenate([second, switches[group : group + 16, :]], axis=0)
    return gaussians(mm(first_rows[index * halo : (index + 1) * halo, :], columns)).astype(BF16)


def prepare(
    points, near_list, near_used, first_rows, first_cols, second_cols, second_rows, switches, place
):
    rows = points.shape[1]
    own = near_list.shape[1]
    width = rows // own
    place[...] = jnp.zeros(place.shape, F32)
    place[0:3, :] = points[...]
    leaf = iota((8, rows), 1) // width
    first, second = features(place[...], leaf, own // LAYER // 2)
    hot_leaf = iota((16, rows), 1) // width
    hot = jnp.where(hot_leaf % 16 == iota((16, rows), 0), 1.0, 0.0).astype(F32)
    first = jnp.concatenate([first, hot], axis=0)
    first_cols[...] = first.astype(BF16)
    second_cols[...] = second.astype(BF16)
    first_rows[...] = first.T.astype(BF16)
    second_rows[...] = rows_of(second)

    start_leaf = lax.axis_index(AXES) * own
    target = iota((1, own), 1)
    base_leaf = start_leaf + target // LAYER * LAYER - LAYER
    found = jnp.zeros((16, own), jnp.bool_)
    place_row = iota((16, own), 0)
    for n in range(near_list.shape[0]):
        spot = jnp.where(near_used[...] > n, near_list[n : n + 1, :] - base_leaf, -1)
        found = jnp.logical_or(found, place_row == spot)
    bias = jnp.where(found, 0.0, OFF).astype(F32)
    span = 3 * LAYER * width
    expand = jnp.where(iota((16, span), 0) == iota((16, span), 1) // width, 1.0, 0.0)
    switches[...] = mm(bias.T.astype(BF16), expand.astype(BF16)).astype(BF16)


def inner_layers(layers, vectors, first_rows, second_cols, switches, out, halo):
    for n, index in enumerate(layers):
        around = slice((index - 1) * halo, (index + 2) * halo)
        weights = near_weights(first_rows, second_cols[:, around], switches, index, halo)
        out[n * halo : (n + 1) * halo, :] = mm(weights, vectors[around, :]).astype(BF16)


def far_blocks(pairs, far_list, second_rows, first_cols, out, width, base, places):
    far, own = far_list.shape
    both = 2 * width
    start_leaf = lax.axis_index(AXES) * own
    square = iota((both, both), 0) // width == iota((both, both), 1) // width
    lane = iota((far * width, both), 1) < width
    exponents = []
    for index in pairs:
        t = 2 * index
        picked = []
        for m in range(2):
            spots = [
                pl.multiple_of((far_list[f, t + m] - start_leaf + base) * width, width)
                for f in range(far)
            ]
            picked.append(
                jnp.concatenate([second_rows[pl.ds(spot, width), :] for spot in spots], axis=0)
            )
        cols = first_cols[:, t * width : t * width + both]
        targets = jnp.where(
            square, jnp.concatenate([cols, cols], axis=0), jnp.zeros((both, both), BF16)
        )
        exponents.append(mm(jnp.where(lane, picked[0], picked[1]), targets))
    for place, exponent in zip(places, exponents):
        high, low = split2(gaussians(exponent))
        at = place * far * width
        out[at : at + far * width, 0:both] = high
        out[at : at + far * width, both : 2 * both] = low


def first_chunk_kernel(layers):
    def body(
        points, near_list, near_used, vectors,
        out, first_rows, first_cols, second_cols, second_rows, switches, place,
    ):
        prepare(
            points,
            near_list,
            near_used,
            first_rows,
            first_cols,
            second_cols,
            second_rows,
            switches,
            place,
        )
        halo = LAYER * points.shape[1] // near_list.shape[1]
        inner_layers(layers, vectors, first_rows, second_cols, switches, out, halo)

    return body


def next_chunk_kernel(layers, pairs):
    def body(
        after, far_list, first_rows, first_cols, second_cols, second_rows, switches, vectors, *outs
    ):
        width = vectors.shape[0] // far_list.shape[1]
        if layers:
            inner_layers(
                layers, vectors, first_rows, second_cols, switches, outs[0], LAYER * width
            )
        if pairs:
            far_blocks(
                pairs, far_list, second_rows, first_cols, outs[-1], width, 0, range(len(pairs))
            )

    return body


def leaves_kernel(chunks, edge_pairs, members, groups, *refs):
    outer = len(chunks)
    inner_near = refs[:outer]
    (
        far_list,
        basis,
        top,
        upper,
        transfer,
        first_rows,
        first_cols,
        second_cols,
        own_rows,
        switches,
        inner,
        outer,
        vectors,
        near,
        high,
        low,
        edge_blocks,
        device_factor,
        group_factor,
        root_factor,
        ends,
        sides,
        place,
        halo_cols,
        second_rows,
        results,
        grams,
        work,
        factors,
        sems,
    ) = refs[outer:]
    width = basis.shape[0]
    own = basis.shape[1] // width
    total = own + 2 * PAD
    halo = LAYER * width
    layers = own // LAYER
    both = 2 * width
    extra = sides.shape[1]
    odd = lax.axis_index("sub") % 2
    arrived = ((inner, 1 - odd), (outer, odd))
    side_copies = [
        pltpu.make_async_copy(block.at[pl.ds(halo, extra), :], sides.at[side], sems.at[n])
        for n, (block, side) in enumerate(arrived)
    ]
    end_copies = [
        pltpu.make_async_copy(block.at[pl.ds(0, halo), :], ends.at[side], sems.at[2 + n])
        for n, (block, side) in enumerate(arrived)
    ]
    near_copies = [
        pltpu.make_async_copy(
            part, near.at[pl.ds(chunk[0] * halo, len(chunk) * halo), :], sems.at[6 + n]
        )
        for n, (part, chunk) in enumerate(zip(inner_near, chunks))
    ]
    for copy in side_copies + end_copies + near_copies:
        copy.start()

    lane = iota((width, both), 1)
    for n in range(own // 2):
        pair = basis[:, n * both : (n + 1) * both]
        zero = jnp.zeros_like(pair)
        stacked = jnp.concatenate(
            [jnp.where(lane < width, pair, zero), jnp.where(lane < width, zero, pair)], axis=0
        )
        value = mm_nt(stacked, pair)
        for m in range(2):
            at = (PAD + 2 * n + m) * STRIDE
            grams[at : at + width, :] = value[m * width : (m + 1) * width]
    spare = (0, LAYER, total - LAYER - 1, total - 1)
    for spot, gram in zip(
        spare,
        (
            top[...],
            upper[0 : width // 2, :] * (1.0 / members),
            upper[width // 2 :, :] * (1.0 / (members * groups)),
            top[...],
        ),
    ):
        if gram.shape[0] < width:
            gram = jnp.concatenate([gram[:, :width], gram[:, width:]], axis=0)
        grams[spot * STRIDE : spot * STRIDE + width, :] = gram
    for copy in side_copies:
        copy.wait()
    for side, spots in enumerate(
        ((1, 2, 3, 5, 6, 7), tuple(PAD + own + m for m in (0, 1, 2, 4, 5, 6)))
    ):
        for n, spot in enumerate(spots):
            piece = sides[side, 0:width, n * width : (n + 1) * width]
            grams[spot * STRIDE : spot * STRIDE + width, :] = mm_nt(piece, piece)

    lanes = PAD * width
    place[...] = jnp.zeros(place.shape, F32)
    for side, first_leaf in enumerate((-PAD, own)):
        for n in range(2):
            base = width + 16 * n
            values = sides[side, base : base + 16, 0:halo].astype(F32)
            place[0:3, n * halo : (n + 1) * halo] = values[0:3, :] + values[8:11, :]
        leaf = iota((8, lanes), 1) // width + (first_leaf + PAD)
        second = features(place[...], leaf, layers // 2 + PAD // LAYER)[1]
        halo_cols[side, :, :] = second.astype(BF16)
        at = (PAD + first_leaf) * width
        second_rows[at : at + lanes, :] = rows_of(second)
    second_rows[lanes : lanes + own * width, :] = own_rows[...]

    copies = [
        pltpu.make_async_copy(results.at[n], near.at[pl.ds(index * halo, halo), :], sems.at[4 + n])
        for n, index in enumerate((0, layers - 1))
    ]

    def edge(n):
        if n == 0:
            columns = [halo_cols[0, :, halo:], second_cols[:, 0 : 2 * halo]]
            index = 0
        else:
            columns = [second_cols[:, (layers - 2) * halo :], halo_cols[1, :, 0:halo]]
            index = layers - 1
        weights = near_weights(
            first_rows, jnp.concatenate(columns, axis=1), switches, index, halo
        )
        if n == 0:
            value = mm(weights[:, 0:halo], ends[0, :, :])
            value = value + mm(weights[:, halo:], vectors[0 : 2 * halo, :])
        else:
            value = mm(weights[:, 0 : 2 * halo], vectors[(layers - 2) * halo :, :])
            value = value + mm(weights[:, 2 * halo :], ends[1, :, :])
        results[n, :, :] = value.astype(BF16)
        copies[n].start()

    panels = width // 8

    def beside(p):
        if p in (1, 3):
            edge(p // 2)
        places = range(p * len(edge_pairs) // panels, (p + 1) * len(edge_pairs) // panels)
        far_blocks(
            [edge_pairs[n] for n in places],
            far_list,
            second_rows,
            first_cols,
            edge_blocks,
            width,
            PAD,
            places,
        )

    to_lanes(grams, work, width, total)
    for copy in end_copies:
        copy.wait()
    factor_lanes(work, width, beside)
    from_lanes(work, factors, width, total)
    device_factor[...] = exact(factors[0:width, 0:width], transfer[...])
    for target, spot in ((group_factor, spare[1]), (root_factor, spare[2])):
        target[...] = factors[spot * STRIDE : spot * STRIDE + width, 0:width]
    for spot in range(total):
        at = slice(spot * width, (spot + 1) * width)
        high[at, :], low[at, :] = split2(factors[spot * STRIDE : spot * STRIDE + width, :])
    for copy in copies + near_copies:
        copy.wait()


def far_kernel(plan, far_list, high, low, *refs):
    blocks, coupling = refs[:-1], refs[-1]
    width = coupling.shape[0]
    far, own = far_list.shape
    both = 2 * width
    start_leaf = lax.axis_index(AXES) * own
    square = iota((both, both), 0) // width == iota((both, both), 1) // width
    lane = iota((width, both), 1) < width
    zero = jnp.zeros((both, both), BF16)

    def diagonal(value):
        return jnp.where(square, value, zero)

    for start in range(0, own // 2, 4):
        indices = range(start, start + 4)
        halves = []
        for index in indices:
            source, place = plan[index]
            at = place * far * width
            kh = blocks[source][at : at + far * width, 0:both]
            kl = blocks[source][at : at + far * width, both : 2 * both]
            at = (PAD + 2 * index) * width
            rh = diagonal(high[at : at + both, :])
            rl = diagonal(low[at : at + both, :])
            halves.append(
                mm_nt(
                    jnp.concatenate([kh, kl, kh], axis=1), jnp.concatenate([rh, rh, rl], axis=1)
                )
            )
        outs = []
        for index, half in zip(indices, halves):
            zh, zl = split2(half * (1.0 / width))
            for f in range(far):
                spots = [
                    pl.multiple_of((far_list[f, 2 * index + m] - start_leaf + PAD) * width, width)
                    for m in range(2)
                ]
                sh, sl = (
                    jnp.where(lane, *(part[pl.ds(spot, width), :] for spot in spots))
                    for part in (high, low)
                )
                a = slice(f * width, (f + 1) * width)
                ph = diagonal(jnp.concatenate([zh[a], zh[a]], axis=0))
                plow = diagonal(jnp.concatenate([zl[a], zl[a]], axis=0))
                outs.append(
                    mm(
                        jnp.concatenate([sh, sh, sl], axis=1),
                        jnp.concatenate([ph, plow, ph], axis=0),
                    )
                )
        for n, index in enumerate(indices):
            three = outs[n * far : (n + 1) * far]
            line = jnp.concatenate(
                [out[:, 0:width] for out in three] + [out[:, width:both] for out in three], axis=1
            )
            at = index * 2 * far * width
            coupling[:, at : at + 2 * far * width] = line.astype(BF16)


def swap_inner(block):
    return lax.ppermute(block, AXES, [(i, i ^ 1) for i in range(lax.axis_size(AXES))])


def swap_outer(block):
    inside = range(1, lax.axis_size(AXES) - 1)
    return lax.ppermute(block, AXES, [(i, i + 1 if i % 2 else i - 1) for i in inside])


def exchange(value, axis, bit):
    mask = 2**bit
    pairs = [(source, source ^ mask) for source in range(lax.axis_size(axis))]
    return value + lax.ppermute(value, axis, pairs)


def per_device(
    points, leaf_basis, inner_transfer, device_transfer, vectors, near_index, near_count, far_index
):
    own = near_index.shape[0]
    width = leaf_basis.shape[1]
    columns = vectors.shape[1]
    halo = LAYER * width
    half = width // 2
    layers = own // LAYER
    total = own + 2 * PAD
    members, groups = lax.axis_size("sub"), lax.axis_size("group")
    vmem = pl.BlockSpec(memory_space=pltpu.VMEM)
    smem = pl.BlockSpec(memory_space=pltpu.SMEM)
    hbm = pl.BlockSpec(memory_space=pl.ANY)
    square = jax.ShapeDtypeStruct((width, width), F32)
    extra = halo + width + 32

    def block_of(rows):
        return jax.ShapeDtypeStruct((rows, columns), BF16)

    basis = leaf_basis.T
    near_list, far_list = near_index.T, far_index.T
    cost = pl.CostEstimate(flops=10**9, bytes_accessed=4 * 10**6, transcendentals=10**6)

    dense, top, to_outer, to_inner = pl.pallas_call(
        tree_kernel,
        out_shape=(
            jax.ShapeDtypeStruct((half, 2 * width), F32),
            square,
            block_of(extra),
            block_of(extra + half),
        ),
        in_specs=[hbm] * 5,
        out_specs=(vmem,) * 4,
        scratch_shapes=[
            pltpu.VMEM((3, own * width), F32),
            pltpu.VMEM((width, own * width), BF16),
            pltpu.VMEM((width, (own - 2) * width), BF16),
            pltpu.VMEM((width, width), F32),
            pltpu.SemaphoreType.DMA((6,)),
        ],
        compiler_params=room(60),
        name="tree",
    )(points, basis, inner_transfer.T, device_transfer, vectors)
    from_inner = swap_inner(to_inner)
    from_outer = swap_outer(to_outer)

    steps = [("group", bit) for bit in range(groups.bit_length() - 1)]
    steps += [("sub", bit) for bit in range(1, members.bit_length() - 1)]
    chunks = [[1, 2, 3], [4], [5], [6], []]
    inner_pairs = list(range(PAD // 2, (own - PAD) // 2))
    pair_chunks = [[], [], inner_pairs[:2], inner_pairs[2:4], inner_pairs[4:]]
    blocks, plan, parts = [], {}, []

    def part_shape(count):
        return jax.ShapeDtypeStruct((count * halo, columns), BF16)

    def block_shape(count):
        return jax.ShapeDtypeStruct((count * far_index.shape[1] * width, 4 * width), BF16)

    late_points, dense = lax.optimization_barrier((points, dense))
    part, *shared = pl.pallas_call(
        first_chunk_kernel(chunks[0]),
        out_shape=(
            part_shape(len(chunks[0])),
            jax.ShapeDtypeStruct((own * width, 64), BF16),
            jax.ShapeDtypeStruct((64, own * width), BF16),
            jax.ShapeDtypeStruct((48, own * width), BF16),
            jax.ShapeDtypeStruct((own * width, 128), BF16),
            jax.ShapeDtypeStruct((own, 3 * halo), BF16),
        ),
        in_specs=[vmem] * 4,
        out_specs=(vmem,) * 6,
        scratch_shapes=[pltpu.VMEM((8, own * width), F32)],
        compiler_params=room(10),
        cost_estimate=cost,
        name="chunk_0",
    )(late_points, near_list, near_count.reshape(1, own), vectors)
    parts.append(part)
    summands = [
        from_inner[extra:, n * 2 * width : (n + 1) * 2 * width].astype(F32) for n in range(3)
    ]
    pair_gram = gram = dense + (summands[0] + (summands[1] + summands[2]))
    gram, parts[0] = lax.optimization_barrier((gram, parts[0]))
    for n in range(max(len(steps) + 1, len(chunks)) - 1):
        before = gram
        if n < len(steps):
            axis, bit = steps[n]
            if n == len(steps) - (members.bit_length() - 2):
                gram = before = jnp.concatenate([pair_gram, gram], axis=0)
            gram = exchange(gram, axis, bit)
        if n + 1 < len(chunks):
            layer_chunk, pair_chunk = chunks[n + 1], pair_chunks[n + 1]
            shapes = [part_shape(len(layer_chunk))] * bool(layer_chunk)
            shapes += [block_shape(len(pair_chunk))] * bool(pair_chunk)
            outs = pl.pallas_call(
                next_chunk_kernel(layer_chunk, pair_chunk),
                out_shape=tuple(shapes),
                in_specs=[hbm, smem] + [vmem] * 6,
                out_specs=(vmem,) * len(shapes),
                compiler_params=room(10),
                cost_estimate=cost,
                name=f"chunk_{n + 1}",
            )(before, far_list, *shared, vectors)
            gram, outs = lax.optimization_barrier((gram, outs))
            if layer_chunk:
                parts.append(outs[0])
            if pair_chunk:
                plan.update((index, (len(blocks), m)) for m, index in enumerate(pair_chunk))
                blocks.append(outs[-1])

    edge_pairs = [index for index in range(own // 2) if index not in plan]
    plan.update((index, (len(blocks), m)) for m, index in enumerate(edge_pairs))
    near_chunks = [chunk for chunk in chunks if chunk]
    split_factors = jax.ShapeDtypeStruct((total * width, 2 * width), BF16)
    near, high, low, edge_blocks, device_factor, group_factor, root_factor = pl.pallas_call(
        functools.partial(leaves_kernel, near_chunks, edge_pairs, members, groups),
        out_shape=(
            jax.ShapeDtypeStruct(vectors.shape, BF16),
            split_factors,
            split_factors,
            block_shape(len(edge_pairs)),
            square,
            square,
            square,
        ),
        in_specs=[hbm] * len(parts) + [smem] + [vmem] * 9 + [hbm] * 2 + [vmem],
        out_specs=(hbm,) + (vmem,) * 6,
        scratch_shapes=[
            pltpu.VMEM((2, halo, columns), BF16),
            pltpu.VMEM((2, width + 32, columns), BF16),
            pltpu.VMEM((8, PAD * width), F32),
            pltpu.VMEM((2, 48, PAD * width), BF16),
            pltpu.VMEM((total * width, 2 * width), BF16),
            pltpu.VMEM((2, halo, columns), BF16),
            pltpu.VMEM((total * STRIDE, width), F32),
            pltpu.VMEM((width, width, 128), F32),
            pltpu.VMEM((total * STRIDE, 2 * width), F32),
            pltpu.SemaphoreType.DMA((6 + len(parts),)),
        ],
        compiler_params=room(24),
        name="leaves",
    )(
        *parts,
        far_list,
        basis,
        top,
        gram,
        device_transfer,
        *shared,
        from_inner,
        from_outer,
        vectors,
    )

    coupling = pl.pallas_call(
        functools.partial(far_kernel, plan),
        out_shape=jax.ShapeDtypeStruct((width, own * far_index.shape[1] * width), BF16),
        in_specs=[smem] + [vmem] * (3 + len(blocks)),
        out_specs=vmem,
        compiler_params=room(16),
        name="far",
    )(far_list, high, low, *blocks, edge_blocks)
    return near, coupling.T, device_factor, group_factor, root_factor


def solution(mesh):
    split = P(AXES, None)
    return jax.shard_map(
        per_device,
        mesh=mesh,
        in_specs=(P(None, AXES), split, split, split, split, split, P(AXES), split),
        out_specs=(split, split, split, split, split),
        check_vma=False,
    )
```

```python
import functools
import math

import jax
import jax.numpy as jnp
from jax import lax
from jax.experimental import pallas as pl
from jax.experimental.pallas import tpu as pltpu
from jax.sharding import PartitionSpec as P

LAYER = 4
PAD = 8
LONG_SQ = 2.25
RATIO = 25.0
SCALE = 0.5 / LONG_SQ
HALF = math.log(0.5)
OFF = -16384.0
STRIDE = 40
AXES = ("group", "sub")
F32 = jnp.float32
BF16 = jnp.bfloat16


def room(megabytes):
    return pltpu.CompilerParams(vmem_limit_bytes=int(megabytes * 1024 * 1024))


def split2(value):
    high = value.astype(BF16)
    return high, (value - high.astype(F32)).astype(BF16)


def split3(value):
    high = value.astype(BF16)
    rest = value - high.astype(F32)
    middle = rest.astype(BF16)
    return high, middle, (rest - middle.astype(F32)).astype(BF16)


def mm(left, right):
    return jnp.dot(left, right, preferred_element_type=F32)


def mm_nt(left, right):
    return lax.dot_general(left, right, (((1,), (1,)), ((), ())), preferred_element_type=F32)


def exact(left, right):
    return jnp.dot(left, right, precision=lax.Precision.HIGHEST, preferred_element_type=F32)


def iota(shape, dim):
    return lax.broadcasted_iota(jnp.int32, shape, dim)


def tree_kernel(
    points_in, basis_in, below_in, transfer_in, vectors,
    dense, top, outer, inner, points, basis, below, transfer, sems,
):
    width = basis.shape[0]
    count = basis.shape[1] // width
    halo = LAYER * width
    span = PAD * width
    rows = vectors.shape[0]
    odd = lax.axis_index("sub") % 2
    sides = ((outer, odd), (inner, 1 - odd))
    basis_copy, below_copy, points_copy, transfer_copy = loads = [
        pltpu.make_async_copy(source, target, sems.at[n])
        for n, (source, target) in enumerate(
            (
                (basis_in, basis),
                (below_in, below),
                (points_in, points),
                (transfer_in, transfer),
            )
        )
    ]
    copies = [
        pltpu.make_async_copy(
            vectors.at[pl.ds(pl.multiple_of(last * (rows - halo), 16), halo), :],
            target.at[pl.ds(0, halo), :],
            sems.at[4 + n],
        )
        for n, (target, last) in enumerate(sides)
    ]
    for copy in loads + copies:
        copy.start()
    basis_copy.wait()
    points_copy.wait()
    transfer_copy.wait()

    for target, last in sides:
        bases = basis[:, count * width - span :], basis[:, 0:span]
        last_three, first_three = (
            jnp.concatenate(
                [block[:, (at + skip) * width : (at + skip + 3) * width] for at in (0, LAYER)],
                axis=1,
            )
            for skip, block in zip((1, 0), bases)
        )
        target[halo : halo + width, :] = jnp.where(last == 1, last_three, first_three)
        coords = jnp.where(last == 1, points[:, count * width - span :], points[:, 0:span])
        for m in range(2):
            high, low = split2(coords[:, m * halo : (m + 1) * halo])
            base = halo + width + 16 * m
            target[base : base + 16, :] = jnp.zeros((16, target.shape[1]), BF16)
            target[base : base + 3, 0:halo] = high
            target[base + 8 : base + 11, 0:halo] = low

    both = 2 * width
    same = iota((both, both), 0) // width == iota((both, both), 1) // width
    half_block = jnp.where(same, 0.5, 0.0).astype(F32)

    def pair(index):
        return below[:, index * both : (index + 1) * both]

    blocks = []
    for n in range(count // 4):
        stacked = jnp.concatenate(
            [basis[:, (2 * n + m) * both : (2 * n + m + 1) * both] for m in range(2)], axis=0
        )
        blocks.append(mm_nt(stacked, stacked) * half_block)
    below_copy.wait()
    offset = 0
    while True:
        nodes = len(blocks)
        xs, ts = [], []
        for n in range(nodes):
            t = pair(offset + n)
            parts = jnp.concatenate(split3(blocks[n]), axis=0)
            xs.append(mm(jnp.concatenate([t, t, t], axis=1), parts))
            ts.append(t)
        offset += nodes
        if nodes == 1:
            break
        blocks = []
        for n in range(nodes // 2):
            x = jnp.concatenate(split3(jnp.concatenate(xs[2 * n : 2 * n + 2], axis=0)), axis=1)
            t = jnp.concatenate(ts[2 * n : 2 * n + 2], axis=0)
            blocks.append(mm_nt(x, jnp.concatenate([t, t, t], axis=1)) * half_block)
    t = ts[0]
    x = jnp.concatenate(split3(xs[0]), axis=1)
    top_gram = mm_nt(x, jnp.concatenate([t, t, t], axis=1)) * 0.5
    top[...] = fold(top_gram)
    matrix = transfer[...]
    gram = exact(exact(matrix.T, top_gram), matrix)
    halves = fold(gram)
    dense[...] = halves
    inner[halo + width + 32 :, :] = jnp.concatenate(split3(halves), axis=1)
    for copy in copies:
        copy.wait()


def factor_lanes(work, width, beside):
    panels = width // 8
    row = iota((8, 128), 0)

    def spread(j, i):
        return jnp.broadcast_to(work[j, i : i + 1, :], (8, 128))

    for p in range(panels):
        at = 8 * p
        entry = {(k, m): spread(at + k, at + m) for k in range(8) for m in range(k, 8)}
        scales = []
        for k in range(8):
            scales.append(lax.rsqrt(entry[k, k]))
            for m in range(k + 1, 8):
                entry[k, m] = entry[k, m] * scales[k]
            for m in range(k + 1, 8):
                for q in range(m, 8):
                    entry[m, q] = entry[m, q] - entry[k, m] * entry[k, q]
        for i in range(p, panels):
            tile = [work[at + k, 8 * i : 8 * i + 8, :] for k in range(8)]
            for k in range(8):
                tile[k] = tile[k] * scales[k]
                for m in range(k + 1, 8):
                    tile[m] = tile[m] - tile[k] * entry[k, m]
            for k in range(8):
                work[at + k, 8 * i : 8 * i + 8, :] = (
                    jnp.where(row >= k, tile[k], 0.0) if i == p else tile[k]
                )
        beside(p)
        for q in range(p + 1, panels):
            for start in range(q, panels, 2):
                group = range(start, min(start + 2, panels))
                accs = {
                    (i, k): work[8 * q + k, 8 * i : 8 * i + 8, :] for i in group for k in range(8)
                }
                for j in range(at, at + 8):
                    factors = [spread(j, 8 * q + k) for k in range(8)]
                    for i in group:
                        column = work[j, 8 * i : 8 * i + 8, :]
                        for k in range(8):
                            accs[i, k] = accs[i, k] - column * factors[k]
                for (i, k), value in accs.items():
                    work[8 * q + k, 8 * i : 8 * i + 8, :] = value


def fold(matrix):
    half = matrix.shape[0] // 2
    return jnp.concatenate([matrix[:half], matrix[half:]], axis=1)


def unfold(matrix):
    half = matrix.shape[1] // 2
    return jnp.concatenate([matrix[:, :half], matrix[:, half:]], axis=0)


def to_lanes(grams, work, width, many):
    for i in range(width // 2):
        both = grams[pl.ds(i, many, stride=STRIDE), :].T
        work[i, :, 0:many] = both[0:width]
        work[i + width // 2, :, 0:many] = both[width:]


def from_lanes(work, factors, width, many):
    for i in range(width // 2):
        both = []
        for j in (i, i + width // 2):
            skip = j // 8 * 8
            both += [jnp.zeros((skip, many), F32)] * bool(skip) + [work[j, skip:, 0:many]]
        factors[pl.ds(i, many, stride=STRIDE), :] = jnp.concatenate(both, axis=0).T


def gaussians(exponent):
    return jnp.exp(exponent) + jnp.exp(exponent * RATIO - RATIO * HALF)


def features(place, leaf, center):
    sub = iota(place.shape, 0)
    corner = jnp.where(sub == 0, leaf % 2 - 1, leaf // 2 % 2 - 1)
    corner = jnp.where(sub == 2, leaf // LAYER - center, corner)
    place = jnp.where(sub < 3, place + corner.astype(F32), 0.0)
    norm = jnp.sum(place * place, axis=0, keepdims=True) * SCALE
    first = jnp.where(sub == 3, -norm, jnp.where(sub == 4, 1.0, place))
    second = jnp.where(
        sub == 3, 1.0, jnp.where(sub == 4, HALF - norm, place * (2.0 * SCALE))
    )
    fh, fm, fl = [v.astype(F32) for v in split3(first)]
    sh, sm, sl = [v.astype(F32) for v in split3(second)]
    return (
        jnp.concatenate([fh, fh, fh, fm, fm, fl], axis=0),
        jnp.concatenate([sh, sm, sl, sh, sm, sh], axis=0),
    )


def rows_of(second):
    blank = jnp.zeros((16, second.shape[1]), F32)
    return jnp.concatenate([second, blank, second, blank], axis=0).T.astype(BF16)


def near_weights(first_rows, second, switches, index, halo):
    group = index // 4 * 16
    columns = jnp.concatenate([second, switches[group : group + 16, :]], axis=0)
    return gaussians(mm(first_rows[index * halo : (index + 1) * halo, :], columns)).astype(BF16)


def prepare(
    points, near_list, near_used, first_rows, first_cols, second_cols, second_rows, switches, place
):
    rows = points.shape[1]
    own = near_list.shape[1]
    width = rows // own
    place[...] = jnp.zeros(place.shape, F32)
    place[0:3, :] = points[...]
    leaf = iota((8, rows), 1) // width
    first, second = features(place[...], leaf, own // LAYER // 2)
    hot_leaf = iota((16, rows), 1) // width
    hot = jnp.where(hot_leaf % 16 == iota((16, rows), 0), 1.0, 0.0).astype(F32)
    first = jnp.concatenate([first, hot], axis=0)
    first_cols[...] = first.astype(BF16)
    second_cols[...] = second.astype(BF16)
    first_rows[...] = first.T.astype(BF16)
    second_rows[...] = rows_of(second)

    start_leaf = lax.axis_index(AXES) * own
    target = iota((1, own), 1)
    base_leaf = start_leaf + target // LAYER * LAYER - LAYER
    found = jnp.zeros((16, own), jnp.bool_)
    place_row = iota((16, own), 0)
    for n in range(near_list.shape[0]):
        spot = jnp.where(near_used[...] > n, near_list[n : n + 1, :] - base_leaf, -1)
        found = jnp.logical_or(found, place_row == spot)
    bias = jnp.where(found, 0.0, OFF).astype(F32)
    span = 3 * LAYER * width
    expand = jnp.where(iota((16, span), 0) == iota((16, span), 1) // width, 1.0, 0.0)
    switches[...] = mm(bias.T.astype(BF16), expand.astype(BF16)).astype(BF16)


def inner_layers(layers, vectors, first_rows, second_cols, switches, out, halo):
    for n, index in enumerate(layers):
        around = slice((index - 1) * halo, (index + 2) * halo)
        weights = near_weights(first_rows, second_cols[:, around], switches, index, halo)
        out[n * halo : (n + 1) * halo, :] = mm(weights, vectors[around, :]).astype(BF16)


def far_blocks(pairs, far_list, second_rows, first_cols, out, width, base, places):
    far, own = far_list.shape
    both = 2 * width
    start_leaf = lax.axis_index(AXES) * own
    square = iota((both, both), 0) // width == iota((both, both), 1) // width
    lane = iota((far * width, both), 1) < width
    exponents = []
    for index in pairs:
        t = 2 * index
        picked = []
        for m in range(2):
            spots = [
                pl.multiple_of((far_list[f, t + m] - start_leaf + base) * width, width)
                for f in range(far)
            ]
            picked.append(
                jnp.concatenate([second_rows[pl.ds(spot, width), :] for spot in spots], axis=0)
            )
        cols = first_cols[:, t * width : t * width + both]
        targets = jnp.where(
            square, jnp.concatenate([cols, cols], axis=0), jnp.zeros((both, both), BF16)
        )
        exponents.append(mm(jnp.where(lane, picked[0], picked[1]), targets))
    for place, exponent in zip(places, exponents):
        high, low = split2(gaussians(exponent))
        at = place * far * width
        out[at : at + far * width, 0:both] = high
        out[at : at + far * width, both : 2 * both] = low


def first_chunk_kernel(layers):
    def body(
        points, near_list, near_used, vectors,
        out, first_rows, first_cols, second_cols, second_rows, switches, place,
    ):
        prepare(
            points,
            near_list,
            near_used,
            first_rows,
            first_cols,
            second_cols,
            second_rows,
            switches,
            place,
        )
        halo = LAYER * points.shape[1] // near_list.shape[1]
        inner_layers(layers, vectors, first_rows, second_cols, switches, out, halo)

    return body


def layers_chunk_kernel(layers, halo):
    def body(after, first_rows, second_cols, switches, vectors, out):
        inner_layers(layers, vectors, first_rows, second_cols, switches, out, halo)

    return body


def pairs_chunk_kernel(pairs, width):
    def body(after, far_list, first_cols, second_rows, out):
        far_blocks(pairs, far_list, second_rows, first_cols, out, width, 0, range(len(pairs)))

    return body


def leaves_kernel(chunks, edge_pairs, members, groups, *refs):
    outer = len(chunks)
    inner_near = refs[:outer]
    (
        far_list,
        basis,
        top,
        upper,
        transfer,
        first_rows,
        first_cols,
        second_cols,
        own_rows,
        switches,
        inner,
        outer,
        vectors,
        near,
        high,
        low,
        edge_blocks,
        device_factor,
        group_factor,
        root_factor,
        ends,
        sides,
        place,
        halo_cols,
        second_rows,
        results,
        grams,
        work,
        factors,
        sems,
    ) = refs[outer:]
    width = basis.shape[0]
    own = basis.shape[1] // width
    total = own + 2 * PAD
    halo = LAYER * width
    layers = own // LAYER
    both = 2 * width
    extra = sides.shape[1]
    odd = lax.axis_index("sub") % 2
    arrived = ((inner, 1 - odd), (outer, odd))
    side_copies = [
        pltpu.make_async_copy(block.at[pl.ds(halo, extra), :], sides.at[side], sems.at[n])
        for n, (block, side) in enumerate(arrived)
    ]
    end_copies = [
        pltpu.make_async_copy(block.at[pl.ds(0, halo), :], ends.at[side], sems.at[2 + n])
        for n, (block, side) in enumerate(arrived)
    ]
    near_copies = [
        pltpu.make_async_copy(
            part, near.at[pl.ds(chunk[0] * halo, len(chunk) * halo), :], sems.at[6 + n]
        )
        for n, (part, chunk) in enumerate(zip(inner_near, chunks))
    ]
    for copy in side_copies + end_copies + near_copies:
        copy.start()

    lane = iota((width, both), 1)
    for n in range(own // 2):
        pair = basis[:, n * both : (n + 1) * both]
        zero = jnp.zeros_like(pair)
        stacked = jnp.concatenate(
            [jnp.where(lane < width, pair, zero), jnp.where(lane < width, zero, pair)], axis=0
        )
        value = mm_nt(stacked, pair)
        for m in range(2):
            at = (PAD + 2 * n + m) * STRIDE
            grams[at : at + width // 2, :] = fold(value[m * width : (m + 1) * width])
    spare = (0, LAYER, total - LAYER - 1, total - 1)
    for spot, gram in zip(
        spare,
        (
            top[...],
            upper[0 : width // 2, :] * (1.0 / members),
            upper[width // 2 :, :] * (1.0 / (members * groups)),
            top[...],
        ),
    ):
        grams[spot * STRIDE : spot * STRIDE + width // 2, :] = gram
    for copy in side_copies:
        copy.wait()
    for side, spots in enumerate(
        ((1, 2, 3, 5, 6, 7), tuple(PAD + own + m for m in (0, 1, 2, 4, 5, 6)))
    ):
        for n, spot in enumerate(spots):
            piece = sides[side, 0:width, n * width : (n + 1) * width]
            grams[spot * STRIDE : spot * STRIDE + width // 2, :] = fold(mm_nt(piece, piece))

    lanes = PAD * width
    place[...] = jnp.zeros(place.shape, F32)
    for side, first_leaf in enumerate((-PAD, own)):
        for n in range(2):
            base = width + 16 * n
            values = sides[side, base : base + 16, 0:halo].astype(F32)
            place[0:3, n * halo : (n + 1) * halo] = values[0:3, :] + values[8:11, :]
        leaf = iota((8, lanes), 1) // width + (first_leaf + PAD)
        second = features(place[...], leaf, layers // 2 + PAD // LAYER)[1]
        halo_cols[side, :, :] = second.astype(BF16)
        at = (PAD + first_leaf) * width
        second_rows[at : at + lanes, :] = rows_of(second)
    second_rows[lanes : lanes + own * width, :] = own_rows[...]

    copies = [
        pltpu.make_async_copy(results.at[n], near.at[pl.ds(index * halo, halo), :], sems.at[4 + n])
        for n, index in enumerate((0, layers - 1))
    ]

    def edge(n):
        if n == 0:
            columns = [halo_cols[0, :, halo:], second_cols[:, 0 : 2 * halo]]
            index = 0
        else:
            columns = [second_cols[:, (layers - 2) * halo :], halo_cols[1, :, 0:halo]]
            index = layers - 1
        weights = near_weights(
            first_rows, jnp.concatenate(columns, axis=1), switches, index, halo
        )
        if n == 0:
            value = mm(weights[:, 0:halo], ends[0, :, :])
            value = value + mm(weights[:, halo:], vectors[0 : 2 * halo, :])
        else:
            value = mm(weights[:, 0 : 2 * halo], vectors[(layers - 2) * halo :, :])
            value = value + mm(weights[:, 2 * halo :], ends[1, :, :])
        results[n, :, :] = value.astype(BF16)
        copies[n].start()

    panels = width // 8

    def beside(p):
        if p in (1, 3):
            edge(p // 2)
        places = range(p * len(edge_pairs) // panels, (p + 1) * len(edge_pairs) // panels)
        far_blocks(
            [edge_pairs[n] for n in places],
            far_list,
            second_rows,
            first_cols,
            edge_blocks,
            width,
            PAD,
            places,
        )

    to_lanes(grams, work, width, total)
    for copy in end_copies:
        copy.wait()
    factor_lanes(work, width, beside)
    from_lanes(work, factors, width, total)
    device_factor[...] = exact(unfold(factors[0 : width // 2, :]), transfer[...])
    for target, spot in ((group_factor, spare[1]), (root_factor, spare[2])):
        target[...] = unfold(factors[spot * STRIDE : spot * STRIDE + width // 2, :])
    left_lanes = iota((width // 2, both), 1) < width
    for spot in range(total):
        rows = factors[spot * STRIDE : spot * STRIDE + width // 2, :]
        turned = pltpu.roll(rows, width, 1)
        twice = jnp.concatenate(
            [jnp.where(left_lanes, rows, turned), jnp.where(left_lanes, turned, rows)], axis=0
        )
        at = slice(spot * width, (spot + 1) * width)
        high[at, :], low[at, :] = split2(twice)
    for copy in copies + near_copies:
        copy.wait()


def far_kernel(plan, far_list, high, low, *refs):
    blocks, coupling = refs[:-1], refs[-1]
    width = coupling.shape[0]
    far, own = far_list.shape
    both = 2 * width
    start_leaf = lax.axis_index(AXES) * own
    square = iota((both, both), 0) // width == iota((both, both), 1) // width
    lane = iota((width, both), 1) < width
    zero = jnp.zeros((both, both), BF16)

    def diagonal(value):
        return jnp.where(square, value, zero)

    for start in range(0, own // 2, 4):
        indices = range(start, start + 4)
        halves = []
        for index in indices:
            source, place = plan[index]
            at = place * far * width
            kh = blocks[source][at : at + far * width, 0:both]
            kl = blocks[source][at : at + far * width, both : 2 * both]
            at = (PAD + 2 * index) * width
            rh = diagonal(high[at : at + both, :])
            rl = diagonal(low[at : at + both, :])
            halves.append(
                mm_nt(
                    jnp.concatenate([kh, kl, kh], axis=1), jnp.concatenate([rh, rh, rl], axis=1)
                )
            )
        outs = []
        for index, half in zip(indices, halves):
            zh, zl = split2(half * (1.0 / width))
            for f in range(far):
                spots = [
                    pl.multiple_of((far_list[f, 2 * index + m] - start_leaf + PAD) * width, width)
                    for m in range(2)
                ]
                sh, sl = (
                    jnp.where(lane, *(part[pl.ds(spot, width), :] for spot in spots))
                    for part in (high, low)
                )
                a = slice(f * width, (f + 1) * width)
                ph = diagonal(jnp.concatenate([zh[a], zh[a]], axis=0))
                plow = diagonal(jnp.concatenate([zl[a], zl[a]], axis=0))
                outs.append(
                    mm(
                        jnp.concatenate([sh, sh, sl], axis=1),
                        jnp.concatenate([ph, plow, ph], axis=0),
                    )
                )
        for n, index in enumerate(indices):
            three = outs[n * far : (n + 1) * far]
            line = jnp.concatenate(
                [out[:, 0:width] for out in three] + [out[:, width:both] for out in three], axis=1
            )
            at = index * 2 * far * width
            coupling[:, at : at + 2 * far * width] = line.astype(BF16)


def swap_inner(block):
    return lax.ppermute(block, AXES, [(i, i ^ 1) for i in range(lax.axis_size(AXES))])


def swap_outer(block):
    inside = range(1, lax.axis_size(AXES) - 1)
    return lax.ppermute(block, AXES, [(i, i + 1 if i % 2 else i - 1) for i in inside])


def exchange(value, distance):
    odd = range(1, lax.axis_size(AXES), 2)
    return value + lax.ppermute(value, AXES, [(i, i ^ distance) for i in odd])


def per_device(
    points, leaf_basis, inner_transfer, device_transfer, vectors, near_index, near_count, far_index
):
    own = near_index.shape[0]
    width = leaf_basis.shape[1]
    columns = vectors.shape[1]
    halo = LAYER * width
    half = width // 2
    layers = own // LAYER
    total = own + 2 * PAD
    members, groups = lax.axis_size("sub"), lax.axis_size("group")
    vmem = pl.BlockSpec(memory_space=pltpu.VMEM)
    smem = pl.BlockSpec(memory_space=pltpu.SMEM)
    hbm = pl.BlockSpec(memory_space=pl.ANY)
    square = jax.ShapeDtypeStruct((width, width), F32)
    extra = halo + width + 32

    def block_of(rows):
        return jax.ShapeDtypeStruct((rows, columns), BF16)

    basis = leaf_basis.T
    near_list, far_list = near_index.T, far_index.T
    cost = pl.CostEstimate(flops=10**9, bytes_accessed=4 * 10**6, transcendentals=10**6)

    dense, top, to_outer, to_inner = pl.pallas_call(
        tree_kernel,
        out_shape=(
            jax.ShapeDtypeStruct((half, 2 * width), F32),
            jax.ShapeDtypeStruct((half, 2 * width), F32),
            block_of(extra),
            block_of(extra + half),
        ),
        in_specs=[hbm] * 5,
        out_specs=(vmem,) * 4,
        scratch_shapes=[
            pltpu.VMEM((3, own * width), F32),
            pltpu.VMEM((width, own * width), BF16),
            pltpu.VMEM((width, (own - 2) * width), BF16),
            pltpu.VMEM((width, width), F32),
            pltpu.SemaphoreType.DMA((6,)),
        ],
        compiler_params=room(60),
        name="tree",
    )(points, basis, inner_transfer.T, device_transfer, vectors)
    from_inner = swap_inner(to_inner)
    from_outer = swap_outer(to_outer)

    sub_bits = members.bit_length() - 1
    steps = [members << bit for bit in range(groups.bit_length() - 1)]
    steps += [1 << bit for bit in range(1, sub_bits)]
    chunks = [[1, 2, 3], [4], [5], [6]]
    inner_pairs = list(range(PAD // 2, (own - PAD) // 2))
    few = len(inner_pairs) // 2
    pair_chunks = [inner_pairs[:few], inner_pairs[few:]]
    blocks, plan, parts = [], {}, []

    def part_shape(count):
        return jax.ShapeDtypeStruct((count * halo, columns), BF16)

    def block_shape(count):
        return jax.ShapeDtypeStruct((count * far_index.shape[1] * width, 4 * width), BF16)

    late_points, dense = lax.optimization_barrier((points, dense))
    part, *shared = pl.pallas_call(
        first_chunk_kernel(chunks[0]),
        out_shape=(
            part_shape(len(chunks[0])),
            jax.ShapeDtypeStruct((own * width, 64), BF16),
            jax.ShapeDtypeStruct((64, own * width), BF16),
            jax.ShapeDtypeStruct((48, own * width), BF16),
            jax.ShapeDtypeStruct((own * width, 128), BF16),
            jax.ShapeDtypeStruct((own, 3 * halo), BF16),
        ),
        in_specs=[vmem] * 4,
        out_specs=(vmem,) * 6,
        scratch_shapes=[pltpu.VMEM((8, own * width), F32)],
        compiler_params=room(10),
        cost_estimate=cost,
        name="chunk_0",
    )(late_points, near_list, near_count.reshape(1, own), vectors)
    parts.append(part)
    summands = [
        from_inner[extra:, n * 2 * width : (n + 1) * 2 * width].astype(F32) for n in range(3)
    ]
    pair_gram = gram = dense + (summands[0] + (summands[1] + summands[2]))
    gram, parts[0] = lax.optimization_barrier((gram, parts[0]))
    work = [("layers", chunk) for chunk in chunks[1:]] + [("pairs", chunk) for chunk in pair_chunks]
    first_rows, first_cols, second_cols, second_rows, switches = shared
    for n in range(max(len(steps) + 1, len(work))):
        before = gram
        if n < len(steps):
            if n == len(steps) - sub_bits + 1:
                gram = before = jnp.concatenate([pair_gram, gram], axis=0)
            gram = exchange(gram, steps[n])
        elif n == len(steps):
            handed = lax.ppermute(
                gram, AXES, [(i, i - 1) for i in range(1, lax.axis_size(AXES), 2)]
            )
            gram = jnp.where(lax.axis_index("sub") % 2 == 1, gram, handed)
        if n < len(work):
            kind, chunk = work[n]
            if kind == "layers":
                out = pl.pallas_call(
                    layers_chunk_kernel(chunk, halo),
                    out_shape=part_shape(len(chunk)),
                    in_specs=[hbm] + [vmem] * 4,
                    out_specs=vmem,
                    compiler_params=room(10),
                    cost_estimate=cost,
                    name=f"chunk_{n + 1}",
                )(before, first_rows, second_cols, switches, vectors)
                parts.append(out)
            else:
                out = pl.pallas_call(
                    pairs_chunk_kernel(chunk, width),
                    out_shape=block_shape(len(chunk)),
                    in_specs=[hbm, smem] + [vmem] * 2,
                    out_specs=vmem,
                    compiler_params=room(10),
                    cost_estimate=cost,
                    name=f"chunk_{n + 1}",
                )(before, far_list, first_cols, second_rows)
                plan.update((index, (len(blocks), m)) for m, index in enumerate(chunk))
                blocks.append(out)
            gram, out = lax.optimization_barrier((gram, out))
            (parts if kind == "layers" else blocks)[-1] = out

    edge_pairs = [index for index in range(own // 2) if index not in plan]
    plan.update((index, (len(blocks), m)) for m, index in enumerate(edge_pairs))
    near_chunks = [chunk for chunk in chunks if chunk]
    split_factors = jax.ShapeDtypeStruct((total * width, 2 * width), BF16)
    near, high, low, edge_blocks, device_factor, group_factor, root_factor = pl.pallas_call(
        functools.partial(leaves_kernel, near_chunks, edge_pairs, members, groups),
        out_shape=(
            jax.ShapeDtypeStruct(vectors.shape, BF16),
            split_factors,
            split_factors,
            block_shape(len(edge_pairs)),
            square,
            square,
            square,
        ),
        in_specs=[hbm] * len(parts) + [smem] + [vmem] * 9 + [hbm] * 2 + [vmem],
        out_specs=(hbm,) + (vmem,) * 6,
        scratch_shapes=[
            pltpu.VMEM((2, halo, columns), BF16),
            pltpu.VMEM((2, width + 32, columns), BF16),
            pltpu.VMEM((8, PAD * width), F32),
            pltpu.VMEM((2, 48, PAD * width), BF16),
            pltpu.VMEM((total * width, 2 * width), BF16),
            pltpu.VMEM((2, halo, columns), BF16),
            pltpu.VMEM((total * STRIDE, 2 * width), F32),
            pltpu.VMEM((width, width, 128), F32),
            pltpu.VMEM((total * STRIDE, 2 * width), F32),
            pltpu.SemaphoreType.DMA((6 + len(parts),)),
        ],
        compiler_params=room(24),
        name="leaves",
    )(
        *parts,
        far_list,
        basis,
        top,
        gram,
        device_transfer,
        *shared,
        from_inner,
        from_outer,
        vectors,
    )

    coupling = pl.pallas_call(
        functools.partial(far_kernel, plan),
        out_shape=jax.ShapeDtypeStruct((width, own * far_index.shape[1] * width), BF16),
        in_specs=[smem] + [vmem] * (3 + len(blocks)),
        out_specs=vmem,
        compiler_params=room(16),
        name="far",
    )(far_list, high, low, *blocks, edge_blocks)
    return near, coupling.T, device_factor, group_factor, root_factor


def solution(mesh):
    split = P(AXES, None)
    return jax.shard_map(
        per_device,
        mesh=mesh,
        in_specs=(P(None, AXES), split, split, split, split, split, P(AXES), split),
        out_specs=(split, split, split, split, split),
        check_vma=False,
    )
```

```python
import functools
import math

import jax
import jax.numpy as jnp
from jax import lax
from jax.experimental import pallas as pl
from jax.experimental.pallas import tpu as pltpu
from jax.sharding import PartitionSpec as P

LAYER = 4
PAD = 8
LONG_SQ = 2.25
RATIO = 25.0
SCALE = 0.5 / LONG_SQ
HALF = math.log(0.5)
OFF = -16384.0
STRIDE = 40
AXES = ("group", "sub")
F32 = jnp.float32
BF16 = jnp.bfloat16


def room(megabytes):
    return pltpu.CompilerParams(vmem_limit_bytes=int(megabytes * 1024 * 1024))


def split2(value):
    high = value.astype(BF16)
    return high, (value - high.astype(F32)).astype(BF16)


def split3(value):
    high = value.astype(BF16)
    rest = value - high.astype(F32)
    middle = rest.astype(BF16)
    return high, middle, (rest - middle.astype(F32)).astype(BF16)


def mm(left, right):
    return jnp.dot(left, right, preferred_element_type=F32)


def mm_nt(left, right):
    return lax.dot_general(left, right, (((1,), (1,)), ((), ())), preferred_element_type=F32)


def exact(left, right):
    return jnp.dot(left, right, precision=lax.Precision.HIGHEST, preferred_element_type=F32)


def iota(shape, dim):
    return lax.broadcasted_iota(jnp.int32, shape, dim)


def tree_kernel(
    points_in, basis_in, below_in, transfer_in, vectors,
    dense, top, outer, inner, points, basis, below, transfer, sems,
):
    width = basis.shape[0]
    count = basis.shape[1] // width
    halo = LAYER * width
    span = PAD * width
    rows = vectors.shape[0]
    odd = lax.axis_index("sub") % 2
    sides = ((outer, odd), (inner, 1 - odd))
    basis_copy, below_copy, points_copy, transfer_copy = loads = [
        pltpu.make_async_copy(source, target, sems.at[n])
        for n, (source, target) in enumerate(
            (
                (basis_in, basis),
                (below_in, below),
                (points_in, points),
                (transfer_in, transfer),
            )
        )
    ]
    copies = [
        pltpu.make_async_copy(
            vectors.at[pl.ds(pl.multiple_of(last * (rows - halo), 16), halo), :],
            target.at[pl.ds(0, halo), :],
            sems.at[4 + n],
        )
        for n, (target, last) in enumerate(sides)
    ]
    for copy in loads + copies:
        copy.start()
    both = 2 * width
    lane = iota((width, 2 * both), 1)

    def times(above, columns):
        found = []
        for n in range(above.shape[1] // both):
            parts = jnp.concatenate(split3(above[:, n * both : (n + 1) * both]), axis=1)
            block = columns(n * 2 * both)
            zero = jnp.zeros_like(block)
            block = jnp.concatenate(
                [jnp.where(lane < both, block, zero), jnp.where(lane < both, zero, block)], axis=0
            )
            found.append(mm(parts, jnp.concatenate([block] * 3, axis=0)))
        return jnp.concatenate(found, axis=1)

    below_copy.wait()
    transfer_copy.wait()
    end = below.shape[1]
    tops = below[:, end - both : end]
    turned = jnp.concatenate(split3(transfer[...].T), axis=1)
    above = jnp.concatenate(
        [tops.astype(F32), mm(turned, jnp.concatenate([tops] * 3, axis=0))], axis=0
    )
    end -= both
    nodes = 4
    while nodes < count:
        start = end - nodes * width
        above = times(above, lambda at, start=start: below[:, start + at : start + at + 2 * both])
        end = start
        nodes *= 2
    basis_copy.wait()
    values = times(above, lambda at: basis[:, at : at + 2 * both])
    high, middle, low = split3(values)
    total = mm_nt(
        jnp.concatenate([high, high, high, middle, middle, low], axis=1),
        jnp.concatenate([high, middle, low, high, middle, high], axis=1),
    ) * (1.0 / count)
    top[...] = fold(total[:width, :width])
    halves = fold(total[width:, width:])
    dense[...] = halves
    inner[halo + width + 32 :, :] = jnp.concatenate(split3(halves), axis=1)

    points_copy.wait()

    for target, last in sides:
        bases = basis[:, count * width - span :], basis[:, 0:span]
        last_three, first_three = (
            jnp.concatenate(
                [block[:, (at + skip) * width : (at + skip + 3) * width] for at in (0, LAYER)],
                axis=1,
            )
            for skip, block in zip((1, 0), bases)
        )
        target[halo : halo + width, :] = jnp.where(last == 1, last_three, first_three)
        coords = jnp.where(last == 1, points[:, count * width - span :], points[:, 0:span])
        for m in range(2):
            high, low = split2(coords[:, m * halo : (m + 1) * halo])
            base = halo + width + 16 * m
            target[base : base + 16, :] = jnp.zeros((16, target.shape[1]), BF16)
            target[base : base + 3, 0:halo] = high
            target[base + 8 : base + 11, 0:halo] = low
    for copy in copies:
        copy.wait()


def factor_lanes(work, width, beside):
    panels = width // 8
    row = iota((8, 128), 0)

    def spread(j, i):
        return jnp.broadcast_to(work[j, i : i + 1, :], (8, 128))

    for p in range(panels):
        at = 8 * p
        entry = {(k, m): spread(at + k, at + m) for k in range(8) for m in range(k, 8)}
        scales = []
        for k in range(8):
            scales.append(lax.rsqrt(entry[k, k]))
            for m in range(k + 1, 8):
                entry[k, m] = entry[k, m] * scales[k]
            for m in range(k + 1, 8):
                for q in range(m, 8):
                    entry[m, q] = entry[m, q] - entry[k, m] * entry[k, q]
        for i in range(p, panels):
            tile = [work[at + k, 8 * i : 8 * i + 8, :] for k in range(8)]
            for k in range(8):
                tile[k] = tile[k] * scales[k]
                for m in range(k + 1, 8):
                    tile[m] = tile[m] - tile[k] * entry[k, m]
            for k in range(8):
                work[at + k, 8 * i : 8 * i + 8, :] = (
                    jnp.where(row >= k, tile[k], 0.0) if i == p else tile[k]
                )
        beside(p)
        for q in range(p + 1, panels):
            for start in range(q, panels, 2):
                group = range(start, min(start + 2, panels))
                accs = {
                    (i, k): work[8 * q + k, 8 * i : 8 * i + 8, :] for i in group for k in range(8)
                }
                for j in range(at, at + 8):
                    factors = [spread(j, 8 * q + k) for k in range(8)]
                    for i in group:
                        column = work[j, 8 * i : 8 * i + 8, :]
                        for k in range(8):
                            accs[i, k] = accs[i, k] - column * factors[k]
                for (i, k), value in accs.items():
                    work[8 * q + k, 8 * i : 8 * i + 8, :] = value


def fold(matrix):
    half = matrix.shape[0] // 2
    return jnp.concatenate([matrix[:half], matrix[half:]], axis=1)


def unfold(matrix):
    half = matrix.shape[1] // 2
    return jnp.concatenate([matrix[:, :half], matrix[:, half:]], axis=0)


def to_lanes(grams, work, width, many):
    for i in range(width // 2):
        both = grams[pl.ds(i, many, stride=STRIDE), :].T
        work[i, :, 0:many] = both[0:width]
        work[i + width // 2, :, 0:many] = both[width:]


def from_lanes(work, factors, width, many):
    for i in range(width // 2):
        both = []
        for j in (i, i + width // 2):
            skip = j // 8 * 8
            both += [jnp.zeros((skip, many), F32)] * bool(skip) + [work[j, skip:, 0:many]]
        factors[pl.ds(i, many, stride=STRIDE), :] = jnp.concatenate(both, axis=0).T


def gaussians(exponent):
    return jnp.exp(exponent) + jnp.exp(exponent * RATIO - RATIO * HALF)


def features(place, leaf, center):
    sub = iota(place.shape, 0)
    corner = jnp.where(sub == 0, leaf % 2 - 1, leaf // 2 % 2 - 1)
    corner = jnp.where(sub == 2, leaf // LAYER - center, corner)
    place = jnp.where(sub < 3, place + corner.astype(F32), 0.0)
    norm = jnp.sum(place * place, axis=0, keepdims=True) * SCALE
    first = jnp.where(sub == 3, -norm, jnp.where(sub == 4, 1.0, place))
    second = jnp.where(
        sub == 3, 1.0, jnp.where(sub == 4, HALF - norm, place * (2.0 * SCALE))
    )
    fh, fm, fl = [v.astype(F32) for v in split3(first)]
    sh, sm, sl = [v.astype(F32) for v in split3(second)]
    return (
        jnp.concatenate([fh, fh, fh, fm, fm, fl], axis=0),
        jnp.concatenate([sh, sm, sl, sh, sm, sh], axis=0),
    )


def rows_of(second):
    blank = jnp.zeros((16, second.shape[1]), F32)
    return jnp.concatenate([second, blank, second, blank], axis=0).T.astype(BF16)


def near_weights(first_rows, second, switches, index, halo):
    group = index // 4 * 16
    columns = jnp.concatenate([second, switches[group : group + 16, :]], axis=0)
    return gaussians(mm(first_rows[index * halo : (index + 1) * halo, :], columns)).astype(BF16)


def prepare(
    points, near_list, near_used, first_rows, first_cols, second_cols, second_rows, switches, place
):
    rows = points.shape[1]
    own = near_list.shape[1]
    width = rows // own
    place[...] = jnp.zeros(place.shape, F32)
    place[0:3, :] = points[...]
    leaf = iota((8, rows), 1) // width
    first, second = features(place[...], leaf, own // LAYER // 2)
    hot_leaf = iota((16, rows), 1) // width
    hot = jnp.where(hot_leaf % 16 == iota((16, rows), 0), 1.0, 0.0).astype(F32)
    first = jnp.concatenate([first, hot], axis=0)
    first_cols[...] = first.astype(BF16)
    second_cols[...] = second.astype(BF16)
    first_rows[...] = first.T.astype(BF16)
    second_rows[...] = rows_of(second)

    start_leaf = lax.axis_index(AXES) * own
    target = iota((1, own), 1)
    base_leaf = start_leaf + target // LAYER * LAYER - LAYER
    found = jnp.zeros((16, own), jnp.bool_)
    place_row = iota((16, own), 0)
    for n in range(near_list.shape[0]):
        spot = jnp.where(near_used[...] > n, near_list[n : n + 1, :] - base_leaf, -1)
        found = jnp.logical_or(found, place_row == spot)
    bias = jnp.where(found, 0.0, OFF).astype(F32)
    span = 3 * LAYER * width
    expand = jnp.where(iota((16, span), 0) == iota((16, span), 1) // width, 1.0, 0.0)
    switches[...] = mm(bias.T.astype(BF16), expand.astype(BF16)).astype(BF16)


def inner_layers(layers, vectors, first_rows, second_cols, switches, out, halo):
    for n, index in enumerate(layers):
        around = slice((index - 1) * halo, (index + 2) * halo)
        weights = near_weights(first_rows, second_cols[:, around], switches, index, halo)
        out[n * halo : (n + 1) * halo, :] = mm(weights, vectors[around, :]).astype(BF16)


def far_blocks(pairs, far_list, second_rows, first_cols, out, width, base, places):
    far, own = far_list.shape
    both = 2 * width
    start_leaf = lax.axis_index(AXES) * own
    square = iota((both, both), 0) // width == iota((both, both), 1) // width
    lane = iota((far * width, both), 1) < width
    exponents = []
    for index in pairs:
        t = 2 * index
        picked = []
        for m in range(2):
            spots = [
                pl.multiple_of((far_list[f, t + m] - start_leaf + base) * width, width)
                for f in range(far)
            ]
            picked.append(
                jnp.concatenate([second_rows[pl.ds(spot, width), :] for spot in spots], axis=0)
            )
        cols = first_cols[:, t * width : t * width + both]
        targets = jnp.where(
            square, jnp.concatenate([cols, cols], axis=0), jnp.zeros((both, both), BF16)
        )
        exponents.append(mm(jnp.where(lane, picked[0], picked[1]), targets))
    for place, exponent in zip(places, exponents):
        high, low = split2(gaussians(exponent))
        at = place * far * width
        out[at : at + far * width, 0:both] = high
        out[at : at + far * width, both : 2 * both] = low


def first_chunk_kernel(layers):
    def body(
        points, near_list, near_used, vectors,
        out, first_rows, first_cols, second_cols, second_rows, switches, place,
    ):
        prepare(
            points,
            near_list,
            near_used,
            first_rows,
            first_cols,
            second_cols,
            second_rows,
            switches,
            place,
        )
        halo = LAYER * points.shape[1] // near_list.shape[1]
        inner_layers(layers, vectors, first_rows, second_cols, switches, out, halo)

    return body


def chunk_kernel(layers, pairs, halo, width):
    def body(after, far_in, *refs):
        first_rows, second_cols, switches, vectors, first_cols, second_rows = refs[:6]
        outs, far_list, sem = refs[6:-2], refs[-2], refs[-1]
        if pairs:
            copy = pltpu.make_async_copy(far_in, far_list, sem)
            copy.start()
        if layers:
            inner_layers(layers, vectors, first_rows, second_cols, switches, outs[0], halo)
        if pairs:
            copy.wait()
            far_blocks(
                pairs, far_list, second_rows, first_cols, outs[-1], width, 0, range(len(pairs))
            )

    return body


def edges_kernel(
    after, inner, outer, first_rows, second_cols, switches, vectors,
    out, halo_rows, ends, sides, place, halo_cols, sems,
):
    halo = ends.shape[1]
    width = halo // LAYER
    own = vectors.shape[0] // width
    layers = own // LAYER
    extra = sides.shape[1]
    odd = lax.axis_index("sub") % 2
    arrived = ((inner, 1 - odd), (outer, odd))
    side_copies = [
        pltpu.make_async_copy(
            block.at[pl.ds(halo + width, extra), :], sides.at[side], sems.at[n]
        )
        for n, (block, side) in enumerate(arrived)
    ]
    end_copies = [
        pltpu.make_async_copy(block.at[pl.ds(0, halo), :], ends.at[side], sems.at[2 + n])
        for n, (block, side) in enumerate(arrived)
    ]
    for copy in side_copies + end_copies:
        copy.start()
    lanes = PAD * width
    place[...] = jnp.zeros(place.shape, F32)
    for copy in side_copies:
        copy.wait()
    for side, first_leaf in enumerate((-PAD, own)):
        for n in range(2):
            values = sides[side, 16 * n : 16 * n + 16, 0:halo].astype(F32)
            place[0:3, n * halo : (n + 1) * halo] = values[0:3, :] + values[8:11, :]
        leaf = iota((8, lanes), 1) // width + (first_leaf + PAD)
        second = features(place[...], leaf, layers // 2 + PAD // LAYER)[1]
        halo_cols[side, :, :] = second.astype(BF16)
        halo_rows[side * lanes : (side + 1) * lanes, :] = rows_of(second)
    weights = [
        near_weights(
            first_rows, jnp.concatenate(columns, axis=1), switches, index, halo
        )
        for index, columns in (
            (0, [halo_cols[0, :, halo:], second_cols[:, 0 : 2 * halo]]),
            (layers - 1, [second_cols[:, (layers - 2) * halo :], halo_cols[1, :, 0:halo]]),
        )
    ]
    for copy in end_copies:
        copy.wait()
    value = mm(weights[0][:, 0:halo], ends[0, :, :])
    value = value + mm(weights[0][:, halo:], vectors[0 : 2 * halo, :])
    out[0:halo, :] = value.astype(BF16)
    value = mm(weights[1][:, 0 : 2 * halo], vectors[(layers - 2) * halo :, :])
    value = value + mm(weights[1][:, 2 * halo :], ends[1, :, :])
    out[halo:, :] = value.astype(BF16)


def leaves_kernel(chunks, edge_pairs, members, groups, *refs):
    outer_count = len(chunks) + 1
    near_parts = refs[:outer_count]
    (
        far_in,
        basis,
        top,
        upper,
        transfer,
        first_cols,
        own_rows,
        halo_rows,
        inner,
        outer,
        near,
        high,
        low,
        edge_blocks,
        device_factor,
        group_factor,
        root_factor,
        far_list,
        sides,
        second_rows,
        grams,
        work,
        factors,
        sems,
    ) = refs[outer_count:]
    width = basis.shape[0]
    own = basis.shape[1] // width
    total = own + 2 * PAD
    halo = LAYER * width
    layers = own // LAYER
    both = 2 * width
    odd = lax.axis_index("sub") % 2
    side_copies = [
        pltpu.make_async_copy(block.at[pl.ds(halo, width), :], sides.at[side], sems.at[n])
        for n, (block, side) in enumerate(((inner, 1 - odd), (outer, odd)))
    ]
    list_copy = pltpu.make_async_copy(far_in, far_list, sems.at[2])
    places = [(part, 0, chunk[0], len(chunk)) for part, chunk in zip(near_parts, chunks)]
    places += [(near_parts[-1], n, index, 1) for n, index in enumerate((0, layers - 1))]
    near_copies = [
        pltpu.make_async_copy(
            part.at[pl.ds(start * halo, many * halo), :],
            near.at[pl.ds(index * halo, many * halo), :],
            sems.at[3 + n],
        )
        for n, (part, start, index, many) in enumerate(places)
    ]
    for copy in side_copies + [list_copy] + near_copies:
        copy.start()

    lane = iota((width, both), 1)
    for n in range(own // 2):
        pair = basis[:, n * both : (n + 1) * both]
        zero = jnp.zeros_like(pair)
        stacked = jnp.concatenate(
            [jnp.where(lane < width, pair, zero), jnp.where(lane < width, zero, pair)], axis=0
        )
        value = mm_nt(stacked, pair)
        for m in range(2):
            at = (PAD + 2 * n + m) * STRIDE
            grams[at : at + width // 2, :] = fold(value[m * width : (m + 1) * width])
    spare = (0, LAYER, total - LAYER - 1, total - 1)
    for spot, gram in zip(
        spare,
        (
            top[...],
            upper[0 : width // 2, :] * (1.0 / members),
            upper[width // 2 :, :] * (1.0 / (members * groups)),
            top[...],
        ),
    ):
        grams[spot * STRIDE : spot * STRIDE + width // 2, :] = gram
    for copy in side_copies:
        copy.wait()
    for side, spots in enumerate(
        ((1, 2, 3, 5, 6, 7), tuple(PAD + own + m for m in (0, 1, 2, 4, 5, 6)))
    ):
        for n, spot in enumerate(spots):
            piece = sides[side, 0:width, n * width : (n + 1) * width]
            grams[spot * STRIDE : spot * STRIDE + width // 2, :] = fold(mm_nt(piece, piece))

    lanes = PAD * width
    second_rows[0:lanes, :] = halo_rows[0:lanes, :]
    second_rows[lanes : lanes + own * width, :] = own_rows[...]
    second_rows[lanes + own * width :, :] = halo_rows[lanes:, :]
    panels = width // 8

    def beside(p):
        places = range(p * len(edge_pairs) // panels, (p + 1) * len(edge_pairs) // panels)
        far_blocks(
            [edge_pairs[n] for n in places],
            far_list,
            second_rows,
            first_cols,
            edge_blocks,
            width,
            PAD,
            places,
        )

    to_lanes(grams, work, width, total)
    list_copy.wait()
    factor_lanes(work, width, beside)
    from_lanes(work, factors, width, total)
    device_factor[...] = exact(unfold(factors[0 : width // 2, :]), transfer[...])
    for target, spot in ((group_factor, spare[1]), (root_factor, spare[2])):
        target[...] = unfold(factors[spot * STRIDE : spot * STRIDE + width // 2, :])
    left_lanes = iota((width // 2, both), 1) < width
    for spot in range(total):
        rows = factors[spot * STRIDE : spot * STRIDE + width // 2, :]
        turned = pltpu.roll(rows, width, 1)
        twice = jnp.concatenate(
            [jnp.where(left_lanes, rows, turned), jnp.where(left_lanes, turned, rows)], axis=0
        )
        at = slice(spot * width, (spot + 1) * width)
        high[at, :], low[at, :] = split2(twice)
    for copy in near_copies:
        copy.wait()


def far_kernel(plan, far_in, high, low, *refs):
    blocks, (coupling, far_list, sem) = refs[:-3], refs[-3:]
    copy = pltpu.make_async_copy(far_in, far_list, sem)
    copy.start()
    width = coupling.shape[0]
    far, own = far_list.shape
    both = 2 * width
    start_leaf = lax.axis_index(AXES) * own
    square = iota((both, both), 0) // width == iota((both, both), 1) // width
    lane = iota((width, both), 1) < width
    zero = jnp.zeros((both, both), BF16)

    def diagonal(value):
        return jnp.where(square, value, zero)

    for start in range(0, own // 2, 4):
        indices = range(start, start + 4)
        halves = []
        for index in indices:
            source, place = plan[index]
            at = place * far * width
            kh = blocks[source][at : at + far * width, 0:both]
            kl = blocks[source][at : at + far * width, both : 2 * both]
            at = (PAD + 2 * index) * width
            rh = diagonal(high[at : at + both, :])
            rl = diagonal(low[at : at + both, :])
            halves.append(
                mm_nt(
                    jnp.concatenate([kh, kl, kh], axis=1), jnp.concatenate([rh, rh, rl], axis=1)
                )
            )
        if start == 0:
            copy.wait()
        outs = []
        for index, half in zip(indices, halves):
            zh, zl = split2(half * (1.0 / width))
            for f in range(far):
                spots = [
                    pl.multiple_of((far_list[f, 2 * index + m] - start_leaf + PAD) * width, width)
                    for m in range(2)
                ]
                sh, sl = (
                    jnp.where(lane, *(part[pl.ds(spot, width), :] for spot in spots))
                    for part in (high, low)
                )
                a = slice(f * width, (f + 1) * width)
                ph = diagonal(jnp.concatenate([zh[a], zh[a]], axis=0))
                plow = diagonal(jnp.concatenate([zl[a], zl[a]], axis=0))
                outs.append(
                    mm(
                        jnp.concatenate([sh, sh, sl], axis=1),
                        jnp.concatenate([ph, plow, ph], axis=0),
                    )
                )
        for n, index in enumerate(indices):
            three = outs[n * far : (n + 1) * far]
            line = jnp.concatenate(
                [out[:, 0:width] for out in three] + [out[:, width:both] for out in three], axis=1
            )
            at = index * 2 * far * width
            coupling[:, at : at + 2 * far * width] = line.astype(BF16)


def swap_inner(block):
    return lax.ppermute(block, AXES, [(i, i ^ 1) for i in range(lax.axis_size(AXES))])


def swap_outer(block):
    many = lax.axis_size(AXES)
    return lax.ppermute(block, AXES, [(i, (i + 1 if i % 2 else i - 1) % many) for i in range(many)])


def exchange(value, distance):
    pairs = [(i, i ^ distance) for i in range(lax.axis_size(AXES))]
    return value + lax.ppermute(value, AXES, pairs)


def per_device(
    points, leaf_basis, inner_transfer, device_transfer, vectors, near_index, near_count, far_index
):
    own = near_index.shape[0]
    width = leaf_basis.shape[1]
    columns = vectors.shape[1]
    halo = LAYER * width
    half = width // 2
    layers = own // LAYER
    total = own + 2 * PAD
    members, groups = lax.axis_size("sub"), lax.axis_size("group")
    vmem = pl.BlockSpec(memory_space=pltpu.VMEM)
    hbm = pl.BlockSpec(memory_space=pl.ANY)
    square = jax.ShapeDtypeStruct((width, width), F32)
    extra = halo + width + 32

    def block_of(rows):
        return jax.ShapeDtypeStruct((rows, columns), BF16)

    basis = leaf_basis.T
    near_list, far_list = near_index.T, far_index.T
    cost = pl.CostEstimate(flops=10**9, bytes_accessed=4 * 10**6, transcendentals=10**6)

    dense, top, to_outer, to_inner = pl.pallas_call(
        tree_kernel,
        out_shape=(
            jax.ShapeDtypeStruct((half, 2 * width), F32),
            jax.ShapeDtypeStruct((half, 2 * width), F32),
            block_of(extra),
            block_of(extra + half),
        ),
        in_specs=[hbm] * 5,
        out_specs=(vmem,) * 4,
        scratch_shapes=[
            pltpu.VMEM((3, own * width), F32),
            pltpu.VMEM((width, own * width), BF16),
            pltpu.VMEM((width, (own - 2) * width), BF16),
            pltpu.VMEM((width, width), F32),
            pltpu.SemaphoreType.DMA((6,)),
        ],
        compiler_params=room(60),
        name="tree",
    )(points, basis, inner_transfer.T, device_transfer, vectors)
    from_inner = swap_inner(to_inner)
    from_outer = swap_outer(to_outer)

    sub_bits = members.bit_length() - 1
    steps = [members << bit for bit in range(groups.bit_length() - 1)]
    steps += [1 << bit for bit in range(1, sub_bits)]
    inner_pairs = list(range(PAD // 2, (own - PAD) // 2))
    few = len(inner_pairs) // 2
    chunks = [[1, 2], [3, 4], [5], [6]]
    pair_chunks = [[], [], inner_pairs[:few], inner_pairs[few:]]
    blocks, plan, parts = [], {}, []

    def part_shape(count):
        return jax.ShapeDtypeStruct((count * halo, columns), BF16)

    def block_shape(count):
        return jax.ShapeDtypeStruct((count * far_index.shape[1] * width, 4 * width), BF16)

    late_points, dense = lax.optimization_barrier((points, dense))
    part, *shared = pl.pallas_call(
        first_chunk_kernel(chunks[0]),
        out_shape=(
            part_shape(len(chunks[0])),
            jax.ShapeDtypeStruct((own * width, 64), BF16),
            jax.ShapeDtypeStruct((64, own * width), BF16),
            jax.ShapeDtypeStruct((48, own * width), BF16),
            jax.ShapeDtypeStruct((own * width, 128), BF16),
            jax.ShapeDtypeStruct((own, 3 * halo), BF16),
        ),
        in_specs=[vmem] * 4,
        out_specs=(vmem,) * 6,
        scratch_shapes=[pltpu.VMEM((8, own * width), F32)],
        compiler_params=room(10),
        cost_estimate=cost,
        name="chunk_0",
    )(late_points, near_list, near_count.reshape(1, own), vectors)
    parts.append(part)
    summands = [
        from_inner[extra:, n * 2 * width : (n + 1) * 2 * width].astype(F32) for n in range(3)
    ]
    pair_gram = gram = dense + (summands[0] + (summands[1] + summands[2]))
    gram, parts[0] = lax.optimization_barrier((gram, parts[0]))
    first_rows, first_cols, second_cols, second_rows, switches = shared
    for n in range(max(len(steps), len(chunks))):
        before = gram
        if n < len(steps):
            if n == len(steps) - sub_bits + 1:
                gram = before = jnp.concatenate([pair_gram, gram], axis=0)
            gram = exchange(gram, steps[n])
        if n + 1 < len(chunks):
            layer_chunk, pair_chunk = chunks[n + 1], pair_chunks[n + 1]
            shapes = [part_shape(len(layer_chunk))] * bool(layer_chunk)
            shapes += [block_shape(len(pair_chunk))] * bool(pair_chunk)
            outs = pl.pallas_call(
                chunk_kernel(layer_chunk, pair_chunk, halo, width),
                out_shape=tuple(shapes),
                in_specs=[hbm] * 2 + [vmem] * 6,
                out_specs=(vmem,) * len(shapes),
                scratch_shapes=[
                    pltpu.SMEM(far_list.shape, jnp.int32),
                    pltpu.SemaphoreType.DMA,
                ],
                compiler_params=room(10),
                cost_estimate=cost,
                name=f"chunk_{n + 1}",
            )(before, far_list, first_rows, second_cols, switches, vectors, first_cols, second_rows)
            gram, outs = lax.optimization_barrier((gram, outs))
            if layer_chunk:
                parts.append(outs[0])
            if pair_chunk:
                plan.update((index, (len(blocks), m)) for m, index in enumerate(pair_chunk))
                blocks.append(outs[-1])
        elif n + 1 == len(chunks):
            edge_part, halo_rows = pl.pallas_call(
                edges_kernel,
                out_shape=(
                    part_shape(2),
                    jax.ShapeDtypeStruct((2 * PAD * width, 2 * width), BF16),
                ),
                in_specs=[hbm] * 3 + [vmem] * 4,
                out_specs=(vmem,) * 2,
                scratch_shapes=[
                    pltpu.VMEM((2, halo, columns), BF16),
                    pltpu.VMEM((2, 32, columns), BF16),
                    pltpu.VMEM((8, PAD * width), F32),
                    pltpu.VMEM((2, 48, PAD * width), BF16),
                    pltpu.SemaphoreType.DMA((4,)),
                ],
                compiler_params=room(10),
                cost_estimate=cost,
                name="edges",
            )(before, from_inner, from_outer, first_rows, second_cols, switches, vectors)
            gram, edge_part = lax.optimization_barrier((gram, edge_part))

    edge_pairs = [index for index in range(own // 2) if index not in plan]
    plan.update((index, (len(blocks), m)) for m, index in enumerate(edge_pairs))
    split_factors = jax.ShapeDtypeStruct((total * width, 2 * width), BF16)
    near, high, low, edge_blocks, device_factor, group_factor, root_factor = pl.pallas_call(
        functools.partial(leaves_kernel, chunks, edge_pairs, members, groups),
        out_shape=(
            jax.ShapeDtypeStruct(vectors.shape, BF16),
            split_factors,
            split_factors,
            block_shape(len(edge_pairs)),
            square,
            square,
            square,
        ),
        in_specs=[hbm] * (len(parts) + 2) + [vmem] * 7 + [hbm] * 2,
        out_specs=(hbm,) + (vmem,) * 6,
        scratch_shapes=[
            pltpu.SMEM(far_list.shape, jnp.int32),
            pltpu.VMEM((2, width, columns), BF16),
            pltpu.VMEM((total * width, 2 * width), BF16),
            pltpu.VMEM((total * STRIDE, 2 * width), F32),
            pltpu.VMEM((width, width, 128), F32),
            pltpu.VMEM((total * STRIDE, 2 * width), F32),
            pltpu.SemaphoreType.DMA((5 + len(parts),)),
        ],
        compiler_params=room(24),
        name="leaves",
    )(
        *parts,
        edge_part,
        far_list,
        basis,
        top,
        gram,
        device_transfer,
        first_cols,
        second_rows,
        halo_rows,
        from_inner,
        from_outer,
    )

    coupling = pl.pallas_call(
        functools.partial(far_kernel, plan),
        out_shape=jax.ShapeDtypeStruct((width, own * far_index.shape[1] * width), BF16),
        in_specs=[hbm] + [vmem] * (3 + len(blocks)),
        out_specs=vmem,
        scratch_shapes=[
            pltpu.SMEM(far_list.shape, jnp.int32),
            pltpu.SemaphoreType.DMA,
        ],
        compiler_params=room(16),
        name="far",
    )(far_list, high, low, *blocks, edge_blocks)
    return near, coupling.T, device_factor, group_factor, root_factor


def solution(mesh):
    split = P(AXES, None)
    return jax.shard_map(
        per_device,
        mesh=mesh,
        in_specs=(P(None, AXES), split, split, split, split, split, P(AXES), split),
        out_specs=(split, split, split, split, split),
        check_vma=False,
    )
```

```python
import functools
import math

import jax
import jax.numpy as jnp
from jax import lax
from jax.experimental import pallas as pl
from jax.experimental.pallas import tpu as pltpu
from jax.sharding import PartitionSpec as P

LAYER = 4
PAD = 8
LONG_SQ = 2.25
RATIO = 25.0
SCALE = 0.5 / LONG_SQ
HALF = math.log(0.5)
OFF = -16384.0
STRIDE = 40
AXES = ("group", "sub")
F32 = jnp.float32
BF16 = jnp.bfloat16


def room(megabytes):
    return pltpu.CompilerParams(vmem_limit_bytes=int(megabytes * 1024 * 1024))


def split2(value):
    high = value.astype(BF16)
    return high, (value - high.astype(F32)).astype(BF16)


def split3(value):
    high = value.astype(BF16)
    rest = value - high.astype(F32)
    middle = rest.astype(BF16)
    return high, middle, (rest - middle.astype(F32)).astype(BF16)


def mm(left, right):
    return jnp.dot(left, right, preferred_element_type=F32)


def mm_nt(left, right):
    return lax.dot_general(left, right, (((1,), (1,)), ((), ())), preferred_element_type=F32)


def exact(left, right):
    return jnp.dot(left, right, precision=lax.Precision.HIGHEST, preferred_element_type=F32)


def iota(shape, dim):
    return lax.broadcasted_iota(jnp.int32, shape, dim)


def tree_kernel(
    points_in, basis_in, below_in, transfer_in, vectors,
    dense, top, outer, inner, points, basis, below, transfer, sems,
):
    width = basis.shape[0]
    count = basis.shape[1] // width
    halo = LAYER * width
    span = PAD * width
    rows = vectors.shape[0]
    odd = lax.axis_index("sub") % 2
    sides = ((outer, odd), (inner, 1 - odd))
    basis_copy, below_copy, points_copy, transfer_copy = loads = [
        pltpu.make_async_copy(source, target, sems.at[n])
        for n, (source, target) in enumerate(
            (
                (basis_in, basis),
                (below_in, below),
                (points_in, points),
                (transfer_in, transfer),
            )
        )
    ]
    copies = [
        pltpu.make_async_copy(
            vectors.at[pl.ds(pl.multiple_of(last * (rows - halo), 16), halo), :],
            target.at[pl.ds(0, halo), :],
            sems.at[4 + n],
        )
        for n, (target, last) in enumerate(sides)
    ]
    for copy in loads + copies:
        copy.start()
    both = 2 * width
    lane = iota((width, 2 * both), 1)

    def times(above, columns):
        found = []
        for n in range(above.shape[1] // both):
            parts = jnp.concatenate(split3(above[:, n * both : (n + 1) * both]), axis=1)
            block = columns(n * 2 * both)
            zero = jnp.zeros_like(block)
            block = jnp.concatenate(
                [jnp.where(lane < both, block, zero), jnp.where(lane < both, zero, block)], axis=0
            )
            found.append(mm(parts, jnp.concatenate([block] * 3, axis=0)))
        return jnp.concatenate(found, axis=1)

    same = iota((both, both), 0) // width == iota((both, both), 1) // width
    half_block = jnp.where(same, 0.5, 0.0).astype(F32)
    basis_copy.wait()
    blocks = []
    for n in range(count // 4):
        stacked = jnp.concatenate(
            [basis[:, (2 * n + m) * both : (2 * n + m + 1) * both] for m in range(2)], axis=0
        )
        blocks.append(mm_nt(stacked, stacked) * half_block)
    below_copy.wait()
    halves = []
    for n, block in enumerate(blocks):
        t = below[:, n * both : (n + 1) * both]
        half = mm(jnp.concatenate([t, t, t], axis=1), jnp.concatenate(split3(block), axis=0))
        halves.append((half, t))
    blocks = []
    for n in range(0, len(halves), 2):
        (first, t), (second, u) = halves[n : n + 2]
        x = jnp.concatenate(split3(jnp.concatenate([first, second], axis=0)), axis=1)
        t = jnp.concatenate([t, u], axis=0)
        blocks.append(mm_nt(x, jnp.concatenate([t, t, t], axis=1)) * half_block)

    transfer_copy.wait()
    end = below.shape[1]
    tops = below[:, end - both : end]
    turned = jnp.concatenate(split3(transfer[...].T), axis=1)
    above = jnp.concatenate(
        [tops.astype(F32), mm(turned, jnp.concatenate([tops] * 3, axis=0))], axis=0
    )
    end -= both
    nodes = 4
    while nodes < count // 2:
        start = end - nodes * width
        above = times(above, lambda at, start=start: below[:, start + at : start + at + 2 * both])
        end = start
        nodes *= 2

    total = jnp.zeros((both, both), F32)
    for n, block in enumerate(blocks):
        rows = above[:, n * both : (n + 1) * both]
        high, middle, low = split3(rows)
        gh, gm, gl = split3(block)
        x = mm(
            jnp.concatenate([high, high, high, middle, middle, low], axis=1),
            jnp.concatenate([gh, gm, gl, gh, gm, gh], axis=0),
        )
        xh, xm, xl = split3(x)
        total = total + mm_nt(
            jnp.concatenate([xh, xh, xh, xm, xm, xl], axis=1),
            jnp.concatenate([high, middle, low, high, middle, high], axis=1),
        )
    total = total * (4.0 / count)
    top[...] = fold(total[:width, :width])
    halves = fold(total[width:, width:])
    dense[...] = halves
    inner[halo + width + 32 :, :] = jnp.concatenate(split3(halves), axis=1)

    points_copy.wait()

    for target, last in sides:
        bases = basis[:, count * width - span :], basis[:, 0:span]
        last_three, first_three = (
            jnp.concatenate(
                [block[:, (at + skip) * width : (at + skip + 3) * width] for at in (0, LAYER)],
                axis=1,
            )
            for skip, block in zip((1, 0), bases)
        )
        target[halo : halo + width, :] = jnp.where(last == 1, last_three, first_three)
        coords = jnp.where(last == 1, points[:, count * width - span :], points[:, 0:span])
        for m in range(2):
            high, low = split2(coords[:, m * halo : (m + 1) * halo])
            base = halo + width + 16 * m
            target[base : base + 16, :] = jnp.zeros((16, target.shape[1]), BF16)
            target[base : base + 3, 0:halo] = high
            target[base + 8 : base + 11, 0:halo] = low
    for copy in copies:
        copy.wait()


def factor_lanes(work, width, beside):
    panels = width // 8
    row = iota((8, 128), 0)

    def spread(j, i):
        return jnp.broadcast_to(work[j, i : i + 1, :], (8, 128))

    for p in range(panels):
        at = 8 * p
        entry = {(k, m): spread(at + k, at + m) for k in range(8) for m in range(k, 8)}
        scales = []
        for k in range(8):
            scales.append(lax.rsqrt(entry[k, k]))
            for m in range(k + 1, 8):
                entry[k, m] = entry[k, m] * scales[k]
            for m in range(k + 1, 8):
                for q in range(m, 8):
                    entry[m, q] = entry[m, q] - entry[k, m] * entry[k, q]
        for i in range(p, panels):
            tile = [work[at + k, 8 * i : 8 * i + 8, :] for k in range(8)]
            for k in range(8):
                tile[k] = tile[k] * scales[k]
                for m in range(k + 1, 8):
                    tile[m] = tile[m] - tile[k] * entry[k, m]
            for k in range(8):
                work[at + k, 8 * i : 8 * i + 8, :] = (
                    jnp.where(row >= k, tile[k], 0.0) if i == p else tile[k]
                )
        beside(p)
        for q in range(p + 1, panels):
            for start in range(q, panels, 2):
                group = range(start, min(start + 2, panels))
                accs = {
                    (i, k): work[8 * q + k, 8 * i : 8 * i + 8, :] for i in group for k in range(8)
                }
                for j in range(at, at + 8):
                    factors = [spread(j, 8 * q + k) for k in range(8)]
                    for i in group:
                        column = work[j, 8 * i : 8 * i + 8, :]
                        for k in range(8):
                            accs[i, k] = accs[i, k] - column * factors[k]
                for (i, k), value in accs.items():
                    work[8 * q + k, 8 * i : 8 * i + 8, :] = value


def fold(matrix):
    half = matrix.shape[0] // 2
    return jnp.concatenate([matrix[:half], matrix[half:]], axis=1)


def unfold(matrix):
    half = matrix.shape[1] // 2
    return jnp.concatenate([matrix[:, :half], matrix[:, half:]], axis=0)


def to_lanes(grams, work, width, many):
    for i in range(width // 2):
        both = grams[pl.ds(i, many, stride=STRIDE), :].T
        work[i, :, 0:many] = both[0:width]
        work[i + width // 2, :, 0:many] = both[width:]


def from_lanes(work, factors, width, many):
    for i in range(width // 2):
        both = []
        for j in (i, i + width // 2):
            skip = j // 8 * 8
            both += [jnp.zeros((skip, many), F32)] * bool(skip) + [work[j, skip:, 0:many]]
        factors[pl.ds(i, many, stride=STRIDE), :] = jnp.concatenate(both, axis=0).T


def gaussians(exponent):
    return jnp.exp(exponent) + jnp.exp(exponent * RATIO - RATIO * HALF)


def features(place, leaf, center):
    sub = iota(place.shape, 0)
    corner = jnp.where(sub == 0, leaf % 2 - 1, leaf // 2 % 2 - 1)
    corner = jnp.where(sub == 2, leaf // LAYER - center, corner)
    place = jnp.where(sub < 3, place + corner.astype(F32), 0.0)
    norm = jnp.sum(place * place, axis=0, keepdims=True) * SCALE
    first = jnp.where(sub == 3, -norm, jnp.where(sub == 4, 1.0, place))
    second = jnp.where(
        sub == 3, 1.0, jnp.where(sub == 4, HALF - norm, place * (2.0 * SCALE))
    )
    fh, fm, fl = [v.astype(F32) for v in split3(first)]
    sh, sm, sl = [v.astype(F32) for v in split3(second)]
    return (
        jnp.concatenate([fh, fh, fh, fm, fm, fl], axis=0),
        jnp.concatenate([sh, sm, sl, sh, sm, sh], axis=0),
    )


def rows_of(second):
    blank = jnp.zeros((16, second.shape[1]), F32)
    return jnp.concatenate([second, blank, second, blank], axis=0).T.astype(BF16)


def near_weights(first_rows, second, switches, index, halo):
    group = index // 4 * 16
    columns = jnp.concatenate([second, switches[group : group + 16, :]], axis=0)
    return gaussians(mm(first_rows[index * halo : (index + 1) * halo, :], columns)).astype(BF16)


def prepare(
    points, near_list, near_used, first_rows, first_cols, second_cols, second_rows, switches, place
):
    rows = points.shape[1]
    own = near_list.shape[1]
    width = rows // own
    place[...] = jnp.zeros(place.shape, F32)
    place[0:3, :] = points[...]
    leaf = iota((8, rows), 1) // width
    first, second = features(place[...], leaf, own // LAYER // 2)
    hot_leaf = iota((16, rows), 1) // width
    hot = jnp.where(hot_leaf % 16 == iota((16, rows), 0), 1.0, 0.0).astype(F32)
    first = jnp.concatenate([first, hot], axis=0)
    first_cols[...] = first.astype(BF16)
    second_cols[...] = second.astype(BF16)
    first_rows[...] = first.T.astype(BF16)
    second_rows[...] = rows_of(second)

    start_leaf = lax.axis_index(AXES) * own
    target = iota((1, own), 1)
    base_leaf = start_leaf + target // LAYER * LAYER - LAYER
    found = jnp.zeros((16, own), jnp.bool_)
    place_row = iota((16, own), 0)
    for n in range(near_list.shape[0]):
        spot = jnp.where(near_used[...] > n, near_list[n : n + 1, :] - base_leaf, -1)
        found = jnp.logical_or(found, place_row == spot)
    bias = jnp.where(found, 0.0, OFF).astype(F32)
    span = 3 * LAYER * width
    expand = jnp.where(iota((16, span), 0) == iota((16, span), 1) // width, 1.0, 0.0)
    switches[...] = mm(bias.T.astype(BF16), expand.astype(BF16)).astype(BF16)


def inner_layers(layers, vectors, first_rows, second_cols, switches, out, halo):
    for n, index in enumerate(layers):
        around = slice((index - 1) * halo, (index + 2) * halo)
        weights = near_weights(first_rows, second_cols[:, around], switches, index, halo)
        out[n * halo : (n + 1) * halo, :] = mm(weights, vectors[around, :]).astype(BF16)


def far_blocks(pairs, far_list, second_rows, first_cols, out, width, base, places):
    far, own = far_list.shape
    both = 2 * width
    start_leaf = lax.axis_index(AXES) * own
    square = iota((both, both), 0) // width == iota((both, both), 1) // width
    lane = iota((far * width, both), 1) < width
    exponents = []
    for index in pairs:
        t = 2 * index
        picked = []
        for m in range(2):
            spots = [
                pl.multiple_of((far_list[f, t + m] - start_leaf + base) * width, width)
                for f in range(far)
            ]
            picked.append(
                jnp.concatenate([second_rows[pl.ds(spot, width), :] for spot in spots], axis=0)
            )
        cols = first_cols[:, t * width : t * width + both]
        targets = jnp.where(
            square, jnp.concatenate([cols, cols], axis=0), jnp.zeros((both, both), BF16)
        )
        exponents.append(mm(jnp.where(lane, picked[0], picked[1]), targets))
    for place, exponent in zip(places, exponents):
        high, low = split2(gaussians(exponent))
        at = place * far * width
        out[at : at + far * width, 0:both] = high
        out[at : at + far * width, both : 2 * both] = low


def first_chunk_kernel(layers):
    def body(
        points, near_list, near_used, vectors,
        out, first_rows, first_cols, second_cols, second_rows, switches, place,
    ):
        prepare(
            points,
            near_list,
            near_used,
            first_rows,
            first_cols,
            second_cols,
            second_rows,
            switches,
            place,
        )
        halo = LAYER * points.shape[1] // near_list.shape[1]
        inner_layers(layers, vectors, first_rows, second_cols, switches, out, halo)

    return body


def chunk_kernel(layers, pairs, halo, width):
    def body(after, far_in, *refs):
        first_rows, second_cols, switches, vectors, first_cols, second_rows = refs[:6]
        outs, far_list, sem = refs[6:-2], refs[-2], refs[-1]
        if pairs:
            copy = pltpu.make_async_copy(far_in, far_list, sem)
            copy.start()
        if layers:
            inner_layers(layers, vectors, first_rows, second_cols, switches, outs[0], halo)
        if pairs:
            copy.wait()
            far_blocks(
                pairs, far_list, second_rows, first_cols, outs[-1], width, 0, range(len(pairs))
            )

    return body


def edges_kernel(
    after, inner, outer, first_rows, second_cols, switches, vectors,
    out, halo_rows, ends, sides, place, halo_cols, sems,
):
    halo = ends.shape[1]
    width = halo // LAYER
    own = vectors.shape[0] // width
    layers = own // LAYER
    extra = sides.shape[1]
    odd = lax.axis_index("sub") % 2
    arrived = ((inner, 1 - odd), (outer, odd))
    side_copies = [
        pltpu.make_async_copy(
            block.at[pl.ds(halo + width, extra), :], sides.at[side], sems.at[n]
        )
        for n, (block, side) in enumerate(arrived)
    ]
    end_copies = [
        pltpu.make_async_copy(block.at[pl.ds(0, halo), :], ends.at[side], sems.at[2 + n])
        for n, (block, side) in enumerate(arrived)
    ]
    for copy in side_copies + end_copies:
        copy.start()
    lanes = PAD * width
    place[...] = jnp.zeros(place.shape, F32)
    for copy in side_copies:
        copy.wait()
    for side, first_leaf in enumerate((-PAD, own)):
        for n in range(2):
            values = sides[side, 16 * n : 16 * n + 16, 0:halo].astype(F32)
            place[0:3, n * halo : (n + 1) * halo] = values[0:3, :] + values[8:11, :]
        leaf = iota((8, lanes), 1) // width + (first_leaf + PAD)
        second = features(place[...], leaf, layers // 2 + PAD // LAYER)[1]
        halo_cols[side, :, :] = second.astype(BF16)
        halo_rows[side * lanes : (side + 1) * lanes, :] = rows_of(second)
    weights = [
        near_weights(
            first_rows, jnp.concatenate(columns, axis=1), switches, index, halo
        )
        for index, columns in (
            (0, [halo_cols[0, :, halo:], second_cols[:, 0 : 2 * halo]]),
            (layers - 1, [second_cols[:, (layers - 2) * halo :], halo_cols[1, :, 0:halo]]),
        )
    ]
    for copy in end_copies:
        copy.wait()
    value = mm(weights[0][:, 0:halo], ends[0, :, :])
    value = value + mm(weights[0][:, halo:], vectors[0 : 2 * halo, :])
    out[0:halo, :] = value.astype(BF16)
    value = mm(weights[1][:, 0 : 2 * halo], vectors[(layers - 2) * halo :, :])
    value = value + mm(weights[1][:, 2 * halo :], ends[1, :, :])
    out[halo:, :] = value.astype(BF16)


def leaves_kernel(chunks, edge_pairs, members, groups, *refs):
    outer_count = len(chunks) + 1
    near_parts = refs[:outer_count]
    (
        far_in,
        basis,
        top,
        upper,
        transfer,
        first_cols,
        own_rows,
        halo_rows,
        inner,
        outer,
        near,
        high,
        low,
        edge_blocks,
        device_factor,
        group_factor,
        root_factor,
        far_list,
        sides,
        second_rows,
        grams,
        work,
        factors,
        sems,
    ) = refs[outer_count:]
    width = basis.shape[0]
    own = basis.shape[1] // width
    total = own + 2 * PAD
    halo = LAYER * width
    layers = own // LAYER
    both = 2 * width
    odd = lax.axis_index("sub") % 2
    side_copies = [
        pltpu.make_async_copy(block.at[pl.ds(halo, width), :], sides.at[side], sems.at[n])
        for n, (block, side) in enumerate(((inner, 1 - odd), (outer, odd)))
    ]
    list_copy = pltpu.make_async_copy(far_in, far_list, sems.at[2])
    places = [(part, 0, chunk[0], len(chunk)) for part, chunk in zip(near_parts, chunks)]
    places += [(near_parts[-1], n, index, 1) for n, index in enumerate((0, layers - 1))]
    near_copies = [
        pltpu.make_async_copy(
            part.at[pl.ds(start * halo, many * halo), :],
            near.at[pl.ds(index * halo, many * halo), :],
            sems.at[3 + n],
        )
        for n, (part, start, index, many) in enumerate(places)
    ]
    for copy in side_copies + [list_copy] + near_copies:
        copy.start()

    lane = iota((width, both), 1)
    for n in range(own // 2):
        pair = basis[:, n * both : (n + 1) * both]
        zero = jnp.zeros_like(pair)
        stacked = jnp.concatenate(
            [jnp.where(lane < width, pair, zero), jnp.where(lane < width, zero, pair)], axis=0
        )
        value = mm_nt(stacked, pair)
        for m in range(2):
            at = (PAD + 2 * n + m) * STRIDE
            grams[at : at + width // 2, :] = fold(value[m * width : (m + 1) * width])
    spare = (0, LAYER, total - LAYER - 1, total - 1)
    for spot, gram in zip(
        spare,
        (
            top[...],
            upper[0 : width // 2, :] * (1.0 / members),
            upper[width // 2 :, :] * (1.0 / (members * groups)),
            top[...],
        ),
    ):
        grams[spot * STRIDE : spot * STRIDE + width // 2, :] = gram
    for copy in side_copies:
        copy.wait()
    for side, spots in enumerate(
        ((1, 2, 3, 5, 6, 7), tuple(PAD + own + m for m in (0, 1, 2, 4, 5, 6)))
    ):
        for n, spot in enumerate(spots):
            piece = sides[side, 0:width, n * width : (n + 1) * width]
            grams[spot * STRIDE : spot * STRIDE + width // 2, :] = fold(mm_nt(piece, piece))

    lanes = PAD * width
    second_rows[0:lanes, :] = halo_rows[0:lanes, :]
    second_rows[lanes : lanes + own * width, :] = own_rows[...]
    second_rows[lanes + own * width :, :] = halo_rows[lanes:, :]
    panels = width // 8

    def beside(p):
        places = range(p * len(edge_pairs) // panels, (p + 1) * len(edge_pairs) // panels)
        far_blocks(
            [edge_pairs[n] for n in places],
            far_list,
            second_rows,
            first_cols,
            edge_blocks,
            width,
            PAD,
            places,
        )

    to_lanes(grams, work, width, total)
    list_copy.wait()
    factor_lanes(work, width, beside)
    from_lanes(work, factors, width, total)
    device_factor[...] = exact(unfold(factors[0 : width // 2, :]), transfer[...])
    for target, spot in ((group_factor, spare[1]), (root_factor, spare[2])):
        target[...] = unfold(factors[spot * STRIDE : spot * STRIDE + width // 2, :])
    left_lanes = iota((width // 2, both), 1) < width
    for spot in range(total):
        rows = factors[spot * STRIDE : spot * STRIDE + width // 2, :]
        turned = pltpu.roll(rows, width, 1)
        twice = jnp.concatenate(
            [jnp.where(left_lanes, rows, turned), jnp.where(left_lanes, turned, rows)], axis=0
        )
        at = slice(spot * width, (spot + 1) * width)
        high[at, :], low[at, :] = split2(twice)
    for copy in near_copies:
        copy.wait()


def far_kernel(plan, far_in, high, low, *refs):
    blocks, (coupling, far_list, sem) = refs[:-3], refs[-3:]
    copy = pltpu.make_async_copy(far_in, far_list, sem)
    copy.start()
    width = coupling.shape[0]
    far, own = far_list.shape
    both = 2 * width
    start_leaf = lax.axis_index(AXES) * own
    square = iota((both, both), 0) // width == iota((both, both), 1) // width
    lane = iota((width, both), 1) < width
    zero = jnp.zeros((both, both), BF16)

    def diagonal(value):
        return jnp.where(square, value, zero)

    for start in range(0, own // 2, 4):
        indices = range(start, start + 4)
        halves = []
        for index in indices:
            source, place = plan[index]
            at = place * far * width
            kh = blocks[source][at : at + far * width, 0:both]
            kl = blocks[source][at : at + far * width, both : 2 * both]
            at = (PAD + 2 * index) * width
            rh = diagonal(high[at : at + both, :])
            rl = diagonal(low[at : at + both, :])
            halves.append(
                mm_nt(
                    jnp.concatenate([kh, kl, kh], axis=1), jnp.concatenate([rh, rh, rl], axis=1)
                )
            )
        if start == 0:
            copy.wait()
        outs = []
        for index, half in zip(indices, halves):
            zh, zl = split2(half * (1.0 / width))
            for f in range(far):
                spots = [
                    pl.multiple_of((far_list[f, 2 * index + m] - start_leaf + PAD) * width, width)
                    for m in range(2)
                ]
                sh, sl = (
                    jnp.where(lane, *(part[pl.ds(spot, width), :] for spot in spots))
                    for part in (high, low)
                )
                a = slice(f * width, (f + 1) * width)
                ph = diagonal(jnp.concatenate([zh[a], zh[a]], axis=0))
                plow = diagonal(jnp.concatenate([zl[a], zl[a]], axis=0))
                outs.append(
                    mm(
                        jnp.concatenate([sh, sh, sl], axis=1),
                        jnp.concatenate([ph, plow, ph], axis=0),
                    )
                )
        for n, index in enumerate(indices):
            three = outs[n * far : (n + 1) * far]
            line = jnp.concatenate(
                [out[:, 0:width] for out in three] + [out[:, width:both] for out in three], axis=1
            )
            at = index * 2 * far * width
            coupling[:, at : at + 2 * far * width] = line.astype(BF16)


def swap_inner(block):
    return lax.ppermute(block, AXES, [(i, i ^ 1) for i in range(lax.axis_size(AXES))])


def swap_outer(block):
    last = lax.axis_size(AXES) - 1
    route = [(i, min(max(i + 1 if i % 2 else i - 1, 0), last)) for i in range(last + 1)]
    return lax.ppermute(block, AXES, route)


def exchange(value, distance):
    pairs = [(i, i ^ distance) for i in range(lax.axis_size(AXES))]
    return value + lax.ppermute(value, AXES, pairs)


def per_device(
    points, leaf_basis, inner_transfer, device_transfer, vectors, near_index, near_count, far_index
):
    own = near_index.shape[0]
    width = leaf_basis.shape[1]
    columns = vectors.shape[1]
    halo = LAYER * width
    half = width // 2
    layers = own // LAYER
    total = own + 2 * PAD
    members, groups = lax.axis_size("sub"), lax.axis_size("group")
    vmem = pl.BlockSpec(memory_space=pltpu.VMEM)
    hbm = pl.BlockSpec(memory_space=pl.ANY)
    square = jax.ShapeDtypeStruct((width, width), F32)
    extra = halo + width + 32

    def block_of(rows):
        return jax.ShapeDtypeStruct((rows, columns), BF16)

    basis = leaf_basis.T
    near_list, far_list = near_index.T, far_index.T
    cost = pl.CostEstimate(flops=10**9, bytes_accessed=4 * 10**6, transcendentals=10**6)

    dense, top, to_outer, to_inner = pl.pallas_call(
        tree_kernel,
        out_shape=(
            jax.ShapeDtypeStruct((half, 2 * width), F32),
            jax.ShapeDtypeStruct((half, 2 * width), F32),
            block_of(extra),
            block_of(extra + half),
        ),
        in_specs=[hbm] * 5,
        out_specs=(vmem,) * 4,
        scratch_shapes=[
            pltpu.VMEM((3, own * width), F32),
            pltpu.VMEM((width, own * width), BF16),
            pltpu.VMEM((width, (own - 2) * width), BF16),
            pltpu.VMEM((width, width), F32),
            pltpu.SemaphoreType.DMA((6,)),
        ],
        compiler_params=room(60),
        name="tree",
    )(points, basis, inner_transfer.T, device_transfer, vectors)
    from_inner = swap_inner(to_inner)
    from_outer = swap_outer(to_outer)

    sub_bits = members.bit_length() - 1
    steps = [members << bit for bit in range(groups.bit_length() - 1)]
    steps += [1 << bit for bit in range(1, sub_bits)]
    inner_pairs = list(range(PAD // 2, (own - PAD) // 2))
    few = len(inner_pairs) // 2
    chunks = [[1, 2], [3, 4], [5], [6]]
    pair_chunks = [[], [], inner_pairs[:few], inner_pairs[few:]]
    blocks, plan, parts = [], {}, []

    def part_shape(count):
        return jax.ShapeDtypeStruct((count * halo, columns), BF16)

    def block_shape(count):
        return jax.ShapeDtypeStruct((count * far_index.shape[1] * width, 4 * width), BF16)

    late_points, dense = lax.optimization_barrier((points, dense))
    part, *shared = pl.pallas_call(
        first_chunk_kernel(chunks[0]),
        out_shape=(
            part_shape(len(chunks[0])),
            jax.ShapeDtypeStruct((own * width, 64), BF16),
            jax.ShapeDtypeStruct((64, own * width), BF16),
            jax.ShapeDtypeStruct((48, own * width), BF16),
            jax.ShapeDtypeStruct((own * width, 128), BF16),
            jax.ShapeDtypeStruct((own, 3 * halo), BF16),
        ),
        in_specs=[vmem] * 4,
        out_specs=(vmem,) * 6,
        scratch_shapes=[pltpu.VMEM((8, own * width), F32)],
        compiler_params=room(10),
        cost_estimate=cost,
        name="chunk_0",
    )(late_points, near_list, near_count.reshape(1, own), vectors)
    parts.append(part)
    summands = [
        from_inner[extra:, n * 2 * width : (n + 1) * 2 * width].astype(F32) for n in range(3)
    ]
    pair_gram = gram = dense + (summands[0] + (summands[1] + summands[2]))
    gram, parts[0] = lax.optimization_barrier((gram, parts[0]))
    first_rows, first_cols, second_cols, second_rows, switches = shared
    for n in range(max(len(steps), len(chunks))):
        before = gram
        if n < len(steps):
            if n == len(steps) - sub_bits + 1:
                gram = before = jnp.concatenate([pair_gram, gram], axis=0)
            gram = exchange(gram, steps[n])
        if n + 1 < len(chunks):
            layer_chunk, pair_chunk = chunks[n + 1], pair_chunks[n + 1]
            shapes = [part_shape(len(layer_chunk))] * bool(layer_chunk)
            shapes += [block_shape(len(pair_chunk))] * bool(pair_chunk)
            outs = pl.pallas_call(
                chunk_kernel(layer_chunk, pair_chunk, halo, width),
                out_shape=tuple(shapes),
                in_specs=[hbm] * 2 + [vmem] * 6,
                out_specs=(vmem,) * len(shapes),
                scratch_shapes=[
                    pltpu.SMEM(far_list.shape, jnp.int32),
                    pltpu.SemaphoreType.DMA,
                ],
                compiler_params=room(10),
                cost_estimate=cost,
                name=f"chunk_{n + 1}",
            )(before, far_list, first_rows, second_cols, switches, vectors, first_cols, second_rows)
            gram, outs = lax.optimization_barrier((gram, outs))
            if layer_chunk:
                parts.append(outs[0])
            if pair_chunk:
                plan.update((index, (len(blocks), m)) for m, index in enumerate(pair_chunk))
                blocks.append(outs[-1])
        elif n + 1 == len(chunks):
            edge_part, halo_rows = pl.pallas_call(
                edges_kernel,
                out_shape=(
                    part_shape(2),
                    jax.ShapeDtypeStruct((2 * PAD * width, 2 * width), BF16),
                ),
                in_specs=[hbm] * 3 + [vmem] * 4,
                out_specs=(vmem,) * 2,
                scratch_shapes=[
                    pltpu.VMEM((2, halo, columns), BF16),
                    pltpu.VMEM((2, 32, columns), BF16),
                    pltpu.VMEM((8, PAD * width), F32),
                    pltpu.VMEM((2, 48, PAD * width), BF16),
                    pltpu.SemaphoreType.DMA((4,)),
                ],
                compiler_params=room(10),
                cost_estimate=cost,
                name="edges",
            )(before, from_inner, from_outer, first_rows, second_cols, switches, vectors)
            gram, edge_part = lax.optimization_barrier((gram, edge_part))

    edge_pairs = [index for index in range(own // 2) if index not in plan]
    plan.update((index, (len(blocks), m)) for m, index in enumerate(edge_pairs))
    split_factors = jax.ShapeDtypeStruct((total * width, 2 * width), BF16)
    near, high, low, edge_blocks, device_factor, group_factor, root_factor = pl.pallas_call(
        functools.partial(leaves_kernel, chunks, edge_pairs, members, groups),
        out_shape=(
            jax.ShapeDtypeStruct(vectors.shape, BF16),
            split_factors,
            split_factors,
            block_shape(len(edge_pairs)),
            square,
            square,
            square,
        ),
        in_specs=[hbm] * (len(parts) + 2) + [vmem] * 7 + [hbm] * 2,
        out_specs=(hbm,) + (vmem,) * 6,
        scratch_shapes=[
            pltpu.SMEM(far_list.shape, jnp.int32),
            pltpu.VMEM((2, width, columns), BF16),
            pltpu.VMEM((total * width, 2 * width), BF16),
            pltpu.VMEM((total * STRIDE, 2 * width), F32),
            pltpu.VMEM((width, width, 128), F32),
            pltpu.VMEM((total * STRIDE, 2 * width), F32),
            pltpu.SemaphoreType.DMA((5 + len(parts),)),
        ],
        compiler_params=room(24),
        name="leaves",
    )(
        *parts,
        edge_part,
        far_list,
        basis,
        top,
        gram,
        device_transfer,
        first_cols,
        second_rows,
        halo_rows,
        from_inner,
        from_outer,
    )

    coupling = pl.pallas_call(
        functools.partial(far_kernel, plan),
        out_shape=jax.ShapeDtypeStruct((width, own * far_index.shape[1] * width), BF16),
        in_specs=[hbm] + [vmem] * (3 + len(blocks)),
        out_specs=vmem,
        scratch_shapes=[
            pltpu.SMEM(far_list.shape, jnp.int32),
            pltpu.SemaphoreType.DMA,
        ],
        compiler_params=room(16),
        name="far",
    )(far_list, high, low, *blocks, edge_blocks)
    return near, coupling.T, device_factor, group_factor, root_factor


def solution(mesh):
    split = P(AXES, None)
    return jax.shard_map(
        per_device,
        mesh=mesh,
        in_specs=(P(None, AXES), split, split, split, split, split, P(AXES), split),
        out_specs=(split, split, split, split, split),
        check_vma=False,
    )
```

```python
import functools
import math

import jax
import jax.numpy as jnp
from jax import lax
from jax.experimental import pallas as pl
from jax.experimental.pallas import tpu as pltpu
from jax.sharding import PartitionSpec as P

LAYER = 4
PAD = 8
LONG_SQ = 2.25
RATIO = 25.0
SCALE = 0.5 / LONG_SQ
HALF = math.log(0.5)
OFF = -16384.0
STRIDE = 40
AXES = ("group", "sub")
F32 = jnp.float32
BF16 = jnp.bfloat16


def room(megabytes):
    return pltpu.CompilerParams(vmem_limit_bytes=int(megabytes * 1024 * 1024))


def split2(value):
    high = value.astype(BF16)
    return high, (value - high.astype(F32)).astype(BF16)


def split3(value):
    high = value.astype(BF16)
    rest = value - high.astype(F32)
    middle = rest.astype(BF16)
    return high, middle, (rest - middle.astype(F32)).astype(BF16)


def mm(left, right):
    return jnp.dot(left, right, preferred_element_type=F32)


def mm_nt(left, right):
    return lax.dot_general(left, right, (((1,), (1,)), ((), ())), preferred_element_type=F32)


def exact(left, right):
    return jnp.dot(left, right, precision=lax.Precision.HIGHEST, preferred_element_type=F32)


def iota(shape, dim):
    return lax.broadcasted_iota(jnp.int32, shape, dim)


def tree_kernel(
    points_in, basis_in, below_in, transfer_in, vectors,
    dense, top, outer, inner, points, basis, below, transfer, packed, staged, sems,
):
    width = basis.shape[0]
    count = basis.shape[1] // width
    halo = LAYER * width
    span = PAD * width
    rows = vectors.shape[0]
    odd = lax.axis_index("sub") % 2
    sides = ((outer, odd), (inner, 1 - odd))
    basis_copy, below_copy, points_copy, transfer_copy = loads = [
        pltpu.make_async_copy(source, target, sems.at[n])
        for n, (source, target) in enumerate(
            (
                (basis_in, basis),
                (below_in, below),
                (points_in, points),
                (transfer_in, transfer),
            )
        )
    ]
    copies = [
        pltpu.make_async_copy(
            vectors.at[pl.ds(pl.multiple_of(last * (rows - halo), 16), halo), :],
            target.at[pl.ds(0, halo), :],
            sems.at[4 + n],
        )
        for n, (target, last) in enumerate(sides)
    ]
    for copy in loads + copies:
        copy.start()
    both = 2 * width
    lane = iota((width, 2 * both), 1)

    def times(above, columns):
        found = []
        for n in range(above.shape[1] // both):
            parts = jnp.concatenate(split3(above[:, n * both : (n + 1) * both]), axis=1)
            block = columns(n * 2 * both)
            zero = jnp.zeros_like(block)
            block = jnp.concatenate(
                [jnp.where(lane < both, block, zero), jnp.where(lane < both, zero, block)], axis=0
            )
            found.append(mm(parts, jnp.concatenate([block] * 3, axis=0)))
        return jnp.concatenate(found, axis=1)

    same = iota((both, both), 0) // width == iota((both, both), 1) // width
    half_block = jnp.where(same, 0.5, 0.0).astype(F32)
    basis_copy.wait()
    points_copy.wait()
    for n, (target, last) in enumerate(sides):
        bases = basis[:, count * width - span :], basis[:, 0:span]
        last_three, first_three = (
            jnp.concatenate(
                [block[:, (at + skip) * width : (at + skip + 3) * width] for at in (0, LAYER)],
                axis=1,
            )
            for skip, block in zip((1, 0), bases)
        )
        packed[n, 0:width, :] = jnp.where(last == 1, last_three, first_three)
        coords = jnp.where(last == 1, points[:, count * width - span :], points[:, 0:span])
        for m in range(2):
            high, low = split2(coords[:, m * halo : (m + 1) * halo])
            base = width + 16 * m
            packed[n, base : base + 16, :] = jnp.zeros((16, target.shape[1]), BF16)
            packed[n, base : base + 3, 0:halo] = high
            packed[n, base + 8 : base + 11, 0:halo] = low
        copies.append(
            pltpu.make_async_copy(
                packed.at[n], target.at[pl.ds(halo, width + 32), :], sems.at[6 + n]
            )
        )
        copies[-1].start()
    blocks = []
    for n in range(count // 4):
        stacked = jnp.concatenate(
            [basis[:, (2 * n + m) * both : (2 * n + m + 1) * both] for m in range(2)], axis=0
        )
        blocks.append(mm_nt(stacked, stacked) * half_block)
    below_copy.wait()
    halves = []
    for n, block in enumerate(blocks):
        t = below[:, n * both : (n + 1) * both]
        half = mm(jnp.concatenate([t, t, t], axis=1), jnp.concatenate(split3(block), axis=0))
        halves.append((half, t))
    blocks = []
    for n in range(0, len(halves), 2):
        (first, t), (second, u) = halves[n : n + 2]
        x = jnp.concatenate(split3(jnp.concatenate([first, second], axis=0)), axis=1)
        t = jnp.concatenate([t, u], axis=0)
        blocks.append(mm_nt(x, jnp.concatenate([t, t, t], axis=1)) * half_block)

    transfer_copy.wait()
    end = below.shape[1]
    tops = below[:, end - both : end]
    turned = jnp.concatenate(split3(transfer[...].T), axis=1)
    above = jnp.concatenate(
        [tops.astype(F32), mm(turned, jnp.concatenate([tops] * 3, axis=0))], axis=0
    )
    end -= both
    nodes = 4
    while nodes < count // 2:
        start = end - nodes * width
        above = times(above, lambda at, start=start: below[:, start + at : start + at + 2 * both])
        end = start
        nodes *= 2

    total = jnp.zeros((both, both), F32)
    for n, block in enumerate(blocks):
        rows = above[:, n * both : (n + 1) * both]
        high, middle, low = split3(rows)
        gh, gm, gl = split3(block)
        x = mm(
            jnp.concatenate([high, high, high, middle, middle, low], axis=1),
            jnp.concatenate([gh, gm, gl, gh, gm, gh], axis=0),
        )
        xh, xm, xl = split3(x)
        total = total + mm_nt(
            jnp.concatenate([xh, xh, xh, xm, xm, xl], axis=1),
            jnp.concatenate([high, middle, low, high, middle, high], axis=1),
        )
    total = total * (4.0 / count)
    top[...] = fold(total[:width, :width])
    halves = fold(total[width:, width:])
    dense[...] = halves
    staged[...] = jnp.concatenate(split3(halves), axis=1)
    copies.append(
        pltpu.make_async_copy(
            staged, inner.at[pl.ds(halo + width + 32, width // 2), :], sems.at[8]
        )
    )
    copies[-1].start()
    for copy in copies:
        copy.wait()


def factor_lanes(work, width):
    panels = width // 8
    row = iota((8, 128), 0)

    def spread(j, i):
        return jnp.broadcast_to(work[j, i : i + 1, :], (8, 128))

    for p in range(panels):
        at = 8 * p
        entry = {(k, m): spread(at + k, at + m) for k in range(8) for m in range(k, 8)}
        scales = []
        for k in range(8):
            scales.append(lax.rsqrt(entry[k, k]))
            for m in range(k + 1, 8):
                entry[k, m] = entry[k, m] * scales[k]
            for m in range(k + 1, 8):
                for q in range(m, 8):
                    entry[m, q] = entry[m, q] - entry[k, m] * entry[k, q]
        for i in range(p, panels):
            tile = [work[at + k, 8 * i : 8 * i + 8, :] for k in range(8)]
            for k in range(8):
                tile[k] = tile[k] * scales[k]
                for m in range(k + 1, 8):
                    tile[m] = tile[m] - tile[k] * entry[k, m]
            for k in range(8):
                work[at + k, 8 * i : 8 * i + 8, :] = (
                    jnp.where(row >= k, tile[k], 0.0) if i == p else tile[k]
                )
        for q in range(p + 1, panels):
            for start in range(q, panels, 2):
                group = range(start, min(start + 2, panels))
                accs = {
                    (i, k): work[8 * q + k, 8 * i : 8 * i + 8, :] for i in group for k in range(8)
                }
                for j in range(at, at + 8):
                    factors = [spread(j, 8 * q + k) for k in range(8)]
                    for i in group:
                        column = work[j, 8 * i : 8 * i + 8, :]
                        for k in range(8):
                            accs[i, k] = accs[i, k] - column * factors[k]
                for (i, k), value in accs.items():
                    work[8 * q + k, 8 * i : 8 * i + 8, :] = value


def fold(matrix):
    half = matrix.shape[0] // 2
    return jnp.concatenate([matrix[:half], matrix[half:]], axis=1)


def unfold(matrix):
    half = matrix.shape[1] // 2
    return jnp.concatenate([matrix[:, :half], matrix[:, half:]], axis=0)


def from_lanes(work, factors, width, many):
    for i in range(width // 2):
        both = []
        for j in (i, i + width // 2):
            skip = j // 8 * 8
            both += [jnp.zeros((skip, many), F32)] * bool(skip) + [work[j, skip:, 0:many]]
        factors[pl.ds(i, many, stride=STRIDE), :] = jnp.concatenate(both, axis=0).T


def gaussians(exponent):
    return jnp.exp(exponent) + jnp.exp(exponent * RATIO - RATIO * HALF)


def features(place, leaf, center):
    sub = iota(place.shape, 0)
    corner = jnp.where(sub == 0, leaf % 2 - 1, leaf // 2 % 2 - 1)
    corner = jnp.where(sub == 2, leaf // LAYER - center, corner)
    place = jnp.where(sub < 3, place + corner.astype(F32), 0.0)
    norm = jnp.sum(place * place, axis=0, keepdims=True) * SCALE
    first = jnp.where(sub == 3, -norm, jnp.where(sub == 4, 1.0, place))
    second = jnp.where(
        sub == 3, 1.0, jnp.where(sub == 4, HALF - norm, place * (2.0 * SCALE))
    )
    fh, fm, fl = [v.astype(F32) for v in split3(first)]
    sh, sm, sl = [v.astype(F32) for v in split3(second)]
    return (
        jnp.concatenate([fh, fh, fh, fm, fm, fl], axis=0),
        jnp.concatenate([sh, sm, sl, sh, sm, sh], axis=0),
    )


def rows_of(second):
    blank = jnp.zeros((16, second.shape[1]), F32)
    return jnp.concatenate([second, blank, second, blank], axis=0).T.astype(BF16)


def near_weights(first_rows, second, switches, index, halo):
    group = index // 4 * 16
    columns = jnp.concatenate([second, switches[group : group + 16, :]], axis=0)
    return gaussians(mm(first_rows[index * halo : (index + 1) * halo, :], columns)).astype(BF16)


def prepare(
    points, near_list, near_used, first_rows, first_cols, second_cols, second_rows, switches, place
):
    rows = points.shape[1]
    own = near_list.shape[1]
    width = rows // own
    place[...] = jnp.zeros(place.shape, F32)
    place[0:3, :] = points[...]
    leaf = iota((8, rows), 1) // width
    first, second = features(place[...], leaf, own // LAYER // 2)
    hot_leaf = iota((16, rows), 1) // width
    hot = jnp.where(hot_leaf % 16 == iota((16, rows), 0), 1.0, 0.0).astype(F32)
    first = jnp.concatenate([first, hot], axis=0)
    first_cols[...] = first.astype(BF16)
    second_cols[...] = second.astype(BF16)
    first_rows[...] = first.T.astype(BF16)
    second_rows[...] = rows_of(second)

    start_leaf = lax.axis_index(AXES) * own
    target = iota((1, own), 1)
    base_leaf = start_leaf + target // LAYER * LAYER - LAYER
    found = jnp.zeros((16, own), jnp.bool_)
    place_row = iota((16, own), 0)
    for n in range(near_list.shape[0]):
        spot = jnp.where(near_used[...] > n, near_list[n : n + 1, :] - base_leaf, -1)
        found = jnp.logical_or(found, place_row == spot)
    bias = jnp.where(found, 0.0, OFF).astype(F32)
    span = 3 * LAYER * width
    expand = jnp.where(iota((16, span), 0) == iota((16, span), 1) // width, 1.0, 0.0)
    switches[...] = mm(bias.T.astype(BF16), expand.astype(BF16)).astype(BF16)


def inner_layers(layers, vectors, first_rows, second_cols, switches, out, halo):
    for n, index in enumerate(layers):
        around = slice((index - 1) * halo, (index + 2) * halo)
        weights = near_weights(first_rows, second_cols[:, around], switches, index, halo)
        out[n * halo : (n + 1) * halo, :] = mm(weights, vectors[around, :]).astype(BF16)


def far_blocks(pairs, far_list, second_rows, first_cols, out, width, base, places):
    far, own = far_list.shape
    both = 2 * width
    start_leaf = lax.axis_index(AXES) * own
    square = iota((both, both), 0) // width == iota((both, both), 1) // width
    lane = iota((far * width, both), 1) < width
    exponents = []
    for index in pairs:
        t = 2 * index
        picked = []
        for m in range(2):
            spots = [
                pl.multiple_of((far_list[f, t + m] - start_leaf + base) * width, width)
                for f in range(far)
            ]
            picked.append(
                jnp.concatenate([second_rows[pl.ds(spot, width), :] for spot in spots], axis=0)
            )
        cols = first_cols[:, t * width : t * width + both]
        targets = jnp.where(
            square, jnp.concatenate([cols, cols], axis=0), jnp.zeros((both, both), BF16)
        )
        exponents.append(mm(jnp.where(lane, picked[0], picked[1]), targets))
    for place, exponent in zip(places, exponents):
        high, low = split2(gaussians(exponent))
        at = place * far * width
        out[at : at + far * width, 0:both] = high
        out[at : at + far * width, both : 2 * both] = low


def first_chunk_kernel(layers):
    def body(
        points, near_list, near_used, vectors,
        out, first_rows, first_cols, second_cols, second_rows, switches, place,
    ):
        prepare(
            points,
            near_list,
            near_used,
            first_rows,
            first_cols,
            second_cols,
            second_rows,
            switches,
            place,
        )
        halo = LAYER * points.shape[1] // near_list.shape[1]
        inner_layers(layers, vectors, first_rows, second_cols, switches, out, halo)

    return body


def chunk_kernel(layers, pairs, halo, width):
    def body(after, far_in, *refs):
        first_rows, second_cols, switches, vectors, first_cols, second_rows = refs[:6]
        outs, far_list, sem = refs[6:-2], refs[-2], refs[-1]
        if pairs:
            copy = pltpu.make_async_copy(far_in, far_list, sem)
            copy.start()
        if layers:
            inner_layers(layers, vectors, first_rows, second_cols, switches, outs[0], halo)
        if pairs:
            copy.wait()
            far_blocks(
                pairs, far_list, second_rows, first_cols, outs[-1], width, 0, range(len(pairs))
            )

    return body


def edges_kernel(
    after, inner, outer, first_rows, second_cols, switches, vectors,
    out, halo_rows, ends, sides, place, halo_cols, sems,
):
    halo = ends.shape[1]
    width = halo // LAYER
    own = vectors.shape[0] // width
    layers = own // LAYER
    extra = sides.shape[1]
    odd = lax.axis_index("sub") % 2
    arrived = ((inner, 1 - odd), (outer, odd))
    side_copies = [
        pltpu.make_async_copy(
            block.at[pl.ds(halo + width, extra), :], sides.at[side], sems.at[n]
        )
        for n, (block, side) in enumerate(arrived)
    ]
    end_copies = [
        pltpu.make_async_copy(block.at[pl.ds(0, halo), :], ends.at[side], sems.at[2 + n])
        for n, (block, side) in enumerate(arrived)
    ]
    for copy in side_copies + end_copies:
        copy.start()
    lanes = PAD * width
    place[...] = jnp.zeros(place.shape, F32)
    for copy in side_copies:
        copy.wait()
    for side, first_leaf in enumerate((-PAD, own)):
        for n in range(2):
            values = sides[side, 16 * n : 16 * n + 16, 0:halo].astype(F32)
            place[0:3, n * halo : (n + 1) * halo] = values[0:3, :] + values[8:11, :]
        leaf = iota((8, lanes), 1) // width + (first_leaf + PAD)
        second = features(place[...], leaf, layers // 2 + PAD // LAYER)[1]
        halo_cols[side, :, :] = second.astype(BF16)
        halo_rows[side * lanes : (side + 1) * lanes, :] = rows_of(second)
    weights = [
        near_weights(
            first_rows, jnp.concatenate(columns, axis=1), switches, index, halo
        )
        for index, columns in (
            (0, [halo_cols[0, :, halo:], second_cols[:, 0 : 2 * halo]]),
            (layers - 1, [second_cols[:, (layers - 2) * halo :], halo_cols[1, :, 0:halo]]),
        )
    ]
    for copy in end_copies:
        copy.wait()
    value = mm(weights[0][:, 0:halo], ends[0, :, :])
    value = value + mm(weights[0][:, halo:], vectors[0 : 2 * halo, :])
    out[0:halo, :] = value.astype(BF16)
    value = mm(weights[1][:, 0 : 2 * halo], vectors[(layers - 2) * halo :, :])
    value = value + mm(weights[1][:, 2 * halo :], ends[1, :, :])
    out[halo:, :] = value.astype(BF16)


def last_chunk_kernel(layers, pairs):
    def body(
        after, far_in, inner, outer, first_rows, second_cols, switches, vectors,
        first_cols, own_rows, halo_rows, basis, top,
        out, blocks, grams, far_list, sides, second_rows, sems,
    ):
        width = basis.shape[0]
        own = basis.shape[1] // width
        total = own + 2 * PAD
        halo = LAYER * width
        both = 2 * width
        odd = lax.axis_index("sub") % 2
        side_copies = [
            pltpu.make_async_copy(block.at[pl.ds(halo, width), :], sides.at[side], sems.at[n])
            for n, (block, side) in enumerate(((inner, 1 - odd), (outer, odd)))
        ]
        list_copy = pltpu.make_async_copy(far_in, far_list, sems.at[2])
        for copy in side_copies + [list_copy]:
            copy.start()
        lanes = PAD * width
        second_rows[0:lanes, :] = halo_rows[0:lanes, :]
        second_rows[lanes : lanes + own * width, :] = own_rows[...]
        second_rows[lanes + own * width :, :] = halo_rows[lanes:, :]
        inner_layers(layers, vectors, first_rows, second_cols, switches, out, halo)

        lane = iota((width, both), 1)
        for n in range(own // 2):
            pair = basis[:, n * both : (n + 1) * both]
            zero = jnp.zeros_like(pair)
            stacked = jnp.concatenate(
                [jnp.where(lane < width, pair, zero), jnp.where(lane < width, zero, pair)], axis=0
            )
            value = mm_nt(stacked, pair)
            for m in range(2):
                at = (PAD + 2 * n + m) * STRIDE
                grams[at : at + width // 2, :] = fold(value[m * width : (m + 1) * width])
        for spot in (0, LAYER, total - LAYER - 1, total - 1):
            grams[spot * STRIDE : spot * STRIDE + width // 2, :] = top[...]
        for copy in side_copies + [list_copy]:
            copy.wait()
        for side, spots in enumerate(
            ((1, 2, 3, 5, 6, 7), tuple(PAD + own + m for m in (0, 1, 2, 4, 5, 6)))
        ):
            for n, spot in enumerate(spots):
                piece = sides[side, 0:width, n * width : (n + 1) * width]
                at = spot * STRIDE
                grams[at : at + width // 2, :] = fold(mm_nt(piece, piece))
        far_blocks(
            pairs, far_list, second_rows, first_cols, blocks, width, PAD, range(len(pairs))
        )

    return body


def leaves_kernel(chunks, members, groups, *refs):
    outer_count = len(chunks) + 1
    near_parts = refs[:outer_count]
    (
        grams,
        upper,
        transfer,
        near,
        high,
        low,
        device_factor,
        group_factor,
        root_factor,
        work,
        factors,
        sems,
    ) = refs[outer_count:]
    width = transfer.shape[0]
    total = high.shape[0] // width
    own = total - 2 * PAD
    halo = LAYER * width
    layers = own // LAYER
    both = 2 * width
    places = [(part, 0, chunk[0], len(chunk)) for part, chunk in zip(near_parts, chunks)]
    places += [(near_parts[-1], n, index, 1) for n, index in enumerate((0, layers - 1))]
    near_copies = [
        pltpu.make_async_copy(
            part.at[pl.ds(start * halo, many * halo), :],
            near.at[pl.ds(index * halo, many * halo), :],
            sems.at[n],
        )
        for n, (part, start, index, many) in enumerate(places)
    ]
    for copy in near_copies:
        copy.start()

    spare = (LAYER, total - LAYER - 1)
    means = (
        upper[0 : width // 2, :] * (1.0 / members),
        upper[width // 2 :, :] * (1.0 / (members * groups)),
    )
    spot_row = iota((total, both), 0)
    for i in range(width // 2):
        rows = grams[pl.ds(i, total, stride=STRIDE), :]
        for spot, mean in zip(spare, means):
            rows = jnp.where(spot_row == spot, mean[i : i + 1, :], rows)
        turned = rows.T
        work[i, :, 0:total] = turned[0:width]
        work[i + width // 2, :, 0:total] = turned[width:]
    factor_lanes(work, width)
    from_lanes(work, factors, width, total)
    device_factor[...] = exact(unfold(factors[0 : width // 2, :]), transfer[...])
    for target, spot in zip((group_factor, root_factor), spare):
        target[...] = unfold(factors[spot * STRIDE : spot * STRIDE + width // 2, :])
    left_lanes = iota((width // 2, both), 1) < width
    for spot in range(total):
        rows = factors[spot * STRIDE : spot * STRIDE + width // 2, :]
        turned = pltpu.roll(rows, width, 1)
        twice = jnp.concatenate(
            [jnp.where(left_lanes, rows, turned), jnp.where(left_lanes, turned, rows)], axis=0
        )
        at = slice(spot * width, (spot + 1) * width)
        high[at, :], low[at, :] = split2(twice)
    for copy in near_copies:
        copy.wait()


def far_kernel(plan, far_in, high, low, *refs):
    blocks, (coupling, far_list, sem) = refs[:-3], refs[-3:]
    copy = pltpu.make_async_copy(far_in, far_list, sem)
    copy.start()
    width = coupling.shape[0]
    far, own = far_list.shape
    both = 2 * width
    start_leaf = lax.axis_index(AXES) * own
    square = iota((both, both), 0) // width == iota((both, both), 1) // width
    lane = iota((width, both), 1) < width
    zero = jnp.zeros((both, both), BF16)

    def diagonal(value):
        return jnp.where(square, value, zero)

    for start in range(0, own // 2, 4):
        indices = range(start, start + 4)
        halves = []
        for index in indices:
            source, place = plan[index]
            at = place * far * width
            kh = blocks[source][at : at + far * width, 0:both]
            kl = blocks[source][at : at + far * width, both : 2 * both]
            at = (PAD + 2 * index) * width
            rh = diagonal(high[at : at + both, :])
            rl = diagonal(low[at : at + both, :])
            halves.append(
                mm_nt(
                    jnp.concatenate([kh, kl, kh], axis=1), jnp.concatenate([rh, rh, rl], axis=1)
                )
            )
        if start == 0:
            copy.wait()
        outs = []
        for index, half in zip(indices, halves):
            zh, zl = split2(half * (1.0 / width))
            for f in range(far):
                spots = [
                    pl.multiple_of((far_list[f, 2 * index + m] - start_leaf + PAD) * width, width)
                    for m in range(2)
                ]
                sh, sl = (
                    jnp.where(lane, *(part[pl.ds(spot, width), :] for spot in spots))
                    for part in (high, low)
                )
                a = slice(f * width, (f + 1) * width)
                ph = diagonal(jnp.concatenate([zh[a], zh[a]], axis=0))
                plow = diagonal(jnp.concatenate([zl[a], zl[a]], axis=0))
                outs.append(
                    mm(
                        jnp.concatenate([sh, sh, sl], axis=1),
                        jnp.concatenate([ph, plow, ph], axis=0),
                    )
                )
        for n, index in enumerate(indices):
            three = outs[n * far : (n + 1) * far]
            line = jnp.concatenate(
                [out[:, 0:width] for out in three] + [out[:, width:both] for out in three], axis=1
            )
            at = index * 2 * far * width
            coupling[:, at : at + 2 * far * width] = line.astype(BF16)


def swap_inner(block):
    return lax.ppermute(block, AXES, [(i, i ^ 1) for i in range(lax.axis_size(AXES))])


def swap_outer(block):
    last = lax.axis_size(AXES) - 1
    route = [(i, min(max(i + 1 if i % 2 else i - 1, 0), last)) for i in range(last + 1)]
    return lax.ppermute(block, AXES, route)


def exchange(value, distance):
    pairs = [(i, i ^ distance ^ 1) for i in range(lax.axis_size(AXES))]
    return value + lax.ppermute(value, AXES, pairs)


def per_device(
    points, leaf_basis, inner_transfer, device_transfer, vectors, near_index, near_count, far_index
):
    own = near_index.shape[0]
    width = leaf_basis.shape[1]
    columns = vectors.shape[1]
    halo = LAYER * width
    half = width // 2
    layers = own // LAYER
    total = own + 2 * PAD
    members, groups = lax.axis_size("sub"), lax.axis_size("group")
    vmem = pl.BlockSpec(memory_space=pltpu.VMEM)
    hbm = pl.BlockSpec(memory_space=pl.ANY)
    square = jax.ShapeDtypeStruct((width, width), F32)
    extra = halo + width + 32

    def block_of(rows):
        return jax.ShapeDtypeStruct((rows, columns), BF16)

    basis = leaf_basis.T
    near_list, far_list = near_index.T, far_index.T
    cost = pl.CostEstimate(flops=10**9, bytes_accessed=4 * 10**6, transcendentals=10**6)

    dense, top, to_outer, to_inner = pl.pallas_call(
        tree_kernel,
        out_shape=(
            jax.ShapeDtypeStruct((half, 2 * width), F32),
            jax.ShapeDtypeStruct((half, 2 * width), F32),
            block_of(extra),
            block_of(extra + half),
        ),
        in_specs=[hbm] * 5,
        out_specs=(vmem, vmem, hbm, hbm),
        scratch_shapes=[
            pltpu.VMEM((3, own * width), F32),
            pltpu.VMEM((width, own * width), BF16),
            pltpu.VMEM((width, (own - 2) * width), BF16),
            pltpu.VMEM((width, width), F32),
            pltpu.VMEM((2, width + 32, columns), BF16),
            pltpu.VMEM((half, columns), BF16),
            pltpu.SemaphoreType.DMA((9,)),
        ],
        compiler_params=room(60),
        name="tree",
    )(points, basis, inner_transfer.T, device_transfer, vectors)
    from_inner = swap_inner(to_inner)
    from_outer = swap_outer(to_outer)

    sub_bits = members.bit_length() - 1
    steps = [members << bit for bit in range(groups.bit_length() - 1)]
    steps += [1 << bit for bit in range(1, sub_bits)]
    inner_pairs = list(range(PAD // 2, (own - PAD) // 2))
    few = len(inner_pairs) // 2
    edge_pairs = [index for index in range(own // 2) if index not in inner_pairs]
    chunks = [[1, 2], [3, 4], [5], [6]]
    pair_chunks = [[], inner_pairs[:few], inner_pairs[few:], edge_pairs]
    blocks, plan, parts = [], {}, []

    def part_shape(count):
        return jax.ShapeDtypeStruct((count * halo, columns), BF16)

    def block_shape(count):
        return jax.ShapeDtypeStruct((count * far_index.shape[1] * width, 4 * width), BF16)

    late_points, dense = lax.optimization_barrier((points, dense))
    part, *shared = pl.pallas_call(
        first_chunk_kernel(chunks[0]),
        out_shape=(
            part_shape(len(chunks[0])),
            jax.ShapeDtypeStruct((own * width, 64), BF16),
            jax.ShapeDtypeStruct((64, own * width), BF16),
            jax.ShapeDtypeStruct((48, own * width), BF16),
            jax.ShapeDtypeStruct((own * width, 128), BF16),
            jax.ShapeDtypeStruct((own, 3 * halo), BF16),
        ),
        in_specs=[vmem] * 4,
        out_specs=(vmem,) * 6,
        scratch_shapes=[pltpu.VMEM((8, own * width), F32)],
        compiler_params=room(10),
        cost_estimate=cost,
        name="chunk_0",
    )(late_points, near_list, near_count.reshape(1, own), vectors)
    parts.append(part)
    summands = [
        from_inner[extra:, n * 2 * width : (n + 1) * 2 * width].astype(F32) for n in range(3)
    ]
    pair_gram = gram = dense + (summands[0] + (summands[1] + summands[2]))
    gram, parts[0] = lax.optimization_barrier((gram, parts[0]))
    first_rows, first_cols, second_cols, second_rows, switches = shared
    jobs = [1, 2, "edges", 3]
    for n in range(max(len(steps), len(jobs))):
        before = gram
        if n < len(steps):
            if n == len(steps) - sub_bits + 1:
                gram = before = jnp.concatenate([pair_gram, gram], axis=0)
            gram = exchange(gram, steps[n])
        job = jobs[n] if n < len(jobs) else None
        if job in (1, 2):
            layer_chunk, pair_chunk = chunks[job], pair_chunks[job]
            shapes = [part_shape(len(layer_chunk))] * bool(layer_chunk)
            shapes += [block_shape(len(pair_chunk))] * bool(pair_chunk)
            outs = pl.pallas_call(
                chunk_kernel(layer_chunk, pair_chunk, halo, width),
                out_shape=tuple(shapes),
                in_specs=[hbm] * 2 + [vmem] * 6,
                out_specs=(vmem,) * len(shapes),
                scratch_shapes=[
                    pltpu.SMEM(far_list.shape, jnp.int32),
                    pltpu.SemaphoreType.DMA,
                ],
                compiler_params=room(10),
                cost_estimate=cost,
                name=f"chunk_{job}",
            )(before, far_list, first_rows, second_cols, switches, vectors, first_cols, second_rows)
            gram, outs = lax.optimization_barrier((gram, outs))
            if layer_chunk:
                parts.append(outs[0])
            if pair_chunk:
                plan.update((index, (len(blocks), m)) for m, index in enumerate(pair_chunk))
                blocks.append(outs[-1])
        elif job == "edges":
            edge_part, halo_rows = pl.pallas_call(
                edges_kernel,
                out_shape=(
                    part_shape(2),
                    jax.ShapeDtypeStruct((2 * PAD * width, 2 * width), BF16),
                ),
                in_specs=[hbm] * 3 + [vmem] * 4,
                out_specs=(vmem,) * 2,
                scratch_shapes=[
                    pltpu.VMEM((2, halo, columns), BF16),
                    pltpu.VMEM((2, 32, columns), BF16),
                    pltpu.VMEM((8, PAD * width), F32),
                    pltpu.VMEM((2, 48, PAD * width), BF16),
                    pltpu.SemaphoreType.DMA((4,)),
                ],
                compiler_params=room(10),
                cost_estimate=cost,
                name="edges",
            )(before, from_inner, from_outer, first_rows, second_cols, switches, vectors)
            gram, edge_part = lax.optimization_barrier((gram, edge_part))
        elif job == 3:
            part, edge_blocks, grams = pl.pallas_call(
                last_chunk_kernel(chunks[3], edge_pairs),
                out_shape=(
                    part_shape(len(chunks[3])),
                    block_shape(len(edge_pairs)),
                    jax.ShapeDtypeStruct((total * STRIDE, 2 * width), F32),
                ),
                in_specs=[hbm] * 4 + [vmem] * 9,
                out_specs=(vmem,) * 3,
                scratch_shapes=[
                    pltpu.SMEM(far_list.shape, jnp.int32),
                    pltpu.VMEM((2, width, columns), BF16),
                    pltpu.VMEM((total * width, 2 * width), BF16),
                    pltpu.SemaphoreType.DMA((3,)),
                ],
                compiler_params=room(14),
                cost_estimate=cost,
                name="chunk_3",
            )(
                before,
                far_list,
                from_inner,
                from_outer,
                first_rows,
                second_cols,
                switches,
                vectors,
                first_cols,
                second_rows,
                halo_rows,
                basis,
                top,
            )
            gram, part = lax.optimization_barrier((gram, part))
            parts.append(part)
            plan.update((index, (len(blocks), m)) for m, index in enumerate(edge_pairs))
            blocks.append(edge_blocks)

    split_factors = jax.ShapeDtypeStruct((total * width, 2 * width), BF16)
    near, high, low, device_factor, group_factor, root_factor = pl.pallas_call(
        functools.partial(leaves_kernel, chunks, members, groups),
        out_shape=(
            jax.ShapeDtypeStruct(vectors.shape, BF16),
            split_factors,
            split_factors,
            square,
            square,
            square,
        ),
        in_specs=[hbm] * (len(parts) + 1) + [vmem] * 3,
        out_specs=(hbm,) + (vmem,) * 5,
        scratch_shapes=[
            pltpu.VMEM((width, width, 128), F32),
            pltpu.VMEM((total * STRIDE, 2 * width), F32),
            pltpu.SemaphoreType.DMA((2 + len(parts),)),
        ],
        compiler_params=room(20),
        name="leaves",
    )(*parts, edge_part, grams, gram, device_transfer)

    coupling = pl.pallas_call(
        functools.partial(far_kernel, plan),
        out_shape=jax.ShapeDtypeStruct((width, own * far_index.shape[1] * width), BF16),
        in_specs=[hbm] + [vmem] * (2 + len(blocks)),
        out_specs=vmem,
        scratch_shapes=[
            pltpu.SMEM(far_list.shape, jnp.int32),
            pltpu.SemaphoreType.DMA,
        ],
        compiler_params=room(16),
        name="far",
    )(far_list, high, low, *blocks)
    return near, coupling.T, device_factor, group_factor, root_factor


def solution(mesh):
    split = P(AXES, None)
    return jax.shard_map(
        per_device,
        mesh=mesh,
        in_specs=(P(None, AXES), split, split, split, split, split, P(AXES), split),
        out_specs=(split, split, split, split, split),
        check_vma=False,
    )
```

```python
import functools
import math

import jax
import jax.numpy as jnp
from jax import lax
from jax.experimental import pallas as pl
from jax.experimental.pallas import tpu as pltpu
from jax.sharding import PartitionSpec as P

LAYER = 4
PAD = 8
LONG_SQ = 2.25
RATIO = 25.0
SCALE = 0.5 / LONG_SQ
HALF = math.log(0.5)
OFF = -16384.0
STRIDE = 40
AXES = ("group", "sub")
F32 = jnp.float32
BF16 = jnp.bfloat16


def room(megabytes):
    return pltpu.CompilerParams(vmem_limit_bytes=int(megabytes * 1024 * 1024))


def split2(value):
    high = value.astype(BF16)
    return high, (value - high.astype(F32)).astype(BF16)


def split3(value):
    high = value.astype(BF16)
    rest = value - high.astype(F32)
    middle = rest.astype(BF16)
    return high, middle, (rest - middle.astype(F32)).astype(BF16)


def mm(left, right):
    return jnp.dot(left, right, preferred_element_type=F32)


def mm_nt(left, right):
    return lax.dot_general(left, right, (((1,), (1,)), ((), ())), preferred_element_type=F32)


def exact(left, right):
    return jnp.dot(left, right, precision=lax.Precision.HIGHEST, preferred_element_type=F32)


def iota(shape, dim):
    return lax.broadcasted_iota(jnp.int32, shape, dim)


def tree_kernel(
    points_in, basis_in, below_in, transfer_in, vectors,
    dense, top, outer, inner, points, basis, below, transfer, passing, packed, staged, sems,
):
    width = basis.shape[0]
    count = basis.shape[1] // width
    halo = LAYER * width
    span = PAD * width
    rows = vectors.shape[0]
    odd = lax.axis_index("sub") % 2
    sides = ((outer, odd), (inner, 1 - odd))
    basis_copy, below_copy, points_copy, transfer_copy = loads = [
        pltpu.make_async_copy(source, target, sems.at[n])
        for n, (source, target) in enumerate(
            (
                (basis_in, basis),
                (below_in, below),
                (points_in, points),
                (transfer_in, transfer),
            )
        )
    ]
    vector_loads = [
        pltpu.make_async_copy(
            vectors.at[pl.ds(pl.multiple_of(last * (rows - halo), 16), halo), :],
            passing.at[n],
            sems.at[4 + n],
        )
        for n, (_, last) in enumerate(sides)
    ]
    copies = [
        pltpu.make_async_copy(passing.at[n], target.at[pl.ds(0, halo), :], sems.at[9 + n])
        for n, (target, _) in enumerate(sides)
    ]
    for copy in loads + vector_loads:
        copy.start()

    both = 2 * width
    lane = iota((width, 2 * both), 1)

    def times(above, columns):
        found = []
        for n in range(above.shape[1] // both):
            parts = jnp.concatenate(split3(above[:, n * both : (n + 1) * both]), axis=1)
            block = columns(n * 2 * both)
            zero = jnp.zeros_like(block)
            block = jnp.concatenate(
                [jnp.where(lane < both, block, zero), jnp.where(lane < both, zero, block)], axis=0
            )
            found.append(mm(parts, jnp.concatenate([block] * 3, axis=0)))
        return jnp.concatenate(found, axis=1)

    same = iota((both, both), 0) // width == iota((both, both), 1) // width
    half_block = jnp.where(same, 0.5, 0.0).astype(F32)
    basis_copy.wait()
    points_copy.wait()
    for n, (target, last) in enumerate(sides):
        bases = basis[:, count * width - span :], basis[:, 0:span]
        last_three, first_three = (
            jnp.concatenate(
                [block[:, (at + skip) * width : (at + skip + 3) * width] for at in (0, LAYER)],
                axis=1,
            )
            for skip, block in zip((1, 0), bases)
        )
        packed[n, 0:width, :] = jnp.where(last == 1, last_three, first_three)
        coords = jnp.where(last == 1, points[:, count * width - span :], points[:, 0:span])
        for m in range(2):
            high, low = split2(coords[:, m * halo : (m + 1) * halo])
            base = width + 16 * m
            packed[n, base : base + 16, :] = jnp.zeros((16, target.shape[1]), BF16)
            packed[n, base : base + 3, 0:halo] = high
            packed[n, base + 8 : base + 11, 0:halo] = low
        copies.append(
            pltpu.make_async_copy(
                packed.at[n], target.at[pl.ds(halo, width + 32), :], sems.at[6 + n]
            )
        )
        copies[-1].start()
    blocks = []
    for n in range(count // 4):
        stacked = jnp.concatenate(
            [basis[:, (2 * n + m) * both : (2 * n + m + 1) * both] for m in range(2)], axis=0
        )
        blocks.append(mm_nt(stacked, stacked) * half_block)
    below_copy.wait()
    for load, copy in zip(vector_loads, copies[:2]):
        load.wait()
        copy.start()
    halves = []
    for n, block in enumerate(blocks):
        t = below[:, n * both : (n + 1) * both]
        half = mm(jnp.concatenate([t, t, t], axis=1), jnp.concatenate(split3(block), axis=0))
        halves.append((half, t))
    blocks = []
    for n in range(0, len(halves), 2):
        (first, t), (second, u) = halves[n : n + 2]
        x = jnp.concatenate(split3(jnp.concatenate([first, second], axis=0)), axis=1)
        t = jnp.concatenate([t, u], axis=0)
        blocks.append(mm_nt(x, jnp.concatenate([t, t, t], axis=1)) * half_block)

    transfer_copy.wait()
    end = below.shape[1]
    tops = below[:, end - both : end]
    turned = jnp.concatenate(split3(transfer[...].T), axis=1)
    above = jnp.concatenate(
        [tops.astype(F32), mm(turned, jnp.concatenate([tops] * 3, axis=0))], axis=0
    )
    end -= both
    nodes = 4
    while nodes < count // 2:
        start = end - nodes * width
        above = times(above, lambda at, start=start: below[:, start + at : start + at + 2 * both])
        end = start
        nodes *= 2

    total = jnp.zeros((both, both), F32)
    for n, block in enumerate(blocks):
        rows = above[:, n * both : (n + 1) * both]
        high, middle, low = split3(rows)
        gh, gm, gl = split3(block)
        x = mm(
            jnp.concatenate([high, high, high, middle, middle, low], axis=1),
            jnp.concatenate([gh, gm, gl, gh, gm, gh], axis=0),
        )
        xh, xm, xl = split3(x)
        total = total + mm_nt(
            jnp.concatenate([xh, xh, xh, xm, xm, xl], axis=1),
            jnp.concatenate([high, middle, low, high, middle, high], axis=1),
        )
    total = total * (4.0 / count)
    top[...] = fold(total[:width, :width])
    halves = fold(total[width:, width:])
    dense[...] = halves
    staged[...] = jnp.concatenate(split3(halves), axis=1)
    copies.append(
        pltpu.make_async_copy(
            staged, inner.at[pl.ds(halo + width + 32, width // 2), :], sems.at[8]
        )
    )
    copies[-1].start()
    for copy in copies:
        copy.wait()


def factor_lanes(work, width):
    panels = width // 8
    row = iota((8, 128), 0)

    def spread(j, i):
        return jnp.broadcast_to(work[j, i : i + 1, :], (8, 128))

    for p in range(panels):
        at = 8 * p
        entry = {(k, m): spread(at + k, at + m) for k in range(8) for m in range(k, 8)}
        scales = []
        for k in range(8):
            scales.append(lax.rsqrt(entry[k, k]))
            for m in range(k + 1, 8):
                entry[k, m] = entry[k, m] * scales[k]
            for m in range(k + 1, 8):
                for q in range(m, 8):
                    entry[m, q] = entry[m, q] - entry[k, m] * entry[k, q]
        for i in range(p, panels):
            tile = [work[at + k, 8 * i : 8 * i + 8, :] for k in range(8)]
            for k in range(8):
                tile[k] = tile[k] * scales[k]
                for m in range(k + 1, 8):
                    tile[m] = tile[m] - tile[k] * entry[k, m]
            for k in range(8):
                work[at + k, 8 * i : 8 * i + 8, :] = (
                    jnp.where(row >= k, tile[k], 0.0) if i == p else tile[k]
                )
        for q in range(p + 1, panels):
            for start in range(q, panels, 2):
                group = range(start, min(start + 2, panels))
                accs = {
                    (i, k): work[8 * q + k, 8 * i : 8 * i + 8, :] for i in group for k in range(8)
                }
                for j in range(at, at + 8):
                    factors = [spread(j, 8 * q + k) for k in range(8)]
                    for i in group:
                        column = work[j, 8 * i : 8 * i + 8, :]
                        for k in range(8):
                            accs[i, k] = accs[i, k] - column * factors[k]
                for (i, k), value in accs.items():
                    work[8 * q + k, 8 * i : 8 * i + 8, :] = value


def fold(matrix):
    half = matrix.shape[0] // 2
    return jnp.concatenate([matrix[:half], matrix[half:]], axis=1)


def unfold(matrix):
    half = matrix.shape[1] // 2
    return jnp.concatenate([matrix[:, :half], matrix[:, half:]], axis=0)


def from_lanes(work, factors, width, many):
    for i in range(width // 2):
        both = []
        for j in (i, i + width // 2):
            skip = j // 8 * 8
            both += [jnp.zeros((skip, many), F32)] * bool(skip) + [work[j, skip:, 0:many]]
        factors[pl.ds(i, many, stride=STRIDE), :] = jnp.concatenate(both, axis=0).T


def gaussians(exponent):
    return jnp.exp(exponent) + jnp.exp(exponent * RATIO - RATIO * HALF)


def features(place, leaf, center):
    sub = iota(place.shape, 0)
    corner = jnp.where(sub == 0, leaf % 2 - 1, leaf // 2 % 2 - 1)
    corner = jnp.where(sub == 2, leaf // LAYER - center, corner)
    place = jnp.where(sub < 3, place + corner.astype(F32), 0.0)
    norm = jnp.sum(place * place, axis=0, keepdims=True) * SCALE
    first = jnp.where(sub == 3, -norm, jnp.where(sub == 4, 1.0, place))
    second = jnp.where(
        sub == 3, 1.0, jnp.where(sub == 4, HALF - norm, place * (2.0 * SCALE))
    )
    fh, fm, fl = [v.astype(F32) for v in split3(first)]
    sh, sm, sl = [v.astype(F32) for v in split3(second)]
    return (
        jnp.concatenate([fh, fh, fh, fm, fm, fl], axis=0),
        jnp.concatenate([sh, sm, sl, sh, sm, sh], axis=0),
    )


def rows_of(second):
    blank = jnp.zeros((16, second.shape[1]), F32)
    return jnp.concatenate([second, blank, second, blank], axis=0).T.astype(BF16)


def near_weights(first_rows, second, switches, index, halo):
    group = index // 4 * 16
    columns = jnp.concatenate([second, switches[group : group + 16, :]], axis=0)
    return gaussians(mm(first_rows[index * halo : (index + 1) * halo, :], columns)).astype(BF16)


def prepare(
    points, near_list, near_used, first_rows, first_cols, second_cols, second_rows, switches, place
):
    rows = points.shape[1]
    own = near_list.shape[1]
    width = rows // own
    place[...] = jnp.zeros(place.shape, F32)
    place[0:3, :] = points[...]
    leaf = iota((8, rows), 1) // width
    first, second = features(place[...], leaf, own // LAYER // 2)
    hot_leaf = iota((16, rows), 1) // width
    hot = jnp.where(hot_leaf % 16 == iota((16, rows), 0), 1.0, 0.0).astype(F32)
    first = jnp.concatenate([first, hot], axis=0)
    first_cols[...] = first.astype(BF16)
    second_cols[...] = second.astype(BF16)
    first_rows[...] = first.T.astype(BF16)
    second_rows[...] = rows_of(second)

    start_leaf = lax.axis_index(AXES) * own
    target = iota((1, own), 1)
    base_leaf = start_leaf + target // LAYER * LAYER - LAYER
    found = jnp.zeros((16, own), jnp.bool_)
    place_row = iota((16, own), 0)
    for n in range(near_list.shape[0]):
        spot = jnp.where(near_used[...] > n, near_list[n : n + 1, :] - base_leaf, -1)
        found = jnp.logical_or(found, place_row == spot)
    bias = jnp.where(found, 0.0, OFF).astype(F32)
    span = 3 * LAYER * width
    expand = jnp.where(iota((16, span), 0) == iota((16, span), 1) // width, 1.0, 0.0)
    switches[...] = mm(bias.T.astype(BF16), expand.astype(BF16)).astype(BF16)


def inner_layers(layers, vectors, first_rows, second_cols, switches, out, halo):
    for n, index in enumerate(layers):
        around = slice((index - 1) * halo, (index + 2) * halo)
        weights = near_weights(first_rows, second_cols[:, around], switches, index, halo)
        out[n * halo : (n + 1) * halo, :] = mm(weights, vectors[around, :]).astype(BF16)


def far_blocks(pairs, far_list, second_rows, first_cols, out, width, base, places):
    far, own = far_list.shape
    both = 2 * width
    start_leaf = lax.axis_index(AXES) * own
    square = iota((both, both), 0) // width == iota((both, both), 1) // width
    lane = iota((far * width, both), 1) < width
    exponents = []
    for index in pairs:
        t = 2 * index
        picked = []
        for m in range(2):
            spots = [
                pl.multiple_of((far_list[f, t + m] - start_leaf + base) * width, width)
                for f in range(far)
            ]
            picked.append(
                jnp.concatenate([second_rows[pl.ds(spot, width), :] for spot in spots], axis=0)
            )
        cols = first_cols[:, t * width : t * width + both]
        targets = jnp.where(
            square, jnp.concatenate([cols, cols], axis=0), jnp.zeros((both, both), BF16)
        )
        exponents.append(mm(jnp.where(lane, picked[0], picked[1]), targets))
    for place, exponent in zip(places, exponents):
        high, low = split2(gaussians(exponent))
        at = place * far * width
        out[at : at + far * width, 0:both] = high
        out[at : at + far * width, both : 2 * both] = low


def first_chunk_kernel(layers):
    def body(
        points, near_list, near_used, vectors,
        out, first_rows, first_cols, second_cols, second_rows, switches, place,
    ):
        prepare(
            points,
            near_list,
            near_used,
            first_rows,
            first_cols,
            second_cols,
            second_rows,
            switches,
            place,
        )
        halo = LAYER * points.shape[1] // near_list.shape[1]
        inner_layers(layers, vectors, first_rows, second_cols, switches, out, halo)

    return body


def chunk_kernel(layers, pairs, halo, width):
    def body(after, far_in, *refs):
        first_rows, second_cols, switches, vectors, first_cols, second_rows = refs[:6]
        outs, far_list, sem = refs[6:-2], refs[-2], refs[-1]
        if pairs:
            copy = pltpu.make_async_copy(far_in, far_list, sem)
            copy.start()
        if layers:
            inner_layers(layers, vectors, first_rows, second_cols, switches, outs[0], halo)
        if pairs:
            copy.wait()
            far_blocks(
                pairs, far_list, second_rows, first_cols, outs[-1], width, 0, range(len(pairs))
            )

    return body


def edges_kernel(
    after, inner, outer, first_rows, second_cols, switches, vectors,
    out, halo_rows, ends, sides, place, halo_cols, sems,
):
    halo = ends.shape[1]
    width = halo // LAYER
    own = vectors.shape[0] // width
    layers = own // LAYER
    extra = sides.shape[1]
    odd = lax.axis_index("sub") % 2
    arrived = ((inner, 1 - odd), (outer, odd))
    side_copies = [
        pltpu.make_async_copy(
            block.at[pl.ds(halo + width, extra), :], sides.at[side], sems.at[n]
        )
        for n, (block, side) in enumerate(arrived)
    ]
    end_copies = [
        pltpu.make_async_copy(block.at[pl.ds(0, halo), :], ends.at[side], sems.at[2 + n])
        for n, (block, side) in enumerate(arrived)
    ]
    for copy in side_copies + end_copies:
        copy.start()
    lanes = PAD * width
    place[...] = jnp.zeros(place.shape, F32)
    for copy in side_copies:
        copy.wait()
    for side, first_leaf in enumerate((-PAD, own)):
        for n in range(2):
            values = sides[side, 16 * n : 16 * n + 16, 0:halo].astype(F32)
            place[0:3, n * halo : (n + 1) * halo] = values[0:3, :] + values[8:11, :]
        leaf = iota((8, lanes), 1) // width + (first_leaf + PAD)
        second = features(place[...], leaf, layers // 2 + PAD // LAYER)[1]
        halo_cols[side, :, :] = second.astype(BF16)
        halo_rows[side * lanes : (side + 1) * lanes, :] = rows_of(second)
    weights = [
        near_weights(
            first_rows, jnp.concatenate(columns, axis=1), switches, index, halo
        )
        for index, columns in (
            (0, [halo_cols[0, :, halo:], second_cols[:, 0 : 2 * halo]]),
            (layers - 1, [second_cols[:, (layers - 2) * halo :], halo_cols[1, :, 0:halo]]),
        )
    ]
    for copy in end_copies:
        copy.wait()
    value = mm(weights[0][:, 0:halo], ends[0, :, :])
    value = value + mm(weights[0][:, halo:], vectors[0 : 2 * halo, :])
    out[0:halo, :] = value.astype(BF16)
    value = mm(weights[1][:, 0 : 2 * halo], vectors[(layers - 2) * halo :, :])
    value = value + mm(weights[1][:, 2 * halo :], ends[1, :, :])
    out[halo:, :] = value.astype(BF16)


def last_chunk_kernel(layers, pairs):
    def body(
        after, far_in, inner, outer, first_rows, second_cols, switches, vectors,
        first_cols, own_rows, halo_rows, basis, top,
        out, blocks, grams, far_list, sides, second_rows, sems,
    ):
        width = basis.shape[0]
        own = basis.shape[1] // width
        total = own + 2 * PAD
        halo = LAYER * width
        both = 2 * width
        odd = lax.axis_index("sub") % 2
        side_copies = [
            pltpu.make_async_copy(block.at[pl.ds(halo, width), :], sides.at[side], sems.at[n])
            for n, (block, side) in enumerate(((inner, 1 - odd), (outer, odd)))
        ]
        list_copy = pltpu.make_async_copy(far_in, far_list, sems.at[2])
        for copy in side_copies + [list_copy]:
            copy.start()
        lanes = PAD * width
        second_rows[0:lanes, :] = halo_rows[0:lanes, :]
        second_rows[lanes : lanes + own * width, :] = own_rows[...]
        second_rows[lanes + own * width :, :] = halo_rows[lanes:, :]
        inner_layers(layers, vectors, first_rows, second_cols, switches, out, halo)

        lane = iota((width, both), 1)
        for n in range(own // 2):
            pair = basis[:, n * both : (n + 1) * both]
            zero = jnp.zeros_like(pair)
            stacked = jnp.concatenate(
                [jnp.where(lane < width, pair, zero), jnp.where(lane < width, zero, pair)], axis=0
            )
            value = mm_nt(stacked, pair)
            for m in range(2):
                at = (PAD + 2 * n + m) * STRIDE
                grams[at : at + width // 2, :] = fold(value[m * width : (m + 1) * width])
        for spot in (0, LAYER, total - LAYER - 1, total - 1):
            grams[spot * STRIDE : spot * STRIDE + width // 2, :] = top[...]
        for copy in side_copies + [list_copy]:
            copy.wait()
        for side, spots in enumerate(
            ((1, 2, 3, 5, 6, 7), tuple(PAD + own + m for m in (0, 1, 2, 4, 5, 6)))
        ):
            for n, spot in enumerate(spots):
                piece = sides[side, 0:width, n * width : (n + 1) * width]
                at = spot * STRIDE
                grams[at : at + width // 2, :] = fold(mm_nt(piece, piece))
        far_blocks(
            pairs, far_list, second_rows, first_cols, blocks, width, PAD, range(len(pairs))
        )

    return body


def leaves_kernel(chunks, members, groups, *refs):
    outer_count = len(chunks) + 1
    near_parts = refs[:outer_count]
    (
        grams,
        upper,
        transfer,
        near,
        high,
        low,
        device_factor,
        group_factor,
        root_factor,
        work,
        factors,
        sems,
    ) = refs[outer_count:]
    width = transfer.shape[0]
    total = high.shape[0] // width
    own = total - 2 * PAD
    halo = LAYER * width
    layers = own // LAYER
    both = 2 * width
    places = [(part, 0, chunk[0], len(chunk)) for part, chunk in zip(near_parts, chunks)]
    places += [(near_parts[-1], n, index, 1) for n, index in enumerate((0, layers - 1))]
    near_copies = [
        pltpu.make_async_copy(
            part.at[pl.ds(start * halo, many * halo), :],
            near.at[pl.ds(index * halo, many * halo), :],
            sems.at[n],
        )
        for n, (part, start, index, many) in enumerate(places)
    ]
    for copy in near_copies:
        copy.start()

    spare = (LAYER, total - LAYER - 1)
    means = (
        upper[0 : width // 2, :] * (1.0 / members),
        upper[width // 2 :, :] * (1.0 / (members * groups)),
    )
    spot_row = iota((total, both), 0)
    for i in range(width // 2):
        rows = grams[pl.ds(i, total, stride=STRIDE), :]
        for spot, mean in zip(spare, means):
            rows = jnp.where(spot_row == spot, mean[i : i + 1, :], rows)
        turned = rows.T
        work[i, :, 0:total] = turned[0:width]
        work[i + width // 2, :, 0:total] = turned[width:]
    factor_lanes(work, width)
    from_lanes(work, factors, width, total)
    device_factor[...] = exact(unfold(factors[0 : width // 2, :]), transfer[...])
    for target, spot in zip((group_factor, root_factor), spare):
        target[...] = unfold(factors[spot * STRIDE : spot * STRIDE + width // 2, :])
    left_lanes = iota((width // 2, both), 1) < width
    for spot in range(total):
        rows = factors[spot * STRIDE : spot * STRIDE + width // 2, :]
        turned = pltpu.roll(rows, width, 1)
        twice = jnp.concatenate(
            [jnp.where(left_lanes, rows, turned), jnp.where(left_lanes, turned, rows)], axis=0
        )
        at = slice(spot * width, (spot + 1) * width)
        high[at, :], low[at, :] = split2(twice)
    for copy in near_copies:
        copy.wait()


def far_kernel(plan, far_in, high, low, *refs):
    blocks, (coupling, far_list, lines, sem, sems) = refs[:-5], refs[-5:]
    copy = pltpu.make_async_copy(far_in, far_list, sem)
    copy.start()
    width = coupling.shape[0]
    far, own = far_list.shape
    both = 2 * width
    start_leaf = lax.axis_index(AXES) * own
    square = iota((both, both), 0) // width == iota((both, both), 1) // width
    lane = iota((width, both), 1) < width
    zero = jnp.zeros((both, both), BF16)

    def diagonal(value):
        return jnp.where(square, value, zero)

    copies = []
    for start in range(0, own // 2, 4):
        indices = range(start, start + 4)
        halves = []
        for index in indices:
            source, place = plan[index]
            at = place * far * width
            kh = blocks[source][at : at + far * width, 0:both]
            kl = blocks[source][at : at + far * width, both : 2 * both]
            at = (PAD + 2 * index) * width
            rh = diagonal(high[at : at + both, :])
            rl = diagonal(low[at : at + both, :])
            halves.append(
                mm_nt(
                    jnp.concatenate([kh, kl, kh], axis=1), jnp.concatenate([rh, rh, rl], axis=1)
                )
            )
        if start == 0:
            copy.wait()
        outs = []
        for index, half in zip(indices, halves):
            zh, zl = split2(half * (1.0 / width))
            for f in range(far):
                spots = [
                    pl.multiple_of((far_list[f, 2 * index + m] - start_leaf + PAD) * width, width)
                    for m in range(2)
                ]
                sh, sl = (
                    jnp.where(lane, *(part[pl.ds(spot, width), :] for spot in spots))
                    for part in (high, low)
                )
                a = slice(f * width, (f + 1) * width)
                ph = diagonal(jnp.concatenate([zh[a], zh[a]], axis=0))
                plow = diagonal(jnp.concatenate([zl[a], zl[a]], axis=0))
                outs.append(
                    mm(
                        jnp.concatenate([sh, sh, sl], axis=1),
                        jnp.concatenate([ph, plow, ph], axis=0),
                    )
                )
        for n, index in enumerate(indices):
            three = outs[n * far : (n + 1) * far]
            line = jnp.concatenate(
                [out[:, 0:width] for out in three] + [out[:, width:both] for out in three], axis=1
            )
            at = index * 2 * far * width
            lines[:, at : at + 2 * far * width] = line.astype(BF16)
        group = pl.ds(start * 2 * far * width, 8 * far * width)
        copies.append(
            pltpu.make_async_copy(lines.at[:, group], coupling.at[:, group], sems.at[start // 4])
        )
        copies[-1].start()
    for copy in copies:
        copy.wait()


def swap_inner(block):
    return lax.ppermute(block, AXES, [(i, i ^ 1) for i in range(lax.axis_size(AXES))])


def swap_outer(block):
    many = lax.axis_size(AXES)
    return lax.ppermute(block, AXES, [(i, (i + 1 if i % 2 else i - 1) % many) for i in range(many)])


def exchange(value, distance):
    pairs = [(i, i ^ distance ^ 1) for i in range(lax.axis_size(AXES))]
    return value + lax.ppermute(value, AXES, pairs)


def per_device(
    points, leaf_basis, inner_transfer, device_transfer, vectors, near_index, near_count, far_index
):
    own = near_index.shape[0]
    width = leaf_basis.shape[1]
    columns = vectors.shape[1]
    halo = LAYER * width
    half = width // 2
    layers = own // LAYER
    total = own + 2 * PAD
    members, groups = lax.axis_size("sub"), lax.axis_size("group")
    vmem = pl.BlockSpec(memory_space=pltpu.VMEM)
    hbm = pl.BlockSpec(memory_space=pl.ANY)
    square = jax.ShapeDtypeStruct((width, width), F32)
    extra = halo + width + 32

    def block_of(rows):
        return jax.ShapeDtypeStruct((rows, columns), BF16)

    basis = leaf_basis.T
    near_list, far_list = near_index.T, far_index.T
    cost = pl.CostEstimate(flops=10**9, bytes_accessed=4 * 10**6, transcendentals=10**6)

    dense, top, to_outer, to_inner = pl.pallas_call(
        tree_kernel,
        out_shape=(
            jax.ShapeDtypeStruct((half, 2 * width), F32),
            jax.ShapeDtypeStruct((half, 2 * width), F32),
            block_of(extra),
            block_of(extra + half),
        ),
        in_specs=[hbm] * 5,
        out_specs=(vmem, vmem, hbm, hbm),
        scratch_shapes=[
            pltpu.VMEM((3, own * width), F32),
            pltpu.VMEM((width, own * width), BF16),
            pltpu.VMEM((width, (own - 2) * width), BF16),
            pltpu.VMEM((width, width), F32),
            pltpu.VMEM((2, halo, columns), BF16),
            pltpu.VMEM((2, width + 32, columns), BF16),
            pltpu.VMEM((half, columns), BF16),
            pltpu.SemaphoreType.DMA((11,)),
        ],
        compiler_params=room(60),
        name="tree",
    )(points, basis, inner_transfer.T, device_transfer, vectors)
    from_inner = swap_inner(to_inner)
    from_outer = swap_outer(to_outer)

    sub_bits = members.bit_length() - 1
    steps = [members << bit for bit in range(groups.bit_length() - 1)]
    steps += [1 << bit for bit in range(1, sub_bits)]
    inner_pairs = list(range(PAD // 2, (own - PAD) // 2))
    few = len(inner_pairs) // 2
    edge_pairs = [index for index in range(own // 2) if index not in inner_pairs]
    chunks = [[1, 2], [3, 4], [5], [6]]
    pair_chunks = [[], inner_pairs[:few], inner_pairs[few:], edge_pairs]
    blocks, plan, parts = [], {}, []

    def part_shape(count):
        return jax.ShapeDtypeStruct((count * halo, columns), BF16)

    def block_shape(count):
        return jax.ShapeDtypeStruct((count * far_index.shape[1] * width, 4 * width), BF16)

    late_points, dense = lax.optimization_barrier((points, dense))
    part, *shared = pl.pallas_call(
        first_chunk_kernel(chunks[0]),
        out_shape=(
            part_shape(len(chunks[0])),
            jax.ShapeDtypeStruct((own * width, 64), BF16),
            jax.ShapeDtypeStruct((64, own * width), BF16),
            jax.ShapeDtypeStruct((48, own * width), BF16),
            jax.ShapeDtypeStruct((own * width, 128), BF16),
            jax.ShapeDtypeStruct((own, 3 * halo), BF16),
        ),
        in_specs=[vmem] * 4,
        out_specs=(vmem,) * 6,
        scratch_shapes=[pltpu.VMEM((8, own * width), F32)],
        compiler_params=room(10),
        cost_estimate=cost,
        name="chunk_0",
    )(late_points, near_list, near_count.reshape(1, own), vectors)
    parts.append(part)
    summands = [
        from_inner[extra:, n * 2 * width : (n + 1) * 2 * width].astype(F32) for n in range(3)
    ]
    pair_gram = gram = dense + (summands[0] + (summands[1] + summands[2]))
    gram, parts[0] = lax.optimization_barrier((gram, parts[0]))
    first_rows, first_cols, second_cols, second_rows, switches = shared
    jobs = [1, 2, "edges", 3]
    for n in range(max(len(steps), len(jobs))):
        before = gram
        if n < len(steps):
            if n == len(steps) - sub_bits + 1:
                gram = before = jnp.concatenate([pair_gram, gram], axis=0)
            gram = exchange(gram, steps[n])
        job = jobs[n] if n < len(jobs) else None
        if job in (1, 2):
            layer_chunk, pair_chunk = chunks[job], pair_chunks[job]
            shapes = [part_shape(len(layer_chunk))] * bool(layer_chunk)
            shapes += [block_shape(len(pair_chunk))] * bool(pair_chunk)
            outs = pl.pallas_call(
                chunk_kernel(layer_chunk, pair_chunk, halo, width),
                out_shape=tuple(shapes),
                in_specs=[hbm] * 2 + [vmem] * 6,
                out_specs=(vmem,) * len(shapes),
                scratch_shapes=[
                    pltpu.SMEM(far_list.shape, jnp.int32),
                    pltpu.SemaphoreType.DMA,
                ],
                compiler_params=room(10),
                cost_estimate=cost,
                name=f"chunk_{job}",
            )(before, far_list, first_rows, second_cols, switches, vectors, first_cols, second_rows)
            gram, outs = lax.optimization_barrier((gram, outs))
            if layer_chunk:
                parts.append(outs[0])
            if pair_chunk:
                plan.update((index, (len(blocks), m)) for m, index in enumerate(pair_chunk))
                blocks.append(outs[-1])
        elif job == "edges":
            edge_part, halo_rows = pl.pallas_call(
                edges_kernel,
                out_shape=(
                    part_shape(2),
                    jax.ShapeDtypeStruct((2 * PAD * width, 2 * width), BF16),
                ),
                in_specs=[hbm] * 3 + [vmem] * 4,
                out_specs=(vmem,) * 2,
                scratch_shapes=[
                    pltpu.VMEM((2, halo, columns), BF16),
                    pltpu.VMEM((2, 32, columns), BF16),
                    pltpu.VMEM((8, PAD * width), F32),
                    pltpu.VMEM((2, 48, PAD * width), BF16),
                    pltpu.SemaphoreType.DMA((4,)),
                ],
                compiler_params=room(10),
                cost_estimate=cost,
                name="edges",
            )(before, from_inner, from_outer, first_rows, second_cols, switches, vectors)
            gram, edge_part = lax.optimization_barrier((gram, edge_part))
        elif job == 3:
            part, edge_blocks, grams = pl.pallas_call(
                last_chunk_kernel(chunks[3], edge_pairs),
                out_shape=(
                    part_shape(len(chunks[3])),
                    block_shape(len(edge_pairs)),
                    jax.ShapeDtypeStruct((total * STRIDE, 2 * width), F32),
                ),
                in_specs=[hbm] * 4 + [vmem] * 9,
                out_specs=(vmem,) * 3,
                scratch_shapes=[
                    pltpu.SMEM(far_list.shape, jnp.int32),
                    pltpu.VMEM((2, width, columns), BF16),
                    pltpu.VMEM((total * width, 2 * width), BF16),
                    pltpu.SemaphoreType.DMA((3,)),
                ],
                compiler_params=room(14),
                cost_estimate=cost,
                name="chunk_3",
            )(
                before,
                far_list,
                from_inner,
                from_outer,
                first_rows,
                second_cols,
                switches,
                vectors,
                first_cols,
                second_rows,
                halo_rows,
                basis,
                top,
            )
            gram, part = lax.optimization_barrier((gram, part))
            parts.append(part)
            plan.update((index, (len(blocks), m)) for m, index in enumerate(edge_pairs))
            blocks.append(edge_blocks)

    split_factors = jax.ShapeDtypeStruct((total * width, 2 * width), BF16)
    near, high, low, device_factor, group_factor, root_factor = pl.pallas_call(
        functools.partial(leaves_kernel, chunks, members, groups),
        out_shape=(
            jax.ShapeDtypeStruct(vectors.shape, BF16),
            split_factors,
            split_factors,
            square,
            square,
            square,
        ),
        in_specs=[hbm] * (len(parts) + 1) + [vmem] * 3,
        out_specs=(hbm,) + (vmem,) * 5,
        scratch_shapes=[
            pltpu.VMEM((width, width, 128), F32),
            pltpu.VMEM((total * STRIDE, 2 * width), F32),
            pltpu.SemaphoreType.DMA((2 + len(parts),)),
        ],
        compiler_params=room(20),
        name="leaves",
    )(*parts, edge_part, grams, gram, device_transfer)

    coupling = pl.pallas_call(
        functools.partial(far_kernel, plan),
        out_shape=jax.ShapeDtypeStruct((width, own * far_index.shape[1] * width), BF16),
        in_specs=[hbm] + [vmem] * (2 + len(blocks)),
        out_specs=hbm,
        scratch_shapes=[
            pltpu.SMEM(far_list.shape, jnp.int32),
            pltpu.VMEM((width, own * far_index.shape[1] * width), BF16),
            pltpu.SemaphoreType.DMA,
            pltpu.SemaphoreType.DMA((own // 8,)),
        ],
        compiler_params=room(16),
        name="far",
    )(far_list, high, low, *blocks)
    return near, coupling.T, device_factor, group_factor, root_factor


def solution(mesh):
    split = P(AXES, None)
    return jax.shard_map(
        per_device,
        mesh=mesh,
        in_specs=(P(None, AXES), split, split, split, split, split, P(AXES), split),
        out_specs=(split, split, split, split, split),
        check_vma=False,
    )
```

```python
import functools
import math

import jax
import jax.numpy as jnp
from jax import lax
from jax.experimental import pallas as pl
from jax.experimental.pallas import tpu as pltpu
from jax.sharding import PartitionSpec as P

LAYER = 4
PAD = 8
LONG_SQ = 2.25
RATIO = 25.0
SCALE = 0.5 / LONG_SQ
HALF = math.log(0.5)
OFF = -16384.0
STRIDE = 40
AXES = ("group", "sub")
F32 = jnp.float32
BF16 = jnp.bfloat16


def room(megabytes):
    return pltpu.CompilerParams(vmem_limit_bytes=int(megabytes * 1024 * 1024))


def split2(value):
    high = value.astype(BF16)
    return high, (value - high.astype(F32)).astype(BF16)


def split3(value):
    high = value.astype(BF16)
    rest = value - high.astype(F32)
    middle = rest.astype(BF16)
    return high, middle, (rest - middle.astype(F32)).astype(BF16)


def mm(left, right):
    return jnp.dot(left, right, preferred_element_type=F32)


def mm_nt(left, right):
    return lax.dot_general(left, right, (((1,), (1,)), ((), ())), preferred_element_type=F32)


def exact(left, right):
    return jnp.dot(left, right, precision=lax.Precision.HIGHEST, preferred_element_type=F32)


def iota(shape, dim):
    return lax.broadcasted_iota(jnp.int32, shape, dim)


def tree_kernel(
    points_in, basis_in, below_in, transfer_in, vectors,
    dense, top, outer, inner, points, basis, below, transfer, passing, packed, staged, small, sems,
):
    width = basis.shape[0]
    count = basis.shape[1] // width
    halo = LAYER * width
    span = PAD * width
    rows = vectors.shape[0]
    odd = lax.axis_index("sub") % 2
    sides = ((outer, odd), (inner, 1 - odd))
    basis_copy, below_copy, points_copy, transfer_copy = loads = [
        pltpu.make_async_copy(source, target, sems.at[n])
        for n, (source, target) in enumerate(
            (
                (basis_in, basis),
                (below_in, below),
                (points_in, points),
                (transfer_in, transfer),
            )
        )
    ]
    vector_loads = [
        pltpu.make_async_copy(
            vectors.at[pl.ds(pl.multiple_of(last * (rows - halo), 16), halo), :],
            passing.at[n],
            sems.at[4 + n],
        )
        for n, (_, last) in enumerate(sides)
    ]
    copies = [
        pltpu.make_async_copy(passing.at[n], target.at[pl.ds(0, halo), :], sems.at[9 + n])
        for n, (target, _) in enumerate(sides)
    ]
    for copy in loads + vector_loads:
        copy.start()

    both = 2 * width
    lane = iota((width, 2 * both), 1)

    def times(above, columns):
        found = []
        for n in range(above.shape[1] // both):
            parts = jnp.concatenate(split3(above[:, n * both : (n + 1) * both]), axis=1)
            block = columns(n * 2 * both)
            zero = jnp.zeros_like(block)
            block = jnp.concatenate(
                [jnp.where(lane < both, block, zero), jnp.where(lane < both, zero, block)], axis=0
            )
            found.append(mm(parts, jnp.concatenate([block] * 3, axis=0)))
        return jnp.concatenate(found, axis=1)

    same = iota((both, both), 0) // width == iota((both, both), 1) // width
    half_block = jnp.where(same, 0.5, 0.0).astype(F32)
    basis_copy.wait()
    points_copy.wait()
    for n, (target, last) in enumerate(sides):
        bases = basis[:, count * width - span :], basis[:, 0:span]
        last_three, first_three = (
            jnp.concatenate(
                [block[:, (at + skip) * width : (at + skip + 3) * width] for at in (0, LAYER)],
                axis=1,
            )
            for skip, block in zip((1, 0), bases)
        )
        packed[n, 0:width, :] = jnp.where(last == 1, last_three, first_three)
        coords = jnp.where(last == 1, points[:, count * width - span :], points[:, 0:span])
        for m in range(2):
            high, low = split2(coords[:, m * halo : (m + 1) * halo])
            base = width + 16 * m
            packed[n, base : base + 16, :] = jnp.zeros((16, target.shape[1]), BF16)
            packed[n, base : base + 3, 0:halo] = high
            packed[n, base + 8 : base + 11, 0:halo] = low
        copies.append(
            pltpu.make_async_copy(
                packed.at[n], target.at[pl.ds(halo, width + 32), :], sems.at[6 + n]
            )
        )
        copies[-1].start()
    blocks = []
    for n in range(count // 4):
        stacked = jnp.concatenate(
            [basis[:, (2 * n + m) * both : (2 * n + m + 1) * both] for m in range(2)], axis=0
        )
        blocks.append(mm_nt(stacked, stacked) * half_block)
    below_copy.wait()
    for load, copy in zip(vector_loads, copies[:2]):
        load.wait()
        copy.start()
    halves = []
    for n, block in enumerate(blocks):
        t = below[:, n * both : (n + 1) * both]
        half = mm(jnp.concatenate([t, t, t], axis=1), jnp.concatenate(split3(block), axis=0))
        halves.append((half, t))
    blocks = []
    for n in range(0, len(halves), 2):
        (first, t), (second, u) = halves[n : n + 2]
        x = jnp.concatenate(split3(jnp.concatenate([first, second], axis=0)), axis=1)
        t = jnp.concatenate([t, u], axis=0)
        blocks.append(mm_nt(x, jnp.concatenate([t, t, t], axis=1)) * half_block)

    transfer_copy.wait()
    end = below.shape[1]
    tops = below[:, end - both : end]
    turned = jnp.concatenate(split3(transfer[...].T), axis=1)
    above = jnp.concatenate(
        [tops.astype(F32), mm(turned, jnp.concatenate([tops] * 3, axis=0))], axis=0
    )
    end -= both
    nodes = 4
    while nodes < count // 2:
        start = end - nodes * width
        above = times(above, lambda at, start=start: below[:, start + at : start + at + 2 * both])
        end = start
        nodes *= 2

    total = jnp.zeros((both, both), F32)
    for n, block in enumerate(blocks):
        rows = above[:, n * both : (n + 1) * both]
        high, middle, low = split3(rows)
        gh, gm, gl = split3(block)
        x = mm(
            jnp.concatenate([high, high, high, middle, middle, low], axis=1),
            jnp.concatenate([gh, gm, gl, gh, gm, gh], axis=0),
        )
        xh, xm, xl = split3(x)
        total = total + mm_nt(
            jnp.concatenate([xh, xh, xh, xm, xm, xl], axis=1),
            jnp.concatenate([high, middle, low, high, middle, high], axis=1),
        )
    total = total * (4.0 / count)
    small[0, :, :] = fold(total[:width, :width])
    halves = fold(total[width:, width:])
    small[1, :, :] = halves
    staged[...] = jnp.concatenate(split3(halves), axis=1)
    copies.append(
        pltpu.make_async_copy(
            staged, inner.at[pl.ds(halo + width + 32, width // 2), :], sems.at[8]
        )
    )
    copies[-1].start()
    for n, target in enumerate((top, dense)):
        copies.append(pltpu.make_async_copy(small.at[n], target, sems.at[11 + n]))
        copies[-1].start()
    for copy in copies:
        copy.wait()


def factor_lanes(work, width):
    panels = width // 8
    row = iota((8, 128), 0)

    def spread(j, i):
        return jnp.broadcast_to(work[j, i : i + 1, :], (8, 128))

    for p in range(panels):
        at = 8 * p
        entry = {(k, m): spread(at + k, at + m) for k in range(8) for m in range(k, 8)}
        scales = []
        for k in range(8):
            scales.append(lax.rsqrt(entry[k, k]))
            for m in range(k + 1, 8):
                entry[k, m] = entry[k, m] * scales[k]
            for m in range(k + 1, 8):
                for q in range(m, 8):
                    entry[m, q] = entry[m, q] - entry[k, m] * entry[k, q]
        for i in range(p, panels):
            tile = [work[at + k, 8 * i : 8 * i + 8, :] for k in range(8)]
            for k in range(8):
                tile[k] = tile[k] * scales[k]
                for m in range(k + 1, 8):
                    tile[m] = tile[m] - tile[k] * entry[k, m]
            for k in range(8):
                work[at + k, 8 * i : 8 * i + 8, :] = (
                    jnp.where(row >= k, tile[k], 0.0) if i == p else tile[k]
                )
        for q in range(p + 1, panels):
            for start in range(q, panels, 4):
                group = range(start, min(start + 4, panels))
                accs = {
                    (i, k): work[8 * q + k, 8 * i : 8 * i + 8, :] for i in group for k in range(8)
                }
                for j in range(at, at + 8):
                    factors = [spread(j, 8 * q + k) for k in range(8)]
                    for i in group:
                        column = work[j, 8 * i : 8 * i + 8, :]
                        for k in range(8):
                            accs[i, k] = accs[i, k] - column * factors[k]
                for (i, k), value in accs.items():
                    work[8 * q + k, 8 * i : 8 * i + 8, :] = value


def fold(matrix):
    half = matrix.shape[0] // 2
    return jnp.concatenate([matrix[:half], matrix[half:]], axis=1)


def unfold(matrix):
    half = matrix.shape[1] // 2
    return jnp.concatenate([matrix[:, :half], matrix[:, half:]], axis=0)


def from_lanes(work, factors, width, many):
    for i in range(width // 2):
        both = []
        for j in (i, i + width // 2):
            skip = j // 8 * 8
            both += [jnp.zeros((skip, many), F32)] * bool(skip) + [work[j, skip:, 0:many]]
        factors[pl.ds(i, many, stride=STRIDE), :] = jnp.concatenate(both, axis=0).T


def gaussians(exponent):
    return jnp.exp(exponent) + jnp.exp(exponent * RATIO - RATIO * HALF)


def features(place, leaf, center):
    sub = iota(place.shape, 0)
    corner = jnp.where(sub == 0, leaf % 2 - 1, leaf // 2 % 2 - 1)
    corner = jnp.where(sub == 2, leaf // LAYER - center, corner)
    place = jnp.where(sub < 3, place + corner.astype(F32), 0.0)
    norm = jnp.sum(place * place, axis=0, keepdims=True) * SCALE
    first = jnp.where(sub == 3, -norm, jnp.where(sub == 4, 1.0, place))
    second = jnp.where(
        sub == 3, 1.0, jnp.where(sub == 4, HALF - norm, place * (2.0 * SCALE))
    )
    fh, fm, fl = [v.astype(F32) for v in split3(first)]
    sh, sm, sl = [v.astype(F32) for v in split3(second)]
    return (
        jnp.concatenate([fh, fh, fh, fm, fm, fl], axis=0),
        jnp.concatenate([sh, sm, sl, sh, sm, sh], axis=0),
    )


def rows_of(second):
    blank = jnp.zeros((16, second.shape[1]), F32)
    return jnp.concatenate([second, blank, second, blank], axis=0).T.astype(BF16)


def near_weights(first_rows, second, switches, index, halo):
    group = index // 4 * 16
    columns = jnp.concatenate([second, switches[group : group + 16, :]], axis=0)
    return gaussians(mm(first_rows[index * halo : (index + 1) * halo, :], columns)).astype(BF16)


def prepare(
    points, near_list, near_used, first_rows, first_cols, second_cols, second_rows, switches, place
):
    rows = points.shape[1]
    own = near_list.shape[1]
    width = rows // own
    place[...] = jnp.zeros(place.shape, F32)
    place[0:3, :] = points[...]
    leaf = iota((8, rows), 1) // width
    first, second = features(place[...], leaf, own // LAYER // 2)
    hot_leaf = iota((16, rows), 1) // width
    hot = jnp.where(hot_leaf % 16 == iota((16, rows), 0), 1.0, 0.0).astype(F32)
    first = jnp.concatenate([first, hot], axis=0)
    first_cols[...] = first.astype(BF16)
    second_cols[...] = second.astype(BF16)
    first_rows[...] = first.T.astype(BF16)
    second_rows[...] = rows_of(second)

    start_leaf = lax.axis_index(AXES) * own
    target = iota((1, own), 1)
    base_leaf = start_leaf + target // LAYER * LAYER - LAYER
    found = jnp.zeros((16, own), jnp.bool_)
    place_row = iota((16, own), 0)
    for n in range(near_list.shape[0]):
        spot = jnp.where(near_used[...] > n, near_list[n : n + 1, :] - base_leaf, -1)
        found = jnp.logical_or(found, place_row == spot)
    bias = jnp.where(found, 0.0, OFF).astype(F32)
    span = 3 * LAYER * width
    expand = jnp.where(iota((16, span), 0) == iota((16, span), 1) // width, 1.0, 0.0)
    switches[...] = mm(bias.T.astype(BF16), expand.astype(BF16)).astype(BF16)


def inner_layers(layers, vectors, first_rows, second_cols, switches, out, halo):
    for n, index in enumerate(layers):
        around = slice((index - 1) * halo, (index + 2) * halo)
        weights = near_weights(first_rows, second_cols[:, around], switches, index, halo)
        out[n * halo : (n + 1) * halo, :] = mm(weights, vectors[around, :]).astype(BF16)


def far_blocks(pairs, far_list, second_rows, first_cols, out, width, base, places):
    far, own = far_list.shape
    both = 2 * width
    start_leaf = lax.axis_index(AXES) * own
    square = iota((both, both), 0) // width == iota((both, both), 1) // width
    lane = iota((far * width, both), 1) < width
    exponents = []
    for index in pairs:
        t = 2 * index
        picked = []
        for m in range(2):
            spots = [
                pl.multiple_of((far_list[f, t + m] - start_leaf + base) * width, width)
                for f in range(far)
            ]
            picked.append(
                jnp.concatenate([second_rows[pl.ds(spot, width), :] for spot in spots], axis=0)
            )
        cols = first_cols[:, t * width : t * width + both]
        targets = jnp.where(
            square, jnp.concatenate([cols, cols], axis=0), jnp.zeros((both, both), BF16)
        )
        exponents.append(mm(jnp.where(lane, picked[0], picked[1]), targets))
    for place, exponent in zip(places, exponents):
        high, low = split2(gaussians(exponent))
        at = place * far * width
        out[at : at + far * width, 0:both] = high
        out[at : at + far * width, both : 2 * both] = low


def first_chunk_kernel(layers):
    def body(
        points, near_list, near_used, vectors,
        out, first_rows, first_cols, second_cols, second_rows, switches, place,
    ):
        prepare(
            points,
            near_list,
            near_used,
            first_rows,
            first_cols,
            second_cols,
            second_rows,
            switches,
            place,
        )
        halo = LAYER * points.shape[1] // near_list.shape[1]
        inner_layers(layers, vectors, first_rows, second_cols, switches, out, halo)

    return body


def chunk_kernel(layers, pairs, halo, width):
    def body(after, far_in, *refs):
        first_rows, second_cols, switches, vectors, first_cols, second_rows = refs[:6]
        outs, far_list, sem = refs[6:-2], refs[-2], refs[-1]
        if pairs:
            copy = pltpu.make_async_copy(far_in, far_list, sem)
            copy.start()
        if layers:
            inner_layers(layers, vectors, first_rows, second_cols, switches, outs[0], halo)
        if pairs:
            copy.wait()
            far_blocks(
                pairs, far_list, second_rows, first_cols, outs[-1], width, 0, range(len(pairs))
            )

    return body


def edges_kernel(
    after, inner, outer, first_rows, second_cols, switches, vectors,
    out, halo_rows, ends, sides, place, halo_cols, sems,
):
    halo = ends.shape[1]
    width = halo // LAYER
    own = vectors.shape[0] // width
    layers = own // LAYER
    extra = sides.shape[1]
    odd = lax.axis_index("sub") % 2
    arrived = ((inner, 1 - odd), (outer, odd))
    side_copies = [
        pltpu.make_async_copy(
            block.at[pl.ds(halo + width, extra), :], sides.at[side], sems.at[n]
        )
        for n, (block, side) in enumerate(arrived)
    ]
    end_copies = [
        pltpu.make_async_copy(block.at[pl.ds(0, halo), :], ends.at[side], sems.at[2 + n])
        for n, (block, side) in enumerate(arrived)
    ]
    for copy in side_copies + end_copies:
        copy.start()
    lanes = PAD * width
    place[...] = jnp.zeros(place.shape, F32)
    for copy in side_copies:
        copy.wait()
    for side, first_leaf in enumerate((-PAD, own)):
        for n in range(2):
            values = sides[side, 16 * n : 16 * n + 16, 0:halo].astype(F32)
            place[0:3, n * halo : (n + 1) * halo] = values[0:3, :] + values[8:11, :]
        leaf = iota((8, lanes), 1) // width + (first_leaf + PAD)
        second = features(place[...], leaf, layers // 2 + PAD // LAYER)[1]
        halo_cols[side, :, :] = second.astype(BF16)
        halo_rows[side * lanes : (side + 1) * lanes, :] = rows_of(second)
    weights = [
        near_weights(
            first_rows, jnp.concatenate(columns, axis=1), switches, index, halo
        )
        for index, columns in (
            (0, [halo_cols[0, :, halo:], second_cols[:, 0 : 2 * halo]]),
            (layers - 1, [second_cols[:, (layers - 2) * halo :], halo_cols[1, :, 0:halo]]),
        )
    ]
    for copy in end_copies:
        copy.wait()
    value = mm(weights[0][:, 0:halo], ends[0, :, :])
    value = value + mm(weights[0][:, halo:], vectors[0 : 2 * halo, :])
    out[0:halo, :] = value.astype(BF16)
    value = mm(weights[1][:, 0 : 2 * halo], vectors[(layers - 2) * halo :, :])
    value = value + mm(weights[1][:, 2 * halo :], ends[1, :, :])
    out[halo:, :] = value.astype(BF16)


def last_chunk_kernel(layers, pairs):
    def body(
        after, far_in, inner, outer, first_rows, second_cols, switches, vectors,
        first_cols, own_rows, halo_rows, basis, top,
        out, blocks, grams, far_list, sides, second_rows, sems,
    ):
        width = basis.shape[0]
        own = basis.shape[1] // width
        total = own + 2 * PAD
        halo = LAYER * width
        both = 2 * width
        odd = lax.axis_index("sub") % 2
        side_copies = [
            pltpu.make_async_copy(block.at[pl.ds(halo, width), :], sides.at[side], sems.at[n])
            for n, (block, side) in enumerate(((inner, 1 - odd), (outer, odd)))
        ]
        list_copy = pltpu.make_async_copy(far_in, far_list, sems.at[2])
        for copy in side_copies + [list_copy]:
            copy.start()
        lanes = PAD * width
        second_rows[0:lanes, :] = halo_rows[0:lanes, :]
        second_rows[lanes : lanes + own * width, :] = own_rows[...]
        second_rows[lanes + own * width :, :] = halo_rows[lanes:, :]
        inner_layers(layers, vectors, first_rows, second_cols, switches, out, halo)

        lane = iota((width, both), 1)
        for n in range(own // 2):
            pair = basis[:, n * both : (n + 1) * both]
            zero = jnp.zeros_like(pair)
            stacked = jnp.concatenate(
                [jnp.where(lane < width, pair, zero), jnp.where(lane < width, zero, pair)], axis=0
            )
            value = mm_nt(stacked, pair)
            for m in range(2):
                at = (PAD + 2 * n + m) * STRIDE
                grams[at : at + width // 2, :] = fold(value[m * width : (m + 1) * width])
        for spot in (0, LAYER, total - LAYER - 1, total - 1):
            grams[spot * STRIDE : spot * STRIDE + width // 2, :] = top[...]
        for copy in side_copies + [list_copy]:
            copy.wait()
        for side, spots in enumerate(
            ((1, 2, 3, 5, 6, 7), tuple(PAD + own + m for m in (0, 1, 2, 4, 5, 6)))
        ):
            for n, spot in enumerate(spots):
                piece = sides[side, 0:width, n * width : (n + 1) * width]
                at = spot * STRIDE
                grams[at : at + width // 2, :] = fold(mm_nt(piece, piece))
        far_blocks(
            pairs, far_list, second_rows, first_cols, blocks, width, PAD, range(len(pairs))
        )

    return body


def leaves_kernel(chunks, members, groups, *refs):
    outer_count = len(chunks) + 1
    near_parts = refs[:outer_count]
    (
        grams,
        upper,
        transfer,
        near,
        high,
        low,
        device_factor,
        group_factor,
        root_factor,
        work,
        factors,
        sems,
    ) = refs[outer_count:]
    width = transfer.shape[0]
    total = high.shape[0] // width
    own = total - 2 * PAD
    halo = LAYER * width
    layers = own // LAYER
    both = 2 * width
    places = [(part, 0, chunk[0], len(chunk)) for part, chunk in zip(near_parts, chunks)]
    places += [(near_parts[-1], n, index, 1) for n, index in enumerate((0, layers - 1))]
    near_copies = [
        pltpu.make_async_copy(
            part.at[pl.ds(start * halo, many * halo), :],
            near.at[pl.ds(index * halo, many * halo), :],
            sems.at[n],
        )
        for n, (part, start, index, many) in enumerate(places)
    ]
    for copy in near_copies:
        copy.start()

    spare = (LAYER, total - LAYER - 1)
    means = (
        upper[0 : width // 2, :] * (1.0 / members),
        upper[width // 2 :, :] * (1.0 / (members * groups)),
    )
    spot_row = iota((total, both), 0)
    for i in range(width // 2):
        rows = grams[pl.ds(i, total, stride=STRIDE), :]
        for spot, mean in zip(spare, means):
            rows = jnp.where(spot_row == spot, mean[i : i + 1, :], rows)
        turned = rows.T
        work[i, :, 0:total] = turned[0:width]
        work[i + width // 2, :, 0:total] = turned[width:]
    factor_lanes(work, width)
    from_lanes(work, factors, width, total)
    device_factor[...] = exact(unfold(factors[0 : width // 2, :]), transfer[...])
    for target, spot in zip((group_factor, root_factor), spare):
        target[...] = unfold(factors[spot * STRIDE : spot * STRIDE + width // 2, :])
    left_lanes = iota((width // 2, both), 1) < width
    for spot in range(total):
        rows = factors[spot * STRIDE : spot * STRIDE + width // 2, :]
        turned = pltpu.roll(rows, width, 1)
        twice = jnp.concatenate(
            [jnp.where(left_lanes, rows, turned), jnp.where(left_lanes, turned, rows)], axis=0
        )
        at = slice(spot * width, (spot + 1) * width)
        high[at, :], low[at, :] = split2(twice)
    for copy in near_copies:
        copy.wait()


def far_kernel(plan, far_in, high, low, *refs):
    blocks, (coupling, far_list, lines, sem, sems) = refs[:-5], refs[-5:]
    copy = pltpu.make_async_copy(far_in, far_list, sem)
    copy.start()
    width = coupling.shape[0]
    far, own = far_list.shape
    both = 2 * width
    start_leaf = lax.axis_index(AXES) * own
    square = iota((both, both), 0) // width == iota((both, both), 1) // width
    lane = iota((width, both), 1) < width
    zero = jnp.zeros((both, both), BF16)

    def diagonal(value):
        return jnp.where(square, value, zero)

    copies = []
    for start in range(0, own // 2, 4):
        indices = range(start, start + 4)
        halves = []
        for index in indices:
            source, place = plan[index]
            at = place * far * width
            kh = blocks[source][at : at + far * width, 0:both]
            kl = blocks[source][at : at + far * width, both : 2 * both]
            at = (PAD + 2 * index) * width
            rh = diagonal(high[at : at + both, :])
            rl = diagonal(low[at : at + both, :])
            halves.append(
                mm_nt(
                    jnp.concatenate([kh, kl, kh], axis=1), jnp.concatenate([rh, rh, rl], axis=1)
                )
            )
        if start == 0:
            copy.wait()
        outs = []
        for index, half in zip(indices, halves):
            zh, zl = split2(half * (1.0 / width))
            for f in range(far):
                spots = [
                    pl.multiple_of((far_list[f, 2 * index + m] - start_leaf + PAD) * width, width)
                    for m in range(2)
                ]
                sh, sl = (
                    jnp.where(lane, *(part[pl.ds(spot, width), :] for spot in spots))
                    for part in (high, low)
                )
                a = slice(f * width, (f + 1) * width)
                ph = diagonal(jnp.concatenate([zh[a], zh[a]], axis=0))
                plow = diagonal(jnp.concatenate([zl[a], zl[a]], axis=0))
                outs.append(
                    mm(
                        jnp.concatenate([sh, sh, sl], axis=1),
                        jnp.concatenate([ph, plow, ph], axis=0),
                    )
                )
        for n, index in enumerate(indices):
            three = outs[n * far : (n + 1) * far]
            line = jnp.concatenate(
                [out[:, 0:width] for out in three] + [out[:, width:both] for out in three], axis=1
            )
            at = index * 2 * far * width
            lines[:, at : at + 2 * far * width] = line.astype(BF16)
        group = pl.ds(start * 2 * far * width, 8 * far * width)
        copies.append(
            pltpu.make_async_copy(lines.at[:, group], coupling.at[:, group], sems.at[start // 4])
        )
        copies[-1].start()
    for copy in copies:
        copy.wait()


def swap_inner(block):
    return lax.ppermute(block, AXES, [(i, i ^ 1) for i in range(lax.axis_size(AXES))])


def swap_outer(block):
    many = lax.axis_size(AXES)
    return lax.ppermute(block, AXES, [(i, (i + 1 if i % 2 else i - 1) % many) for i in range(many)])


def exchange(value, distance):
    pairs = [(i, i ^ distance ^ 1) for i in range(lax.axis_size(AXES))]
    return value + lax.ppermute(value, AXES, pairs)


def per_device(
    points, leaf_basis, inner_transfer, device_transfer, vectors, near_index, near_count, far_index
):
    own = near_index.shape[0]
    width = leaf_basis.shape[1]
    columns = vectors.shape[1]
    halo = LAYER * width
    half = width // 2
    layers = own // LAYER
    total = own + 2 * PAD
    members, groups = lax.axis_size("sub"), lax.axis_size("group")
    vmem = pl.BlockSpec(memory_space=pltpu.VMEM)
    hbm = pl.BlockSpec(memory_space=pl.ANY)
    square = jax.ShapeDtypeStruct((width, width), F32)
    extra = halo + width + 32

    def block_of(rows):
        return jax.ShapeDtypeStruct((rows, columns), BF16)

    basis = leaf_basis.T
    near_list, far_list = near_index.T, far_index.T
    cost = pl.CostEstimate(flops=10**9, bytes_accessed=4 * 10**6, transcendentals=10**6)

    dense, top, to_outer, to_inner = pl.pallas_call(
        tree_kernel,
        out_shape=(
            jax.ShapeDtypeStruct((half, 2 * width), F32),
            jax.ShapeDtypeStruct((half, 2 * width), F32),
            block_of(extra),
            block_of(extra + half),
        ),
        in_specs=[hbm] * 5,
        out_specs=(hbm,) * 4,
        scratch_shapes=[
            pltpu.VMEM((3, own * width), F32),
            pltpu.VMEM((width, own * width), BF16),
            pltpu.VMEM((width, (own - 2) * width), BF16),
            pltpu.VMEM((width, width), F32),
            pltpu.VMEM((2, halo, columns), BF16),
            pltpu.VMEM((2, width + 32, columns), BF16),
            pltpu.VMEM((half, columns), BF16),
            pltpu.VMEM((2, half, 2 * width), F32),
            pltpu.SemaphoreType.DMA((13,)),
        ],
        compiler_params=room(60),
        name="tree",
    )(points, basis, inner_transfer.T, device_transfer, vectors)
    from_inner = swap_inner(to_inner)

    sub_bits = members.bit_length() - 1
    steps = [members << bit for bit in range(groups.bit_length() - 1)]
    steps += [1 << bit for bit in range(1, sub_bits)]
    inner_pairs = list(range(PAD // 2, (own - PAD) // 2))
    few = len(inner_pairs) // 2
    edge_pairs = [index for index in range(own // 2) if index not in inner_pairs]
    chunks = [[1, 2], [3, 4], [5], [6]]
    pair_chunks = [[], inner_pairs[:few], inner_pairs[few:], edge_pairs]
    blocks, plan, parts = [], {}, []

    def part_shape(count):
        return jax.ShapeDtypeStruct((count * halo, columns), BF16)

    def block_shape(count):
        return jax.ShapeDtypeStruct((count * far_index.shape[1] * width, 4 * width), BF16)

    late_points, dense = lax.optimization_barrier((points, dense))
    part, *shared = pl.pallas_call(
        first_chunk_kernel(chunks[0]),
        out_shape=(
            part_shape(len(chunks[0])),
            jax.ShapeDtypeStruct((own * width, 64), BF16),
            jax.ShapeDtypeStruct((64, own * width), BF16),
            jax.ShapeDtypeStruct((48, own * width), BF16),
            jax.ShapeDtypeStruct((own * width, 128), BF16),
            jax.ShapeDtypeStruct((own, 3 * halo), BF16),
        ),
        in_specs=[vmem] * 4,
        out_specs=(vmem,) * 6,
        scratch_shapes=[pltpu.VMEM((8, own * width), F32)],
        compiler_params=room(10),
        cost_estimate=cost,
        name="chunk_0",
    )(late_points, near_list, near_count.reshape(1, own), vectors)
    parts.append(part)
    summands = [
        from_inner[extra:, n * 2 * width : (n + 1) * 2 * width].astype(F32) for n in range(3)
    ]
    pair_gram = gram = dense + (summands[0] + (summands[1] + summands[2]))
    gram, parts[0], to_outer = lax.optimization_barrier((gram, parts[0], to_outer))
    from_outer = swap_outer(to_outer)
    first_rows, first_cols, second_cols, second_rows, switches = shared
    jobs = [1, 2, "edges", 3]
    for n in range(max(len(steps), len(jobs))):
        before = gram
        if n < len(steps):
            if n == len(steps) - sub_bits + 1:
                gram = before = jnp.concatenate([pair_gram, gram], axis=0)
            gram = exchange(gram, steps[n])
        job = jobs[n] if n < len(jobs) else None
        if job in (1, 2):
            layer_chunk, pair_chunk = chunks[job], pair_chunks[job]
            shapes = [part_shape(len(layer_chunk))] * bool(layer_chunk)
            shapes += [block_shape(len(pair_chunk))] * bool(pair_chunk)
            outs = pl.pallas_call(
                chunk_kernel(layer_chunk, pair_chunk, halo, width),
                out_shape=tuple(shapes),
                in_specs=[hbm] * 2 + [vmem] * 6,
                out_specs=(vmem,) * len(shapes),
                scratch_shapes=[
                    pltpu.SMEM(far_list.shape, jnp.int32),
                    pltpu.SemaphoreType.DMA,
                ],
                compiler_params=room(10),
                cost_estimate=cost,
                name=f"chunk_{job}",
            )(before, far_list, first_rows, second_cols, switches, vectors, first_cols, second_rows)
            gram, outs = lax.optimization_barrier((gram, outs))
            if layer_chunk:
                parts.append(outs[0])
            if pair_chunk:
                plan.update((index, (len(blocks), m)) for m, index in enumerate(pair_chunk))
                blocks.append(outs[-1])
        elif job == "edges":
            edge_part, halo_rows = pl.pallas_call(
                edges_kernel,
                out_shape=(
                    part_shape(2),
                    jax.ShapeDtypeStruct((2 * PAD * width, 2 * width), BF16),
                ),
                in_specs=[hbm] * 3 + [vmem] * 4,
                out_specs=(vmem,) * 2,
                scratch_shapes=[
                    pltpu.VMEM((2, halo, columns), BF16),
                    pltpu.VMEM((2, 32, columns), BF16),
                    pltpu.VMEM((8, PAD * width), F32),
                    pltpu.VMEM((2, 48, PAD * width), BF16),
                    pltpu.SemaphoreType.DMA((4,)),
                ],
                compiler_params=room(10),
                cost_estimate=cost,
                name="edges",
            )(before, from_inner, from_outer, first_rows, second_cols, switches, vectors)
            gram, edge_part = lax.optimization_barrier((gram, edge_part))
        elif job == 3:
            part, edge_blocks, grams = pl.pallas_call(
                last_chunk_kernel(chunks[3], edge_pairs),
                out_shape=(
                    part_shape(len(chunks[3])),
                    block_shape(len(edge_pairs)),
                    jax.ShapeDtypeStruct((total * STRIDE, 2 * width), F32),
                ),
                in_specs=[hbm] * 4 + [vmem] * 9,
                out_specs=(vmem,) * 3,
                scratch_shapes=[
                    pltpu.SMEM(far_list.shape, jnp.int32),
                    pltpu.VMEM((2, width, columns), BF16),
                    pltpu.VMEM((total * width, 2 * width), BF16),
                    pltpu.SemaphoreType.DMA((3,)),
                ],
                compiler_params=room(14),
                cost_estimate=cost,
                name="chunk_3",
            )(
                before,
                far_list,
                from_inner,
                from_outer,
                first_rows,
                second_cols,
                switches,
                vectors,
                first_cols,
                second_rows,
                halo_rows,
                basis,
                top,
            )
            gram, part = lax.optimization_barrier((gram, part))
            parts.append(part)
            plan.update((index, (len(blocks), m)) for m, index in enumerate(edge_pairs))
            blocks.append(edge_blocks)

    split_factors = jax.ShapeDtypeStruct((total * width, 2 * width), BF16)
    near, high, low, device_factor, group_factor, root_factor = pl.pallas_call(
        functools.partial(leaves_kernel, chunks, members, groups),
        out_shape=(
            jax.ShapeDtypeStruct(vectors.shape, BF16),
            split_factors,
            split_factors,
            square,
            square,
            square,
        ),
        in_specs=[hbm] * (len(parts) + 1) + [vmem] * 3,
        out_specs=(hbm,) + (vmem,) * 5,
        scratch_shapes=[
            pltpu.VMEM((width, width, 128), F32),
            pltpu.VMEM((total * STRIDE, 2 * width), F32),
            pltpu.SemaphoreType.DMA((2 + len(parts),)),
        ],
        compiler_params=room(20),
        name="leaves",
    )(*parts, edge_part, grams, gram, device_transfer)

    coupling = pl.pallas_call(
        functools.partial(far_kernel, plan),
        out_shape=jax.ShapeDtypeStruct((width, own * far_index.shape[1] * width), BF16),
        in_specs=[hbm] + [vmem] * (2 + len(blocks)),
        out_specs=hbm,
        scratch_shapes=[
            pltpu.SMEM(far_list.shape, jnp.int32),
            pltpu.VMEM((width, own * far_index.shape[1] * width), BF16),
            pltpu.SemaphoreType.DMA,
            pltpu.SemaphoreType.DMA((own // 8,)),
        ],
        compiler_params=room(16),
        name="far",
    )(far_list, high, low, *blocks)
    return near, coupling.T, device_factor, group_factor, root_factor


def solution(mesh):
    split = P(AXES, None)
    return jax.shard_map(
        per_device,
        mesh=mesh,
        in_specs=(P(None, AXES), split, split, split, split, split, P(AXES), split),
        out_specs=(split, split, split, split, split),
        check_vma=False,
    )
```

```python
import functools
import math

import jax
import jax.numpy as jnp
from jax import lax
from jax.experimental import pallas as pl
from jax.experimental.pallas import tpu as pltpu
from jax.sharding import PartitionSpec as P

LAYER = 4
PAD = 8
LONG_SQ = 2.25
RATIO = 25.0
SCALE = 0.5 / LONG_SQ
HALF = math.log(0.5)
OFF = -16384.0
STRIDE = 40
AXES = ("group", "sub")
F32 = jnp.float32
BF16 = jnp.bfloat16


def room(megabytes):
    return pltpu.CompilerParams(vmem_limit_bytes=int(megabytes * 1024 * 1024))


def split2(value):
    high = value.astype(BF16)
    return high, (value - high.astype(F32)).astype(BF16)


def split3(value):
    high = value.astype(BF16)
    rest = value - high.astype(F32)
    middle = rest.astype(BF16)
    return high, middle, (rest - middle.astype(F32)).astype(BF16)


def mm(left, right):
    return jnp.dot(left, right, preferred_element_type=F32)


def mm_nt(left, right):
    return lax.dot_general(left, right, (((1,), (1,)), ((), ())), preferred_element_type=F32)


def exact(left, right):
    return jnp.dot(left, right, precision=lax.Precision.HIGHEST, preferred_element_type=F32)


def iota(shape, dim):
    return lax.broadcasted_iota(jnp.int32, shape, dim)


def tree_kernel(
    points_in, basis_in, below_in, transfer_in, vectors,
    dense, top, outer, inner, points, basis, below, transfer, passing, packed, staged, small, sems,
):
    width = basis.shape[0]
    count = basis.shape[1] // width
    halo = LAYER * width
    span = PAD * width
    rows = vectors.shape[0]
    odd = lax.axis_index("sub") % 2
    sides = ((outer, odd), (inner, 1 - odd))
    basis_copy, below_copy, points_copy, transfer_copy = loads = [
        pltpu.make_async_copy(source, target, sems.at[n])
        for n, (source, target) in enumerate(
            (
                (basis_in, basis),
                (below_in, below),
                (points_in, points),
                (transfer_in, transfer),
            )
        )
    ]
    vector_loads = [
        pltpu.make_async_copy(
            vectors.at[pl.ds(pl.multiple_of(last * (rows - halo), 16), halo), :],
            passing.at[n],
            sems.at[4 + n],
        )
        for n, (_, last) in enumerate(sides)
    ]
    copies = [
        pltpu.make_async_copy(passing.at[n], target.at[pl.ds(0, halo), :], sems.at[9 + n])
        for n, (target, _) in enumerate(sides)
    ]
    for copy in loads + vector_loads:
        copy.start()

    both = 2 * width
    lane = iota((width, 2 * both), 1)

    def times(above, columns):
        found = []
        for n in range(above.shape[1] // both):
            parts = jnp.concatenate(split3(above[:, n * both : (n + 1) * both]), axis=1)
            block = columns(n * 2 * both)
            zero = jnp.zeros_like(block)
            block = jnp.concatenate(
                [jnp.where(lane < both, block, zero), jnp.where(lane < both, zero, block)], axis=0
            )
            found.append(mm(parts, jnp.concatenate([block] * 3, axis=0)))
        return jnp.concatenate(found, axis=1)

    same = iota((both, both), 0) // width == iota((both, both), 1) // width
    half_block = jnp.where(same, 0.5, 0.0).astype(F32)
    basis_copy.wait()
    points_copy.wait()
    for n, (target, last) in enumerate(sides):
        bases = basis[:, count * width - span :], basis[:, 0:span]
        last_three, first_three = (
            jnp.concatenate(
                [block[:, (at + skip) * width : (at + skip + 3) * width] for at in (0, LAYER)],
                axis=1,
            )
            for skip, block in zip((1, 0), bases)
        )
        packed[n, 0:width, :] = jnp.where(last == 1, last_three, first_three)
        coords = jnp.where(last == 1, points[:, count * width - span :], points[:, 0:span])
        for m in range(2):
            high, low = split2(coords[:, m * halo : (m + 1) * halo])
            base = width + 16 * m
            packed[n, base : base + 16, :] = jnp.zeros((16, target.shape[1]), BF16)
            packed[n, base : base + 3, 0:halo] = high
            packed[n, base + 8 : base + 11, 0:halo] = low
        copies.append(
            pltpu.make_async_copy(
                packed.at[n], target.at[pl.ds(halo, width + 32), :], sems.at[6 + n]
            )
        )
        copies[-1].start()
    blocks = []
    for n in range(count // 4):
        stacked = jnp.concatenate(
            [basis[:, (2 * n + m) * both : (2 * n + m + 1) * both] for m in range(2)], axis=0
        )
        blocks.append(mm_nt(stacked, stacked) * half_block)
    below_copy.wait()
    for load, copy in zip(vector_loads, copies[:2]):
        load.wait()
        copy.start()
    halves = []
    for n, block in enumerate(blocks):
        t = below[:, n * both : (n + 1) * both]
        half = mm(jnp.concatenate([t, t, t], axis=1), jnp.concatenate(split3(block), axis=0))
        halves.append((half, t))
    blocks = []
    for n in range(0, len(halves), 2):
        (first, t), (second, u) = halves[n : n + 2]
        x = jnp.concatenate(split3(jnp.concatenate([first, second], axis=0)), axis=1)
        t = jnp.concatenate([t, u], axis=0)
        blocks.append(mm_nt(x, jnp.concatenate([t, t, t], axis=1)) * half_block)

    transfer_copy.wait()
    end = below.shape[1]
    tops = below[:, end - both : end]
    turned = jnp.concatenate(split3(transfer[...].T), axis=1)
    above = jnp.concatenate(
        [tops.astype(F32), mm(turned, jnp.concatenate([tops] * 3, axis=0))], axis=0
    )
    end -= both
    nodes = 4
    while nodes < count // 2:
        start = end - nodes * width
        above = times(above, lambda at, start=start: below[:, start + at : start + at + 2 * both])
        end = start
        nodes *= 2

    total = jnp.zeros((both, both), F32)
    for n, block in enumerate(blocks):
        rows = above[:, n * both : (n + 1) * both]
        high, middle, low = split3(rows)
        gh, gm, gl = split3(block)
        x = mm(
            jnp.concatenate([high, high, high, middle, middle, low], axis=1),
            jnp.concatenate([gh, gm, gl, gh, gm, gh], axis=0),
        )
        xh, xm, xl = split3(x)
        total = total + mm_nt(
            jnp.concatenate([xh, xh, xh, xm, xm, xl], axis=1),
            jnp.concatenate([high, middle, low, high, middle, high], axis=1),
        )
    total = total * (4.0 / count)
    small[0, :, :] = fold(total[:width, :width])
    halves = fold(total[width:, width:])
    small[1, :, :] = halves
    staged[...] = jnp.concatenate(split3(halves), axis=1)
    copies.append(
        pltpu.make_async_copy(
            staged, inner.at[pl.ds(halo + width + 32, width // 2), :], sems.at[8]
        )
    )
    copies[-1].start()
    for n, target in enumerate((top, dense)):
        copies.append(pltpu.make_async_copy(small.at[n], target, sems.at[11 + n]))
        copies[-1].start()
    for copy in copies:
        copy.wait()


def factor_lanes(work, width):
    panels = width // 8
    row = iota((8, 128), 0)

    def spread(j, i):
        return jnp.broadcast_to(work[j, i : i + 1, :], (8, 128))

    for p in range(panels):
        at = 8 * p
        entry = {(k, m): spread(at + k, at + m) for k in range(8) for m in range(k, 8)}
        scales = []
        for k in range(8):
            scales.append(lax.rsqrt(entry[k, k]))
            for m in range(k + 1, 8):
                entry[k, m] = entry[k, m] * scales[k]
            for m in range(k + 1, 8):
                for q in range(m, 8):
                    entry[m, q] = entry[m, q] - entry[k, m] * entry[k, q]
        for i in range(p, panels):
            tile = [work[at + k, 8 * i : 8 * i + 8, :] for k in range(8)]
            for k in range(8):
                tile[k] = tile[k] * scales[k]
                for m in range(k + 1, 8):
                    tile[m] = tile[m] - tile[k] * entry[k, m]
            for k in range(8):
                work[at + k, 8 * i : 8 * i + 8, :] = (
                    jnp.where(row >= k, tile[k], 0.0) if i == p else tile[k]
                )
        for q in range(p + 1, panels):
            for start in range(q, panels, 4):
                group = range(start, min(start + 4, panels))
                accs = {
                    (i, k): work[8 * q + k, 8 * i : 8 * i + 8, :] for i in group for k in range(8)
                }
                for j in range(at, at + 8):
                    factors = [spread(j, 8 * q + k) for k in range(8)]
                    for i in group:
                        column = work[j, 8 * i : 8 * i + 8, :]
                        for k in range(8):
                            accs[i, k] = accs[i, k] - column * factors[k]
                for (i, k), value in accs.items():
                    work[8 * q + k, 8 * i : 8 * i + 8, :] = value


def fold(matrix):
    half = matrix.shape[0] // 2
    return jnp.concatenate([matrix[:half], matrix[half:]], axis=1)


def unfold(matrix):
    half = matrix.shape[1] // 2
    return jnp.concatenate([matrix[:, :half], matrix[:, half:]], axis=0)


def from_lanes(work, factors, width, many):
    for i in range(width // 2):
        both = []
        for j in (i, i + width // 2):
            skip = j // 8 * 8
            both += [jnp.zeros((skip, many), F32)] * bool(skip) + [work[j, skip:, 0:many]]
        factors[pl.ds(i, many, stride=STRIDE), :] = jnp.concatenate(both, axis=0).T


def gaussians(exponent):
    return jnp.exp(exponent) + jnp.exp(exponent * RATIO - RATIO * HALF)


def features(place, leaf, center):
    sub = iota(place.shape, 0)
    corner = jnp.where(sub == 0, leaf % 2 - 1, leaf // 2 % 2 - 1)
    corner = jnp.where(sub == 2, leaf // LAYER - center, corner)
    place = jnp.where(sub < 3, place + corner.astype(F32), 0.0)
    norm = jnp.sum(place * place, axis=0, keepdims=True) * SCALE
    first = jnp.where(sub == 3, -norm, jnp.where(sub == 4, 1.0, place))
    second = jnp.where(
        sub == 3, 1.0, jnp.where(sub == 4, HALF - norm, place * (2.0 * SCALE))
    )
    fh, fm, fl = [v.astype(F32) for v in split3(first)]
    sh, sm, sl = [v.astype(F32) for v in split3(second)]
    return (
        jnp.concatenate([fh, fh, fh, fm, fm, fl], axis=0),
        jnp.concatenate([sh, sm, sl, sh, sm, sh], axis=0),
    )


def rows_of(second):
    blank = jnp.zeros((16, second.shape[1]), F32)
    return jnp.concatenate([second, blank, second, blank], axis=0).T.astype(BF16)


def near_weights(first_rows, second, switches, index, halo):
    group = index // 4 * 16
    columns = jnp.concatenate([second, switches[group : group + 16, :]], axis=0)
    return gaussians(mm(first_rows[index * halo : (index + 1) * halo, :], columns)).astype(BF16)


def prepare(
    points, near_list, near_used, first_rows, first_cols, second_cols, second_rows, switches, place
):
    rows = points.shape[1]
    own = near_list.shape[1]
    width = rows // own
    place[...] = jnp.zeros(place.shape, F32)
    place[0:3, :] = points[...]
    leaf = iota((8, rows), 1) // width
    first, second = features(place[...], leaf, own // LAYER // 2)
    hot_leaf = iota((16, rows), 1) // width
    hot = jnp.where(hot_leaf % 16 == iota((16, rows), 0), 1.0, 0.0).astype(F32)
    first = jnp.concatenate([first, hot], axis=0)
    first_cols[...] = first.astype(BF16)
    second_cols[...] = second.astype(BF16)
    first_rows[...] = first.T.astype(BF16)
    second_rows[...] = rows_of(second)

    start_leaf = lax.axis_index(AXES) * own
    target = iota((1, own), 1)
    base_leaf = start_leaf + target // LAYER * LAYER - LAYER
    found = jnp.zeros((16, own), jnp.bool_)
    place_row = iota((16, own), 0)
    for n in range(near_list.shape[0]):
        spot = jnp.where(near_used[...] > n, near_list[n : n + 1, :] - base_leaf, -1)
        found = jnp.logical_or(found, place_row == spot)
    bias = jnp.where(found, 0.0, OFF).astype(F32)
    span = 3 * LAYER * width
    expand = jnp.where(iota((16, span), 0) == iota((16, span), 1) // width, 1.0, 0.0)
    switches[...] = mm(bias.T.astype(BF16), expand.astype(BF16)).astype(BF16)


def inner_layers(layers, vectors, first_rows, second_cols, switches, out, halo):
    for n, index in enumerate(layers):
        around = slice((index - 1) * halo, (index + 2) * halo)
        weights = near_weights(first_rows, second_cols[:, around], switches, index, halo)
        out[n * halo : (n + 1) * halo, :] = mm(weights, vectors[around, :]).astype(BF16)


def far_blocks(pairs, far_list, second_rows, first_cols, out, width, base, places):
    far, own = far_list.shape
    both = 2 * width
    start_leaf = lax.axis_index(AXES) * own
    square = iota((both, both), 0) // width == iota((both, both), 1) // width
    lane = iota((far * width, both), 1) < width
    exponents = []
    for index in pairs:
        t = 2 * index
        picked = []
        for m in range(2):
            spots = [
                pl.multiple_of((far_list[f, t + m] - start_leaf + base) * width, width)
                for f in range(far)
            ]
            picked.append(
                jnp.concatenate([second_rows[pl.ds(spot, width), :] for spot in spots], axis=0)
            )
        cols = first_cols[:, t * width : t * width + both]
        targets = jnp.where(
            square, jnp.concatenate([cols, cols], axis=0), jnp.zeros((both, both), BF16)
        )
        exponents.append(mm(jnp.where(lane, picked[0], picked[1]), targets))
    for place, exponent in zip(places, exponents):
        high, low = split2(gaussians(exponent))
        at = place * far * width
        out[at : at + far * width, 0:both] = high
        out[at : at + far * width, both : 2 * both] = low


def first_chunk_kernel(layers):
    def body(
        points, near_list, near_used, vectors,
        out, first_rows, first_cols, second_cols, second_rows, switches, place,
    ):
        prepare(
            points,
            near_list,
            near_used,
            first_rows,
            first_cols,
            second_cols,
            second_rows,
            switches,
            place,
        )
        halo = LAYER * points.shape[1] // near_list.shape[1]
        inner_layers(layers, vectors, first_rows, second_cols, switches, out, halo)

    return body


def chunk_kernel(layers, pairs, halo, width):
    def body(after, far_in, *refs):
        first_rows, second_cols, switches, vectors, first_cols, second_rows = refs[:6]
        outs, far_list, sem = refs[6:-2], refs[-2], refs[-1]
        if pairs:
            copy = pltpu.make_async_copy(far_in, far_list, sem)
            copy.start()
        if layers:
            inner_layers(layers, vectors, first_rows, second_cols, switches, outs[0], halo)
        if pairs:
            copy.wait()
            far_blocks(
                pairs, far_list, second_rows, first_cols, outs[-1], width, 0, range(len(pairs))
            )

    return body


def edges_kernel(
    pairs, after, far_in, inner, outer, first_rows, second_cols, switches, vectors,
    first_cols, own_rows, top,
    out, blocks, grams, ends, sides, place, halo_cols, far_list, second_rows, sems,
):
    halo = ends.shape[1]
    width = halo // LAYER
    own = vectors.shape[0] // width
    layers = own // LAYER
    extra = sides.shape[1]
    odd = lax.axis_index("sub") % 2
    arrived = ((inner, 1 - odd), (outer, odd))
    side_copies = [
        pltpu.make_async_copy(
            block.at[pl.ds(halo, extra), :], sides.at[side], sems.at[n]
        )
        for n, (block, side) in enumerate(arrived)
    ]
    end_copies = [
        pltpu.make_async_copy(block.at[pl.ds(0, halo), :], ends.at[side], sems.at[2 + n])
        for n, (block, side) in enumerate(arrived)
    ]
    list_copy = pltpu.make_async_copy(far_in, far_list, sems.at[4])
    for copy in side_copies + end_copies + [list_copy]:
        copy.start()
    lanes = PAD * width
    second_rows[lanes : lanes + own * width, :] = own_rows[...]
    place[...] = jnp.zeros(place.shape, F32)
    for copy in side_copies:
        copy.wait()
    for side, first_leaf in enumerate((-PAD, own)):
        for n in range(2):
            base = width + 16 * n
            values = sides[side, base : base + 16, 0:halo].astype(F32)
            place[0:3, n * halo : (n + 1) * halo] = values[0:3, :] + values[8:11, :]
        leaf = iota((8, lanes), 1) // width + (first_leaf + PAD)
        second = features(place[...], leaf, layers // 2 + PAD // LAYER)[1]
        halo_cols[side, :, :] = second.astype(BF16)
        at = (PAD + first_leaf) * width
        second_rows[at : at + lanes, :] = rows_of(second)
        for n in range(6):
            piece = sides[side, 0:width, n * width : (n + 1) * width]
            at = (6 * side + n) * STRIDE
            grams[at : at + width // 2, :] = fold(mm_nt(piece, piece))
    for n in range(12, 16):
        grams[n * STRIDE : n * STRIDE + width // 2, :] = top[...]
    weights = [
        near_weights(
            first_rows, jnp.concatenate(columns, axis=1), switches, index, halo
        )
        for index, columns in (
            (0, [halo_cols[0, :, halo:], second_cols[:, 0 : 2 * halo]]),
            (layers - 1, [second_cols[:, (layers - 2) * halo :], halo_cols[1, :, 0:halo]]),
        )
    ]
    for copy in end_copies:
        copy.wait()
    value = mm(weights[0][:, 0:halo], ends[0, :, :])
    value = value + mm(weights[0][:, halo:], vectors[0 : 2 * halo, :])
    out[0:halo, :] = value.astype(BF16)
    value = mm(weights[1][:, 0 : 2 * halo], vectors[(layers - 2) * halo :, :])
    value = value + mm(weights[1][:, 2 * halo :], ends[1, :, :])
    out[halo:, :] = value.astype(BF16)
    list_copy.wait()
    far_blocks(pairs, far_list, second_rows, first_cols, blocks, width, PAD, range(len(pairs)))


def own_chunk_kernel(layers):
    def body(after, first_rows, second_cols, switches, vectors, basis, out, grams):
        width = basis.shape[0]
        own = basis.shape[1] // width
        both = 2 * width
        inner_layers(layers, vectors, first_rows, second_cols, switches, out, LAYER * width)
        lane = iota((width, both), 1)
        for n in range(own // 2):
            pair = basis[:, n * both : (n + 1) * both]
            zero = jnp.zeros_like(pair)
            stacked = jnp.concatenate(
                [jnp.where(lane < width, pair, zero), jnp.where(lane < width, zero, pair)], axis=0
            )
            value = mm_nt(stacked, pair)
            for m in range(2):
                at = (2 * n + m) * STRIDE
                grams[at : at + width // 2, :] = fold(value[m * width : (m + 1) * width])

    return body


def leaves_kernel(chunks, members, groups, *refs):
    outer_count = len(chunks) + 1
    near_parts = refs[:outer_count]
    (
        own_grams,
        halo_grams,
        upper,
        transfer,
        near,
        high,
        low,
        device_factor,
        group_factor,
        root_factor,
        work,
        factors,
        sems,
    ) = refs[outer_count:]
    width = transfer.shape[0]
    total = high.shape[0] // width
    own = total - 2 * PAD
    halo = LAYER * width
    layers = own // LAYER
    both = 2 * width
    places = [(part, 0, chunk[0], len(chunk)) for part, chunk in zip(near_parts, chunks)]
    places += [(near_parts[-1], n, index, 1) for n, index in enumerate((0, layers - 1))]
    near_copies = [
        pltpu.make_async_copy(
            part.at[pl.ds(start * halo, many * halo), :],
            near.at[pl.ds(index * halo, many * halo), :],
            sems.at[n],
        )
        for n, (part, start, index, many) in enumerate(places)
    ]
    for copy in near_copies:
        copy.start()

    spare = (own + 13, own + 14)
    means = (
        upper[0 : width // 2, :] * (1.0 / members),
        upper[width // 2 :, :] * (1.0 / (members * groups)),
    )
    spot_row = iota((2 * PAD, both), 0)
    for i in range(width // 2):
        rows = halo_grams[pl.ds(i, 2 * PAD, stride=STRIDE), :]
        for spot, mean in zip(spare, means):
            rows = jnp.where(spot_row == spot - own, mean[i : i + 1, :], rows)
        turned = jnp.concatenate([own_grams[pl.ds(i, own, stride=STRIDE), :], rows], axis=0).T
        work[i, :, 0:total] = turned[0:width]
        work[i + width // 2, :, 0:total] = turned[width:]
    factor_lanes(work, width)
    from_lanes(work, factors, width, total)
    at = (own + 12) * STRIDE
    device_factor[...] = exact(unfold(factors[at : at + width // 2, :]), transfer[...])
    for target, spot in zip((group_factor, root_factor), spare):
        target[...] = unfold(factors[spot * STRIDE : spot * STRIDE + width // 2, :])
    left_lanes = iota((width // 2, both), 1) < width
    spots = [(PAD + t, t) for t in range(own)]
    spots += [(spot, own + n) for n, spot in enumerate((1, 2, 3, 5, 6, 7))]
    spots += [(PAD + own + m, own + 6 + n) for n, m in enumerate((0, 1, 2, 4, 5, 6))]
    for spot, n in spots:
        rows = factors[n * STRIDE : n * STRIDE + width // 2, :]
        turned = pltpu.roll(rows, width, 1)
        twice = jnp.concatenate(
            [jnp.where(left_lanes, rows, turned), jnp.where(left_lanes, turned, rows)], axis=0
        )
        at = slice(spot * width, (spot + 1) * width)
        high[at, :], low[at, :] = split2(twice)
    for copy in near_copies:
        copy.wait()


def far_kernel(plan, far_in, high, low, *refs):
    blocks, (coupling, far_list, lines, sem, sems) = refs[:-5], refs[-5:]
    copy = pltpu.make_async_copy(far_in, far_list, sem)
    copy.start()
    width = coupling.shape[0]
    far, own = far_list.shape
    both = 2 * width
    start_leaf = lax.axis_index(AXES) * own
    square = iota((both, both), 0) // width == iota((both, both), 1) // width
    lane = iota((width, both), 1) < width
    zero = jnp.zeros((both, both), BF16)

    def diagonal(value):
        return jnp.where(square, value, zero)

    copies = []
    for start in range(0, own // 2, 4):
        indices = range(start, start + 4)
        halves = []
        for index in indices:
            source, place = plan[index]
            at = place * far * width
            kh = blocks[source][at : at + far * width, 0:both]
            kl = blocks[source][at : at + far * width, both : 2 * both]
            at = (PAD + 2 * index) * width
            rh = diagonal(high[at : at + both, :])
            rl = diagonal(low[at : at + both, :])
            halves.append(
                mm_nt(
                    jnp.concatenate([kh, kl, kh], axis=1), jnp.concatenate([rh, rh, rl], axis=1)
                )
            )
        if start == 0:
            copy.wait()
        outs = []
        for index, half in zip(indices, halves):
            zh, zl = split2(half * (1.0 / width))
            for f in range(far):
                spots = [
                    pl.multiple_of((far_list[f, 2 * index + m] - start_leaf + PAD) * width, width)
                    for m in range(2)
                ]
                sh, sl = (
                    jnp.where(lane, *(part[pl.ds(spot, width), :] for spot in spots))
                    for part in (high, low)
                )
                a = slice(f * width, (f + 1) * width)
                ph = diagonal(jnp.concatenate([zh[a], zh[a]], axis=0))
                plow = diagonal(jnp.concatenate([zl[a], zl[a]], axis=0))
                outs.append(
                    mm(
                        jnp.concatenate([sh, sh, sl], axis=1),
                        jnp.concatenate([ph, plow, ph], axis=0),
                    )
                )
        for n, index in enumerate(indices):
            three = outs[n * far : (n + 1) * far]
            line = jnp.concatenate(
                [out[:, 0:width] for out in three] + [out[:, width:both] for out in three], axis=1
            )
            at = index * 2 * far * width
            lines[:, at : at + 2 * far * width] = line.astype(BF16)
        group = pl.ds(start * 2 * far * width, 8 * far * width)
        copies.append(
            pltpu.make_async_copy(lines.at[:, group], coupling.at[:, group], sems.at[start // 4])
        )
        copies[-1].start()
    for copy in copies:
        copy.wait()


def swap_inner(block):
    return lax.ppermute(block, AXES, [(i, i ^ 1) for i in range(lax.axis_size(AXES))])


def swap_outer(block):
    many = lax.axis_size(AXES)
    return lax.ppermute(block, AXES, [(i, (i + 1 if i % 2 else i - 1) % many) for i in range(many)])


def exchange(value, distance):
    pairs = [(i, i ^ distance ^ 1) for i in range(lax.axis_size(AXES))]
    return value + lax.ppermute(value, AXES, pairs)


def per_device(
    points, leaf_basis, inner_transfer, device_transfer, vectors, near_index, near_count, far_index
):
    own = near_index.shape[0]
    width = leaf_basis.shape[1]
    columns = vectors.shape[1]
    halo = LAYER * width
    half = width // 2
    layers = own // LAYER
    total = own + 2 * PAD
    members, groups = lax.axis_size("sub"), lax.axis_size("group")
    vmem = pl.BlockSpec(memory_space=pltpu.VMEM)
    hbm = pl.BlockSpec(memory_space=pl.ANY)
    square = jax.ShapeDtypeStruct((width, width), F32)
    extra = halo + width + 32

    def block_of(rows):
        return jax.ShapeDtypeStruct((rows, columns), BF16)

    basis = leaf_basis.T
    near_list, far_list = near_index.T, far_index.T
    cost = pl.CostEstimate(flops=10**9, bytes_accessed=4 * 10**6, transcendentals=10**6)

    dense, top, to_outer, to_inner = pl.pallas_call(
        tree_kernel,
        out_shape=(
            jax.ShapeDtypeStruct((half, 2 * width), F32),
            jax.ShapeDtypeStruct((half, 2 * width), F32),
            block_of(extra),
            block_of(extra + half),
        ),
        in_specs=[hbm] * 5,
        out_specs=(hbm,) * 4,
        scratch_shapes=[
            pltpu.VMEM((3, own * width), F32),
            pltpu.VMEM((width, own * width), BF16),
            pltpu.VMEM((width, (own - 2) * width), BF16),
            pltpu.VMEM((width, width), F32),
            pltpu.VMEM((2, halo, columns), BF16),
            pltpu.VMEM((2, width + 32, columns), BF16),
            pltpu.VMEM((half, columns), BF16),
            pltpu.VMEM((2, half, 2 * width), F32),
            pltpu.SemaphoreType.DMA((13,)),
        ],
        compiler_params=room(60),
        name="tree",
    )(points, basis, inner_transfer.T, device_transfer, vectors)
    from_inner = swap_inner(to_inner)

    sub_bits = members.bit_length() - 1
    steps = [members << bit for bit in range(groups.bit_length() - 1)]
    steps += [1 << bit for bit in range(1, sub_bits)]
    inner_pairs = list(range(PAD // 2, (own - PAD) // 2))
    few = len(inner_pairs) // 2
    edge_pairs = [index for index in range(own // 2) if index not in inner_pairs]
    chunks = [[1, 2], [3, 4], [5], [6]]
    pair_chunks = [[], inner_pairs[:few], inner_pairs[few:], edge_pairs]
    blocks, plan, parts = [], {}, []

    def part_shape(count):
        return jax.ShapeDtypeStruct((count * halo, columns), BF16)

    def block_shape(count):
        return jax.ShapeDtypeStruct((count * far_index.shape[1] * width, 4 * width), BF16)

    late_points, dense = lax.optimization_barrier((points, dense))
    part, *shared = pl.pallas_call(
        first_chunk_kernel(chunks[0]),
        out_shape=(
            part_shape(len(chunks[0])),
            jax.ShapeDtypeStruct((own * width, 64), BF16),
            jax.ShapeDtypeStruct((64, own * width), BF16),
            jax.ShapeDtypeStruct((48, own * width), BF16),
            jax.ShapeDtypeStruct((own * width, 128), BF16),
            jax.ShapeDtypeStruct((own, 3 * halo), BF16),
        ),
        in_specs=[vmem] * 4,
        out_specs=(vmem,) * 6,
        scratch_shapes=[pltpu.VMEM((8, own * width), F32)],
        compiler_params=room(10),
        cost_estimate=cost,
        name="chunk_0",
    )(late_points, near_list, near_count.reshape(1, own), vectors)
    parts.append(part)
    summands = [
        from_inner[extra:, n * 2 * width : (n + 1) * 2 * width].astype(F32) for n in range(3)
    ]
    pair_gram = gram = dense + (summands[0] + (summands[1] + summands[2]))
    gram, parts[0], to_outer = lax.optimization_barrier((gram, parts[0], to_outer))
    from_outer = swap_outer(to_outer)
    first_rows, first_cols, second_cols, second_rows, switches = shared
    jobs = [1, 2, 3, "edges"]
    for n in range(max(len(steps), len(jobs))):
        if n < len(jobs) and jobs[n] == "edges":
            gram, from_outer = lax.optimization_barrier((gram, from_outer))
        before = gram
        if n < len(steps):
            if n == len(steps) - sub_bits + 1:
                gram = before = jnp.concatenate([pair_gram, gram], axis=0)
            gram = exchange(gram, steps[n])
        job = jobs[n] if n < len(jobs) else None
        if job in (1, 2):
            layer_chunk, pair_chunk = chunks[job], pair_chunks[job]
            shapes = [part_shape(len(layer_chunk))] * bool(layer_chunk)
            shapes += [block_shape(len(pair_chunk))] * bool(pair_chunk)
            outs = pl.pallas_call(
                chunk_kernel(layer_chunk, pair_chunk, halo, width),
                out_shape=tuple(shapes),
                in_specs=[hbm] * 2 + [vmem] * 6,
                out_specs=(vmem,) * len(shapes),
                scratch_shapes=[
                    pltpu.SMEM(far_list.shape, jnp.int32),
                    pltpu.SemaphoreType.DMA,
                ],
                compiler_params=room(10),
                cost_estimate=cost,
                name=f"chunk_{job}",
            )(before, far_list, first_rows, second_cols, switches, vectors, first_cols, second_rows)
            gram, outs = lax.optimization_barrier((gram, outs))
            if layer_chunk:
                parts.append(outs[0])
            if pair_chunk:
                plan.update((index, (len(blocks), m)) for m, index in enumerate(pair_chunk))
                blocks.append(outs[-1])
        elif job == 3:
            part, own_grams = pl.pallas_call(
                own_chunk_kernel(chunks[3]),
                out_shape=(
                    part_shape(len(chunks[3])),
                    jax.ShapeDtypeStruct((own * STRIDE, 2 * width), F32),
                ),
                in_specs=[hbm] + [vmem] * 5,
                out_specs=(vmem,) * 2,
                compiler_params=room(10),
                cost_estimate=cost,
                name="chunk_3",
            )(before, first_rows, second_cols, switches, vectors, basis)
            gram, part = lax.optimization_barrier((gram, part))
            parts.append(part)
        elif job == "edges":
            edge_part, edge_blocks, halo_grams = pl.pallas_call(
                functools.partial(edges_kernel, edge_pairs),
                out_shape=(
                    part_shape(2),
                    block_shape(len(edge_pairs)),
                    jax.ShapeDtypeStruct((2 * PAD * STRIDE, 2 * width), F32),
                ),
                in_specs=[hbm] * 4 + [vmem] * 7,
                out_specs=(vmem,) * 3,
                scratch_shapes=[
                    pltpu.VMEM((2, halo, columns), BF16),
                    pltpu.VMEM((2, width + 32, columns), BF16),
                    pltpu.VMEM((8, PAD * width), F32),
                    pltpu.VMEM((2, 48, PAD * width), BF16),
                    pltpu.SMEM(far_list.shape, jnp.int32),
                    pltpu.VMEM((total * width, 2 * width), BF16),
                    pltpu.SemaphoreType.DMA((5,)),
                ],
                compiler_params=room(14),
                cost_estimate=cost,
                name="edges",
            )(
                before,
                far_list,
                from_inner,
                from_outer,
                first_rows,
                second_cols,
                switches,
                vectors,
                first_cols,
                second_rows,
                top,
            )
            gram, edge_part = lax.optimization_barrier((gram, edge_part))
            plan.update((index, (len(blocks), m)) for m, index in enumerate(edge_pairs))
            blocks.append(edge_blocks)

    split_factors = jax.ShapeDtypeStruct((total * width, 2 * width), BF16)
    near, high, low, device_factor, group_factor, root_factor = pl.pallas_call(
        functools.partial(leaves_kernel, chunks, members, groups),
        out_shape=(
            jax.ShapeDtypeStruct(vectors.shape, BF16),
            split_factors,
            split_factors,
            square,
            square,
            square,
        ),
        in_specs=[hbm] * (len(parts) + 1) + [vmem] * 4,
        out_specs=(hbm,) + (vmem,) * 5,
        scratch_shapes=[
            pltpu.VMEM((width, width, 128), F32),
            pltpu.VMEM((total * STRIDE, 2 * width), F32),
            pltpu.SemaphoreType.DMA((2 + len(parts),)),
        ],
        compiler_params=room(20),
        name="leaves",
    )(*parts, edge_part, own_grams, halo_grams, gram, device_transfer)

    coupling = pl.pallas_call(
        functools.partial(far_kernel, plan),
        out_shape=jax.ShapeDtypeStruct((width, own * far_index.shape[1] * width), BF16),
        in_specs=[hbm] + [vmem] * (2 + len(blocks)),
        out_specs=hbm,
        scratch_shapes=[
            pltpu.SMEM(far_list.shape, jnp.int32),
            pltpu.VMEM((width, own * far_index.shape[1] * width), BF16),
            pltpu.SemaphoreType.DMA,
            pltpu.SemaphoreType.DMA((own // 8,)),
        ],
        compiler_params=room(16),
        name="far",
    )(far_list, high, low, *blocks)
    return near, coupling.T, device_factor, group_factor, root_factor


def solution(mesh):
    split = P(AXES, None)
    return jax.shard_map(
        per_device,
        mesh=mesh,
        in_specs=(P(None, AXES), split, split, split, split, split, P(AXES), split),
        out_specs=(split, split, split, split, split),
        check_vma=False,
    )
```

```python
import functools
import math

import jax
import jax.numpy as jnp
from jax import lax
from jax.experimental import pallas as pl
from jax.experimental.pallas import tpu as pltpu
from jax.sharding import PartitionSpec as P

LAYER = 4
PAD = 8
LONG_SQ = 2.25
RATIO = 25.0
SCALE = 0.5 / LONG_SQ
HALF = math.log(0.5)
OFF = -16384.0
STRIDE = 40
AXES = ("group", "sub")
F32 = jnp.float32
BF16 = jnp.bfloat16


def room(megabytes):
    return pltpu.CompilerParams(vmem_limit_bytes=int(megabytes * 1024 * 1024))


def split2(value):
    high = value.astype(BF16)
    return high, (value - high.astype(F32)).astype(BF16)


def split3(value):
    high = value.astype(BF16)
    rest = value - high.astype(F32)
    middle = rest.astype(BF16)
    return high, middle, (rest - middle.astype(F32)).astype(BF16)


def mm(left, right):
    return jnp.dot(left, right, preferred_element_type=F32)


def mm_nt(left, right):
    return lax.dot_general(left, right, (((1,), (1,)), ((), ())), preferred_element_type=F32)


def exact(left, right):
    return jnp.dot(left, right, precision=lax.Precision.HIGHEST, preferred_element_type=F32)


def iota(shape, dim):
    return lax.broadcasted_iota(jnp.int32, shape, dim)


def tree_kernel(
    points_in, basis_in, below_in, transfer_in, vectors,
    dense, top, outer, inner, points, basis, below, transfer, passing, packed, staged, small, sems,
):
    width = basis.shape[0]
    count = basis.shape[1] // width
    halo = LAYER * width
    span = PAD * width
    rows = vectors.shape[0]
    odd = lax.axis_index("sub") % 2
    sides = ((outer, odd), (inner, 1 - odd))
    basis_copy, below_copy, points_copy, transfer_copy = loads = [
        pltpu.make_async_copy(source, target, sems.at[n])
        for n, (source, target) in enumerate(
            (
                (basis_in, basis),
                (below_in, below),
                (points_in, points),
                (transfer_in, transfer),
            )
        )
    ]
    vector_loads = [
        pltpu.make_async_copy(
            vectors.at[pl.ds(pl.multiple_of(last * (rows - halo), 16), halo), :],
            passing.at[n],
            sems.at[4 + n],
        )
        for n, (_, last) in enumerate(sides)
    ]
    copies = [
        pltpu.make_async_copy(passing.at[n], target.at[pl.ds(0, halo), :], sems.at[9 + n])
        for n, (target, _) in enumerate(sides)
    ]
    for copy in loads + vector_loads:
        copy.start()

    both = 2 * width
    lane = iota((width, 2 * both), 1)

    def times(above, columns):
        found = []
        for n in range(above.shape[1] // both):
            parts = jnp.concatenate(split3(above[:, n * both : (n + 1) * both]), axis=1)
            block = columns(n * 2 * both)
            zero = jnp.zeros_like(block)
            block = jnp.concatenate(
                [jnp.where(lane < both, block, zero), jnp.where(lane < both, zero, block)], axis=0
            )
            found.append(mm(parts, jnp.concatenate([block] * 3, axis=0)))
        return jnp.concatenate(found, axis=1)

    same = iota((both, both), 0) // width == iota((both, both), 1) // width
    half_block = jnp.where(same, 0.5, 0.0).astype(F32)
    basis_copy.wait()
    points_copy.wait()
    for n, (target, last) in enumerate(sides):
        bases = basis[:, count * width - span :], basis[:, 0:span]
        last_three, first_three = (
            jnp.concatenate(
                [block[:, (at + skip) * width : (at + skip + 3) * width] for at in (0, LAYER)],
                axis=1,
            )
            for skip, block in zip((1, 0), bases)
        )
        packed[n, 0:width, :] = jnp.where(last == 1, last_three, first_three)
        coords = jnp.where(last == 1, points[:, count * width - span :], points[:, 0:span])
        for m in range(2):
            high, low = split2(coords[:, m * halo : (m + 1) * halo])
            base = width + 16 * m
            packed[n, base : base + 16, :] = jnp.zeros((16, target.shape[1]), BF16)
            packed[n, base : base + 3, 0:halo] = high
            packed[n, base + 8 : base + 11, 0:halo] = low
        copies.append(
            pltpu.make_async_copy(
                packed.at[n], target.at[pl.ds(halo, width + 32), :], sems.at[6 + n]
            )
        )
        copies[-1].start()
    blocks = []
    for n in range(count // 4):
        stacked = jnp.concatenate(
            [basis[:, (2 * n + m) * both : (2 * n + m + 1) * both] for m in range(2)], axis=0
        )
        blocks.append(mm_nt(stacked, stacked) * half_block)
    below_copy.wait()
    halves = []
    for n, block in enumerate(blocks):
        t = below[:, n * both : (n + 1) * both]
        half = mm(jnp.concatenate([t, t, t], axis=1), jnp.concatenate(split3(block), axis=0))
        halves.append((half, t))
    blocks = []
    for n in range(0, len(halves), 2):
        (first, t), (second, u) = halves[n : n + 2]
        x = jnp.concatenate(split3(jnp.concatenate([first, second], axis=0)), axis=1)
        t = jnp.concatenate([t, u], axis=0)
        blocks.append(mm_nt(x, jnp.concatenate([t, t, t], axis=1)) * half_block)

    for load, copy in zip(vector_loads, copies[:2]):
        load.wait()
        copy.start()

    transfer_copy.wait()
    end = below.shape[1]
    tops = below[:, end - both : end]
    turned = jnp.concatenate(split3(transfer[...].T), axis=1)
    above = jnp.concatenate(
        [tops.astype(F32), mm(turned, jnp.concatenate([tops] * 3, axis=0))], axis=0
    )
    end -= both
    nodes = 4
    while nodes < count // 2:
        start = end - nodes * width
        above = times(above, lambda at, start=start: below[:, start + at : start + at + 2 * both])
        end = start
        nodes *= 2

    total = jnp.zeros((both, both), F32)
    for n, block in enumerate(blocks):
        rows = above[:, n * both : (n + 1) * both]
        high, middle, low = split3(rows)
        gh, gm, gl = split3(block)
        x = mm(
            jnp.concatenate([high, high, high, middle, middle, low], axis=1),
            jnp.concatenate([gh, gm, gl, gh, gm, gh], axis=0),
        )
        xh, xm, xl = split3(x)
        total = total + mm_nt(
            jnp.concatenate([xh, xh, xh, xm, xm, xl], axis=1),
            jnp.concatenate([high, middle, low, high, middle, high], axis=1),
        )
    total = total * (4.0 / count)
    small[0, :, :] = fold(total[:width, :width])
    halves = fold(total[width:, width:])
    small[1, :, :] = halves
    staged[...] = jnp.concatenate(split3(halves), axis=1)
    copies.append(
        pltpu.make_async_copy(
            staged, inner.at[pl.ds(halo + width + 32, width // 2), :], sems.at[8]
        )
    )
    copies[-1].start()
    for n, target in enumerate((top, dense)):
        copies.append(pltpu.make_async_copy(small.at[n], target, sems.at[11 + n]))
        copies[-1].start()
    for copy in copies:
        copy.wait()


def factor_lanes(work, width):
    panels = width // 8
    row = iota((8, 128), 0)

    def spread(j, i):
        return jnp.broadcast_to(work[j, i : i + 1, :], (8, 128))

    for p in range(panels):
        at = 8 * p
        entry = {(k, m): spread(at + k, at + m) for k in range(8) for m in range(k, 8)}
        scales = []
        for k in range(8):
            scales.append(lax.rsqrt(entry[k, k]))
            for m in range(k + 1, 8):
                entry[k, m] = entry[k, m] * scales[k]
            for m in range(k + 1, 8):
                for q in range(m, 8):
                    entry[m, q] = entry[m, q] - entry[k, m] * entry[k, q]
        for i in range(p, panels):
            tile = [work[at + k, 8 * i : 8 * i + 8, :] for k in range(8)]
            for k in range(8):
                tile[k] = tile[k] * scales[k]
                for m in range(k + 1, 8):
                    tile[m] = tile[m] - tile[k] * entry[k, m]
            for k in range(8):
                work[at + k, 8 * i : 8 * i + 8, :] = (
                    jnp.where(row >= k, tile[k], 0.0) if i == p else tile[k]
                )
        for q in range(p + 1, panels):
            for start in range(q, panels, 4):
                group = range(start, min(start + 4, panels))
                accs = {
                    (i, k): work[8 * q + k, 8 * i : 8 * i + 8, :] for i in group for k in range(8)
                }
                for j in range(at, at + 8):
                    factors = [spread(j, 8 * q + k) for k in range(8)]
                    for i in group:
                        column = work[j, 8 * i : 8 * i + 8, :]
                        for k in range(8):
                            accs[i, k] = accs[i, k] - column * factors[k]
                for (i, k), value in accs.items():
                    work[8 * q + k, 8 * i : 8 * i + 8, :] = value


def fold(matrix):
    half = matrix.shape[0] // 2
    return jnp.concatenate([matrix[:half], matrix[half:]], axis=1)


def unfold(matrix):
    half = matrix.shape[1] // 2
    return jnp.concatenate([matrix[:, :half], matrix[:, half:]], axis=0)


def from_lanes(work, factors, width, many):
    for i in range(width // 2):
        both = []
        for j in (i, i + width // 2):
            skip = j // 8 * 8
            both += [jnp.zeros((skip, many), F32)] * bool(skip) + [work[j, skip:, 0:many]]
        factors[pl.ds(i, many, stride=STRIDE), :] = jnp.concatenate(both, axis=0).T


def gaussians(exponent):
    return jnp.exp(exponent) + jnp.exp(exponent * RATIO - RATIO * HALF)


def features(place, leaf, center):
    sub = iota(place.shape, 0)
    corner = jnp.where(sub == 0, leaf % 2 - 1, leaf // 2 % 2 - 1)
    corner = jnp.where(sub == 2, leaf // LAYER - center, corner)
    place = jnp.where(sub < 3, place + corner.astype(F32), 0.0)
    norm = jnp.sum(place * place, axis=0, keepdims=True) * SCALE
    first = jnp.where(sub == 3, -norm, jnp.where(sub == 4, 1.0, place))
    second = jnp.where(
        sub == 3, 1.0, jnp.where(sub == 4, HALF - norm, place * (2.0 * SCALE))
    )
    fh, fm, fl = [v.astype(F32) for v in split3(first)]
    sh, sm, sl = [v.astype(F32) for v in split3(second)]
    return (
        jnp.concatenate([fh, fh, fh, fm, fm, fl], axis=0),
        jnp.concatenate([sh, sm, sl, sh, sm, sh], axis=0),
    )


def rows_of(second):
    blank = jnp.zeros((16, second.shape[1]), F32)
    return jnp.concatenate([second, blank, second, blank], axis=0).T.astype(BF16)


def near_weights(first_rows, second, switches, index, halo):
    group = index // 4 * 16
    columns = jnp.concatenate([second, switches[group : group + 16, :]], axis=0)
    return gaussians(mm(first_rows[index * halo : (index + 1) * halo, :], columns)).astype(BF16)


def prepare(
    points, near_list, near_used, first_rows, first_cols, second_cols, second_rows, switches, place
):
    rows = points.shape[1]
    own = near_list.shape[1]
    width = rows // own
    place[...] = jnp.zeros(place.shape, F32)
    place[0:3, :] = points[...]
    leaf = iota((8, rows), 1) // width
    first, second = features(place[...], leaf, own // LAYER // 2)
    hot_leaf = iota((16, rows), 1) // width
    hot = jnp.where(hot_leaf % 16 == iota((16, rows), 0), 1.0, 0.0).astype(F32)
    first = jnp.concatenate([first, hot], axis=0)
    first_cols[...] = first.astype(BF16)
    second_cols[...] = second.astype(BF16)
    first_rows[...] = first.T.astype(BF16)
    second_rows[...] = rows_of(second)

    start_leaf = lax.axis_index(AXES) * own
    target = iota((1, own), 1)
    base_leaf = start_leaf + target // LAYER * LAYER - LAYER
    found = jnp.zeros((16, own), jnp.bool_)
    place_row = iota((16, own), 0)
    for n in range(near_list.shape[0]):
        spot = jnp.where(near_used[...] > n, near_list[n : n + 1, :] - base_leaf, -1)
        found = jnp.logical_or(found, place_row == spot)
    bias = jnp.where(found, 0.0, OFF).astype(F32)
    span = 3 * LAYER * width
    expand = jnp.where(iota((16, span), 0) == iota((16, span), 1) // width, 1.0, 0.0)
    switches[...] = mm(bias.T.astype(BF16), expand.astype(BF16)).astype(BF16)


def inner_layers(layers, vectors, first_rows, second_cols, switches, out, halo):
    for n, index in enumerate(layers):
        around = slice((index - 1) * halo, (index + 2) * halo)
        weights = near_weights(first_rows, second_cols[:, around], switches, index, halo)
        out[n * halo : (n + 1) * halo, :] = mm(weights, vectors[around, :]).astype(BF16)


def far_blocks(pairs, far_list, second_rows, first_cols, out, width, base, places):
    far, own = far_list.shape
    both = 2 * width
    start_leaf = lax.axis_index(AXES) * own
    square = iota((both, both), 0) // width == iota((both, both), 1) // width
    lane = iota((far * width, both), 1) < width
    exponents = []
    for index in pairs:
        t = 2 * index
        picked = []
        for m in range(2):
            spots = [
                pl.multiple_of((far_list[f, t + m] - start_leaf + base) * width, width)
                for f in range(far)
            ]
            picked.append(
                jnp.concatenate([second_rows[pl.ds(spot, width), :] for spot in spots], axis=0)
            )
        cols = first_cols[:, t * width : t * width + both]
        targets = jnp.where(
            square, jnp.concatenate([cols, cols], axis=0), jnp.zeros((both, both), BF16)
        )
        exponents.append(mm(jnp.where(lane, picked[0], picked[1]), targets))
    for place, exponent in zip(places, exponents):
        high, low = split2(gaussians(exponent))
        at = place * far * width
        out[at : at + far * width, 0:both] = high
        out[at : at + far * width, both : 2 * both] = low


def first_chunk_kernel(layers):
    def body(
        points, near_list, near_used, vectors,
        out, first_rows, first_cols, second_cols, second_rows, switches, place,
    ):
        prepare(
            points,
            near_list,
            near_used,
            first_rows,
            first_cols,
            second_cols,
            second_rows,
            switches,
            place,
        )
        halo = LAYER * points.shape[1] // near_list.shape[1]
        inner_layers(layers, vectors, first_rows, second_cols, switches, out, halo)

    return body


def chunk_kernel(layers, pairs, halo, width):
    def body(after, far_in, *refs):
        first_rows, second_cols, switches, vectors, first_cols, second_rows = refs[:6]
        outs, far_list, sem = refs[6:-2], refs[-2], refs[-1]
        if pairs:
            copy = pltpu.make_async_copy(far_in, far_list, sem)
            copy.start()
        if layers:
            inner_layers(layers, vectors, first_rows, second_cols, switches, outs[0], halo)
        if pairs:
            copy.wait()
            far_blocks(
                pairs, far_list, second_rows, first_cols, outs[-1], width, 0, range(len(pairs))
            )

    return body


def edges_kernel(
    pairs, after, far_in, inner, outer, first_rows, second_cols, switches, vectors,
    first_cols, own_rows, top,
    out, blocks, grams, ends, sides, place, halo_cols, far_list, second_rows, sems,
):
    halo = ends.shape[1]
    width = halo // LAYER
    own = vectors.shape[0] // width
    layers = own // LAYER
    extra = sides.shape[1]
    odd = lax.axis_index("sub") % 2
    arrived = ((inner, 1 - odd), (outer, odd))
    side_copies = [
        pltpu.make_async_copy(
            block.at[pl.ds(halo, extra), :], sides.at[side], sems.at[n]
        )
        for n, (block, side) in enumerate(arrived)
    ]
    end_copies = [
        pltpu.make_async_copy(block.at[pl.ds(0, halo), :], ends.at[side], sems.at[2 + n])
        for n, (block, side) in enumerate(arrived)
    ]
    list_copy = pltpu.make_async_copy(far_in, far_list, sems.at[4])
    for copy in side_copies + end_copies + [list_copy]:
        copy.start()
    lanes = PAD * width
    second_rows[lanes : lanes + own * width, :] = own_rows[...]
    place[...] = jnp.zeros(place.shape, F32)
    for copy in side_copies:
        copy.wait()
    for side, first_leaf in enumerate((-PAD, own)):
        for n in range(2):
            base = width + 16 * n
            values = sides[side, base : base + 16, 0:halo].astype(F32)
            place[0:3, n * halo : (n + 1) * halo] = values[0:3, :] + values[8:11, :]
        leaf = iota((8, lanes), 1) // width + (first_leaf + PAD)
        second = features(place[...], leaf, layers // 2 + PAD // LAYER)[1]
        halo_cols[side, :, :] = second.astype(BF16)
        at = (PAD + first_leaf) * width
        second_rows[at : at + lanes, :] = rows_of(second)
        for n in range(6):
            piece = sides[side, 0:width, n * width : (n + 1) * width]
            at = (6 * side + n) * STRIDE
            grams[at : at + width // 2, :] = fold(mm_nt(piece, piece))
    for n in range(12, 16):
        grams[n * STRIDE : n * STRIDE + width // 2, :] = top[...]
    weights = [
        near_weights(
            first_rows, jnp.concatenate(columns, axis=1), switches, index, halo
        )
        for index, columns in (
            (0, [halo_cols[0, :, halo:], second_cols[:, 0 : 2 * halo]]),
            (layers - 1, [second_cols[:, (layers - 2) * halo :], halo_cols[1, :, 0:halo]]),
        )
    ]
    for copy in end_copies:
        copy.wait()
    value = mm(weights[0][:, 0:halo], ends[0, :, :])
    value = value + mm(weights[0][:, halo:], vectors[0 : 2 * halo, :])
    out[0:halo, :] = value.astype(BF16)
    value = mm(weights[1][:, 0 : 2 * halo], vectors[(layers - 2) * halo :, :])
    value = value + mm(weights[1][:, 2 * halo :], ends[1, :, :])
    out[halo:, :] = value.astype(BF16)
    list_copy.wait()
    far_blocks(pairs, far_list, second_rows, first_cols, blocks, width, PAD, range(len(pairs)))


def own_chunk_kernel(layers, pairs):
    def body(
        after, far_in, first_rows, second_cols, switches, vectors, first_cols, second_rows, basis,
        out, blocks, grams, far_list, sem,
    ):
        copy = pltpu.make_async_copy(far_in, far_list, sem)
        copy.start()
        width = basis.shape[0]
        own = basis.shape[1] // width
        both = 2 * width
        inner_layers(layers, vectors, first_rows, second_cols, switches, out, LAYER * width)
        lane = iota((width, both), 1)
        for n in range(own // 2):
            pair = basis[:, n * both : (n + 1) * both]
            zero = jnp.zeros_like(pair)
            stacked = jnp.concatenate(
                [jnp.where(lane < width, pair, zero), jnp.where(lane < width, zero, pair)], axis=0
            )
            value = mm_nt(stacked, pair)
            for m in range(2):
                at = (2 * n + m) * STRIDE
                grams[at : at + width // 2, :] = fold(value[m * width : (m + 1) * width])

        copy.wait()
        far_blocks(pairs, far_list, second_rows, first_cols, blocks, width, 0, range(len(pairs)))

    return body


def leaves_kernel(chunks, members, groups, *refs):
    outer_count = len(chunks) + 1
    near_parts = refs[:outer_count]
    (
        own_grams,
        halo_grams,
        upper,
        transfer,
        near,
        high,
        low,
        device_factor,
        group_factor,
        root_factor,
        work,
        factors,
        sems,
    ) = refs[outer_count:]
    width = transfer.shape[0]
    total = high.shape[0] // width
    own = total - 2 * PAD
    halo = LAYER * width
    layers = own // LAYER
    both = 2 * width
    places = [(part, 0, chunk[0], len(chunk)) for part, chunk in zip(near_parts, chunks)]
    places += [(near_parts[-1], n, index, 1) for n, index in enumerate((0, layers - 1))]
    near_copies = [
        pltpu.make_async_copy(
            part.at[pl.ds(start * halo, many * halo), :],
            near.at[pl.ds(index * halo, many * halo), :],
            sems.at[n],
        )
        for n, (part, start, index, many) in enumerate(places)
    ]
    for copy in near_copies:
        copy.start()

    spare = (own + 13, own + 14)
    means = (
        upper[0 : width // 2, :] * (1.0 / members),
        upper[width // 2 :, :] * (1.0 / (members * groups)),
    )
    spot_row = iota((2 * PAD, both), 0)
    for i in range(width // 2):
        rows = halo_grams[pl.ds(i, 2 * PAD, stride=STRIDE), :]
        for spot, mean in zip(spare, means):
            rows = jnp.where(spot_row == spot - own, mean[i : i + 1, :], rows)
        turned = jnp.concatenate([own_grams[pl.ds(i, own, stride=STRIDE), :], rows], axis=0).T
        work[i, :, 0:total] = turned[0:width]
        work[i + width // 2, :, 0:total] = turned[width:]
    factor_lanes(work, width)
    from_lanes(work, factors, width, total)
    at = (own + 12) * STRIDE
    device_factor[...] = exact(unfold(factors[at : at + width // 2, :]), transfer[...])
    for target, spot in zip((group_factor, root_factor), spare):
        target[...] = unfold(factors[spot * STRIDE : spot * STRIDE + width // 2, :])
    left_lanes = iota((width // 2, both), 1) < width
    spots = [(PAD + t, t) for t in range(own)]
    spots += [(spot, own + n) for n, spot in enumerate((1, 2, 3, 5, 6, 7))]
    spots += [(PAD + own + m, own + 6 + n) for n, m in enumerate((0, 1, 2, 4, 5, 6))]
    for spot, n in spots:
        rows = factors[n * STRIDE : n * STRIDE + width // 2, :]
        turned = pltpu.roll(rows, width, 1)
        twice = jnp.concatenate(
            [jnp.where(left_lanes, rows, turned), jnp.where(left_lanes, turned, rows)], axis=0
        )
        at = slice(spot * width, (spot + 1) * width)
        high[at, :], low[at, :] = split2(twice)
    for copy in near_copies:
        copy.wait()


def far_kernel(plan, far_in, high, low, *refs):
    blocks, (coupling, far_list, lines, sem, sems) = refs[:-5], refs[-5:]
    copy = pltpu.make_async_copy(far_in, far_list, sem)
    copy.start()
    width = coupling.shape[0]
    far, own = far_list.shape
    both = 2 * width
    start_leaf = lax.axis_index(AXES) * own
    square = iota((both, both), 0) // width == iota((both, both), 1) // width
    lane = iota((width, both), 1) < width
    zero = jnp.zeros((both, both), BF16)

    def diagonal(value):
        return jnp.where(square, value, zero)

    copies = []
    for start in range(0, own // 2, 4):
        indices = range(start, start + 4)
        halves = []
        for index in indices:
            source, place = plan[index]
            at = place * far * width
            kh = blocks[source][at : at + far * width, 0:both]
            kl = blocks[source][at : at + far * width, both : 2 * both]
            at = (PAD + 2 * index) * width
            rh = diagonal(high[at : at + both, :])
            rl = diagonal(low[at : at + both, :])
            halves.append(
                mm_nt(
                    jnp.concatenate([kh, kl, kh], axis=1), jnp.concatenate([rh, rh, rl], axis=1)
                )
            )
        if start == 0:
            copy.wait()
        outs = []
        for index, half in zip(indices, halves):
            zh, zl = split2(half * (1.0 / width))
            for f in range(far):
                spots = [
                    pl.multiple_of((far_list[f, 2 * index + m] - start_leaf + PAD) * width, width)
                    for m in range(2)
                ]
                sh, sl = (
                    jnp.where(lane, *(part[pl.ds(spot, width), :] for spot in spots))
                    for part in (high, low)
                )
                a = slice(f * width, (f + 1) * width)
                ph = diagonal(jnp.concatenate([zh[a], zh[a]], axis=0))
                plow = diagonal(jnp.concatenate([zl[a], zl[a]], axis=0))
                outs.append(
                    mm(
                        jnp.concatenate([sh, sh, sl], axis=1),
                        jnp.concatenate([ph, plow, ph], axis=0),
                    )
                )
        for n, index in enumerate(indices):
            three = outs[n * far : (n + 1) * far]
            line = jnp.concatenate(
                [out[:, 0:width] for out in three] + [out[:, width:both] for out in three], axis=1
            )
            at = index * 2 * far * width
            lines[:, at : at + 2 * far * width] = line.astype(BF16)
        group = pl.ds(start * 2 * far * width, 8 * far * width)
        copies.append(
            pltpu.make_async_copy(lines.at[:, group], coupling.at[:, group], sems.at[start // 4])
        )
        copies[-1].start()
    for copy in copies:
        copy.wait()


def swap_inner(block):
    return lax.ppermute(block, AXES, [(i, i ^ 1) for i in range(lax.axis_size(AXES))])


def swap_outer(block):
    many = lax.axis_size(AXES)
    return lax.ppermute(block, AXES, [(i, (i + 1 if i % 2 else i - 1) % many) for i in range(many)])


def exchange(value, distance):
    pairs = [(i, i ^ distance ^ 1) for i in range(lax.axis_size(AXES))]
    return value + lax.ppermute(value, AXES, pairs)


def per_device(
    points, leaf_basis, inner_transfer, device_transfer, vectors, near_index, near_count, far_index
):
    own = near_index.shape[0]
    width = leaf_basis.shape[1]
    columns = vectors.shape[1]
    halo = LAYER * width
    half = width // 2
    layers = own // LAYER
    total = own + 2 * PAD
    members, groups = lax.axis_size("sub"), lax.axis_size("group")
    vmem = pl.BlockSpec(memory_space=pltpu.VMEM)
    hbm = pl.BlockSpec(memory_space=pl.ANY)
    square = jax.ShapeDtypeStruct((width, width), F32)
    extra = halo + width + 32

    def block_of(rows):
        return jax.ShapeDtypeStruct((rows, columns), BF16)

    basis = leaf_basis.T
    near_list, far_list = near_index.T, far_index.T
    cost = pl.CostEstimate(flops=10**9, bytes_accessed=4 * 10**6, transcendentals=10**6)

    dense, top, to_outer, to_inner = pl.pallas_call(
        tree_kernel,
        out_shape=(
            jax.ShapeDtypeStruct((half, 2 * width), F32),
            jax.ShapeDtypeStruct((half, 2 * width), F32),
            block_of(extra),
            block_of(extra + half),
        ),
        in_specs=[hbm] * 5,
        out_specs=(hbm,) * 4,
        scratch_shapes=[
            pltpu.VMEM((3, own * width), F32),
            pltpu.VMEM((width, own * width), BF16),
            pltpu.VMEM((width, (own - 2) * width), BF16),
            pltpu.VMEM((width, width), F32),
            pltpu.VMEM((2, halo, columns), BF16),
            pltpu.VMEM((2, width + 32, columns), BF16),
            pltpu.VMEM((half, columns), BF16),
            pltpu.VMEM((2, half, 2 * width), F32),
            pltpu.SemaphoreType.DMA((13,)),
        ],
        compiler_params=room(60),
        name="tree",
    )(points, basis, inner_transfer.T, device_transfer, vectors)
    from_inner = swap_inner(to_inner)

    sub_bits = members.bit_length() - 1
    steps = [members << bit for bit in range(groups.bit_length() - 1)]
    steps += [1 << bit for bit in range(1, sub_bits)]
    inner_pairs = list(range(PAD // 2, (own - PAD) // 2))
    few = len(inner_pairs) // 2
    edge_pairs = [index for index in range(own // 2) if index not in inner_pairs]
    chunks = [[1, 2], [3], [4, 5], [6]]
    pair_chunks = [[], [], inner_pairs[:few], inner_pairs[few:]]
    blocks, plan, parts = [], {}, []

    def part_shape(count):
        return jax.ShapeDtypeStruct((count * halo, columns), BF16)

    def block_shape(count):
        return jax.ShapeDtypeStruct((count * far_index.shape[1] * width, 4 * width), BF16)

    late_points, dense = lax.optimization_barrier((points, dense))
    part, *shared = pl.pallas_call(
        first_chunk_kernel(chunks[0]),
        out_shape=(
            part_shape(len(chunks[0])),
            jax.ShapeDtypeStruct((own * width, 64), BF16),
            jax.ShapeDtypeStruct((64, own * width), BF16),
            jax.ShapeDtypeStruct((48, own * width), BF16),
            jax.ShapeDtypeStruct((own * width, 128), BF16),
            jax.ShapeDtypeStruct((own, 3 * halo), BF16),
        ),
        in_specs=[vmem] * 4,
        out_specs=(vmem,) * 6,
        scratch_shapes=[pltpu.VMEM((8, own * width), F32)],
        compiler_params=room(10),
        cost_estimate=cost,
        name="chunk_0",
    )(late_points, near_list, near_count.reshape(1, own), vectors)
    parts.append(part)
    summands = [
        from_inner[extra:, n * 2 * width : (n + 1) * 2 * width].astype(F32) for n in range(3)
    ]
    pair_gram = gram = dense + (summands[0] + (summands[1] + summands[2]))
    gram, parts[0], to_outer = lax.optimization_barrier((gram, parts[0], to_outer))
    from_outer = swap_outer(to_outer)
    first_rows, first_cols, second_cols, second_rows, switches = shared
    jobs = [1, 2, 3, "edges"]
    for n in range(max(len(steps), len(jobs))):
        if n < len(jobs) and jobs[n] == "edges":
            gram, from_outer = lax.optimization_barrier((gram, from_outer))
        before = gram
        if n < len(steps):
            if n == len(steps) - sub_bits + 1:
                gram = before = jnp.concatenate([pair_gram, gram], axis=0)
            gram = exchange(gram, steps[n])
        job = jobs[n] if n < len(jobs) else None
        if job in (1, 2):
            layer_chunk, pair_chunk = chunks[job], pair_chunks[job]
            shapes = [part_shape(len(layer_chunk))] * bool(layer_chunk)
            shapes += [block_shape(len(pair_chunk))] * bool(pair_chunk)
            outs = pl.pallas_call(
                chunk_kernel(layer_chunk, pair_chunk, halo, width),
                out_shape=tuple(shapes),
                in_specs=[hbm] * 2 + [vmem] * 6,
                out_specs=(vmem,) * len(shapes),
                scratch_shapes=[
                    pltpu.SMEM(far_list.shape, jnp.int32),
                    pltpu.SemaphoreType.DMA,
                ],
                compiler_params=room(10),
                cost_estimate=cost,
                name=f"chunk_{job}",
            )(before, far_list, first_rows, second_cols, switches, vectors, first_cols, second_rows)
            gram, outs = lax.optimization_barrier((gram, outs))
            if layer_chunk:
                parts.append(outs[0])
            if pair_chunk:
                plan.update((index, (len(blocks), m)) for m, index in enumerate(pair_chunk))
                blocks.append(outs[-1])
        elif job == 3:
            part, own_blocks, own_grams = pl.pallas_call(
                own_chunk_kernel(chunks[3], pair_chunks[3]),
                out_shape=(
                    part_shape(len(chunks[3])),
                    block_shape(len(pair_chunks[3])),
                    jax.ShapeDtypeStruct((own * STRIDE, 2 * width), F32),
                ),
                in_specs=[hbm] * 2 + [vmem] * 7,
                out_specs=(vmem,) * 3,
                scratch_shapes=[
                    pltpu.SMEM(far_list.shape, jnp.int32),
                    pltpu.SemaphoreType.DMA,
                ],
                compiler_params=room(10),
                cost_estimate=cost,
                name="chunk_3",
            )(
                before,
                far_list,
                first_rows,
                second_cols,
                switches,
                vectors,
                first_cols,
                second_rows,
                basis,
            )
            gram, part = lax.optimization_barrier((gram, part))
            parts.append(part)
            plan.update((index, (len(blocks), m)) for m, index in enumerate(pair_chunks[3]))
            blocks.append(own_blocks)
        elif job == "edges":
            edge_part, edge_blocks, halo_grams = pl.pallas_call(
                functools.partial(edges_kernel, edge_pairs),
                out_shape=(
                    part_shape(2),
                    block_shape(len(edge_pairs)),
                    jax.ShapeDtypeStruct((2 * PAD * STRIDE, 2 * width), F32),
                ),
                in_specs=[hbm] * 4 + [vmem] * 7,
                out_specs=(vmem,) * 3,
                scratch_shapes=[
                    pltpu.VMEM((2, halo, columns), BF16),
                    pltpu.VMEM((2, width + 32, columns), BF16),
                    pltpu.VMEM((8, PAD * width), F32),
                    pltpu.VMEM((2, 48, PAD * width), BF16),
                    pltpu.SMEM(far_list.shape, jnp.int32),
                    pltpu.VMEM((total * width, 2 * width), BF16),
                    pltpu.SemaphoreType.DMA((5,)),
                ],
                compiler_params=room(14),
                cost_estimate=cost,
                name="edges",
            )(
                before,
                far_list,
                from_inner,
                from_outer,
                first_rows,
                second_cols,
                switches,
                vectors,
                first_cols,
                second_rows,
                top,
            )
            gram, edge_part = lax.optimization_barrier((gram, edge_part))
            plan.update((index, (len(blocks), m)) for m, index in enumerate(edge_pairs))
            blocks.append(edge_blocks)

    split_factors = jax.ShapeDtypeStruct((total * width, 2 * width), BF16)
    near, high, low, device_factor, group_factor, root_factor = pl.pallas_call(
        functools.partial(leaves_kernel, chunks, members, groups),
        out_shape=(
            jax.ShapeDtypeStruct(vectors.shape, BF16),
            split_factors,
            split_factors,
            square,
            square,
            square,
        ),
        in_specs=[hbm] * (len(parts) + 1) + [vmem] * 4,
        out_specs=(hbm,) + (vmem,) * 5,
        scratch_shapes=[
            pltpu.VMEM((width, width, 128), F32),
            pltpu.VMEM((total * STRIDE, 2 * width), F32),
            pltpu.SemaphoreType.DMA((2 + len(parts),)),
        ],
        compiler_params=room(20),
        name="leaves",
    )(*parts, edge_part, own_grams, halo_grams, gram, device_transfer)

    coupling = pl.pallas_call(
        functools.partial(far_kernel, plan),
        out_shape=jax.ShapeDtypeStruct((width, own * far_index.shape[1] * width), BF16),
        in_specs=[hbm] + [vmem] * (2 + len(blocks)),
        out_specs=hbm,
        scratch_shapes=[
            pltpu.SMEM(far_list.shape, jnp.int32),
            pltpu.VMEM((width, own * far_index.shape[1] * width), BF16),
            pltpu.SemaphoreType.DMA,
            pltpu.SemaphoreType.DMA((own // 8,)),
        ],
        compiler_params=room(16),
        name="far",
    )(far_list, high, low, *blocks)
    return near, coupling.T, device_factor, group_factor, root_factor


def solution(mesh):
    split = P(AXES, None)
    return jax.shard_map(
        per_device,
        mesh=mesh,
        in_specs=(P(None, AXES), split, split, split, split, split, P(AXES), split),
        out_specs=(split, split, split, split, split),
        check_vma=False,
    )
```

```python
import functools
import math

import jax
import jax.numpy as jnp
from jax import lax
from jax.experimental import pallas as pl
from jax.experimental.pallas import tpu as pltpu
from jax.sharding import PartitionSpec as P

LAYER = 4
PAD = 8
LONG_SQ = 2.25
RATIO = 25.0
SCALE = 0.5 / LONG_SQ
HALF = math.log(0.5)
OFF = -16384.0
STRIDE = 40
AXES = ("group", "sub")
F32 = jnp.float32
BF16 = jnp.bfloat16


def room(megabytes):
    return pltpu.CompilerParams(vmem_limit_bytes=int(megabytes * 1024 * 1024))


def split2(value):
    high = value.astype(BF16)
    return high, (value - high.astype(F32)).astype(BF16)


def split3(value):
    high = value.astype(BF16)
    rest = value - high.astype(F32)
    middle = rest.astype(BF16)
    return high, middle, (rest - middle.astype(F32)).astype(BF16)


def mm(left, right):
    return jnp.dot(left, right, preferred_element_type=F32)


def mm_nt(left, right):
    return lax.dot_general(left, right, (((1,), (1,)), ((), ())), preferred_element_type=F32)


def exact(left, right):
    return jnp.dot(left, right, precision=lax.Precision.HIGHEST, preferred_element_type=F32)


def iota(shape, dim):
    return lax.broadcasted_iota(jnp.int32, shape, dim)


def tree_kernel(
    points_in, basis_in, below_in, transfer_in, vectors,
    dense, top, outer, inner, points, basis, below, transfer, passing, packed, small, sems,
):
    width = basis.shape[0]
    count = basis.shape[1] // width
    halo = LAYER * width
    span = PAD * width
    rows = vectors.shape[0]
    odd = lax.axis_index("sub") % 2
    sides = ((outer, odd), (inner, 1 - odd))
    basis_copy, below_copy, points_copy, transfer_copy = loads = [
        pltpu.make_async_copy(source, target, sems.at[n])
        for n, (source, target) in enumerate(
            (
                (basis_in, basis),
                (below_in, below),
                (points_in, points),
                (transfer_in, transfer),
            )
        )
    ]
    vector_loads = [
        pltpu.make_async_copy(
            vectors.at[pl.ds(pl.multiple_of(last * (rows - halo), 16), halo), :],
            passing.at[n],
            sems.at[4 + n],
        )
        for n, (_, last) in enumerate(sides)
    ]
    copies = [
        pltpu.make_async_copy(passing.at[n], target.at[pl.ds(0, halo), :], sems.at[9 + n])
        for n, (target, _) in enumerate(sides)
    ]
    for copy in loads + vector_loads:
        copy.start()

    both = 2 * width
    lane = iota((width, 2 * both), 1)

    def times(above, columns):
        found = []
        for n in range(above.shape[1] // both):
            parts = jnp.concatenate(split3(above[:, n * both : (n + 1) * both]), axis=1)
            block = columns(n * 2 * both)
            zero = jnp.zeros_like(block)
            block = jnp.concatenate(
                [jnp.where(lane < both, block, zero), jnp.where(lane < both, zero, block)], axis=0
            )
            found.append(mm(parts, jnp.concatenate([block] * 3, axis=0)))
        return jnp.concatenate(found, axis=1)

    same = iota((both, both), 0) // width == iota((both, both), 1) // width
    half_block = jnp.where(same, 0.5, 0.0).astype(F32)
    basis_copy.wait()
    points_copy.wait()
    for n, (target, last) in enumerate(sides):
        bases = basis[:, count * width - span :], basis[:, 0:span]
        last_three, first_three = (
            jnp.concatenate(
                [block[:, (at + skip) * width : (at + skip + 3) * width] for at in (0, LAYER)],
                axis=1,
            )
            for skip, block in zip((1, 0), bases)
        )
        packed[n, 0:width, :] = jnp.where(last == 1, last_three, first_three)
        coords = jnp.where(last == 1, points[:, count * width - span :], points[:, 0:span])
        for m in range(2):
            high, low = split2(coords[:, m * halo : (m + 1) * halo])
            base = width + 16 * m
            packed[n, base : base + 16, :] = jnp.zeros((16, target.shape[1]), BF16)
            packed[n, base : base + 3, 0:halo] = high
            packed[n, base + 8 : base + 11, 0:halo] = low
        copies.append(
            pltpu.make_async_copy(
                packed.at[n], target.at[pl.ds(halo, width + 32), :], sems.at[6 + n]
            )
        )
        copies[-1].start()
    blocks = []
    for n in range(count // 4):
        stacked = jnp.concatenate(
            [basis[:, (2 * n + m) * both : (2 * n + m + 1) * both] for m in range(2)], axis=0
        )
        blocks.append(mm_nt(stacked, stacked) * half_block)
    below_copy.wait()
    halves = []
    for n, block in enumerate(blocks):
        t = below[:, n * both : (n + 1) * both]
        half = mm(jnp.concatenate([t, t, t], axis=1), jnp.concatenate(split3(block), axis=0))
        halves.append((half, t))
    blocks = []
    for n in range(0, len(halves), 2):
        (first, t), (second, u) = halves[n : n + 2]
        x = jnp.concatenate(split3(jnp.concatenate([first, second], axis=0)), axis=1)
        t = jnp.concatenate([t, u], axis=0)
        blocks.append(mm_nt(x, jnp.concatenate([t, t, t], axis=1)) * half_block)

    for load, copy in zip(vector_loads, copies[:2]):
        load.wait()
        copy.start()

    transfer_copy.wait()
    end = below.shape[1]
    tops = below[:, end - both : end]
    turned = jnp.concatenate(split3(transfer[...].T), axis=1)
    above = jnp.concatenate(
        [tops.astype(F32), mm(turned, jnp.concatenate([tops] * 3, axis=0))], axis=0
    )
    end -= both
    nodes = 4
    while nodes < count // 2:
        start = end - nodes * width
        above = times(above, lambda at, start=start: below[:, start + at : start + at + 2 * both])
        end = start
        nodes *= 2

    total = jnp.zeros((both, both), F32)
    for n, block in enumerate(blocks):
        rows = above[:, n * both : (n + 1) * both]
        high, middle, low = split3(rows)
        gh, gm, gl = split3(block)
        x = mm(
            jnp.concatenate([high, high, high, middle, middle, low], axis=1),
            jnp.concatenate([gh, gm, gl, gh, gm, gh], axis=0),
        )
        xh, xm, xl = split3(x)
        total = total + mm_nt(
            jnp.concatenate([xh, xh, xh, xm, xm, xl], axis=1),
            jnp.concatenate([high, middle, low, high, middle, high], axis=1),
        )
    total = total * (4.0 / count)
    small[0, :, :] = fold(total[:width, :width])
    halves = fold(total[width:, width:])
    small[1, :, :] = halves
    for n, target in enumerate((top, dense)):
        copies.append(pltpu.make_async_copy(small.at[n], target, sems.at[11 + n]))
        copies[-1].start()
    for copy in copies:
        copy.wait()


def factor_lanes(work, width):
    panels = width // 8
    row = iota((8, 128), 0)

    def spread(j, i):
        return jnp.broadcast_to(work[j, i : i + 1, :], (8, 128))

    for p in range(panels):
        at = 8 * p
        entry = {(k, m): spread(at + k, at + m) for k in range(8) for m in range(k, 8)}
        scales = []
        for k in range(8):
            scales.append(lax.rsqrt(entry[k, k]))
            for m in range(k + 1, 8):
                entry[k, m] = entry[k, m] * scales[k]
            for m in range(k + 1, 8):
                for q in range(m, 8):
                    entry[m, q] = entry[m, q] - entry[k, m] * entry[k, q]
        for i in range(p, panels):
            tile = [work[at + k, 8 * i : 8 * i + 8, :] for k in range(8)]
            for k in range(8):
                tile[k] = tile[k] * scales[k]
                for m in range(k + 1, 8):
                    tile[m] = tile[m] - tile[k] * entry[k, m]
            for k in range(8):
                work[at + k, 8 * i : 8 * i + 8, :] = (
                    jnp.where(row >= k, tile[k], 0.0) if i == p else tile[k]
                )
        for q in range(p + 1, panels):
            for start in range(q, panels, 4):
                group = range(start, min(start + 4, panels))
                accs = {
                    (i, k): work[8 * q + k, 8 * i : 8 * i + 8, :] for i in group for k in range(8)
                }
                for j in range(at, at + 8):
                    factors = [spread(j, 8 * q + k) for k in range(8)]
                    for i in group:
                        column = work[j, 8 * i : 8 * i + 8, :]
                        for k in range(8):
                            accs[i, k] = accs[i, k] - column * factors[k]
                for (i, k), value in accs.items():
                    work[8 * q + k, 8 * i : 8 * i + 8, :] = value


def fold(matrix):
    half = matrix.shape[0] // 2
    return jnp.concatenate([matrix[:half], matrix[half:]], axis=1)


def unfold(matrix):
    half = matrix.shape[1] // 2
    return jnp.concatenate([matrix[:, :half], matrix[:, half:]], axis=0)


def from_lanes(work, factors, width, many):
    for i in range(width // 2):
        both = []
        for j in (i, i + width // 2):
            skip = j // 8 * 8
            both += [jnp.zeros((skip, many), F32)] * bool(skip) + [work[j, skip:, 0:many]]
        factors[pl.ds(i, many, stride=STRIDE), :] = jnp.concatenate(both, axis=0).T


def gaussians(exponent):
    return jnp.exp(exponent) + jnp.exp(exponent * RATIO - RATIO * HALF)


def features(place, leaf, center):
    sub = iota(place.shape, 0)
    corner = jnp.where(sub == 0, leaf % 2 - 1, leaf // 2 % 2 - 1)
    corner = jnp.where(sub == 2, leaf // LAYER - center, corner)
    place = jnp.where(sub < 3, place + corner.astype(F32), 0.0)
    norm = jnp.sum(place * place, axis=0, keepdims=True) * SCALE
    first = jnp.where(sub == 3, -norm, jnp.where(sub == 4, 1.0, place))
    second = jnp.where(
        sub == 3, 1.0, jnp.where(sub == 4, HALF - norm, place * (2.0 * SCALE))
    )
    fh, fm, fl = [v.astype(F32) for v in split3(first)]
    sh, sm, sl = [v.astype(F32) for v in split3(second)]
    return (
        jnp.concatenate([fh, fh, fh, fm, fm, fl], axis=0),
        jnp.concatenate([sh, sm, sl, sh, sm, sh], axis=0),
    )


def rows_of(second):
    blank = jnp.zeros((16, second.shape[1]), F32)
    return jnp.concatenate([second, blank, second, blank], axis=0).T.astype(BF16)


def near_weights(first_rows, second, switches, index, halo):
    group = index // 4 * 16
    columns = jnp.concatenate([second, switches[group : group + 16, :]], axis=0)
    return gaussians(mm(first_rows[index * halo : (index + 1) * halo, :], columns)).astype(BF16)


def prepare(
    points, near_list, near_used, first_rows, first_cols, second_cols, second_rows, switches, place
):
    rows = points.shape[1]
    own = near_list.shape[1]
    width = rows // own
    place[...] = jnp.zeros(place.shape, F32)
    place[0:3, :] = points[...]
    leaf = iota((8, rows), 1) // width
    first, second = features(place[...], leaf, own // LAYER // 2)
    hot_leaf = iota((16, rows), 1) // width
    hot = jnp.where(hot_leaf % 16 == iota((16, rows), 0), 1.0, 0.0).astype(F32)
    first = jnp.concatenate([first, hot], axis=0)
    first_cols[...] = first.astype(BF16)
    second_cols[...] = second.astype(BF16)
    first_rows[...] = first.T.astype(BF16)
    second_rows[...] = rows_of(second)

    start_leaf = lax.axis_index(AXES) * own
    target = iota((1, own), 1)
    base_leaf = start_leaf + target // LAYER * LAYER - LAYER
    found = jnp.zeros((16, own), jnp.bool_)
    place_row = iota((16, own), 0)
    for n in range(near_list.shape[0]):
        spot = jnp.where(near_used[...] > n, near_list[n : n + 1, :] - base_leaf, -1)
        found = jnp.logical_or(found, place_row == spot)
    bias = jnp.where(found, 0.0, OFF).astype(F32)
    span = 3 * LAYER * width
    expand = jnp.where(iota((16, span), 0) == iota((16, span), 1) // width, 1.0, 0.0)
    switches[...] = mm(bias.T.astype(BF16), expand.astype(BF16)).astype(BF16)


def inner_layers(layers, vectors, first_rows, second_cols, switches, out, halo):
    for n, index in enumerate(layers):
        around = slice((index - 1) * halo, (index + 2) * halo)
        weights = near_weights(first_rows, second_cols[:, around], switches, index, halo)
        out[n * halo : (n + 1) * halo, :] = mm(weights, vectors[around, :]).astype(BF16)


def far_blocks(pairs, far_list, second_rows, first_cols, out, width, base, places):
    far, own = far_list.shape
    both = 2 * width
    start_leaf = lax.axis_index(AXES) * own
    square = iota((both, both), 0) // width == iota((both, both), 1) // width
    lane = iota((far * width, both), 1) < width
    exponents = []
    for index in pairs:
        t = 2 * index
        picked = []
        for m in range(2):
            spots = [
                pl.multiple_of((far_list[f, t + m] - start_leaf + base) * width, width)
                for f in range(far)
            ]
            picked.append(
                jnp.concatenate([second_rows[pl.ds(spot, width), :] for spot in spots], axis=0)
            )
        cols = first_cols[:, t * width : t * width + both]
        targets = jnp.where(
            square, jnp.concatenate([cols, cols], axis=0), jnp.zeros((both, both), BF16)
        )
        exponents.append(mm(jnp.where(lane, picked[0], picked[1]), targets))
    for place, exponent in zip(places, exponents):
        high, low = split2(gaussians(exponent))
        at = place * far * width
        out[at : at + far * width, 0:both] = high
        out[at : at + far * width, both : 2 * both] = low


def first_chunk_kernel(layers):
    def body(
        points, near_list, near_used, vectors,
        out, first_rows, first_cols, second_cols, second_rows, switches, place,
    ):
        prepare(
            points,
            near_list,
            near_used,
            first_rows,
            first_cols,
            second_cols,
            second_rows,
            switches,
            place,
        )
        halo = LAYER * points.shape[1] // near_list.shape[1]
        inner_layers(layers, vectors, first_rows, second_cols, switches, out, halo)

    return body


def chunk_kernel(layers, pairs, halo, width):
    def body(after, far_in, *refs):
        first_rows, second_cols, switches, vectors, first_cols, second_rows = refs[:6]
        outs, far_list, sem = refs[6:-2], refs[-2], refs[-1]
        if pairs:
            copy = pltpu.make_async_copy(far_in, far_list, sem)
            copy.start()
        if layers:
            inner_layers(layers, vectors, first_rows, second_cols, switches, outs[0], halo)
        if pairs:
            copy.wait()
            far_blocks(
                pairs, far_list, second_rows, first_cols, outs[-1], width, 0, range(len(pairs))
            )

    return body


def edges_kernel(
    pairs, after, far_in, inner, outer, first_rows, second_cols, switches, vectors,
    first_cols, own_rows, top,
    out, blocks, grams, ends, sides, place, halo_cols, far_list, second_rows, sems,
):
    halo = ends.shape[1]
    width = halo // LAYER
    own = vectors.shape[0] // width
    layers = own // LAYER
    extra = sides.shape[1]
    odd = lax.axis_index("sub") % 2
    arrived = ((inner, 1 - odd), (outer, odd))
    side_copies = [
        pltpu.make_async_copy(
            block.at[pl.ds(halo, extra), :], sides.at[side], sems.at[n]
        )
        for n, (block, side) in enumerate(arrived)
    ]
    end_copies = [
        pltpu.make_async_copy(block.at[pl.ds(0, halo), :], ends.at[side], sems.at[2 + n])
        for n, (block, side) in enumerate(arrived)
    ]
    list_copy = pltpu.make_async_copy(far_in, far_list, sems.at[4])
    for copy in side_copies + end_copies + [list_copy]:
        copy.start()
    lanes = PAD * width
    second_rows[lanes : lanes + own * width, :] = own_rows[...]
    place[...] = jnp.zeros(place.shape, F32)
    for copy in side_copies:
        copy.wait()
    for side, first_leaf in enumerate((-PAD, own)):
        for n in range(2):
            base = width + 16 * n
            values = sides[side, base : base + 16, 0:halo].astype(F32)
            place[0:3, n * halo : (n + 1) * halo] = values[0:3, :] + values[8:11, :]
        leaf = iota((8, lanes), 1) // width + (first_leaf + PAD)
        second = features(place[...], leaf, layers // 2 + PAD // LAYER)[1]
        halo_cols[side, :, :] = second.astype(BF16)
        at = (PAD + first_leaf) * width
        second_rows[at : at + lanes, :] = rows_of(second)
        for n in range(6):
            piece = sides[side, 0:width, n * width : (n + 1) * width]
            at = (6 * side + n) * STRIDE
            grams[at : at + width // 2, :] = fold(mm_nt(piece, piece))
    for n in range(12, 16):
        grams[n * STRIDE : n * STRIDE + width // 2, :] = top[...]
    weights = [
        near_weights(
            first_rows, jnp.concatenate(columns, axis=1), switches, index, halo
        )
        for index, columns in (
            (0, [halo_cols[0, :, halo:], second_cols[:, 0 : 2 * halo]]),
            (layers - 1, [second_cols[:, (layers - 2) * halo :], halo_cols[1, :, 0:halo]]),
        )
    ]
    for copy in end_copies:
        copy.wait()
    value = mm(weights[0][:, 0:halo], ends[0, :, :])
    value = value + mm(weights[0][:, halo:], vectors[0 : 2 * halo, :])
    out[0:halo, :] = value.astype(BF16)
    value = mm(weights[1][:, 0 : 2 * halo], vectors[(layers - 2) * halo :, :])
    value = value + mm(weights[1][:, 2 * halo :], ends[1, :, :])
    out[halo:, :] = value.astype(BF16)
    list_copy.wait()
    far_blocks(pairs, far_list, second_rows, first_cols, blocks, width, PAD, range(len(pairs)))


def own_chunk_kernel(layers, pairs):
    def body(
        after, far_in, first_rows, second_cols, switches, vectors, first_cols, second_rows, basis,
        out, blocks, grams, far_list, sem,
    ):
        copy = pltpu.make_async_copy(far_in, far_list, sem)
        copy.start()
        width = basis.shape[0]
        own = basis.shape[1] // width
        both = 2 * width
        inner_layers(layers, vectors, first_rows, second_cols, switches, out, LAYER * width)
        lane = iota((width, both), 1)
        for n in range(own // 2):
            pair = basis[:, n * both : (n + 1) * both]
            zero = jnp.zeros_like(pair)
            stacked = jnp.concatenate(
                [jnp.where(lane < width, pair, zero), jnp.where(lane < width, zero, pair)], axis=0
            )
            value = mm_nt(stacked, pair)
            for m in range(2):
                at = (2 * n + m) * STRIDE
                grams[at : at + width // 2, :] = fold(value[m * width : (m + 1) * width])

        copy.wait()
        far_blocks(pairs, far_list, second_rows, first_cols, blocks, width, 0, range(len(pairs)))

    return body


def leaves_kernel(chunks, members, groups, *refs):
    outer_count = len(chunks) + 1
    near_parts = refs[:outer_count]
    (
        own_grams,
        halo_grams,
        upper,
        transfer,
        near,
        high,
        low,
        device_factor,
        group_factor,
        root_factor,
        work,
        factors,
        sems,
    ) = refs[outer_count:]
    width = transfer.shape[0]
    total = high.shape[0] // width
    own = total - 2 * PAD
    halo = LAYER * width
    layers = own // LAYER
    both = 2 * width
    places = [(part, 0, chunk[0], len(chunk)) for part, chunk in zip(near_parts, chunks)]
    places += [(near_parts[-1], n, index, 1) for n, index in enumerate((0, layers - 1))]
    near_copies = [
        pltpu.make_async_copy(
            part.at[pl.ds(start * halo, many * halo), :],
            near.at[pl.ds(index * halo, many * halo), :],
            sems.at[n],
        )
        for n, (part, start, index, many) in enumerate(places)
    ]
    for copy in near_copies:
        copy.start()

    spare = (own + 13, own + 14)
    means = (
        upper[0 : width // 2, :] * (1.0 / members),
        upper[width // 2 :, :] * (1.0 / (members * groups)),
    )
    spot_row = iota((2 * PAD, both), 0)
    for i in range(width // 2):
        rows = halo_grams[pl.ds(i, 2 * PAD, stride=STRIDE), :]
        for spot, mean in zip(spare, means):
            rows = jnp.where(spot_row == spot - own, mean[i : i + 1, :], rows)
        turned = jnp.concatenate([own_grams[pl.ds(i, own, stride=STRIDE), :], rows], axis=0).T
        work[i, :, 0:total] = turned[0:width]
        work[i + width // 2, :, 0:total] = turned[width:]
    factor_lanes(work, width)
    from_lanes(work, factors, width, total)
    at = (own + 12) * STRIDE
    device_factor[...] = exact(unfold(factors[at : at + width // 2, :]), transfer[...])
    for target, spot in zip((group_factor, root_factor), spare):
        target[...] = unfold(factors[spot * STRIDE : spot * STRIDE + width // 2, :])
    left_lanes = iota((width // 2, both), 1) < width
    spots = [(PAD + t, t) for t in range(own)]
    spots += [(spot, own + n) for n, spot in enumerate((1, 2, 3, 5, 6, 7))]
    spots += [(PAD + own + m, own + 6 + n) for n, m in enumerate((0, 1, 2, 4, 5, 6))]
    for spot, n in spots:
        rows = factors[n * STRIDE : n * STRIDE + width // 2, :]
        turned = pltpu.roll(rows, width, 1)
        twice = jnp.concatenate(
            [jnp.where(left_lanes, rows, turned), jnp.where(left_lanes, turned, rows)], axis=0
        )
        at = slice(spot * width, (spot + 1) * width)
        high[at, :], low[at, :] = split2(twice)
    for copy in near_copies:
        copy.wait()


def far_kernel(plan, far_in, high, low, *refs):
    blocks, (coupling, far_list, lines, sem, sems) = refs[:-5], refs[-5:]
    copy = pltpu.make_async_copy(far_in, far_list, sem)
    copy.start()
    width = coupling.shape[0]
    far, own = far_list.shape
    both = 2 * width
    start_leaf = lax.axis_index(AXES) * own
    square = iota((both, both), 0) // width == iota((both, both), 1) // width
    lane = iota((width, both), 1) < width
    zero = jnp.zeros((both, both), BF16)

    def diagonal(value):
        return jnp.where(square, value, zero)

    copies = []
    for start in range(0, own // 2, 4):
        indices = range(start, start + 4)
        halves = []
        for index in indices:
            source, place = plan[index]
            at = place * far * width
            kh = blocks[source][at : at + far * width, 0:both]
            kl = blocks[source][at : at + far * width, both : 2 * both]
            at = (PAD + 2 * index) * width
            rh = diagonal(high[at : at + both, :])
            rl = diagonal(low[at : at + both, :])
            halves.append(
                mm_nt(
                    jnp.concatenate([kh, kl, kh], axis=1), jnp.concatenate([rh, rh, rl], axis=1)
                )
            )
        if start == 0:
            copy.wait()
        outs = []
        for index, half in zip(indices, halves):
            zh, zl = split2(half * (1.0 / width))
            for f in range(far):
                spots = [
                    pl.multiple_of((far_list[f, 2 * index + m] - start_leaf + PAD) * width, width)
                    for m in range(2)
                ]
                sh, sl = (
                    jnp.where(lane, *(part[pl.ds(spot, width), :] for spot in spots))
                    for part in (high, low)
                )
                a = slice(f * width, (f + 1) * width)
                ph = diagonal(jnp.concatenate([zh[a], zh[a]], axis=0))
                plow = diagonal(jnp.concatenate([zl[a], zl[a]], axis=0))
                outs.append(
                    mm(
                        jnp.concatenate([sh, sh, sl], axis=1),
                        jnp.concatenate([ph, plow, ph], axis=0),
                    )
                )
        for n, index in enumerate(indices):
            three = outs[n * far : (n + 1) * far]
            line = jnp.concatenate(
                [out[:, 0:width] for out in three] + [out[:, width:both] for out in three], axis=1
            )
            at = index * 2 * far * width
            lines[:, at : at + 2 * far * width] = line.astype(BF16)
        group = pl.ds(start * 2 * far * width, 8 * far * width)
        copies.append(
            pltpu.make_async_copy(lines.at[:, group], coupling.at[:, group], sems.at[start // 4])
        )
        copies[-1].start()
    for copy in copies:
        copy.wait()


def swap_inner(block):
    return lax.ppermute(block, AXES, [(i, i ^ 1) for i in range(lax.axis_size(AXES))])


def swap_outer(block):
    many = lax.axis_size(AXES)
    return lax.ppermute(block, AXES, [(i, (i + 1 if i % 2 else i - 1) % many) for i in range(many)])


def exchange(value, distance):
    pairs = [(i, i ^ distance ^ 1) for i in range(lax.axis_size(AXES))]
    return value + lax.ppermute(value, AXES, pairs)


def per_device(
    points, leaf_basis, inner_transfer, device_transfer, vectors, near_index, near_count, far_index
):
    own = near_index.shape[0]
    width = leaf_basis.shape[1]
    columns = vectors.shape[1]
    halo = LAYER * width
    half = width // 2
    layers = own // LAYER
    total = own + 2 * PAD
    members, groups = lax.axis_size("sub"), lax.axis_size("group")
    vmem = pl.BlockSpec(memory_space=pltpu.VMEM)
    hbm = pl.BlockSpec(memory_space=pl.ANY)
    square = jax.ShapeDtypeStruct((width, width), F32)
    extra = halo + width + 32

    def block_of(rows):
        return jax.ShapeDtypeStruct((rows, columns), BF16)

    basis = leaf_basis.T
    near_list, far_list = near_index.T, far_index.T
    cost = pl.CostEstimate(flops=10**9, bytes_accessed=4 * 10**6, transcendentals=10**6)

    dense, top, to_outer, to_inner = pl.pallas_call(
        tree_kernel,
        out_shape=(
            jax.ShapeDtypeStruct((half, 2 * width), F32),
            jax.ShapeDtypeStruct((half, 2 * width), F32),
            block_of(extra),
            block_of(extra),
        ),
        in_specs=[hbm] * 5,
        out_specs=(hbm,) * 4,
        scratch_shapes=[
            pltpu.VMEM((3, own * width), F32),
            pltpu.VMEM((width, own * width), BF16),
            pltpu.VMEM((width, (own - 2) * width), BF16),
            pltpu.VMEM((width, width), F32),
            pltpu.VMEM((2, halo, columns), BF16),
            pltpu.VMEM((2, width + 32, columns), BF16),
            pltpu.VMEM((2, half, 2 * width), F32),
            pltpu.SemaphoreType.DMA((13,)),
        ],
        compiler_params=room(60),
        name="tree",
    )(points, basis, inner_transfer.T, device_transfer, vectors)
    pair_gram = gram = exchange(dense, 0)

    sub_bits = members.bit_length() - 1
    steps = [members << bit for bit in range(groups.bit_length() - 1)]
    steps += [1 << bit for bit in range(1, sub_bits)]
    inner_pairs = list(range(PAD // 2, (own - PAD) // 2))
    few = len(inner_pairs) // 2
    edge_pairs = [index for index in range(own // 2) if index not in inner_pairs]
    chunks = [[1, 2], [3, 4, 5], [6]]
    pair_chunks = [[], inner_pairs[:few], inner_pairs[few:]]
    blocks, plan, parts = [], {}, []

    def part_shape(count):
        return jax.ShapeDtypeStruct((count * halo, columns), BF16)

    def block_shape(count):
        return jax.ShapeDtypeStruct((count * far_index.shape[1] * width, 4 * width), BF16)

    late_points, gram = lax.optimization_barrier((points, gram))
    part, *shared = pl.pallas_call(
        first_chunk_kernel(chunks[0]),
        out_shape=(
            part_shape(len(chunks[0])),
            jax.ShapeDtypeStruct((own * width, 64), BF16),
            jax.ShapeDtypeStruct((64, own * width), BF16),
            jax.ShapeDtypeStruct((48, own * width), BF16),
            jax.ShapeDtypeStruct((own * width, 128), BF16),
            jax.ShapeDtypeStruct((own, 3 * halo), BF16),
        ),
        in_specs=[vmem] * 4,
        out_specs=(vmem,) * 6,
        scratch_shapes=[pltpu.VMEM((8, own * width), F32)],
        compiler_params=room(10),
        cost_estimate=cost,
        name="chunk_0",
    )(late_points, near_list, near_count.reshape(1, own), vectors)
    parts.append(part)
    gram, to_inner, to_outer = lax.optimization_barrier((gram, to_inner, to_outer))
    from_inner = swap_inner(to_inner)
    from_outer = swap_outer(to_outer)
    first_rows, first_cols, second_cols, second_rows, switches = shared
    jobs = ["first", 1, 2, "edges"]
    for n in range(max(len(steps), len(jobs))):
        if n < len(jobs) and jobs[n] == "edges":
            gram, from_outer = lax.optimization_barrier((gram, from_outer))
        before = gram
        if n < len(steps):
            if n == len(steps) - sub_bits + 1:
                gram = before = jnp.concatenate([pair_gram, gram], axis=0)
            gram = exchange(gram, steps[n])
        job = jobs[n] if n < len(jobs) else None
        if job == "first":
            gram, parts[0] = lax.optimization_barrier((gram, parts[0]))
        elif job == 1:
            layer_chunk, pair_chunk = chunks[job], pair_chunks[job]
            shapes = [part_shape(len(layer_chunk))] * bool(layer_chunk)
            shapes += [block_shape(len(pair_chunk))] * bool(pair_chunk)
            outs = pl.pallas_call(
                chunk_kernel(layer_chunk, pair_chunk, halo, width),
                out_shape=tuple(shapes),
                in_specs=[hbm] * 2 + [vmem] * 6,
                out_specs=(vmem,) * len(shapes),
                scratch_shapes=[
                    pltpu.SMEM(far_list.shape, jnp.int32),
                    pltpu.SemaphoreType.DMA,
                ],
                compiler_params=room(10),
                cost_estimate=cost,
                name=f"chunk_{job}",
            )(before, far_list, first_rows, second_cols, switches, vectors, first_cols, second_rows)
            gram, outs = lax.optimization_barrier((gram, outs))
            if layer_chunk:
                parts.append(outs[0])
            if pair_chunk:
                plan.update((index, (len(blocks), m)) for m, index in enumerate(pair_chunk))
                blocks.append(outs[-1])
        elif job == 2:
            part, own_blocks, own_grams = pl.pallas_call(
                own_chunk_kernel(chunks[2], pair_chunks[2]),
                out_shape=(
                    part_shape(len(chunks[2])),
                    block_shape(len(pair_chunks[2])),
                    jax.ShapeDtypeStruct((own * STRIDE, 2 * width), F32),
                ),
                in_specs=[hbm] * 2 + [vmem] * 7,
                out_specs=(vmem,) * 3,
                scratch_shapes=[
                    pltpu.SMEM(far_list.shape, jnp.int32),
                    pltpu.SemaphoreType.DMA,
                ],
                compiler_params=room(10),
                cost_estimate=cost,
                name="chunk_2",
            )(
                before,
                far_list,
                first_rows,
                second_cols,
                switches,
                vectors,
                first_cols,
                second_rows,
                basis,
            )
            gram, part = lax.optimization_barrier((gram, part))
            parts.append(part)
            plan.update((index, (len(blocks), m)) for m, index in enumerate(pair_chunks[2]))
            blocks.append(own_blocks)
        elif job == "edges":
            edge_part, edge_blocks, halo_grams = pl.pallas_call(
                functools.partial(edges_kernel, edge_pairs),
                out_shape=(
                    part_shape(2),
                    block_shape(len(edge_pairs)),
                    jax.ShapeDtypeStruct((2 * PAD * STRIDE, 2 * width), F32),
                ),
                in_specs=[hbm] * 4 + [vmem] * 7,
                out_specs=(vmem,) * 3,
                scratch_shapes=[
                    pltpu.VMEM((2, halo, columns), BF16),
                    pltpu.VMEM((2, width + 32, columns), BF16),
                    pltpu.VMEM((8, PAD * width), F32),
                    pltpu.VMEM((2, 48, PAD * width), BF16),
                    pltpu.SMEM(far_list.shape, jnp.int32),
                    pltpu.VMEM((total * width, 2 * width), BF16),
                    pltpu.SemaphoreType.DMA((5,)),
                ],
                compiler_params=room(14),
                cost_estimate=cost,
                name="edges",
            )(
                before,
                far_list,
                from_inner,
                from_outer,
                first_rows,
                second_cols,
                switches,
                vectors,
                first_cols,
                second_rows,
                top,
            )
            gram, edge_part = lax.optimization_barrier((gram, edge_part))
            plan.update((index, (len(blocks), m)) for m, index in enumerate(edge_pairs))
            blocks.append(edge_blocks)

    split_factors = jax.ShapeDtypeStruct((total * width, 2 * width), BF16)
    near, high, low, device_factor, group_factor, root_factor = pl.pallas_call(
        functools.partial(leaves_kernel, chunks, members, groups),
        out_shape=(
            jax.ShapeDtypeStruct(vectors.shape, BF16),
            split_factors,
            split_factors,
            square,
            square,
            square,
        ),
        in_specs=[hbm] * (len(parts) + 1) + [vmem] * 4,
        out_specs=(hbm,) + (vmem,) * 5,
        scratch_shapes=[
            pltpu.VMEM((width, width, 128), F32),
            pltpu.VMEM((total * STRIDE, 2 * width), F32),
            pltpu.SemaphoreType.DMA((2 + len(parts),)),
        ],
        compiler_params=room(20),
        name="leaves",
    )(*parts, edge_part, own_grams, halo_grams, gram, device_transfer)

    coupling = pl.pallas_call(
        functools.partial(far_kernel, plan),
        out_shape=jax.ShapeDtypeStruct((width, own * far_index.shape[1] * width), BF16),
        in_specs=[hbm] + [vmem] * (2 + len(blocks)),
        out_specs=hbm,
        scratch_shapes=[
            pltpu.SMEM(far_list.shape, jnp.int32),
            pltpu.VMEM((width, own * far_index.shape[1] * width), BF16),
            pltpu.SemaphoreType.DMA,
            pltpu.SemaphoreType.DMA((own // 8,)),
        ],
        compiler_params=room(16),
        name="far",
    )(far_list, high, low, *blocks)
    return near, coupling.T, device_factor, group_factor, root_factor


def solution(mesh):
    split = P(AXES, None)
    return jax.shard_map(
        per_device,
        mesh=mesh,
        in_specs=(P(None, AXES), split, split, split, split, split, P(AXES), split),
        out_specs=(split, split, split, split, split),
        check_vma=False,
    )
```

```python
import functools
import math

import jax
import jax.numpy as jnp
from jax import lax
from jax.experimental import pallas as pl
from jax.experimental.pallas import tpu as pltpu
from jax.sharding import PartitionSpec as P

LAYER = 4
PAD = 8
LONG_SQ = 2.25
RATIO = 25.0
SCALE = 0.5 / LONG_SQ
HALF = math.log(0.5)
OFF = -16384.0
STRIDE = 40
AXES = ("group", "sub")
F32 = jnp.float32
BF16 = jnp.bfloat16


def room(megabytes):
    return pltpu.CompilerParams(vmem_limit_bytes=int(megabytes * 1024 * 1024))


def split2(value):
    high = value.astype(BF16)
    return high, (value - high.astype(F32)).astype(BF16)


def split3(value):
    high = value.astype(BF16)
    rest = value - high.astype(F32)
    middle = rest.astype(BF16)
    return high, middle, (rest - middle.astype(F32)).astype(BF16)


def mm(left, right):
    return jnp.dot(left, right, preferred_element_type=F32)


def mm_nt(left, right):
    return lax.dot_general(left, right, (((1,), (1,)), ((), ())), preferred_element_type=F32)


def exact(left, right):
    return jnp.dot(left, right, precision=lax.Precision.HIGHEST, preferred_element_type=F32)


def iota(shape, dim):
    return lax.broadcasted_iota(jnp.int32, shape, dim)


def tree_kernel(
    points_in, basis_in, below_in, transfer_in, vectors,
    dense, top, outer, inner, points, basis, below, transfer, passing, packed, staged, small, sems,
):
    width = basis.shape[0]
    count = basis.shape[1] // width
    halo = LAYER * width
    span = PAD * width
    rows = vectors.shape[0]
    odd = lax.axis_index("sub") % 2
    sides = ((outer, odd), (inner, 1 - odd))
    basis_copy, below_copy, points_copy, transfer_copy = loads = [
        pltpu.make_async_copy(source, target, sems.at[n])
        for n, (source, target) in enumerate(
            (
                (basis_in, basis),
                (below_in, below),
                (points_in, points),
                (transfer_in, transfer),
            )
        )
    ]
    vector_loads = [
        pltpu.make_async_copy(
            vectors.at[pl.ds(pl.multiple_of(last * (rows - halo), 16), halo), :],
            passing.at[n],
            sems.at[4 + n],
        )
        for n, (_, last) in enumerate(sides)
    ]
    copies = [
        pltpu.make_async_copy(passing.at[n], target.at[pl.ds(0, halo), :], sems.at[9 + n])
        for n, (target, _) in enumerate(sides)
    ]
    for copy in loads + vector_loads:
        copy.start()

    both = 2 * width
    lane = iota((width, 2 * both), 1)

    def times(above, columns):
        found = []
        for n in range(above.shape[1] // both):
            parts = jnp.concatenate(split3(above[:, n * both : (n + 1) * both]), axis=1)
            block = columns(n * 2 * both)
            zero = jnp.zeros_like(block)
            block = jnp.concatenate(
                [jnp.where(lane < both, block, zero), jnp.where(lane < both, zero, block)], axis=0
            )
            found.append(mm(parts, jnp.concatenate([block] * 3, axis=0)))
        return jnp.concatenate(found, axis=1)

    same = iota((both, both), 0) // width == iota((both, both), 1) // width
    half_block = jnp.where(same, 0.5, 0.0).astype(F32)
    basis_copy.wait()
    points_copy.wait()
    for n, (target, last) in enumerate(sides):
        bases = basis[:, count * width - span :], basis[:, 0:span]
        last_three, first_three = (
            jnp.concatenate(
                [block[:, (at + skip) * width : (at + skip + 3) * width] for at in (0, LAYER)],
                axis=1,
            )
            for skip, block in zip((1, 0), bases)
        )
        packed[n, 0:width, :] = jnp.where(last == 1, last_three, first_three)
        coords = jnp.where(last == 1, points[:, count * width - span :], points[:, 0:span])
        for m in range(2):
            high, low = split2(coords[:, m * halo : (m + 1) * halo])
            base = width + 16 * m
            packed[n, base : base + 16, :] = jnp.zeros((16, target.shape[1]), BF16)
            packed[n, base : base + 3, 0:halo] = high
            packed[n, base + 8 : base + 11, 0:halo] = low
        copies.append(
            pltpu.make_async_copy(
                packed.at[n], target.at[pl.ds(halo, width + 32), :], sems.at[6 + n]
            )
        )
        copies[-1].start()
    blocks = []
    for n in range(count // 4):
        stacked = jnp.concatenate(
            [basis[:, (2 * n + m) * both : (2 * n + m + 1) * both] for m in range(2)], axis=0
        )
        blocks.append(mm_nt(stacked, stacked) * half_block)
    below_copy.wait()
    halves = []
    for n, block in enumerate(blocks):
        t = below[:, n * both : (n + 1) * both]
        half = mm(jnp.concatenate([t, t, t], axis=1), jnp.concatenate(split3(block), axis=0))
        halves.append((half, t))
    blocks = []
    for n in range(0, len(halves), 2):
        (first, t), (second, u) = halves[n : n + 2]
        x = jnp.concatenate(split3(jnp.concatenate([first, second], axis=0)), axis=1)
        t = jnp.concatenate([t, u], axis=0)
        blocks.append(mm_nt(x, jnp.concatenate([t, t, t], axis=1)) * half_block)

    for load, copy in zip(vector_loads, copies[:2]):
        load.wait()
        copy.start()

    transfer_copy.wait()
    end = below.shape[1]
    tops = below[:, end - both : end]
    turned = jnp.concatenate(split3(transfer[...].T), axis=1)
    above = jnp.concatenate(
        [tops.astype(F32), mm(turned, jnp.concatenate([tops] * 3, axis=0))], axis=0
    )
    end -= both
    nodes = 4
    while nodes < count // 2:
        start = end - nodes * width
        above = times(above, lambda at, start=start: below[:, start + at : start + at + 2 * both])
        end = start
        nodes *= 2

    total = jnp.zeros((both, both), F32)
    for n, block in enumerate(blocks):
        rows = above[:, n * both : (n + 1) * both]
        high, middle, low = split3(rows)
        gh, gm, gl = split3(block)
        x = mm(
            jnp.concatenate([high, high, high, middle, middle, low], axis=1),
            jnp.concatenate([gh, gm, gl, gh, gm, gh], axis=0),
        )
        xh, xm, xl = split3(x)
        total = total + mm_nt(
            jnp.concatenate([xh, xh, xh, xm, xm, xl], axis=1),
            jnp.concatenate([high, middle, low, high, middle, high], axis=1),
        )
    total = total * (4.0 / count)
    small[0, :, :] = fold(total[:width, :width])
    halves = fold(total[width:, width:])
    small[1, :, :] = halves
    staged[...] = jnp.concatenate(split3(halves), axis=1)
    copies.append(
        pltpu.make_async_copy(
            staged, inner.at[pl.ds(halo + width + 32, width // 2), :], sems.at[8]
        )
    )
    copies[-1].start()
    for n, target in enumerate((top, dense)):
        copies.append(pltpu.make_async_copy(small.at[n], target, sems.at[11 + n]))
        copies[-1].start()
    for copy in copies:
        copy.wait()


def factor_lanes(work, width):
    panels = width // 8
    row = iota((8, 128), 0)

    def spread(j, i):
        return jnp.broadcast_to(work[j, i : i + 1, :], (8, 128))

    for p in range(panels):
        at = 8 * p
        entry = {(k, m): spread(at + k, at + m) for k in range(8) for m in range(k, 8)}
        scales = []
        for k in range(8):
            scales.append(lax.rsqrt(entry[k, k]))
            for m in range(k + 1, 8):
                entry[k, m] = entry[k, m] * scales[k]
            for m in range(k + 1, 8):
                for q in range(m, 8):
                    entry[m, q] = entry[m, q] - entry[k, m] * entry[k, q]
        for i in range(p, panels):
            tile = [work[at + k, 8 * i : 8 * i + 8, :] for k in range(8)]
            for k in range(8):
                tile[k] = tile[k] * scales[k]
                for m in range(k + 1, 8):
                    tile[m] = tile[m] - tile[k] * entry[k, m]
            for k in range(8):
                work[at + k, 8 * i : 8 * i + 8, :] = (
                    jnp.where(row >= k, tile[k], 0.0) if i == p else tile[k]
                )
        for q in range(p + 1, panels):
            for start in range(q, panels, 4):
                group = range(start, min(start + 4, panels))
                accs = {
                    (i, k): work[8 * q + k, 8 * i : 8 * i + 8, :] for i in group for k in range(8)
                }
                for j in range(at, at + 8):
                    factors = [spread(j, 8 * q + k) for k in range(8)]
                    for i in group:
                        column = work[j, 8 * i : 8 * i + 8, :]
                        for k in range(8):
                            accs[i, k] = accs[i, k] - column * factors[k]
                for (i, k), value in accs.items():
                    work[8 * q + k, 8 * i : 8 * i + 8, :] = value


def fold(matrix):
    half = matrix.shape[0] // 2
    return jnp.concatenate([matrix[:half], matrix[half:]], axis=1)


def unfold(matrix):
    half = matrix.shape[1] // 2
    return jnp.concatenate([matrix[:, :half], matrix[:, half:]], axis=0)


def from_lanes(work, factors, width, many):
    for i in range(width // 2):
        both = []
        for j in (i, i + width // 2):
            skip = j // 8 * 8
            both += [jnp.zeros((skip, many), F32)] * bool(skip) + [work[j, skip:, 0:many]]
        factors[pl.ds(i, many, stride=STRIDE), :] = jnp.concatenate(both, axis=0).T


def gaussians(exponent):
    return jnp.exp(exponent) + jnp.exp(exponent * RATIO - RATIO * HALF)


def features(place, leaf, center):
    sub = iota(place.shape, 0)
    corner = jnp.where(sub == 0, leaf % 2 - 1, leaf // 2 % 2 - 1)
    corner = jnp.where(sub == 2, leaf // LAYER - center, corner)
    place = jnp.where(sub < 3, place + corner.astype(F32), 0.0)
    norm = jnp.sum(place * place, axis=0, keepdims=True) * SCALE
    first = jnp.where(sub == 3, -norm, jnp.where(sub == 4, 1.0, place))
    second = jnp.where(
        sub == 3, 1.0, jnp.where(sub == 4, HALF - norm, place * (2.0 * SCALE))
    )
    fh, fm, fl = [v.astype(F32) for v in split3(first)]
    sh, sm, sl = [v.astype(F32) for v in split3(second)]
    return (
        jnp.concatenate([fh, fh, fh, fm, fm, fl], axis=0),
        jnp.concatenate([sh, sm, sl, sh, sm, sh], axis=0),
    )


def rows_of(second):
    blank = jnp.zeros((16, second.shape[1]), F32)
    return jnp.concatenate([second, blank, second, blank], axis=0).T.astype(BF16)


def near_weights(first_rows, second, switches, index, halo):
    group = index // 4 * 16
    columns = jnp.concatenate([second, switches[group : group + 16, :]], axis=0)
    return gaussians(mm(first_rows[index * halo : (index + 1) * halo, :], columns)).astype(BF16)


def prepare(
    points, near_list, near_used, first_rows, first_cols, second_cols, second_rows, switches, place
):
    rows = points.shape[1]
    own = near_list.shape[1]
    width = rows // own
    place[...] = jnp.zeros(place.shape, F32)
    place[0:3, :] = points[...]
    leaf = iota((8, rows), 1) // width
    first, second = features(place[...], leaf, own // LAYER // 2)
    hot_leaf = iota((16, rows), 1) // width
    hot = jnp.where(hot_leaf % 16 == iota((16, rows), 0), 1.0, 0.0).astype(F32)
    first = jnp.concatenate([first, hot], axis=0)
    first_cols[...] = first.astype(BF16)
    second_cols[...] = second.astype(BF16)
    first_rows[...] = first.T.astype(BF16)
    second_rows[...] = rows_of(second)

    start_leaf = lax.axis_index(AXES) * own
    target = iota((1, own), 1)
    base_leaf = start_leaf + target // LAYER * LAYER - LAYER
    found = jnp.zeros((16, own), jnp.bool_)
    place_row = iota((16, own), 0)
    for n in range(near_list.shape[0]):
        spot = jnp.where(near_used[...] > n, near_list[n : n + 1, :] - base_leaf, -1)
        found = jnp.logical_or(found, place_row == spot)
    bias = jnp.where(found, 0.0, OFF).astype(F32)
    span = 3 * LAYER * width
    expand = jnp.where(iota((16, span), 0) == iota((16, span), 1) // width, 1.0, 0.0)
    switches[...] = mm(bias.T.astype(BF16), expand.astype(BF16)).astype(BF16)


def inner_layers(layers, vectors, first_rows, second_cols, switches, out, halo):
    for n, index in enumerate(layers):
        around = slice((index - 1) * halo, (index + 2) * halo)
        weights = near_weights(first_rows, second_cols[:, around], switches, index, halo)
        out[n * halo : (n + 1) * halo, :] = mm(weights, vectors[around, :]).astype(BF16)


def far_blocks(pairs, far_list, second_rows, first_cols, out, width, base, places):
    far, own = far_list.shape
    both = 2 * width
    start_leaf = lax.axis_index(AXES) * own
    square = iota((both, both), 0) // width == iota((both, both), 1) // width
    lane = iota((far * width, both), 1) < width
    exponents = []
    for index in pairs:
        t = 2 * index
        picked = []
        for m in range(2):
            spots = [
                pl.multiple_of((far_list[f, t + m] - start_leaf + base) * width, width)
                for f in range(far)
            ]
            picked.append(
                jnp.concatenate([second_rows[pl.ds(spot, width), :] for spot in spots], axis=0)
            )
        cols = first_cols[:, t * width : t * width + both]
        targets = jnp.where(
            square, jnp.concatenate([cols, cols], axis=0), jnp.zeros((both, both), BF16)
        )
        exponents.append(mm(jnp.where(lane, picked[0], picked[1]), targets))
    for place, exponent in zip(places, exponents):
        high, low = split2(gaussians(exponent))
        at = place * far * width
        out[at : at + far * width, 0:both] = high
        out[at : at + far * width, both : 2 * both] = low


def first_chunk_kernel(layers):
    def body(
        points, near_list, near_used, vectors,
        out, first_rows, first_cols, second_cols, second_rows, switches, place,
    ):
        prepare(
            points,
            near_list,
            near_used,
            first_rows,
            first_cols,
            second_cols,
            second_rows,
            switches,
            place,
        )
        halo = LAYER * points.shape[1] // near_list.shape[1]
        inner_layers(layers, vectors, first_rows, second_cols, switches, out, halo)

    return body


def chunk_kernel(layers, pairs, halo, width):
    def body(after, far_in, *refs):
        first_rows, second_cols, switches, vectors, first_cols, second_rows = refs[:6]
        outs, far_list, sem = refs[6:-2], refs[-2], refs[-1]
        if pairs:
            copy = pltpu.make_async_copy(far_in, far_list, sem)
            copy.start()
        if layers:
            inner_layers(layers, vectors, first_rows, second_cols, switches, outs[0], halo)
        if pairs:
            copy.wait()
            far_blocks(
                pairs, far_list, second_rows, first_cols, outs[-1], width, 0, range(len(pairs))
            )

    return body


def edges_kernel(
    pairs, after, far_in, inner, outer, first_rows, second_cols, switches, vectors,
    first_cols, own_rows, top,
    out, blocks, grams, ends, sides, place, halo_cols, far_list, second_rows, sems,
):
    halo = ends.shape[1]
    width = halo // LAYER
    own = vectors.shape[0] // width
    layers = own // LAYER
    extra = sides.shape[1]
    odd = lax.axis_index("sub") % 2
    arrived = ((inner, 1 - odd), (outer, odd))
    side_copies = [
        pltpu.make_async_copy(
            block.at[pl.ds(halo, extra), :], sides.at[side], sems.at[n]
        )
        for n, (block, side) in enumerate(arrived)
    ]
    end_copies = [
        pltpu.make_async_copy(block.at[pl.ds(0, halo), :], ends.at[side], sems.at[2 + n])
        for n, (block, side) in enumerate(arrived)
    ]
    list_copy = pltpu.make_async_copy(far_in, far_list, sems.at[4])
    for copy in side_copies + end_copies + [list_copy]:
        copy.start()
    lanes = PAD * width
    second_rows[lanes : lanes + own * width, :] = own_rows[...]
    place[...] = jnp.zeros(place.shape, F32)
    for copy in side_copies:
        copy.wait()
    for side, first_leaf in enumerate((-PAD, own)):
        for n in range(2):
            base = width + 16 * n
            values = sides[side, base : base + 16, 0:halo].astype(F32)
            place[0:3, n * halo : (n + 1) * halo] = values[0:3, :] + values[8:11, :]
        leaf = iota((8, lanes), 1) // width + (first_leaf + PAD)
        second = features(place[...], leaf, layers // 2 + PAD // LAYER)[1]
        halo_cols[side, :, :] = second.astype(BF16)
        at = (PAD + first_leaf) * width
        second_rows[at : at + lanes, :] = rows_of(second)
        for n in range(6):
            piece = sides[side, 0:width, n * width : (n + 1) * width]
            at = (6 * side + n) * STRIDE
            grams[at : at + width // 2, :] = fold(mm_nt(piece, piece))
    for n in range(12, 16):
        grams[n * STRIDE : n * STRIDE + width // 2, :] = top[...]
    weights = [
        near_weights(
            first_rows, jnp.concatenate(columns, axis=1), switches, index, halo
        )
        for index, columns in (
            (0, [halo_cols[0, :, halo:], second_cols[:, 0 : 2 * halo]]),
            (layers - 1, [second_cols[:, (layers - 2) * halo :], halo_cols[1, :, 0:halo]]),
        )
    ]
    for copy in end_copies:
        copy.wait()
    value = mm(weights[0][:, 0:halo], ends[0, :, :])
    value = value + mm(weights[0][:, halo:], vectors[0 : 2 * halo, :])
    out[0:halo, :] = value.astype(BF16)
    value = mm(weights[1][:, 0 : 2 * halo], vectors[(layers - 2) * halo :, :])
    value = value + mm(weights[1][:, 2 * halo :], ends[1, :, :])
    out[halo:, :] = value.astype(BF16)
    list_copy.wait()
    far_blocks(pairs, far_list, second_rows, first_cols, blocks, width, PAD, range(len(pairs)))


def own_chunk_kernel(layers, pairs):
    def body(
        after, far_in, first_rows, second_cols, switches, vectors, first_cols, second_rows, basis,
        out, blocks, grams, far_list, sem,
    ):
        copy = pltpu.make_async_copy(far_in, far_list, sem)
        copy.start()
        width = basis.shape[0]
        own = basis.shape[1] // width
        both = 2 * width
        inner_layers(layers, vectors, first_rows, second_cols, switches, out, LAYER * width)
        lane = iota((width, both), 1)
        for n in range(own // 2):
            pair = basis[:, n * both : (n + 1) * both]
            zero = jnp.zeros_like(pair)
            stacked = jnp.concatenate(
                [jnp.where(lane < width, pair, zero), jnp.where(lane < width, zero, pair)], axis=0
            )
            value = mm_nt(stacked, pair)
            for m in range(2):
                at = (2 * n + m) * STRIDE
                grams[at : at + width // 2, :] = fold(value[m * width : (m + 1) * width])

        copy.wait()
        far_blocks(pairs, far_list, second_rows, first_cols, blocks, width, 0, range(len(pairs)))

    return body


def leaves_kernel(chunks, members, groups, *refs):
    outer_count = len(chunks) + 1
    near_parts = refs[:outer_count]
    (
        own_grams,
        halo_grams,
        upper,
        transfer,
        near,
        high,
        low,
        device_factor,
        group_factor,
        root_factor,
        work,
        factors,
        sems,
    ) = refs[outer_count:]
    width = transfer.shape[0]
    total = high.shape[0] // width
    own = total - 2 * PAD
    halo = LAYER * width
    layers = own // LAYER
    both = 2 * width
    places = [(part, 0, chunk[0], len(chunk)) for part, chunk in zip(near_parts, chunks)]
    places += [(near_parts[-1], n, index, 1) for n, index in enumerate((0, layers - 1))]
    near_copies = [
        pltpu.make_async_copy(
            part.at[pl.ds(start * halo, many * halo), :],
            near.at[pl.ds(index * halo, many * halo), :],
            sems.at[n],
        )
        for n, (part, start, index, many) in enumerate(places)
    ]
    for copy in near_copies:
        copy.start()

    spare = (own + 13, own + 14)
    means = (
        upper[0 : width // 2, :] * (1.0 / members),
        upper[width // 2 :, :] * (1.0 / (members * groups)),
    )
    spot_row = iota((2 * PAD, both), 0)
    for i in range(width // 2):
        rows = halo_grams[pl.ds(i, 2 * PAD, stride=STRIDE), :]
        for spot, mean in zip(spare, means):
            rows = jnp.where(spot_row == spot - own, mean[i : i + 1, :], rows)
        turned = jnp.concatenate([own_grams[pl.ds(i, own, stride=STRIDE), :], rows], axis=0).T
        work[i, :, 0:total] = turned[0:width]
        work[i + width // 2, :, 0:total] = turned[width:]
    factor_lanes(work, width)
    from_lanes(work, factors, width, total)
    at = (own + 12) * STRIDE
    device_factor[...] = exact(unfold(factors[at : at + width // 2, :]), transfer[...])
    for target, spot in zip((group_factor, root_factor), spare):
        target[...] = unfold(factors[spot * STRIDE : spot * STRIDE + width // 2, :])
    left_lanes = iota((width // 2, both), 1) < width
    spots = [(PAD + t, t) for t in range(own)]
    spots += [(spot, own + n) for n, spot in enumerate((1, 2, 3, 5, 6, 7))]
    spots += [(PAD + own + m, own + 6 + n) for n, m in enumerate((0, 1, 2, 4, 5, 6))]
    for spot, n in spots:
        rows = factors[n * STRIDE : n * STRIDE + width // 2, :]
        turned = pltpu.roll(rows, width, 1)
        twice = jnp.concatenate(
            [jnp.where(left_lanes, rows, turned), jnp.where(left_lanes, turned, rows)], axis=0
        )
        at = slice(spot * width, (spot + 1) * width)
        high[at, :], low[at, :] = split2(twice)
    for copy in near_copies:
        copy.wait()


def far_kernel(plan, far_in, high, low, *refs):
    blocks, (coupling, far_list, lines, sem, sems) = refs[:-5], refs[-5:]
    copy = pltpu.make_async_copy(far_in, far_list, sem)
    copy.start()
    width = coupling.shape[0]
    far, own = far_list.shape
    both = 2 * width
    start_leaf = lax.axis_index(AXES) * own
    square = iota((both, both), 0) // width == iota((both, both), 1) // width
    lane = iota((width, both), 1) < width
    zero = jnp.zeros((both, both), BF16)

    def diagonal(value):
        return jnp.where(square, value, zero)

    copies = []
    for start in range(0, own // 2, 4):
        indices = range(start, start + 4)
        halves = []
        for index in indices:
            source, place = plan[index]
            at = place * far * width
            kh = blocks[source][at : at + far * width, 0:both]
            kl = blocks[source][at : at + far * width, both : 2 * both]
            at = (PAD + 2 * index) * width
            rh = diagonal(high[at : at + both, :])
            rl = diagonal(low[at : at + both, :])
            halves.append(
                mm_nt(
                    jnp.concatenate([kh, kl, kh], axis=1), jnp.concatenate([rh, rh, rl], axis=1)
                )
            )
        if start == 0:
            copy.wait()
        outs = []
        for index, half in zip(indices, halves):
            zh, zl = split2(half * (1.0 / width))
            for f in range(far):
                spots = [
                    pl.multiple_of((far_list[f, 2 * index + m] - start_leaf + PAD) * width, width)
                    for m in range(2)
                ]
                sh, sl = (
                    jnp.where(lane, *(part[pl.ds(spot, width), :] for spot in spots))
                    for part in (high, low)
                )
                a = slice(f * width, (f + 1) * width)
                ph = diagonal(jnp.concatenate([zh[a], zh[a]], axis=0))
                plow = diagonal(jnp.concatenate([zl[a], zl[a]], axis=0))
                outs.append(
                    mm(
                        jnp.concatenate([sh, sh, sl], axis=1),
                        jnp.concatenate([ph, plow, ph], axis=0),
                    )
                )
        for n, index in enumerate(indices):
            three = outs[n * far : (n + 1) * far]
            line = jnp.concatenate(
                [out[:, 0:width] for out in three] + [out[:, width:both] for out in three], axis=1
            )
            at = index * 2 * far * width
            lines[:, at : at + 2 * far * width] = line.astype(BF16)
        group = pl.ds(start * 2 * far * width, 8 * far * width)
        copies.append(
            pltpu.make_async_copy(lines.at[:, group], coupling.at[:, group], sems.at[start // 4])
        )
        copies[-1].start()
    for copy in copies:
        copy.wait()


def swap_inner(block):
    return lax.ppermute(block, AXES, [(i, i ^ 1) for i in range(lax.axis_size(AXES))])


def swap_outer(block):
    many = lax.axis_size(AXES)
    return lax.ppermute(block, AXES, [(i, (i + 1 if i % 2 else i - 1) % many) for i in range(many)])


def exchange(value, distance):
    pairs = [(i, i ^ distance ^ 1) for i in range(lax.axis_size(AXES))]
    return value + lax.ppermute(value, AXES, pairs)


def per_device(
    points, leaf_basis, inner_transfer, device_transfer, vectors, near_index, near_count, far_index
):
    own = near_index.shape[0]
    width = leaf_basis.shape[1]
    columns = vectors.shape[1]
    halo = LAYER * width
    half = width // 2
    layers = own // LAYER
    total = own + 2 * PAD
    members, groups = lax.axis_size("sub"), lax.axis_size("group")
    vmem = pl.BlockSpec(memory_space=pltpu.VMEM)
    hbm = pl.BlockSpec(memory_space=pl.ANY)
    square = jax.ShapeDtypeStruct((width, width), F32)
    extra = halo + width + 32

    def block_of(rows):
        return jax.ShapeDtypeStruct((rows, columns), BF16)

    basis = leaf_basis.T
    near_list, far_list = near_index.T, far_index.T
    cost = pl.CostEstimate(flops=10**9, bytes_accessed=4 * 10**6, transcendentals=10**6)

    dense, top, to_outer, to_inner = pl.pallas_call(
        tree_kernel,
        out_shape=(
            jax.ShapeDtypeStruct((half, 2 * width), F32),
            jax.ShapeDtypeStruct((half, 2 * width), F32),
            block_of(extra),
            block_of(extra + half),
        ),
        in_specs=[hbm] * 5,
        out_specs=(hbm,) * 4,
        scratch_shapes=[
            pltpu.VMEM((3, own * width), F32),
            pltpu.VMEM((width, own * width), BF16),
            pltpu.VMEM((width, (own - 2) * width), BF16),
            pltpu.VMEM((width, width), F32),
            pltpu.VMEM((2, halo, columns), BF16),
            pltpu.VMEM((2, width + 32, columns), BF16),
            pltpu.VMEM((half, columns), BF16),
            pltpu.VMEM((2, half, 2 * width), F32),
            pltpu.SemaphoreType.DMA((13,)),
        ],
        compiler_params=room(60),
        name="tree",
    )(points, basis, inner_transfer.T, device_transfer, vectors)
    from_inner = swap_inner(to_inner)

    sub_bits = members.bit_length() - 1
    steps = [members << bit for bit in range(groups.bit_length() - 1)]
    steps += [1 << bit for bit in range(1, sub_bits)]
    inner_pairs = list(range(PAD // 2, (own - PAD) // 2))
    few = len(inner_pairs) // 2
    edge_pairs = [index for index in range(own // 2) if index not in inner_pairs]
    chunks = [[1, 2], [3], [4, 5], [6]]
    pair_chunks = [[], [], inner_pairs[:few], inner_pairs[few:]]
    blocks, plan, parts = [], {}, []

    def part_shape(count):
        return jax.ShapeDtypeStruct((count * halo, columns), BF16)

    def block_shape(count):
        return jax.ShapeDtypeStruct((count * far_index.shape[1] * width, 4 * width), BF16)

    late_points, dense = lax.optimization_barrier((points, dense))
    part, *shared = pl.pallas_call(
        first_chunk_kernel(chunks[0]),
        out_shape=(
            part_shape(len(chunks[0])),
            jax.ShapeDtypeStruct((own * width, 64), BF16),
            jax.ShapeDtypeStruct((64, own * width), BF16),
            jax.ShapeDtypeStruct((48, own * width), BF16),
            jax.ShapeDtypeStruct((own * width, 128), BF16),
            jax.ShapeDtypeStruct((own, 3 * halo), BF16),
        ),
        in_specs=[vmem] * 4,
        out_specs=(vmem,) * 6,
        scratch_shapes=[pltpu.VMEM((8, own * width), F32)],
        compiler_params=room(10),
        cost_estimate=cost,
        name="chunk_0",
    )(late_points, near_list, near_count.reshape(1, own), vectors)
    parts.append(part)
    summands = [
        from_inner[extra:, n * 2 * width : (n + 1) * 2 * width].astype(F32) for n in range(3)
    ]
    pair_gram = gram = dense + (summands[0] + (summands[1] + summands[2]))
    gram, parts[0], to_outer = lax.optimization_barrier((gram, parts[0], to_outer))
    from_outer = swap_outer(to_outer)
    first_rows, first_cols, second_cols, second_rows, switches = shared
    jobs = [1, 2, 3, "edges"]
    for n in range(max(len(steps), len(jobs))):
        if n < len(jobs) and jobs[n] == "edges":
            gram, from_outer = lax.optimization_barrier((gram, from_outer))
        before = gram
        if n < len(steps):
            if n == len(steps) - sub_bits + 1:
                gram = before = jnp.concatenate([pair_gram, gram], axis=0)
            gram = exchange(gram, steps[n])
        job = jobs[n] if n < len(jobs) else None
        if job in (1, 2):
            layer_chunk, pair_chunk = chunks[job], pair_chunks[job]
            shapes = [part_shape(len(layer_chunk))] * bool(layer_chunk)
            shapes += [block_shape(len(pair_chunk))] * bool(pair_chunk)
            outs = pl.pallas_call(
                chunk_kernel(layer_chunk, pair_chunk, halo, width),
                out_shape=tuple(shapes),
                in_specs=[hbm] * 2 + [vmem] * 6,
                out_specs=(vmem,) * len(shapes),
                scratch_shapes=[
                    pltpu.SMEM(far_list.shape, jnp.int32),
                    pltpu.SemaphoreType.DMA,
                ],
                compiler_params=room(10),
                cost_estimate=cost,
                name=f"chunk_{job}",
            )(before, far_list, first_rows, second_cols, switches, vectors, first_cols, second_rows)
            gram, outs = lax.optimization_barrier((gram, outs))
            if layer_chunk:
                parts.append(outs[0])
            if pair_chunk:
                plan.update((index, (len(blocks), m)) for m, index in enumerate(pair_chunk))
                blocks.append(outs[-1])
        elif job == 3:
            part, own_blocks, own_grams = pl.pallas_call(
                own_chunk_kernel(chunks[3], pair_chunks[3]),
                out_shape=(
                    part_shape(len(chunks[3])),
                    block_shape(len(pair_chunks[3])),
                    jax.ShapeDtypeStruct(((own + 1) * STRIDE, 2 * width), F32),
                ),
                in_specs=[hbm] * 2 + [vmem] * 7,
                out_specs=(vmem,) * 3,
                scratch_shapes=[
                    pltpu.SMEM(far_list.shape, jnp.int32),
                    pltpu.SemaphoreType.DMA,
                ],
                compiler_params=room(10),
                cost_estimate=cost,
                name="chunk_3",
            )(
                before,
                far_list,
                first_rows,
                second_cols,
                switches,
                vectors,
                first_cols,
                second_rows,
                basis,
            )
            gram, part = lax.optimization_barrier((gram, part))
            parts.append(part)
            plan.update((index, (len(blocks), m)) for m, index in enumerate(pair_chunks[3]))
            blocks.append(own_blocks)
        elif job == "edges":
            edge_part, edge_blocks, halo_grams = pl.pallas_call(
                functools.partial(edges_kernel, edge_pairs),
                out_shape=(
                    part_shape(2),
                    block_shape(len(edge_pairs)),
                    jax.ShapeDtypeStruct(((2 * PAD + 1) * STRIDE, 2 * width), F32),
                ),
                in_specs=[hbm] * 4 + [vmem] * 7,
                out_specs=(vmem,) * 3,
                scratch_shapes=[
                    pltpu.VMEM((2, halo, columns), BF16),
                    pltpu.VMEM((2, width + 32, columns), BF16),
                    pltpu.VMEM((8, PAD * width), F32),
                    pltpu.VMEM((2, 48, PAD * width), BF16),
                    pltpu.SMEM(far_list.shape, jnp.int32),
                    pltpu.VMEM((total * width, 2 * width), BF16),
                    pltpu.SemaphoreType.DMA((5,)),
                ],
                compiler_params=room(14),
                cost_estimate=cost,
                name="edges",
            )(
                before,
                far_list,
                from_inner,
                from_outer,
                first_rows,
                second_cols,
                switches,
                vectors,
                first_cols,
                second_rows,
                top,
            )
            gram, edge_part = lax.optimization_barrier((gram, edge_part))
            plan.update((index, (len(blocks), m)) for m, index in enumerate(edge_pairs))
            blocks.append(edge_blocks)

    split_factors = jax.ShapeDtypeStruct((total * width, 2 * width), BF16)
    near, high, low, device_factor, group_factor, root_factor = pl.pallas_call(
        functools.partial(leaves_kernel, chunks, members, groups),
        out_shape=(
            jax.ShapeDtypeStruct(vectors.shape, BF16),
            split_factors,
            split_factors,
            square,
            square,
            square,
        ),
        in_specs=[hbm] * (len(parts) + 1) + [vmem] * 4,
        out_specs=(hbm,) + (vmem,) * 5,
        scratch_shapes=[
            pltpu.VMEM((width, width, 128), F32),
            pltpu.VMEM(((total + 1) * STRIDE, 2 * width), F32),
            pltpu.SemaphoreType.DMA((2 + len(parts),)),
        ],
        compiler_params=room(20),
        name="leaves",
    )(*parts, edge_part, own_grams, halo_grams, gram, device_transfer)

    coupling = pl.pallas_call(
        functools.partial(far_kernel, plan),
        out_shape=jax.ShapeDtypeStruct((width, own * far_index.shape[1] * width), BF16),
        in_specs=[hbm] + [vmem] * (2 + len(blocks)),
        out_specs=hbm,
        scratch_shapes=[
            pltpu.SMEM(far_list.shape, jnp.int32),
            pltpu.VMEM((width, own * far_index.shape[1] * width), BF16),
            pltpu.SemaphoreType.DMA,
            pltpu.SemaphoreType.DMA((own // 8,)),
        ],
        compiler_params=room(16),
        name="far",
    )(far_list, high, low, *blocks)
    return near, coupling.T, device_factor, group_factor, root_factor


def solution(mesh):
    split = P(AXES, None)
    return jax.shard_map(
        per_device,
        mesh=mesh,
        in_specs=(P(None, AXES), split, split, split, split, split, P(AXES), split),
        out_specs=(split, split, split, split, split),
        check_vma=False,
    )
```
